32 devices in a mesh: group: 2 (over x), row: 16 (over z, y, core).
Axes of the slice: x: 2, y: 2, z: 4, core: 2. Of those that a mesh axis runs over, the one named last changes fastest.
Arguments:
- voxels: bfloat16 [128, 4, 8, 768], P(('group', 'row')), parts along dimension 0, may hold values from -6 to 6
- dw_kernel: float32 [343, 768], replicated, may hold values from -0.3125 to 0.3125
- norm_gain: float32 [768], replicated, may hold values from 0.25 to 1.75
- norm_bias: float32 [768], replicated, may hold values from -3 to 3
- weight_in: bfloat16 [3072, 768], replicated, may hold values from -0.21875 to 0.21875
- weight_out: bfloat16 [3072, 768], replicated, may hold values from -0.109375 to 0.109375
- layer_scale: float32 [768], replicated, may hold values from 0.3 to 1
- cotangent: bfloat16 [128, 4, 8, 768], P(('group', 'row')), parts along dimension 0, may hold values from -6 to 6
Outputs:
- block_out: bfloat16 [128, 4, 8, 768], P(('group', 'row')), parts along dimension 0
- voxel_grad: bfloat16 [128, 4, 8, 768], P(('group', 'row')), parts along dimension 0
- kernel_grad: float32 [686, 768], P('group'), parts along dimension 0
- gain_grad: float32 [1536], P('group'), parts along dimension 0
- bias_grad: float32 [1536], P('group'), parts along dimension 0
- scale_grad: float32 [1536], P('group'), parts along dimension 0
- weight_in_grad: float32 [6144, 768], P(('group', 'row')), parts along dimension 0
- weight_out_grad: float32 [6144, 768], P(('group', 'row')), parts along dimension 0
The draws below stay inside these ranges and needn't reach their ends.
There are 2 independent parts, one for each index of `group`. The reference program is written for one: setup_inputs(seed, part) draws one part's arguments, and reference() takes and returns one part's arrays. A program takes and returns all parts, laid end to end along the dimension named above; an argument that names none is the same for every part. Nothing has to cross between parts.
All inputs are finite; a program needn't handle non-finite values.
Results may differ from the reference program's by a relative error of at most 0.0064.
Values may be sent and summed in bfloat16 or wider, within the bound.
No kernel may reach another device: no remote copies, remote signals or barrier semaphores. Data moves between devices by JAX's collectives and lax.ppermute only.
A program may use at most 128 MiB of HBM per device.

```python
import math
import jax
import jax.numpy as jnp
from jax import lax

C = 768
FF = 3072
KS = 7
SY = 4
SZ = 8
NX = 64


def level_of(rng, shape, pieces, smallest, largest):
    factor_of = 1.0
    for position, shards_of in pieces:
        heights = jax.random.uniform(jax.random.fold_in(jax.random.fold_in(rng, 6), position), (shards_of,), jnp.float32, smallest / len(pieces), largest / len(pieces))
        factor_of = factor_of * jnp.repeat(jnp.exp(heights), shape[position] // shards_of).reshape((-1,) + (1,) * (len(shape) - 1 - position))
    return factor_of


def gaussian(key, extent, scale, bound, split=(), held_as=jnp.bfloat16):
    drawn = jax.random.normal(key, extent, jnp.float32) * scale
    if len(split) > 0:
        drawn = level_of(key, extent, split, -0.22, 0.18) * drawn
    return jnp.clip(drawn, min=-bound, max=bound).astype(held_as)


def setup_inputs(seed: int = 0, part: int = 0) -> dict:
    arg_keys = jax.random.split(jax.random.key(seed), 9)
    part_keys = jax.random.split(jax.random.fold_in(arg_keys[8], part), 9)
    return {
        "voxels": gaussian(part_keys[0], (NX, SY, SZ, C), 1.0, 6.0, ((0, 16),)),
        "dw_kernel": gaussian(arg_keys[1], (KS * KS * KS, C), (KS * KS * KS) ** -0.5, 0.3125, (), jnp.float32),
        "norm_gain": jnp.clip(1.0 + 0.15 * jax.random.normal(arg_keys[2], (C,), jnp.float32), 0.25, 1.75),
        "norm_bias": gaussian(arg_keys[3], (C,), 0.5, 3.0, (), jnp.float32),
        "weight_in": gaussian(arg_keys[4], (FF, C), C ** -0.5, 0.21875),
        "weight_out": gaussian(arg_keys[5], (FF, C), FF ** -0.5, 0.109375),
        "layer_scale": jnp.clip(jnp.exp(jax.random.uniform(arg_keys[6], (C,), jnp.float32, math.log(0.3), math.log(1.0))), 0.3, 1.0),
        "cotangent": gaussian(part_keys[7], (NX, SY, SZ, C), 1.0, 6.0, ((0, 16),)),
    }


root_half = 0.7071067811865476
inv_root_tau = 0.3989422804014327
norm_eps = 1e-06

def gelu_value(values):
    return 0.5 * values * (1.0 + lax.erf(values * root_half))

def gelu_slope(values):
    return 0.5 * (1.0 + lax.erf(values * root_half)) + values * jnp.exp(-0.5 * values * values) * inv_root_tau

def depthwise_apply(padded, kernel, window_shape, flipped):
    planes = window_shape[0]
    height = window_shape[1]
    breadth = window_shape[2]

    def advance(along_x, running):
        along_x = along_x.astype(jnp.int32)
        start_x = KS - 1 - along_x if flipped else along_x
        slab = lax.dynamic_slice_in_dim(padded, start_x, planes, 0).astype(jnp.float32)
        taps = lax.dynamic_slice_in_dim(kernel, along_x * (KS * KS), KS * KS, 0)
        for along_y in range(KS):
            for along_z in range(KS):
                start_y = KS - 1 - along_y if flipped else along_y
                start_z = KS - 1 - along_z if flipped else along_z
                window = slab[:, start_y:start_y + height, start_z:start_z + breadth, :]
                running = running + window * taps[along_y * KS + along_z]
        return running
    return lax.fori_loop(0, KS, advance, jnp.zeros(window_shape, jnp.float32))

def kernel_terms(padded, grads, window_shape):
    planes = window_shape[0]
    height = window_shape[1]
    breadth = window_shape[2]
    grads_wide = grads.astype(jnp.float32)

    def one_plane(along_x):
        slab = lax.dynamic_slice_in_dim(padded, along_x, planes, 0).astype(jnp.float32)
        rows_out = []
        for along_y in range(KS):
            for along_z in range(KS):
                window = slab[:, along_y:along_y + height, along_z:along_z + breadth, :]
                rows_out.append(lax.optimization_barrier(jnp.sum(window * grads_wide, axis=(0, 1, 2))))
        return jnp.stack(rows_out)
    stacked = lax.map(one_plane, jnp.arange(KS, dtype=jnp.int32))
    return stacked.reshape(KS * KS * KS, grads.shape[3])

def reference(voxels, dw_kernel, norm_gain, norm_bias, weight_in, weight_out, layer_scale, cotangent):
    margin = KS // 2
    window_shape = voxels.shape
    channels = voxels.shape[3]
    padded = jnp.pad(voxels, ((margin, margin), (margin, margin), (margin, margin), (0, 0)))
    convolved = depthwise_apply(padded, dw_kernel, window_shape, False).reshape(-1, channels)
    average = lax.optimization_barrier(jnp.mean(convolved, axis=-1, keepdims=True))
    centered = convolved - average
    variance = lax.optimization_barrier(jnp.mean(centered * centered, axis=-1, keepdims=True))
    inverse_std = lax.rsqrt(variance + norm_eps)
    unit = centered * inverse_std
    normed = (unit * norm_gain + norm_bias).astype(jnp.bfloat16)
    hidden = jnp.dot(normed, weight_in.T, preferred_element_type=jnp.float32)
    activated = gelu_value(hidden).astype(jnp.bfloat16)
    mixed = jnp.dot(activated, weight_out, preferred_element_type=jnp.float32)
    block_out = (voxels.reshape(-1, channels).astype(jnp.float32) + layer_scale * mixed).astype(jnp.bfloat16)
    upstream = cotangent.reshape(-1, channels).astype(jnp.float32)
    scale_grad = lax.optimization_barrier(jnp.sum(upstream * mixed, axis=0))
    mixed_grad = (layer_scale * upstream).astype(jnp.bfloat16)
    weight_out_grad = jnp.dot(activated.T, mixed_grad, preferred_element_type=jnp.float32)
    activated_grad = jnp.dot(mixed_grad, weight_out.T, preferred_element_type=jnp.float32)
    hidden_grad = (activated_grad * gelu_slope(hidden)).astype(jnp.bfloat16)
    weight_in_grad = jnp.dot(hidden_grad.T, normed, preferred_element_type=jnp.float32)
    normed_grad = jnp.dot(hidden_grad, weight_in, preferred_element_type=jnp.float32)
    bias_grad = lax.optimization_barrier(jnp.sum(normed_grad, axis=0))
    gain_grad = lax.optimization_barrier(jnp.sum(normed_grad * unit, axis=0))
    scaled = normed_grad * norm_gain
    convolved_grad = inverse_std * (scaled - lax.optimization_barrier(jnp.mean(scaled, axis=-1, keepdims=True)) - unit * lax.optimization_barrier(jnp.mean(scaled * unit, axis=-1, keepdims=True)))
    convolved_grad = convolved_grad.astype(jnp.bfloat16).reshape(window_shape)
    kernel_grad = kernel_terms(padded, convolved_grad, window_shape)
    grad_padded = jnp.pad(convolved_grad, ((margin, margin), (margin, margin), (margin, margin), (0, 0)))
    back_conv = depthwise_apply(grad_padded, dw_kernel, window_shape, True)
    voxel_grad = (cotangent.astype(jnp.float32) + back_conv).astype(jnp.bfloat16)
    return (block_out.reshape(window_shape), voxel_grad, kernel_grad, gain_grad, bias_grad, scale_grad, weight_in_grad, weight_out_grad)
```

```python
import functools

import jax
import jax.numpy as jnp
from jax import lax
from jax.experimental import pallas as pl
from jax.experimental.pallas import tpu as pltpu
from jax.sharding import PartitionSpec as P

KS = 7
MARGIN = KS // 2
LANES = 128
SUB = 8
PAD = 3 * SUB
TAP_ROWS = KS * KS * KS

root_half = 0.7071067811865476
inv_root_tau = 0.3989422804014327
norm_eps = 1e-06

F32 = jnp.float32
BF16 = jnp.bfloat16


def split_source(v):
    terms = []
    for a, b in ((v[0] + v[2], v[1] + v[3]), (v[2], v[3]), (v[0], v[1])):
        terms += [a + b, b, a]
    return terms


def split_taps(t):
    terms = []
    for s in (
        (t[2], t[3], t[4]),
        (t[4] - t[2], t[5] - t[3], t[6] - t[4]),
        (t[0] - t[2], t[1] - t[3], t[2] - t[4]),
    ):
        terms += [s[1], s[2] - s[1], s[0] - s[1]]
    return terms


def split_grads(g):
    terms = []
    for a, b in ((g[0] + g[2], g[1] + g[3]), (g[0], g[1]), (g[2], g[3])):
        terms += [a + b, a, b]
    return terms


def join_outputs(m):
    pair = [(m[3 * k] + m[3 * k + 1], m[3 * k] + m[3 * k + 2]) for k in range(3)]
    return [
        pair[0][0] + pair[1][0],
        pair[0][1] + pair[1][1],
        pair[0][0] + pair[2][0],
        pair[0][1] + pair[2][1],
    ]


def join_taps(m):
    p, q, r = [
        (m[3 * k + 2], m[3 * k] - m[3 * k + 1] - m[3 * k + 2], m[3 * k + 1]) for k in range(3)
    ]
    return [
        r[0],
        r[1],
        p[0] - q[0] - r[0] + r[2],
        p[1] - q[1] - r[1],
        p[2] - q[2] - r[2] + q[0],
        q[1],
        q[2],
    ]


def tree_sum(terms):
    while len(terms) > 1:
        terms = [
            terms[k] + terms[k + 1] if k + 1 < len(terms) else terms[k]
            for k in range(0, len(terms), 2)
        ]
    return terms[0]


def stage_source(blocks, height, spread):
    row = height * SUB
    at = 0
    for block in blocks:
        for x in range(block.shape[0] // row):
            plane = block[x * row : (x + 1) * row, :].astype(F32)
            lines = [plane[y * SUB : (y + 1) * SUB, :] for y in range(height)]
            for j, term in enumerate(split_source(lines)):
                spread[j, at, SUB : 2 * SUB, :] = term
            at += 1


def clear_rims(spread):
    zeros = jnp.zeros(spread.shape[:2] + (SUB, LANES), F32)
    spread[:, :, :SUB, :] = zeros
    spread[:, :, 2 * SUB :, :] = zeros


def stage_taps(taps, flipped, split):
    for dx in range(KS):
        rows = []
        for dy in range(KS):
            first = dx * KS * KS + dy * KS
            if first + SUB <= TAP_ROWS:
                rows.append(taps[first : first + SUB, :])
            else:
                rows.append(pltpu.roll(taps[TAP_ROWS - SUB : TAP_ROWS, :], SUB - 1, 0))
        if flipped:
            rows = rows[::-1]
        for j, term in enumerate(split_taps(rows)):
            split[j, KS - 1 - dx if flipped else dx] = term


def convolve(spread, split, planes, flipped):
    terms = []
    for j in range(9):
        sums = [None] * planes
        for dz in range(KS):
            first = SUB - MARGIN + dz
            source = [
                spread[j, x, first : first + SUB, :] for x in range(planes + KS - 1)
            ]
            at = KS - 1 - dz if flipped else dz
            weights = [
                jnp.broadcast_to(split[j, dx, at : at + 1, :], (SUB, LANES)) for dx in range(KS)
            ]
            for x in range(planes):
                part = tree_sum([source[x + dx] * weights[dx] for dx in range(KS)])
                sums[x] = part if sums[x] is None else sums[x] + part
        terms.append(sums)
    return [join_outputs([terms[j][x] for j in range(9)]) for x in range(planes)]


def forward_kernel(
    planes, height, left, own, right, taps, gain, bias, normed, unit, inv, spread, split, conv
):
    step = pl.program_id(0)

    @pl.when(step == 0)
    def _():
        clear_rims(spread)

    stage_source((left, own, right), height, spread)
    stage_taps(taps, False, split)
    rows = convolve(spread, split, planes, False)
    for x in range(planes):
        for y in range(height):
            at = (x * height + y) * SUB
            conv[step, at : at + SUB, :] = rows[x][y]

    @pl.when(step == pl.num_programs(0) - 1)
    def _():
        tiles = conv.shape[0]
        channels = tiles * LANES
        parts = [conv[k] for k in range(tiles)]
        average = jnp.sum(tree_sum(parts), axis=1, keepdims=True) * (1.0 / channels)
        parts = [part - average for part in parts]
        variance = jnp.sum(
            tree_sum([part * part for part in parts]), axis=1, keepdims=True
        ) * (1.0 / channels)
        inverse = lax.rsqrt(variance + norm_eps)
        inv[...] = jnp.broadcast_to(inverse, inv.shape)
        for k in range(tiles):
            lanes = slice(k * LANES, (k + 1) * LANES)
            value = parts[k] * inverse
            unit[:, lanes] = value
            normed[:, lanes] = (value * gain[:, lanes] + bias[:, lanes]).astype(BF16)


def input_grad_kernel(planes, height, left, own, right, taps, cotangent, out, spread, split):
    @pl.when(pl.program_id(0) == 0)
    def _():
        clear_rims(spread)

    stage_source((left, own, right), height, spread)
    stage_taps(taps, True, split)
    rows = convolve(spread, split, planes, True)
    for x in range(planes):
        at = x * height * SUB
        whole = jnp.concatenate(rows[x], axis=0)
        upstream = cotangent[at : at + height * SUB, :].astype(F32)
        out[at : at + height * SUB, :] = (upstream + whole).astype(BF16)


def kernel_grad_kernel(
    planes, height, left, own, right, grads, small, out, spread, products, joined, flat
):
    @pl.when(pl.program_id(0) == 0)
    def _():
        clear_rims(spread)
        products[...] = jnp.zeros(products.shape, F32)
        flat[...] = jnp.zeros(flat.shape, F32)

    stage_source((left, own, right), height, spread)
    upstream = []
    for x in range(planes):
        plane = grads[x * height * SUB : (x + 1) * height * SUB, :].astype(F32)
        upstream.append(
            split_grads([plane[y * SUB : (y + 1) * SUB, :] for y in range(height)])
        )
    for j in range(9):
        for dz in range(KS):
            first = SUB - MARGIN + dz
            source = [
                spread[j, x, first : first + SUB, :] for x in range(planes + KS - 1)
            ]
            for dx in range(KS):
                products[j % 2, dx, dz * SUB : (dz + 1) * SUB, :] = tree_sum(
                    [source[x + dx] * upstream[x][j] for x in range(planes)]
                )
        for dx in range(KS):
            joined[j, dx] = tree_sum(
                [products[j % 2, dx, pl.ds(s, SUB, stride=SUB), :] for s in range(SUB)]
            )
    for dx in range(KS):
        for dy, tile in enumerate(join_taps([joined[j, dx] for j in range(9)])):
            first = dx * KS * KS + dy * KS
            flat[first : first + SUB, :] = tile
    flat[TAP_ROWS : TAP_ROWS + SUB, :] = small[...]
    out[...] = flat[...].astype(out.dtype)


def mlp_kernel(
    normed,
    mixed_grad,
    weight_in,
    weight_out,
    unit,
    inv,
    gain,
    scale,
    voxels,
    cotangent,
    act_out,
    hid_out,
    block_out,
    conv_grad,
    small,
    mixed,
    back,
):
    step = pl.program_id(0)
    hidden = lax.dot_general(
        normed[...], weight_in[...], (((1,), (1,)), ((), ())), preferred_element_type=F32
    )
    act_grad = lax.dot_general(
        mixed_grad[...], weight_out[...], (((1,), (1,)), ((), ())), preferred_element_type=F32
    )
    cover = 0.5 * (1.0 + lax.erf(hidden * root_half))
    activated = (hidden * cover).astype(BF16)
    slope = cover + hidden * jnp.exp(-0.5 * hidden * hidden) * inv_root_tau
    hidden_grad = (act_grad * slope).astype(BF16)
    act_out[...] = activated.T
    hid_out[...] = hidden_grad.T
    forward = jnp.dot(activated, weight_out[...], preferred_element_type=F32)
    backward = jnp.dot(hidden_grad, weight_in[...], preferred_element_type=F32)

    @pl.when(step == 0)
    def _():
        mixed[...] = forward
        back[...] = backward

    @pl.when(step > 0)
    def _():
        mixed[...] += forward
        back[...] += backward

    @pl.when(step == pl.num_programs(0) - 1)
    def _():
        channels = gain.shape[1]
        whole = mixed[...]
        block_out[...] = (voxels[...].astype(F32) + scale[...] * whole).astype(BF16)
        scale_local = jnp.sum(cotangent[...].astype(F32) * whole, axis=0, keepdims=True)
        grad = back[...]
        one = unit[...]
        bias_local = jnp.sum(grad, axis=0, keepdims=True)
        gain_local = jnp.sum(grad * one, axis=0, keepdims=True)
        small[...] = jnp.concatenate(
            [gain_local, bias_local, scale_local, jnp.zeros((SUB - 3, channels), F32)], axis=0
        )
        scaled = grad * gain[...]
        average = jnp.sum(scaled, axis=1, keepdims=True) * (1.0 / channels)
        slant = jnp.sum(scaled * one, axis=1, keepdims=True) * (1.0 / channels)
        conv_grad[...] = (inv[:, :1] * (scaled - average - one * slant)).astype(BF16)


def weight_grad_kernel(which, act, hid, mixed_grad, normed, out_grad, in_grad):
    del which
    tokens = act.shape[2]
    for lhs, rhs, out in ((act, mixed_grad, out_grad), (hid, normed, in_grad)):
        total = None
        for k in range(act.shape[0]):
            part = jnp.dot(
                lhs[k], rhs[k * tokens : (k + 1) * tokens, :], preferred_element_type=F32
            )
            total = part if total is None else total + part
        out[...] = total


def params(limit=48):
    return pltpu.CompilerParams(vmem_limit_bytes=limit * 1024 * 1024)


def lane_block(rows):
    return pl.BlockSpec((rows, LANES), lambda c: (0, c))


def whole_block(*shape):
    return pl.BlockSpec(shape, lambda *_: (0,) * len(shape))


def halo(cells, axis, width):
    count = lax.axis_size(axis)
    ends = count - 1
    tail = cells[cells.shape[0] - width :]
    head = cells[:width]
    return (
        lax.ppermute(tail, axis, [(i, i + 1) for i in range(ends)]),
        lax.ppermute(head, axis, [(i + 1, i) for i in range(ends)]),
    )


def conv_cost(rows, channels):
    return pl.CostEstimate(
        flops=rows * channels * TAP_ROWS * 2, bytes_accessed=4 * rows * channels * 4, transcendentals=0
    )


def on_device(
    voxels, dw_kernel, norm_gain, norm_bias, weight_in, weight_out, layer_scale, cotangent
):
    planes, height, breadth, channels = voxels.shape
    rows = planes * height * breadth
    width = MARGIN * height * breadth
    units = weight_in.shape[0]
    count = lax.axis_size("row")
    me = lax.axis_index("row")
    half = count // 2
    alike = [[2 * k + p for k in range(half)] for p in range(2)]
    swap = [(i, i ^ 1) for i in range(count)]
    tiles = channels // LANES

    own = voxels.reshape(rows, channels)
    upstream = cotangent.reshape(rows, channels)
    gain = norm_gain.reshape(1, channels)
    bias = norm_bias.reshape(1, channels)
    scale = layer_scale.reshape(1, channels)

    left, right = halo(own, "row", width)
    mixed_grad = (scale * upstream.astype(F32)).astype(BF16)
    mixed_all = lax.all_gather(
        mixed_grad, "row", axis=0, tiled=True, axis_index_groups=alike
    )

    spread = pltpu.VMEM((9, planes + KS - 1, PAD, LANES), F32)
    split = pltpu.VMEM((9, KS, SUB, LANES), F32)

    normed, unit, inv = pl.pallas_call(
        functools.partial(forward_kernel, planes, height),
        grid=(tiles,),
        in_specs=[
            lane_block(width),
            lane_block(rows),
            lane_block(width),
            lane_block(TAP_ROWS),
            whole_block(1, channels),
            whole_block(1, channels),
        ],
        out_specs=[
            whole_block(rows, channels),
            whole_block(rows, channels),
            whole_block(rows, LANES),
        ],
        out_shape=[
            jax.ShapeDtypeStruct((rows, channels), BF16),
            jax.ShapeDtypeStruct((rows, channels), F32),
            jax.ShapeDtypeStruct((rows, LANES), F32),
        ],
        scratch_shapes=[spread, split, pltpu.VMEM((tiles, rows, LANES), F32)],
        compiler_params=params(),
        cost_estimate=conv_cost(rows, channels),
        name="forward_conv",
    )(left, own, right, dw_kernel, gain, bias)

    normed_all = lax.all_gather(normed, "row", axis=0, tiled=True, axis_index_groups=alike)

    block = 512
    whole = whole_block(rows, channels)
    line = whole_block(1, channels)
    act, hid, block_out, conv_grad, small = pl.pallas_call(
        mlp_kernel,
        grid=(units // block,),
        in_specs=[
            whole,
            whole,
            pl.BlockSpec((block, channels), lambda f: (f, 0)),
            pl.BlockSpec((block, channels), lambda f: (f, 0)),
            whole,
            whole_block(rows, LANES),
            line,
            line,
            whole,
            whole,
        ],
        out_specs=[
            pl.BlockSpec((block, rows), lambda f: (f, 0)),
            pl.BlockSpec((block, rows), lambda f: (f, 0)),
            whole,
            whole,
            whole_block(SUB, channels),
        ],
        out_shape=[
            jax.ShapeDtypeStruct((units, rows), BF16),
            jax.ShapeDtypeStruct((units, rows), BF16),
            jax.ShapeDtypeStruct((rows, channels), BF16),
            jax.ShapeDtypeStruct((rows, channels), BF16),
            jax.ShapeDtypeStruct((SUB, channels), F32),
        ],
        scratch_shapes=[pltpu.VMEM((rows, channels), F32), pltpu.VMEM((rows, channels), F32)],
        compiler_params=params(),
        cost_estimate=pl.CostEstimate(
            flops=8 * rows * channels * units,
            bytes_accessed=4 * units * channels + 4 * units * rows,
            transcendentals=2 * rows * units,
        ),
        name="mlp_both_ways",
    )(
        normed,
        mixed_grad,
        weight_in,
        weight_out,
        unit,
        inv,
        gain,
        scale,
        own,
        upstream,
    )

    grad_left, grad_right = halo(conv_grad, "row", width)

    piece = -(-(TAP_ROWS + SUB) // count)
    piece += -piece % SUB if count <= 16 else 0
    padded = piece * count
    sums = pl.pallas_call(
        functools.partial(kernel_grad_kernel, planes, height),
        grid=(tiles,),
        in_specs=[
            lane_block(width),
            lane_block(rows),
            lane_block(width),
            lane_block(rows),
            lane_block(SUB),
        ],
        out_specs=lane_block(padded),
        out_shape=jax.ShapeDtypeStruct((padded, channels), BF16),
        scratch_shapes=[
            spread,
            pltpu.VMEM((2, KS, SUB * SUB, LANES), F32),
            pltpu.VMEM((9, KS, SUB, LANES), F32),
            pltpu.VMEM((padded, LANES), F32),
        ],
        compiler_params=params(),
        cost_estimate=conv_cost(rows, channels),
        name="kernel_grad_terms",
    )(left, own, right, conv_grad, small)

    scattered = lax.all_to_all(sums, "row", split_axis=0, concat_axis=0, tiled=True)
    act_all = lax.all_to_all(
        act.reshape(half, units // half, rows),
        "row",
        split_axis=0,
        concat_axis=0,
        tiled=True,
        axis_index_groups=alike,
    )
    hid_all = lax.all_to_all(
        hid.reshape(half, units // half, rows),
        "row",
        split_axis=0,
        concat_axis=0,
        tiled=True,
        axis_index_groups=alike,
    )

    voxel_grad = pl.pallas_call(
        functools.partial(input_grad_kernel, planes, height),
        grid=(tiles,),
        in_specs=[
            lane_block(width),
            lane_block(rows),
            lane_block(width),
            lane_block(TAP_ROWS),
            lane_block(rows),
        ],
        out_specs=lane_block(rows),
        out_shape=jax.ShapeDtypeStruct((rows, channels), BF16),
        scratch_shapes=[spread, split],
        compiler_params=params(),
        cost_estimate=conv_cost(rows, channels),
        name="input_grad_conv",
    )(grad_left, conv_grad, grad_right, dw_kernel, upstream)

    summed = jnp.sum(scattered.reshape(count, piece, channels).astype(F32), axis=0)
    gathered = lax.all_gather(summed.astype(BF16), "row", axis=0, tiled=True)
    totals = gathered.astype(F32)
    kernel_grad = totals[:TAP_ROWS]
    gain_grad = totals[TAP_ROWS]
    bias_grad = totals[TAP_ROWS + 1]
    scale_grad = totals[TAP_ROWS + 2]

    mine = units // count
    tokens = half * rows

    def weight_grads(which, name):
        return pl.pallas_call(
            weight_grad_kernel,
            grid_spec=pltpu.PrefetchScalarGridSpec(
                num_scalar_prefetch=1,
                grid=(1,),
                in_specs=[
                    pl.BlockSpec((half, mine, rows), lambda _, w: (0, w[0], 0)),
                    pl.BlockSpec((half, mine, rows), lambda _, w: (0, w[0], 0)),
                    whole_block(tokens, channels),
                    whole_block(tokens, channels),
                ],
                out_specs=[whole_block(mine, channels), whole_block(mine, channels)],
            ),
            out_shape=[
                jax.ShapeDtypeStruct((mine, channels), F32),
                jax.ShapeDtypeStruct((mine, channels), F32),
            ],
            compiler_params=params(),
            cost_estimate=pl.CostEstimate(
                flops=4 * tokens * channels * mine,
                bytes_accessed=4 * tokens * channels + 4 * mine * tokens,
                transcendentals=0,
            ),
            name=name,
        )(which.reshape(1), act_all, hid_all, mixed_all, normed_all)

    core = lax.rem(me, 2).astype(jnp.int32)
    sent = weight_grads(1 - core, "weight_grads_sent")
    got = [lax.ppermute(part, "row", swap) for part in sent]
    kept = weight_grads(core, "weight_grads_kept")
    weight_out_grad = kept[0] + got[0]
    weight_in_grad = kept[1] + got[1]

    return (
        block_out.reshape(voxels.shape),
        voxel_grad.reshape(voxels.shape),
        kernel_grad,
        gain_grad,
        bias_grad,
        scale_grad,
        weight_in_grad,
        weight_out_grad,
    )


def solution(mesh):
    in_specs = (
        P(("group", "row"), None, None, None),
        P(),
        P(),
        P(),
        P(),
        P(),
        P(),
        P(("group", "row"), None, None, None),
    )
    out_specs = (
        P(("group", "row"), None, None, None),
        P(("group", "row"), None, None, None),
        P("group", None),
        P("group"),
        P("group"),
        P("group"),
        P(("group", "row"), None),
        P(("group", "row"), None),
    )
    return jax.shard_map(
        on_device, mesh=mesh, in_specs=in_specs, out_specs=out_specs, check_vma=False
    )
```

```python
import functools

import jax
import jax.numpy as jnp
from jax import lax
from jax.experimental import pallas as pl
from jax.experimental.pallas import tpu as pltpu
from jax.sharding import PartitionSpec as P

KS = 7
MARGIN = KS // 2
LANES = 128
SUB = 8
PAD = 3 * SUB
TAP_ROWS = KS * KS * KS

root_half = 0.7071067811865476
inv_root_tau = 0.3989422804014327
norm_eps = 1e-06

F32 = jnp.float32
BF16 = jnp.bfloat16


def split_source(v):
    terms = []
    for a, b in ((v[0] + v[2], v[1] + v[3]), (v[2], v[3]), (v[0], v[1])):
        terms += [a + b, b, a]
    return terms


def split_taps(t):
    terms = []
    for s in (
        (t[2], t[3], t[4]),
        (t[4] - t[2], t[5] - t[3], t[6] - t[4]),
        (t[0] - t[2], t[1] - t[3], t[2] - t[4]),
    ):
        terms += [s[1], s[2] - s[1], s[0] - s[1]]
    return terms


def split_grads(g):
    terms = []
    for a, b in ((g[0] + g[2], g[1] + g[3]), (g[0], g[1]), (g[2], g[3])):
        terms += [a + b, a, b]
    return terms


def join_outputs(m):
    pair = [(m[3 * k] + m[3 * k + 1], m[3 * k] + m[3 * k + 2]) for k in range(3)]
    return [
        pair[0][0] + pair[1][0],
        pair[0][1] + pair[1][1],
        pair[0][0] + pair[2][0],
        pair[0][1] + pair[2][1],
    ]


def join_taps(m):
    p, q, r = [
        (m[3 * k + 2], m[3 * k] - m[3 * k + 1] - m[3 * k + 2], m[3 * k + 1]) for k in range(3)
    ]
    return [
        r[0],
        r[1],
        p[0] - q[0] - r[0] + r[2],
        p[1] - q[1] - r[1],
        p[2] - q[2] - r[2] + q[0],
        q[1],
        q[2],
    ]


def tree_sum(terms):
    while len(terms) > 1:
        terms = [
            terms[k] + terms[k + 1] if k + 1 < len(terms) else terms[k]
            for k in range(0, len(terms), 2)
        ]
    return terms[0]


def stage_source(left, own, right, planes, height, spread):
    row = height * SUB
    wanted = [(left, x) for x in range(planes - MARGIN, planes)]
    wanted += [(own, x) for x in range(planes)]
    wanted += [(right, x) for x in range(MARGIN)]
    for at, (block, x) in enumerate(wanted):
        plane = block[x * row : (x + 1) * row, :].astype(F32)
        lines = [plane[y * SUB : (y + 1) * SUB, :] for y in range(height)]
        for j, term in enumerate(split_source(lines)):
            spread[j, at, SUB : 2 * SUB, :] = term


def clear_rims(spread):
    zeros = jnp.zeros(spread.shape[:2] + (SUB, LANES), F32)
    spread[:, :, :SUB, :] = zeros
    spread[:, :, 2 * SUB :, :] = zeros


def stage_taps(taps, flipped, split):
    for dx in range(KS):
        rows = []
        for dy in range(KS):
            first = dx * KS * KS + dy * KS
            if first + SUB <= TAP_ROWS:
                rows.append(taps[first : first + SUB, :])
            else:
                rows.append(pltpu.roll(taps[TAP_ROWS - SUB : TAP_ROWS, :], SUB - 1, 0))
        if flipped:
            rows = rows[::-1]
        for j, term in enumerate(split_taps(rows)):
            split[j, KS - 1 - dx if flipped else dx] = term


def convolve(spread, split, planes, flipped):
    terms = []
    for j in range(9):
        sums = [None] * planes
        for dz in range(KS):
            first = SUB - MARGIN + dz
            source = [
                spread[j, x, first : first + SUB, :] for x in range(planes + KS - 1)
            ]
            at = KS - 1 - dz if flipped else dz
            weights = [
                jnp.broadcast_to(split[j, dx, at : at + 1, :], (SUB, LANES)) for dx in range(KS)
            ]
            for x in range(planes):
                part = tree_sum([source[x + dx] * weights[dx] for dx in range(KS)])
                sums[x] = part if sums[x] is None else sums[x] + part
        terms.append(sums)
    return [join_outputs([terms[j][x] for j in range(9)]) for x in range(planes)]


def forward_kernel(
    planes, height, left, own, right, taps, gain, bias, normed, unit, inv, spread, split, conv
):
    step = pl.program_id(0)

    @pl.when(step == 0)
    def _():
        clear_rims(spread)

    stage_source(left, own, right, planes, height, spread)
    stage_taps(taps, False, split)
    rows = convolve(spread, split, planes, False)
    for x in range(planes):
        for y in range(height):
            at = (x * height + y) * SUB
            conv[step, at : at + SUB, :] = rows[x][y]

    @pl.when(step == pl.num_programs(0) - 1)
    def _():
        tiles = conv.shape[0]
        channels = tiles * LANES
        parts = [conv[k] for k in range(tiles)]
        average = jnp.sum(tree_sum(parts), axis=1, keepdims=True) * (1.0 / channels)
        parts = [part - average for part in parts]
        variance = jnp.sum(
            tree_sum([part * part for part in parts]), axis=1, keepdims=True
        ) * (1.0 / channels)
        inverse = lax.rsqrt(variance + norm_eps)
        inv[...] = jnp.broadcast_to(inverse, inv.shape)
        for k in range(tiles):
            lanes = slice(k * LANES, (k + 1) * LANES)
            value = parts[k] * inverse
            unit[:, lanes] = value
            whole = (value * gain[:, lanes] + bias[:, lanes]).astype(BF16)
            for copy in range(normed.shape[0]):
                normed[copy, :, lanes] = whole


def input_grad_kernel(planes, height, left, own, right, taps, cotangent, out, spread, split):
    @pl.when(pl.program_id(0) == 0)
    def _():
        clear_rims(spread)

    stage_source(left, own, right, planes, height, spread)
    stage_taps(taps, True, split)
    rows = convolve(spread, split, planes, True)
    for x in range(planes):
        at = x * height * SUB
        whole = jnp.concatenate(rows[x], axis=0)
        upstream = cotangent[at : at + height * SUB, :].astype(F32)
        out[at : at + height * SUB, :] = (upstream + whole).astype(BF16)


def kernel_grad_kernel(
    planes, height, which, left, own, right, grads, small, out, spread, products, joined, flat
):
    del which

    @pl.when(pl.program_id(0) == 0)
    def _():
        clear_rims(spread)
        products[...] = jnp.zeros(products.shape, F32)
        flat[...] = jnp.zeros(flat.shape, F32)

    stage_source(left, own, right, planes, height, spread)
    upstream = []
    for x in range(planes):
        plane = grads[x * height * SUB : (x + 1) * height * SUB, :].astype(F32)
        upstream.append(
            split_grads([plane[y * SUB : (y + 1) * SUB, :] for y in range(height)])
        )
    for j in range(9):
        for dz in range(KS):
            first = SUB - MARGIN + dz
            source = [
                spread[j, x, first : first + SUB, :] for x in range(planes + KS - 1)
            ]
            for dx in range(KS):
                products[j % 2, dx, dz * SUB : (dz + 1) * SUB, :] = tree_sum(
                    [source[x + dx] * upstream[x][j] for x in range(planes)]
                )
        for dx in range(KS):
            joined[j, dx] = tree_sum(
                [products[j % 2, dx, pl.ds(s, SUB, stride=SUB), :] for s in range(SUB)]
            )
    for dx in range(KS):
        for dy, tile in enumerate(join_taps([joined[j, dx] for j in range(9)])):
            first = dx * KS * KS + dy * KS
            flat[first : first + SUB, :] = tile
    flat[TAP_ROWS : TAP_ROWS + SUB, :] = small[...]
    out[...] = flat[...].astype(out.dtype)


def mlp_kernel(
    normed,
    weight_in,
    weight_out,
    unit,
    inv,
    gain,
    scale,
    voxels,
    cotangent,
    block_out,
    conv_grad,
    small,
    mixed,
    back,
    mixed_grad,
):
    step = pl.program_id(0)

    @pl.when(step == 0)
    def _():
        mixed_grad[...] = (scale[...] * cotangent[...].astype(F32)).astype(BF16)

    hidden = lax.dot_general(
        normed[...], weight_in[...], (((1,), (1,)), ((), ())), preferred_element_type=F32
    )
    act_grad = lax.dot_general(
        mixed_grad[...], weight_out[...], (((1,), (1,)), ((), ())), preferred_element_type=F32
    )
    activated, hidden_grad = slopes(hidden, act_grad)
    forward = jnp.dot(activated, weight_out[...], preferred_element_type=F32)
    backward = jnp.dot(hidden_grad, weight_in[...], preferred_element_type=F32)

    @pl.when(step == 0)
    def _():
        mixed[...] = forward
        back[...] = backward

    @pl.when(step > 0)
    def _():
        mixed[...] += forward
        back[...] += backward

    @pl.when(step == pl.num_programs(0) - 1)
    def _():
        channels = gain.shape[1]
        whole = mixed[...]
        block_out[...] = (voxels[...].astype(F32) + scale[...] * whole).astype(BF16)
        scale_local = jnp.sum(cotangent[...].astype(F32) * whole, axis=0, keepdims=True)
        grad = back[...]
        one = unit[...]
        bias_local = jnp.sum(grad, axis=0, keepdims=True)
        gain_local = jnp.sum(grad * one, axis=0, keepdims=True)
        small[...] = jnp.concatenate(
            [gain_local, bias_local, scale_local, jnp.zeros((SUB - 3, channels), F32)], axis=0
        )
        scaled = grad * gain[...]
        average = jnp.sum(scaled, axis=1, keepdims=True) * (1.0 / channels)
        slant = jnp.sum(scaled * one, axis=1, keepdims=True) * (1.0 / channels)
        conv_grad[...] = (inv[:, :1] * (scaled - average - one * slant)).astype(BF16)


def slopes(hidden, act_grad):
    cover = 0.5 * (1.0 + lax.erf(hidden * root_half))
    activated = (hidden * cover).astype(BF16)
    slope = cover + hidden * jnp.exp(-0.5 * hidden * hidden) * inv_root_tau
    return activated, (act_grad * slope).astype(BF16)


def weight_grad_terms(which, weight_in, weight_out, scale, cotangent, normed, aligned):
    rows = cotangent.shape[1]
    for k in range(cotangent.shape[0]):
        upstream = cotangent[which[2 + k]].astype(F32)
        aligned[k * rows : (k + 1) * rows, :] = (scale[...] * upstream).astype(BF16)
    mixed_grad = aligned[...]
    across = (((1,), (1,)), ((), ()))
    hidden = lax.dot_general(weight_in[...], normed[...], across, preferred_element_type=F32)
    act_grad = lax.dot_general(weight_out[...], mixed_grad, across, preferred_element_type=F32)
    activated, hidden_grad = slopes(hidden, act_grad)
    return (
        jnp.dot(hidden_grad, normed[...], preferred_element_type=F32),
        jnp.dot(activated, mixed_grad, preferred_element_type=F32),
    )


def first_terms_kernel(which, weight_in, weight_out, scale, cotangent, normed, out, aligned):
    terms = weight_grad_terms(which, weight_in, weight_out, scale, cotangent, normed, aligned)
    for k in range(2):
        out[0, k] = terms[k]


def sent_terms_kernel(
    which, weight_in, weight_out, scale, cotangent, normed, before, out, aligned
):
    terms = weight_grad_terms(which, weight_in, weight_out, scale, cotangent, normed, aligned)
    for k in range(2):
        out[k] = before[0, k] + terms[k]


def last_terms_kernel(
    which, weight_in, weight_out, scale, cotangent, normed, before, got, in_grad, out_grad, aligned
):
    terms = weight_grad_terms(which, weight_in, weight_out, scale, cotangent, normed, aligned)
    for k, out in enumerate((in_grad, out_grad)):
        out[...] = before[0, k] + terms[k] + got[k]


def spread_sum_kernel(parts, out):
    total = tree_sum([parts[k].astype(F32) for k in range(parts.shape[0])]).astype(BF16)
    for copy in range(out.shape[0]):
        out[copy] = total


def unpack_kernel(parts, out, small):
    piece = parts.shape[1]
    for k in range(-(-TAP_ROWS // piece)):
        first = k * piece
        length = min(piece, TAP_ROWS - first)
        out[first : first + length, :] = parts[k].astype(F32)[:length, :]
    k = TAP_ROWS // piece
    first = TAP_ROWS - k * piece
    rows = parts[k].astype(F32)
    if first + SUB > piece:
        rows = jnp.concatenate([rows, parts[k + 1].astype(F32)], axis=0)
    small[...] = rows[first : first + SUB, :]


def params(limit=48):
    return pltpu.CompilerParams(vmem_limit_bytes=limit * 1024 * 1024)


def lane_block(rows):
    return pl.BlockSpec((rows, LANES), lambda c: (0, c))


def whole_block(*shape):
    return pl.BlockSpec(shape, lambda *_: (0,) * len(shape))


def neighbours(cells):
    ends = lax.axis_size("row") - 1
    return (
        lax.ppermute(cells, "row", [(i, i + 1) for i in range(ends)]),
        lax.ppermute(cells, "row", [(i + 1, i) for i in range(ends)]),
    )


def conv_cost(rows, channels):
    return pl.CostEstimate(
        flops=rows * channels * TAP_ROWS * 2, bytes_accessed=4 * rows * channels * 4, transcendentals=0
    )


def on_device(
    voxels, dw_kernel, norm_gain, norm_bias, weight_in, weight_out, layer_scale, cotangent
):
    planes, height, breadth, channels = voxels.shape
    rows = planes * height * breadth
    units = weight_in.shape[0]
    count = lax.axis_size("row")
    me = lax.axis_index("row")
    half = count // 2
    quad = 4
    line = count // quad
    alike = [[2 * k + p for k in range(half)] for p in range(2)]
    lines = [[quad * k + p for k in range(line)] for p in range(quad)]
    other_core = [(i, i ^ 1) for i in range(count)]
    other_side = [(i, i ^ 2) for i in range(count)]
    tiles = channels // LANES
    half_tiles = tiles // 2

    own = voxels.reshape(rows, channels)
    upstream = cotangent.reshape(rows, channels)
    gain = norm_gain.reshape(1, channels)
    bias = norm_bias.reshape(1, channels)
    scale = layer_scale.reshape(1, channels)
    core = lax.rem(me, 2).astype(jnp.int32)
    mine = me.astype(jnp.int32)
    theirs = mine + 1 - 2 * core

    left, right = neighbours(own)
    upstream_line = [upstream] + [
        lax.ppermute(upstream, "row", [(i, (i + quad * k) % count) for i in range(count)])
        for k in range(1, line)
    ]
    upstream_near = jnp.concatenate(upstream_line, axis=0).reshape(line, rows, channels)
    upstream_far = lax.ppermute(upstream_near, "row", other_side)

    spread = pltpu.VMEM((9, planes + KS - 1, PAD, LANES), F32)
    split = pltpu.VMEM((9, KS, SUB, LANES), F32)

    normed, unit, inv = pl.pallas_call(
        functools.partial(forward_kernel, planes, height),
        grid=(tiles,),
        in_specs=[
            lane_block(rows),
            lane_block(rows),
            lane_block(rows),
            lane_block(TAP_ROWS),
            whole_block(1, channels),
            whole_block(1, channels),
        ],
        out_specs=[
            whole_block(line, rows, channels),
            whole_block(rows, channels),
            whole_block(rows, LANES),
        ],
        out_shape=[
            jax.ShapeDtypeStruct((line, rows, channels), BF16),
            jax.ShapeDtypeStruct((rows, channels), F32),
            jax.ShapeDtypeStruct((rows, LANES), F32),
        ],
        scratch_shapes=[spread, split, pltpu.VMEM((tiles, rows, LANES), F32)],
        compiler_params=params(),
        cost_estimate=conv_cost(rows, channels),
        name="forward_conv",
    )(left, own, right, dw_kernel, gain, bias)

    gathered = lax.all_to_all(
        normed, "row", split_axis=0, concat_axis=0, tiled=True, axis_index_groups=lines
    )
    normed_near = gathered.reshape(line * rows, channels)
    normed_far = lax.ppermute(normed_near, "row", other_side)

    block = 512
    whole = whole_block(rows, channels)
    vector = whole_block(1, channels)
    block_out, conv_grad, small = pl.pallas_call(
        mlp_kernel,
        grid=(units // block,),
        in_specs=[
            pl.BlockSpec((None, rows, channels), lambda f: (0, 0, 0)),
            pl.BlockSpec((block, channels), lambda f: (f, 0)),
            pl.BlockSpec((block, channels), lambda f: (f, 0)),
            whole,
            whole_block(rows, LANES),
            vector,
            vector,
            whole,
            whole,
        ],
        out_specs=[
            whole,
            whole,
            whole_block(SUB, channels),
        ],
        out_shape=[
            jax.ShapeDtypeStruct((rows, channels), BF16),
            jax.ShapeDtypeStruct((rows, channels), BF16),
            jax.ShapeDtypeStruct((SUB, channels), F32),
        ],
        scratch_shapes=[
            pltpu.VMEM((rows, channels), F32),
            pltpu.VMEM((rows, channels), F32),
            pltpu.VMEM((rows, channels), BF16),
        ],
        compiler_params=params(),
        cost_estimate=pl.CostEstimate(
            flops=8 * rows * channels * units,
            bytes_accessed=4 * units * channels,
            transcendentals=2 * rows * units,
        ),
        name="mlp_both_ways",
    )(normed, weight_in, weight_out, unit, inv, gain, scale, own, upstream)

    grad_left, grad_right = neighbours(conv_grad)

    piece = -(-(TAP_ROWS + SUB) // half)
    piece += -piece % (2 * SUB)
    padded = piece * half

    def kernel_grad_half(which, name):
        def at(block_rows):
            return pl.BlockSpec((block_rows, LANES), lambda c, w: (0, w[0] * half_tiles + c))

        return pl.pallas_call(
            functools.partial(kernel_grad_kernel, planes, height),
            grid_spec=pltpu.PrefetchScalarGridSpec(
                num_scalar_prefetch=1,
                grid=(half_tiles,),
                in_specs=[at(rows), at(rows), at(rows), at(rows), at(SUB)],
                out_specs=pl.BlockSpec((padded, LANES), lambda c, w: (0, c)),
                scratch_shapes=[
                    spread,
                    pltpu.VMEM((2, KS, SUB * SUB, LANES), F32),
                    pltpu.VMEM((9, KS, SUB, LANES), F32),
                    pltpu.VMEM((padded, LANES), F32),
                ],
            ),
            out_shape=jax.ShapeDtypeStruct((padded, half_tiles * LANES), BF16),
            compiler_params=params(),
            cost_estimate=conv_cost(rows, channels // 2),
            name=name,
        )(which.reshape(1), left, own, right, conv_grad, small)

    for_other = kernel_grad_half(1 - core, "kernel_grad_sent")
    from_other = lax.ppermute(for_other, "row", other_core)
    for_self = kernel_grad_half(core, "kernel_grad_kept")
    chip_sum = (for_self.astype(F32) + from_other.astype(F32)).astype(BF16)
    wide = half_tiles * LANES
    scattered = lax.all_to_all(
        chip_sum.reshape(half, piece, wide),
        "row",
        split_axis=0,
        concat_axis=0,
        tiled=True,
        axis_index_groups=alike,
    )
    copies = pl.pallas_call(
        spread_sum_kernel,
        in_specs=[whole_block(half, piece, wide)],
        out_specs=whole_block(count, piece, wide),
        out_shape=jax.ShapeDtypeStruct((count, piece, wide), BF16),
        grid=(1,),
        compiler_params=params(),
        name="kernel_grad_sum",
    )(scattered)
    totals = lax.all_to_all(copies, "row", split_axis=0, concat_axis=0, tiled=True)

    voxel_grad = pl.pallas_call(
        functools.partial(input_grad_kernel, planes, height),
        grid=(tiles,),
        in_specs=[
            lane_block(rows),
            lane_block(rows),
            lane_block(rows),
            lane_block(TAP_ROWS),
            lane_block(rows),
        ],
        out_specs=lane_block(rows),
        out_shape=jax.ShapeDtypeStruct((rows, channels), BF16),
        scratch_shapes=[spread, split],
        compiler_params=params(),
        cost_estimate=conv_cost(rows, channels),
        name="input_grad_conv",
    )(grad_left, conv_grad, grad_right, dw_kernel, upstream)

    kernel_grad, vectors = pl.pallas_call(
        unpack_kernel,
        grid=(2,),
        in_specs=[pl.BlockSpec((half, None, piece, wide), lambda p: (0, p, 0, 0))],
        out_specs=[
            pl.BlockSpec((TAP_ROWS, wide), lambda p: (0, p)),
            pl.BlockSpec((SUB, wide), lambda p: (0, p)),
        ],
        out_shape=[
            jax.ShapeDtypeStruct((TAP_ROWS, channels), F32),
            jax.ShapeDtypeStruct((SUB, channels), F32),
        ],
        compiler_params=params(),
        name="kernel_grad_unpack",
    )(totals.reshape(half, 2, piece, wide))

    share = units // count
    tokens = line * rows
    terms_cost = pl.CostEstimate(
        flops=8 * tokens * channels * share,
        bytes_accessed=4 * tokens * channels + 4 * share * channels,
        transcendentals=2 * tokens * share,
    )
    both = jax.ShapeDtypeStruct((2, share, channels), F32)
    sets = [
        whole_block(1, channels),
        whole_block(line, rows, channels),
        whole_block(tokens, channels),
    ]
    aligned = [pltpu.VMEM((tokens, channels), BF16)]
    place = lax.rem(me // quad + line - jnp.arange(line, dtype=jnp.int32), line)
    which = jnp.concatenate([theirs.reshape(1), mine.reshape(1), place.astype(jnp.int32)])

    def chunk(at):
        return pl.BlockSpec((share, channels), lambda s, w: (w[s + at], 0))

    first = pl.pallas_call(
        first_terms_kernel,
        grid_spec=pltpu.PrefetchScalarGridSpec(
            num_scalar_prefetch=1,
            grid=(2,),
            in_specs=[chunk(0), chunk(0)] + sets,
            out_specs=pl.BlockSpec((1, 2, share, channels), lambda s, w: (s, 0, 0, 0)),
            scratch_shapes=aligned,
        ),
        out_shape=jax.ShapeDtypeStruct((2, 2, share, channels), F32),
        compiler_params=params(),
        cost_estimate=terms_cost,
        name="weight_grads_near",
    )(which, weight_in, weight_out, scale, upstream_near, normed_near)
    sent = pl.pallas_call(
        sent_terms_kernel,
        grid_spec=pltpu.PrefetchScalarGridSpec(
            num_scalar_prefetch=1,
            grid=(1,),
            in_specs=[chunk(0), chunk(0)]
            + sets
            + [pl.BlockSpec((1, 2, share, channels), lambda s, w: (0, 0, 0, 0))],
            out_specs=whole_block(2, share, channels),
            scratch_shapes=aligned,
        ),
        out_shape=both,
        compiler_params=params(),
        cost_estimate=terms_cost,
        name="weight_grads_sent",
    )(which, weight_in, weight_out, scale, upstream_far, normed_far, first)
    got = lax.ppermute(sent, "row", other_core)
    weight_in_grad, weight_out_grad = pl.pallas_call(
        last_terms_kernel,
        grid_spec=pltpu.PrefetchScalarGridSpec(
            num_scalar_prefetch=1,
            grid=(1,),
            in_specs=[chunk(1), chunk(1)]
            + sets
            + [
                pl.BlockSpec((1, 2, share, channels), lambda s, w: (1, 0, 0, 0)),
                whole_block(2, share, channels),
            ],
            out_specs=[whole_block(share, channels), whole_block(share, channels)],
            scratch_shapes=aligned,
        ),
        out_shape=[jax.ShapeDtypeStruct((share, channels), F32)] * 2,
        compiler_params=params(),
        cost_estimate=terms_cost,
        name="weight_grads_kept",
    )(which, weight_in, weight_out, scale, upstream_far, normed_far, first, got)

    return (
        block_out.reshape(voxels.shape),
        voxel_grad.reshape(voxels.shape),
        kernel_grad,
        vectors[0],
        vectors[1],
        vectors[2],
        weight_in_grad,
        weight_out_grad,
    )


def solution(mesh):
    in_specs = (
        P(("group", "row"), None, None, None),
        P(),
        P(),
        P(),
        P(),
        P(),
        P(),
        P(("group", "row"), None, None, None),
    )
    out_specs = (
        P(("group", "row"), None, None, None),
        P(("group", "row"), None, None, None),
        P("group", None),
        P("group"),
        P("group"),
        P("group"),
        P(("group", "row"), None),
        P(("group", "row"), None),
    )
    return jax.shard_map(
        on_device, mesh=mesh, in_specs=in_specs, out_specs=out_specs, check_vma=False
    )
```

```python
import functools

import jax
import jax.numpy as jnp
from jax import lax
from jax.experimental import pallas as pl
from jax.experimental.pallas import tpu as pltpu
from jax.sharding import PartitionSpec as P

KS = 7
MARGIN = KS // 2
LANES = 128
SUB = 8
PAD = 3 * SUB
TAP_ROWS = KS * KS * KS

root_half = 0.7071067811865476
inv_root_tau = 0.3989422804014327
norm_eps = 1e-06

F32 = jnp.float32
BF16 = jnp.bfloat16


def split_source(v):
    terms = []
    for a, b in ((v[0] + v[2], v[1] + v[3]), (v[2], v[3]), (v[0], v[1])):
        terms += [a + b, b, a]
    return terms


def split_taps(t):
    terms = []
    for s in (
        (t[2], t[3], t[4]),
        (t[4] - t[2], t[5] - t[3], t[6] - t[4]),
        (t[0] - t[2], t[1] - t[3], t[2] - t[4]),
    ):
        terms += [s[1], s[2] - s[1], s[0] - s[1]]
    return terms


def split_grads(g):
    terms = []
    for a, b in ((g[0] + g[2], g[1] + g[3]), (g[0], g[1]), (g[2], g[3])):
        terms += [a + b, a, b]
    return terms


def join_outputs(m):
    pair = [(m[3 * k] + m[3 * k + 1], m[3 * k] + m[3 * k + 2]) for k in range(3)]
    return [
        pair[0][0] + pair[1][0],
        pair[0][1] + pair[1][1],
        pair[0][0] + pair[2][0],
        pair[0][1] + pair[2][1],
    ]


def join_taps(m):
    p, q, r = [
        (m[3 * k + 2], m[3 * k] - m[3 * k + 1] - m[3 * k + 2], m[3 * k + 1]) for k in range(3)
    ]
    return [
        r[0],
        r[1],
        p[0] - q[0] - r[0] + r[2],
        p[1] - q[1] - r[1],
        p[2] - q[2] - r[2] + q[0],
        q[1],
        q[2],
    ]


def tree_sum(terms):
    while len(terms) > 1:
        terms = [
            terms[k] + terms[k + 1] if k + 1 < len(terms) else terms[k]
            for k in range(0, len(terms), 2)
        ]
    return terms[0]


def stage_source(left, own, right, planes, height, spread):
    row = height * SUB
    wanted = [(left, x) for x in range(planes - MARGIN, planes)]
    wanted += [(own, x) for x in range(planes)]
    wanted += [(right, x) for x in range(MARGIN)]
    for at, (block, x) in enumerate(wanted):
        plane = block[x * row : (x + 1) * row, :].astype(F32)
        lines = [plane[y * SUB : (y + 1) * SUB, :] for y in range(height)]
        for j, term in enumerate(split_source(lines)):
            spread[j, at, SUB : 2 * SUB, :] = term


def clear_rims(spread):
    zeros = jnp.zeros(spread.shape[:2] + (SUB, LANES), F32)
    spread[:, :, :SUB, :] = zeros
    spread[:, :, 2 * SUB :, :] = zeros


def stage_taps(taps, flipped, split):
    for dx in range(KS):
        rows = []
        for dy in range(KS):
            first = dx * KS * KS + dy * KS
            if first + SUB <= TAP_ROWS:
                rows.append(taps[first : first + SUB, :])
            else:
                rows.append(pltpu.roll(taps[TAP_ROWS - SUB : TAP_ROWS, :], SUB - 1, 0))
        if flipped:
            rows = rows[::-1]
        for j, term in enumerate(split_taps(rows)):
            split[j, KS - 1 - dx if flipped else dx] = term


def convolve(spread, split, planes, flipped):
    terms = []
    for j in range(9):
        sums = [None] * planes
        for dz in range(KS):
            first = SUB - MARGIN + dz
            source = [
                spread[j, x, first : first + SUB, :] for x in range(planes + KS - 1)
            ]
            at = KS - 1 - dz if flipped else dz
            weights = [
                jnp.broadcast_to(split[j, dx, at : at + 1, :], (SUB, LANES)) for dx in range(KS)
            ]
            for x in range(planes):
                part = tree_sum([source[x + dx] * weights[dx] for dx in range(KS)])
                sums[x] = part if sums[x] is None else sums[x] + part
        terms.append(sums)
    return [join_outputs([terms[j][x] for j in range(9)]) for x in range(planes)]


def forward_kernel(
    planes, height, left, own, right, taps, gain, bias, normed, unit, inv, spread, split, conv
):
    step = pl.program_id(0)

    @pl.when(step == 0)
    def _():
        clear_rims(spread)

    stage_source(left, own, right, planes, height, spread)
    stage_taps(taps, False, split)
    rows = convolve(spread, split, planes, False)
    for x in range(planes):
        for y in range(height):
            at = (x * height + y) * SUB
            conv[step, at : at + SUB, :] = rows[x][y]

    @pl.when(step == pl.num_programs(0) - 1)
    def _():
        tiles = conv.shape[0]
        channels = tiles * LANES
        parts = [conv[k] for k in range(tiles)]
        average = jnp.sum(tree_sum(parts), axis=1, keepdims=True) * (1.0 / channels)
        parts = [part - average for part in parts]
        variance = jnp.sum(
            tree_sum([part * part for part in parts]), axis=1, keepdims=True
        ) * (1.0 / channels)
        inverse = lax.rsqrt(variance + norm_eps)
        inv[...] = jnp.broadcast_to(inverse, inv.shape)
        for k in range(tiles):
            lanes = slice(k * LANES, (k + 1) * LANES)
            value = parts[k] * inverse
            unit[:, lanes] = value
            whole = (value * gain[:, lanes] + bias[:, lanes]).astype(BF16)
            for copy in range(normed.shape[0]):
                normed[copy, :, lanes] = whole


def input_grad_kernel(planes, height, left, own, right, taps, cotangent, out, spread, split):
    @pl.when(pl.program_id(0) == 0)
    def _():
        clear_rims(spread)

    stage_source(left, own, right, planes, height, spread)
    stage_taps(taps, True, split)
    rows = convolve(spread, split, planes, True)
    for x in range(planes):
        at = x * height * SUB
        whole = jnp.concatenate(rows[x], axis=0)
        upstream = cotangent[at : at + height * SUB, :].astype(F32)
        out[at : at + height * SUB, :] = (upstream + whole).astype(BF16)


def kernel_grad_kernel(
    planes, height, left, own, right, grads, small, out, spread, products, joined, flat
):
    @pl.when(pl.program_id(0) == 0)
    def _():
        clear_rims(spread)
        products[...] = jnp.zeros(products.shape, F32)
        flat[...] = jnp.zeros(flat.shape, F32)

    stage_source(left, own, right, planes, height, spread)
    upstream = []
    for x in range(planes):
        plane = grads[x * height * SUB : (x + 1) * height * SUB, :].astype(F32)
        upstream.append(
            split_grads([plane[y * SUB : (y + 1) * SUB, :] for y in range(height)])
        )
    for j in range(9):
        for dz in range(KS):
            first = SUB - MARGIN + dz
            source = [
                spread[j, x, first : first + SUB, :] for x in range(planes + KS - 1)
            ]
            for dx in range(KS):
                products[j % 2, dx, dz * SUB : (dz + 1) * SUB, :] = tree_sum(
                    [source[x + dx] * upstream[x][j] for x in range(planes)]
                )
        for dx in range(KS):
            joined[j, dx] = tree_sum(
                [products[j % 2, dx, pl.ds(s, SUB, stride=SUB), :] for s in range(SUB)]
            )
    for dx in range(KS):
        for dy, tile in enumerate(join_taps([joined[j, dx] for j in range(9)])):
            first = dx * KS * KS + dy * KS
            flat[first : first + SUB, :] = tile
    flat[TAP_ROWS : TAP_ROWS + SUB, :] = small[...]
    out[...] = flat[...].astype(out.dtype)


def mlp_kernel(
    normed,
    weight_in,
    weight_out,
    unit,
    inv,
    gain,
    scale,
    voxels,
    cotangent,
    block_out,
    conv_grad,
    small,
    mixed,
    back,
    mixed_grad,
):
    step = pl.program_id(0)

    @pl.when(step == 0)
    def _():
        mixed_grad[...] = (scale[...] * cotangent[...].astype(F32)).astype(BF16)

    hidden = lax.dot_general(
        normed[...], weight_in[...], (((1,), (1,)), ((), ())), preferred_element_type=F32
    )
    act_grad = lax.dot_general(
        mixed_grad[...], weight_out[...], (((1,), (1,)), ((), ())), preferred_element_type=F32
    )
    activated, hidden_grad = slopes(hidden, act_grad)
    forward = jnp.dot(activated, weight_out[...], preferred_element_type=F32)
    backward = jnp.dot(hidden_grad, weight_in[...], preferred_element_type=F32)

    @pl.when(step == 0)
    def _():
        mixed[...] = forward
        back[...] = backward

    @pl.when(step > 0)
    def _():
        mixed[...] += forward
        back[...] += backward

    @pl.when(step == pl.num_programs(0) - 1)
    def _():
        channels = gain.shape[1]
        whole = mixed[...]
        block_out[...] = (voxels[...].astype(F32) + scale[...] * whole).astype(BF16)
        scale_local = jnp.sum(cotangent[...].astype(F32) * whole, axis=0, keepdims=True)
        grad = back[...]
        one = unit[...]
        bias_local = jnp.sum(grad, axis=0, keepdims=True)
        gain_local = jnp.sum(grad * one, axis=0, keepdims=True)
        small[...] = jnp.concatenate(
            [gain_local, bias_local, scale_local, jnp.zeros((SUB - 3, channels), F32)], axis=0
        )
        scaled = grad * gain[...]
        average = jnp.sum(scaled, axis=1, keepdims=True) * (1.0 / channels)
        slant = jnp.sum(scaled * one, axis=1, keepdims=True) * (1.0 / channels)
        conv_grad[...] = (inv[:, :1] * (scaled - average - one * slant)).astype(BF16)


def slopes(hidden, act_grad):
    cover = 0.5 * (1.0 + lax.erf(hidden * root_half))
    activated = (hidden * cover).astype(BF16)
    slope = cover + hidden * jnp.exp(-0.5 * hidden * hidden) * inv_root_tau
    return activated, (act_grad * slope).astype(BF16)


def weight_grad_terms(which, weight_in, weight_out, scale, normed, cotangents, aligned):
    rows = normed.shape[1]
    line = len(cotangents)
    mixed_grad = jnp.concatenate(
        [(scale[...] * part[...].astype(F32)).astype(BF16) for part in cotangents], axis=0
    )
    for k in range(line):
        aligned[k * rows : (k + 1) * rows, :] = normed[which[4 + k]]
    across = (((1,), (1,)), ((), ()))
    hidden = lax.dot_general(weight_in[...], aligned[...], across, preferred_element_type=F32)
    act_grad = lax.dot_general(weight_out[...], mixed_grad, across, preferred_element_type=F32)
    activated, hidden_grad = slopes(hidden, act_grad)
    return (
        jnp.dot(hidden_grad, aligned[...], preferred_element_type=F32),
        jnp.dot(activated, mixed_grad, preferred_element_type=F32),
    )


def other_core_terms_kernel(which, weight_in, weight_out, scale, normed, *rest):
    *cotangents, out, aligned = rest
    terms = weight_grad_terms(which, weight_in, weight_out, scale, normed, cotangents, aligned)
    for k in range(2):
        out[0, k] = terms[k].astype(BF16)


def own_core_terms_kernel(which, weight_in, weight_out, scale, normed, got, *rest):
    *cotangents, sent, kept, aligned = rest
    terms = weight_grad_terms(which, weight_in, weight_out, scale, normed, cotangents, aligned)
    step = pl.program_id(0)
    for k in range(2):
        total = terms[k] + got[0, k].astype(F32)

        @pl.when(step == 0)
        def _():
            sent[k] = total.astype(BF16)

        @pl.when(step == 1)
        def _():
            kept[k] = total


def last_sum_kernel(kept, got, in_grad, out_grad):
    for k, out in enumerate((in_grad, out_grad)):
        out[...] = kept[k] + got[k].astype(F32)


def spread_sum_kernel(parts, out):
    total = tree_sum([parts[k].astype(F32) for k in range(parts.shape[0])]).astype(BF16)
    for copy in range(out.shape[0]):
        out[copy] = total


def unpack_kernel(parts, out, small):
    piece = parts.shape[1]
    for k in range(-(-TAP_ROWS // piece)):
        first = k * piece
        length = min(piece, TAP_ROWS - first)
        out[first : first + length, :] = parts[k].astype(F32)[:length, :]
    k = TAP_ROWS // piece
    first = TAP_ROWS - k * piece
    rows = parts[k].astype(F32)
    if first + SUB > piece:
        rows = jnp.concatenate([rows, parts[k + 1].astype(F32)], axis=0)
    small[...] = rows[first : first + SUB, :]


def params(limit=48):
    return pltpu.CompilerParams(vmem_limit_bytes=limit * 1024 * 1024)


def lane_block(rows):
    return pl.BlockSpec((rows, LANES), lambda c: (0, c))


def whole_block(*shape):
    return pl.BlockSpec(shape, lambda *_: (0,) * len(shape))


def neighbours(cells):
    ends = lax.axis_size("row") - 1
    return (
        lax.ppermute(cells, "row", [(i, i + 1) for i in range(ends)]),
        lax.ppermute(cells, "row", [(i + 1, i) for i in range(ends)]),
    )


def conv_cost(rows, channels):
    return pl.CostEstimate(
        flops=rows * channels * TAP_ROWS * 2, bytes_accessed=4 * rows * channels * 4, transcendentals=0
    )


def on_device(
    voxels, dw_kernel, norm_gain, norm_bias, weight_in, weight_out, layer_scale, cotangent
):
    planes, height, breadth, channels = voxels.shape
    rows = planes * height * breadth
    units = weight_in.shape[0]
    count = lax.axis_size("row")
    me = lax.axis_index("row")
    quad = 4
    line = count // quad
    lines = [[quad * k + p for k in range(line)] for p in range(quad)]
    other_core = [(i, i ^ 1) for i in range(count)]
    other_side = [(i, i ^ 2) for i in range(count)]
    tiles = channels // LANES

    own = voxels.reshape(rows, channels)
    upstream = cotangent.reshape(rows, channels)
    gain = norm_gain.reshape(1, channels)
    bias = norm_bias.reshape(1, channels)
    scale = layer_scale.reshape(1, channels)
    core = lax.rem(me, 2).astype(jnp.int32)
    left, right = neighbours(own)
    upstream_line = [upstream] + [
        lax.ppermute(upstream, "row", [(i, (i + quad * k) % count) for i in range(count)])
        for k in range(1, line)
    ]

    spread = pltpu.VMEM((9, planes + KS - 1, PAD, LANES), F32)
    split = pltpu.VMEM((9, KS, SUB, LANES), F32)

    normed, unit, inv = pl.pallas_call(
        functools.partial(forward_kernel, planes, height),
        grid=(tiles,),
        in_specs=[
            lane_block(rows),
            lane_block(rows),
            lane_block(rows),
            lane_block(TAP_ROWS),
            whole_block(1, channels),
            whole_block(1, channels),
        ],
        out_specs=[
            whole_block(line, rows, channels),
            whole_block(rows, channels),
            whole_block(rows, LANES),
        ],
        out_shape=[
            jax.ShapeDtypeStruct((line, rows, channels), BF16),
            jax.ShapeDtypeStruct((rows, channels), F32),
            jax.ShapeDtypeStruct((rows, LANES), F32),
        ],
        scratch_shapes=[spread, split, pltpu.VMEM((tiles, rows, LANES), F32)],
        compiler_params=params(),
        cost_estimate=conv_cost(rows, channels),
        name="forward_conv",
    )(left, own, right, dw_kernel, gain, bias)

    gathered = lax.all_to_all(
        normed, "row", split_axis=0, concat_axis=0, tiled=True, axis_index_groups=lines
    )

    block = 512
    whole = whole_block(rows, channels)
    vector = whole_block(1, channels)
    block_out, conv_grad, small = pl.pallas_call(
        mlp_kernel,
        grid=(units // block,),
        in_specs=[
            pl.BlockSpec((None, rows, channels), lambda f: (0, 0, 0)),
            pl.BlockSpec((block, channels), lambda f: (f, 0)),
            pl.BlockSpec((block, channels), lambda f: (f, 0)),
            whole,
            whole_block(rows, LANES),
            vector,
            vector,
            whole,
            whole,
        ],
        out_specs=[
            whole,
            whole,
            whole_block(SUB, channels),
        ],
        out_shape=[
            jax.ShapeDtypeStruct((rows, channels), BF16),
            jax.ShapeDtypeStruct((rows, channels), BF16),
            jax.ShapeDtypeStruct((SUB, channels), F32),
        ],
        scratch_shapes=[
            pltpu.VMEM((rows, channels), F32),
            pltpu.VMEM((rows, channels), F32),
            pltpu.VMEM((rows, channels), BF16),
        ],
        compiler_params=params(),
        cost_estimate=pl.CostEstimate(
            flops=8 * rows * channels * units,
            bytes_accessed=4 * units * channels,
            transcendentals=2 * rows * units,
        ),
        name="mlp_both_ways",
    )(normed, weight_in, weight_out, unit, inv, gain, scale, own, upstream)

    grad_left, grad_right = neighbours(conv_grad)

    piece = -(-(TAP_ROWS + SUB) // count)
    piece += -piece % SUB
    padded = piece * count
    sums = pl.pallas_call(
        functools.partial(kernel_grad_kernel, planes, height),
        grid=(tiles,),
        in_specs=[
            lane_block(rows),
            lane_block(rows),
            lane_block(rows),
            lane_block(rows),
            lane_block(SUB),
        ],
        out_specs=lane_block(padded),
        out_shape=jax.ShapeDtypeStruct((padded, channels), BF16),
        scratch_shapes=[
            spread,
            pltpu.VMEM((2, KS, SUB * SUB, LANES), F32),
            pltpu.VMEM((9, KS, SUB, LANES), F32),
            pltpu.VMEM((padded, LANES), F32),
        ],
        compiler_params=params(),
        cost_estimate=conv_cost(rows, channels),
        name="kernel_grad_terms",
    )(left, own, right, conv_grad, small)

    share = units // count
    tokens = line * rows
    base = me // quad * quad
    side = lax.rem(me, quad) // 2
    place = lax.rem(me // quad + line - jnp.arange(line, dtype=jnp.int32), line)
    which = jnp.concatenate(
        [
            jnp.stack(
                [
                    base + 1 - core,
                    base + 3 - core,
                    base + 2 - 2 * side + core,
                    base + 2 * side + core,
                ]
            ).astype(jnp.int32),
            place.astype(jnp.int32),
        ]
    )
    terms_cost = pl.CostEstimate(
        flops=16 * tokens * channels * share,
        bytes_accessed=4 * tokens * channels + 8 * share * channels,
        transcendentals=4 * tokens * share,
    )
    pair = (2, 2, share, channels)

    def chunk(at):
        return pl.BlockSpec((share, channels), lambda s, w: (w[s + at], 0))

    sets = [whole_block(1, channels), whole_block(line, rows, channels)]
    cotangents = [whole_block(rows, channels)] * line
    aligned = [pltpu.VMEM((tokens, channels), BF16)]

    which, sums = lax.optimization_barrier((which, sums))
    for_other = pl.pallas_call(
        other_core_terms_kernel,
        grid_spec=pltpu.PrefetchScalarGridSpec(
            num_scalar_prefetch=1,
            grid=(2,),
            in_specs=[chunk(0), chunk(0)] + sets + cotangents,
            out_specs=pl.BlockSpec((1,) + pair[1:], lambda s, w: (s, 0, 0, 0)),
            scratch_shapes=aligned,
        ),
        out_shape=jax.ShapeDtypeStruct(pair, BF16),
        compiler_params=params(),
        cost_estimate=terms_cost,
        name="weight_grads_other_core",
    )(which, weight_in, weight_out, scale, gathered, *upstream_line)
    from_other = lax.ppermute(for_other, "row", other_core)

    scattered = lax.all_to_all(
        sums.reshape(count, piece, channels), "row", split_axis=0, concat_axis=0, tiled=True
    )
    scattered, for_other = lax.optimization_barrier((scattered, for_other))
    copies = pl.pallas_call(
        spread_sum_kernel,
        in_specs=[whole_block(count, piece, channels)],
        out_specs=whole_block(count, piece, channels),
        out_shape=jax.ShapeDtypeStruct((count, piece, channels), BF16),
        grid=(1,),
        compiler_params=params(),
        name="kernel_grad_sum",
    )(scattered)
    totals = lax.all_to_all(copies, "row", split_axis=0, concat_axis=0, tiled=True)

    which, copies = lax.optimization_barrier((which, copies))
    sent, kept = pl.pallas_call(
        own_core_terms_kernel,
        grid_spec=pltpu.PrefetchScalarGridSpec(
            num_scalar_prefetch=1,
            grid=(2,),
            in_specs=[chunk(2), chunk(2)]
            + sets
            + [pl.BlockSpec((1,) + pair[1:], lambda s, w: ((w[s + 2] - w[0] // 4 * 4) // 2, 0, 0, 0))]
            + cotangents,
            out_specs=[whole_block(2, share, channels)] * 2,
            scratch_shapes=aligned,
        ),
        out_shape=[
            jax.ShapeDtypeStruct(pair[1:], BF16),
            jax.ShapeDtypeStruct(pair[1:], F32),
        ],
        compiler_params=params(),
        cost_estimate=terms_cost,
        name="weight_grads_own_core",
    )(which, weight_in, weight_out, scale, gathered, from_other, *upstream_line)
    got = lax.ppermute(sent, "row", other_side)

    conv_own, sent = lax.optimization_barrier((conv_grad, sent))
    voxel_grad = pl.pallas_call(
        functools.partial(input_grad_kernel, planes, height),
        grid=(tiles,),
        in_specs=[
            lane_block(rows),
            lane_block(rows),
            lane_block(rows),
            lane_block(TAP_ROWS),
            lane_block(rows),
        ],
        out_specs=lane_block(rows),
        out_shape=jax.ShapeDtypeStruct((rows, channels), BF16),
        scratch_shapes=[spread, split],
        compiler_params=params(),
        cost_estimate=conv_cost(rows, channels),
        name="input_grad_conv",
    )(grad_left, conv_own, grad_right, dw_kernel, upstream)

    kernel_grad, vectors = pl.pallas_call(
        unpack_kernel,
        grid=(1,),
        in_specs=[whole_block(count, piece, channels)],
        out_specs=[whole_block(TAP_ROWS, channels), whole_block(SUB, channels)],
        out_shape=[
            jax.ShapeDtypeStruct((TAP_ROWS, channels), F32),
            jax.ShapeDtypeStruct((SUB, channels), F32),
        ],
        compiler_params=params(),
        name="kernel_grad_unpack",
    )(totals)

    weight_in_grad, weight_out_grad = pl.pallas_call(
        last_sum_kernel,
        grid=(1,),
        in_specs=[whole_block(2, share, channels)] * 2,
        out_specs=[whole_block(share, channels)] * 2,
        out_shape=[jax.ShapeDtypeStruct((share, channels), F32)] * 2,
        compiler_params=params(),
        name="weight_grads_sum",
    )(kept, got)

    return (
        block_out.reshape(voxels.shape),
        voxel_grad.reshape(voxels.shape),
        kernel_grad,
        vectors[0],
        vectors[1],
        vectors[2],
        weight_in_grad,
        weight_out_grad,
    )


def solution(mesh):
    in_specs = (
        P(("group", "row"), None, None, None),
        P(),
        P(),
        P(),
        P(),
        P(),
        P(),
        P(("group", "row"), None, None, None),
    )
    out_specs = (
        P(("group", "row"), None, None, None),
        P(("group", "row"), None, None, None),
        P("group", None),
        P("group"),
        P("group"),
        P("group"),
        P(("group", "row"), None),
        P(("group", "row"), None),
    )
    return jax.shard_map(
        on_device, mesh=mesh, in_specs=in_specs, out_specs=out_specs, check_vma=False
    )
```

```python
import functools

import jax
import jax.numpy as jnp
from jax import lax
from jax.experimental import pallas as pl
from jax.experimental.pallas import tpu as pltpu
from jax.sharding import PartitionSpec as P

KS = 7
MARGIN = KS // 2
LANES = 128
SUB = 8
PAD = 3 * SUB
TAP_ROWS = KS * KS * KS

root_half = 0.7071067811865476
inv_root_tau = 0.3989422804014327
norm_eps = 1e-06

F32 = jnp.float32
BF16 = jnp.bfloat16


def split_source(v):
    terms = []
    for a, b in ((v[0] + v[2], v[1] + v[3]), (v[2], v[3]), (v[0], v[1])):
        terms += [a + b, b, a]
    return terms


def split_taps(t):
    terms = []
    for s in (
        (t[2], t[3], t[4]),
        (t[4] - t[2], t[5] - t[3], t[6] - t[4]),
        (t[0] - t[2], t[1] - t[3], t[2] - t[4]),
    ):
        terms += [s[1], s[2] - s[1], s[0] - s[1]]
    return terms


def split_grads(g):
    terms = []
    for a, b in ((g[0] + g[2], g[1] + g[3]), (g[0], g[1]), (g[2], g[3])):
        terms += [a + b, a, b]
    return terms


def join_outputs(m):
    pair = [(m[3 * k] + m[3 * k + 1], m[3 * k] + m[3 * k + 2]) for k in range(3)]
    return [
        pair[0][0] + pair[1][0],
        pair[0][1] + pair[1][1],
        pair[0][0] + pair[2][0],
        pair[0][1] + pair[2][1],
    ]


def join_taps(m):
    p, q, r = [
        (m[3 * k + 2], m[3 * k] - m[3 * k + 1] - m[3 * k + 2], m[3 * k + 1]) for k in range(3)
    ]
    return [
        r[0],
        r[1],
        p[0] - q[0] - r[0] + r[2],
        p[1] - q[1] - r[1],
        p[2] - q[2] - r[2] + q[0],
        q[1],
        q[2],
    ]


def tree_sum(terms):
    while len(terms) > 1:
        terms = [
            terms[k] + terms[k + 1] if k + 1 < len(terms) else terms[k]
            for k in range(0, len(terms), 2)
        ]
    return terms[0]


def stage_source(wanted, height, spread):
    row = height * SUB
    for at, (block, x) in enumerate(wanted):
        plane = block[x * row : (x + 1) * row, :].astype(F32)
        lines = [plane[y * SUB : (y + 1) * SUB, :] for y in range(height)]
        for j, term in enumerate(split_source(lines)):
            spread[j, at, SUB : 2 * SUB, :] = term


def rim_planes(left, right, planes):
    wanted = [(left, x) for x in range(planes - MARGIN, planes)]
    return wanted + [(right, x) for x in range(MARGIN)]


def all_planes(left, own, right, planes):
    rim = rim_planes(left, right, planes)
    return rim[:MARGIN] + [(own, x) for x in range(planes)] + rim[MARGIN:]


def clear_rims(spread):
    zeros = jnp.zeros(spread.shape[:2] + (SUB, LANES), F32)
    spread[:, :, :SUB, :] = zeros
    spread[:, :, 2 * SUB :, :] = zeros


def stage_taps(taps, split):
    for dx in range(KS):
        rows = []
        for dy in range(KS):
            first = dx * KS * KS + dy * KS
            if first + SUB <= TAP_ROWS:
                rows.append(taps[first : first + SUB, :])
            else:
                rows.append(pltpu.roll(taps[TAP_ROWS - SUB : TAP_ROWS, :], SUB - 1, 0))
        for j, term in enumerate(split_taps(rows)):
            split[j, dx] = term


REVERSED = (0, 2, 1, 6, 8, 7, 3, 5, 4)


def convolve(spread, split, planes, held, flipped):
    terms = []
    for j in range(9):
        sums = [None] * planes
        for dz in range(KS):
            first = SUB - MARGIN + dz
            source = {x: spread[j, at, first : first + SUB, :] for at, x in enumerate(held)}
            weights = []
            for dx in range(KS):
                if flipped:
                    tap = split[REVERSED[j], KS - 1 - dx, KS - 1 - dz : KS - dz, :]
                else:
                    tap = split[j, dx, dz : dz + 1, :]
                weights.append(jnp.broadcast_to(tap, (SUB, LANES)))
            for x in range(planes):
                part = tree_sum(
                    [source[x + dx] * weights[dx] for dx in range(KS) if x + dx in source]
                )
                sums[x] = part if sums[x] is None else sums[x] + part
        terms.append(sums)
    return [join_outputs([terms[j][x] for j in range(9)]) for x in range(planes)]


def own_conv_kernel(planes, height, own, taps, out, split, spread):
    @pl.when(pl.program_id(0) == 0)
    def _():
        clear_rims(spread)

    stage_source([(own, x) for x in range(planes)], height, spread)
    stage_taps(taps, split)
    rows = convolve(spread, split, planes, range(MARGIN, MARGIN + planes), False)
    for x in range(planes):
        for y in range(height):
            at = (x * height + y) * SUB
            out[at : at + SUB, :] = rows[x][y]


def rim_conv_kernel(
    planes, height, left, right, split, partial, gain, bias, normed, unit, inv, spread, conv
):
    step = pl.program_id(0)

    @pl.when(step == 0)
    def _():
        clear_rims(spread)

    stage_source(rim_planes(left, right, planes), height, spread)
    held = list(range(MARGIN)) + list(range(MARGIN + planes, 2 * MARGIN + planes))
    rows = convolve(spread, split, planes, held, False)
    for x in range(planes):
        for y in range(height):
            at = (x * height + y) * SUB
            conv[step, at : at + SUB, :] = rows[x][y] + partial[at : at + SUB, :]

    @pl.when(step == pl.num_programs(0) - 1)
    def _():
        tiles = conv.shape[0]
        channels = tiles * LANES
        parts = [conv[k] for k in range(tiles)]
        average = jnp.sum(tree_sum(parts), axis=1, keepdims=True) * (1.0 / channels)
        parts = [part - average for part in parts]
        variance = jnp.sum(
            tree_sum([part * part for part in parts]), axis=1, keepdims=True
        ) * (1.0 / channels)
        inverse = lax.rsqrt(variance + norm_eps)
        inv[...] = jnp.broadcast_to(inverse, inv.shape)
        for k in range(tiles):
            lanes = slice(k * LANES, (k + 1) * LANES)
            value = parts[k] * inverse
            unit[:, lanes] = value
            whole = (value * gain[:, lanes] + bias[:, lanes]).astype(BF16)
            for copy in range(normed.shape[0]):
                normed[copy, :, lanes] = whole


def input_grad_kernel(planes, height, left, own, right, split, cotangent, out, spread):
    @pl.when(pl.program_id(0) == 0)
    def _():
        clear_rims(spread)

    stage_source(all_planes(left, own, right, planes), height, spread)
    rows = convolve(spread, split, planes, range(2 * MARGIN + planes), True)
    for x in range(planes):
        at = x * height * SUB
        whole = jnp.concatenate(rows[x], axis=0)
        upstream = cotangent[at : at + height * SUB, :].astype(F32)
        out[at : at + height * SUB, :] = (upstream + whole).astype(BF16)


def kernel_grad_kernel(
    planes, height, left, own, right, grads, small, out, spread, products, joined, flat
):
    @pl.when(pl.program_id(0) == 0)
    def _():
        clear_rims(spread)
        products[...] = jnp.zeros(products.shape, F32)
        flat[...] = jnp.zeros(flat.shape, F32)

    stage_source(all_planes(left, own, right, planes), height, spread)
    upstream = []
    for x in range(planes):
        plane = grads[x * height * SUB : (x + 1) * height * SUB, :].astype(F32)
        upstream.append(
            split_grads([plane[y * SUB : (y + 1) * SUB, :] for y in range(height)])
        )
    for j in range(9):
        for dz in range(KS):
            first = SUB - MARGIN + dz
            source = [
                spread[j, x, first : first + SUB, :] for x in range(planes + KS - 1)
            ]
            for dx in range(KS):
                products[j % 2, dx, dz * SUB : (dz + 1) * SUB, :] = tree_sum(
                    [source[x + dx] * upstream[x][j] for x in range(planes)]
                )
        for dx in range(KS):
            joined[j, dx] = tree_sum(
                [products[j % 2, dx, pl.ds(s, SUB, stride=SUB), :] for s in range(SUB)]
            )
    for dx in range(KS):
        for dy, tile in enumerate(join_taps([joined[j, dx] for j in range(9)])):
            first = dx * KS * KS + dy * KS
            flat[first : first + SUB, :] = tile
    flat[TAP_ROWS : TAP_ROWS + SUB, :] = small[...]
    out[...] = flat[...].astype(out.dtype)


def mlp_kernel(
    normed,
    weight_in,
    weight_out,
    unit,
    inv,
    gain,
    scale,
    voxels,
    cotangent,
    block_out,
    conv_grad,
    small,
    mixed,
    back,
    mixed_grad,
):
    step = pl.program_id(0)

    @pl.when(step == 0)
    def _():
        mixed_grad[...] = (scale[...] * cotangent[...].astype(F32)).astype(BF16)

    hidden = lax.dot_general(
        normed[...], weight_in[...], (((1,), (1,)), ((), ())), preferred_element_type=F32
    )
    act_grad = lax.dot_general(
        mixed_grad[...], weight_out[...], (((1,), (1,)), ((), ())), preferred_element_type=F32
    )
    activated, hidden_grad = slopes(hidden, act_grad)
    forward = jnp.dot(activated, weight_out[...], preferred_element_type=F32)
    backward = jnp.dot(hidden_grad, weight_in[...], preferred_element_type=F32)

    @pl.when(step == 0)
    def _():
        mixed[...] = forward
        back[...] = backward

    @pl.when(step > 0)
    def _():
        mixed[...] += forward
        back[...] += backward

    @pl.when(step == pl.num_programs(0) - 1)
    def _():
        channels = gain.shape[1]
        whole = mixed[...]
        block_out[...] = (voxels[...].astype(F32) + scale[...] * whole).astype(BF16)
        scale_local = jnp.sum(cotangent[...].astype(F32) * whole, axis=0, keepdims=True)
        grad = back[...]
        one = unit[...]
        bias_local = jnp.sum(grad, axis=0, keepdims=True)
        gain_local = jnp.sum(grad * one, axis=0, keepdims=True)
        small[...] = jnp.concatenate(
            [gain_local, bias_local, scale_local, jnp.zeros((SUB - 3, channels), F32)], axis=0
        )
        scaled = grad * gain[...]
        average = jnp.sum(scaled, axis=1, keepdims=True) * (1.0 / channels)
        slant = jnp.sum(scaled * one, axis=1, keepdims=True) * (1.0 / channels)
        conv_grad[...] = (inv[:, :1] * (scaled - average - one * slant)).astype(BF16)


def slopes(hidden, act_grad):
    cover = 0.5 * (1.0 + lax.erf(hidden * root_half))
    activated = (hidden * cover).astype(BF16)
    slope = cover + hidden * jnp.exp(-0.5 * hidden * hidden) * inv_root_tau
    return activated, (act_grad * slope).astype(BF16)


def weight_grad_terms(which, weight_in, weight_out, scale, normed, cotangents, aligned):
    rows = normed.shape[1]
    line = len(cotangents)
    mixed_grad = jnp.concatenate(
        [(scale[...] * part[...].astype(F32)).astype(BF16) for part in cotangents], axis=0
    )
    for k in range(line):
        aligned[k * rows : (k + 1) * rows, :] = normed[which[4 + k]]
    across = (((1,), (1,)), ((), ()))
    hidden = lax.dot_general(weight_in[...], aligned[...], across, preferred_element_type=F32)
    act_grad = lax.dot_general(weight_out[...], mixed_grad, across, preferred_element_type=F32)
    activated, hidden_grad = slopes(hidden, act_grad)
    return (
        jnp.dot(hidden_grad, aligned[...], preferred_element_type=F32),
        jnp.dot(activated, mixed_grad, preferred_element_type=F32),
    )


def other_core_terms_kernel(which, weight_in, weight_out, scale, normed, *rest):
    *cotangents, out, aligned = rest
    terms = weight_grad_terms(which, weight_in, weight_out, scale, normed, cotangents, aligned)
    for k in range(2):
        out[0, k] = terms[k].astype(BF16)


def own_core_terms_kernel(which, weight_in, weight_out, scale, normed, got, *rest):
    *cotangents, sent, kept, aligned = rest
    terms = weight_grad_terms(which, weight_in, weight_out, scale, normed, cotangents, aligned)
    step = pl.program_id(0)
    for k in range(2):
        total = terms[k] + got[0, k].astype(F32)

        @pl.when(step == 0)
        def _():
            sent[k] = total.astype(BF16)

        @pl.when(step == 1)
        def _():
            kept[k] = total


def last_sum_kernel(kept, got, in_grad, out_grad):
    for k, out in enumerate((in_grad, out_grad)):
        out[...] = kept[k] + got[k].astype(F32)


def spread_sum_kernel(parts, out):
    total = tree_sum([parts[k].astype(F32) for k in range(parts.shape[0])]).astype(BF16)
    for copy in range(out.shape[0]):
        out[copy] = total


def unpack_kernel(parts, out, small):
    piece = parts.shape[1]
    for k in range(-(-TAP_ROWS // piece)):
        first = k * piece
        length = min(piece, TAP_ROWS - first)
        out[first : first + length, :] = parts[k].astype(F32)[:length, :]
    k = TAP_ROWS // piece
    first = TAP_ROWS - k * piece
    rows = parts[k].astype(F32)
    if first + SUB > piece:
        rows = jnp.concatenate([rows, parts[k + 1].astype(F32)], axis=0)
    small[...] = rows[first : first + SUB, :]


def params(limit=48):
    return pltpu.CompilerParams(vmem_limit_bytes=limit * 1024 * 1024)


def lane_block(rows):
    return pl.BlockSpec((rows, LANES), lambda c: (0, c))


def whole_block(*shape):
    return pl.BlockSpec(shape, lambda *_: (0,) * len(shape))


def neighbours(cells):
    ends = lax.axis_size("row") - 1
    return (
        lax.ppermute(cells, "row", [(i, i + 1) for i in range(ends)]),
        lax.ppermute(cells, "row", [(i + 1, i) for i in range(ends)]),
    )


def conv_cost(rows, channels):
    return pl.CostEstimate(
        flops=rows * channels * TAP_ROWS * 2, bytes_accessed=4 * rows * channels * 4, transcendentals=0
    )


def on_device(
    voxels, dw_kernel, norm_gain, norm_bias, weight_in, weight_out, layer_scale, cotangent
):
    planes, height, breadth, channels = voxels.shape
    rows = planes * height * breadth
    units = weight_in.shape[0]
    count = lax.axis_size("row")
    me = lax.axis_index("row")
    quad = 4
    line = count // quad
    lines = [[quad * k + p for k in range(line)] for p in range(quad)]
    other_core = [(i, i ^ 1) for i in range(count)]
    other_side = [(i, i ^ 2) for i in range(count)]
    tiles = channels // LANES

    own = voxels.reshape(rows, channels)
    upstream = cotangent.reshape(rows, channels)
    gain = norm_gain.reshape(1, channels)
    bias = norm_bias.reshape(1, channels)
    scale = layer_scale.reshape(1, channels)
    core = lax.rem(me, 2).astype(jnp.int32)
    left, right = neighbours(own)

    def next_in_line(cells):
        return lax.ppermute(cells, "row", [(i, (i + quad) % count) for i in range(count)])

    upstream_line = [upstream, next_in_line(upstream)]

    def spread_of(held):
        return pltpu.VMEM((9, held, PAD, LANES), F32)

    split_block = pl.BlockSpec((None, 9, KS, SUB, LANES), lambda c: (c, 0, 0, 0, 0))
    partial, split = pl.pallas_call(
        functools.partial(own_conv_kernel, planes, height),
        grid=(tiles,),
        in_specs=[lane_block(rows), lane_block(TAP_ROWS)],
        out_specs=[lane_block(rows), split_block],
        out_shape=[
            jax.ShapeDtypeStruct((rows, channels), F32),
            jax.ShapeDtypeStruct((tiles, 9, KS, SUB, LANES), F32),
        ],
        scratch_shapes=[spread_of(planes)],
        compiler_params=params(),
        cost_estimate=conv_cost(rows, channels // 2),
        name="own_conv",
    )(own, dw_kernel)

    left, right, partial, upstream_line[-1] = lax.optimization_barrier(
        (left, right, partial, upstream_line[-1])
    )
    upstream_line.append(next_in_line(upstream_line[-1]))
    normed, unit, inv = pl.pallas_call(
        functools.partial(rim_conv_kernel, planes, height),
        grid=(tiles,),
        in_specs=[
            lane_block(rows),
            lane_block(rows),
            split_block,
            lane_block(rows),
            whole_block(1, channels),
            whole_block(1, channels),
        ],
        out_specs=[
            whole_block(line, rows, channels),
            whole_block(rows, channels),
            whole_block(rows, LANES),
        ],
        out_shape=[
            jax.ShapeDtypeStruct((line, rows, channels), BF16),
            jax.ShapeDtypeStruct((rows, channels), F32),
            jax.ShapeDtypeStruct((rows, LANES), F32),
        ],
        scratch_shapes=[spread_of(2 * MARGIN), pltpu.VMEM((tiles, rows, LANES), F32)],
        compiler_params=params(),
        cost_estimate=conv_cost(rows, channels // 2),
        name="rim_conv",
    )(left, right, split, partial, gain, bias)

    gathered = lax.all_to_all(
        normed, "row", split_axis=0, concat_axis=0, tiled=True, axis_index_groups=lines
    )

    unit, upstream_line[-1] = lax.optimization_barrier((unit, upstream_line[-1]))
    for _ in range(3, line):
        upstream_line.append(next_in_line(upstream_line[-1]))

    block = 512
    whole = whole_block(rows, channels)
    vector = whole_block(1, channels)
    block_out, conv_grad, small = pl.pallas_call(
        mlp_kernel,
        grid=(units // block,),
        in_specs=[
            pl.BlockSpec((None, rows, channels), lambda f: (0, 0, 0)),
            pl.BlockSpec((block, channels), lambda f: (f, 0)),
            pl.BlockSpec((block, channels), lambda f: (f, 0)),
            whole,
            whole_block(rows, LANES),
            vector,
            vector,
            whole,
            whole,
        ],
        out_specs=[
            whole,
            whole,
            whole_block(SUB, channels),
        ],
        out_shape=[
            jax.ShapeDtypeStruct((rows, channels), BF16),
            jax.ShapeDtypeStruct((rows, channels), BF16),
            jax.ShapeDtypeStruct((SUB, channels), F32),
        ],
        scratch_shapes=[
            pltpu.VMEM((rows, channels), F32),
            pltpu.VMEM((rows, channels), F32),
            pltpu.VMEM((rows, channels), BF16),
        ],
        compiler_params=params(),
        cost_estimate=pl.CostEstimate(
            flops=8 * rows * channels * units,
            bytes_accessed=4 * units * channels,
            transcendentals=2 * rows * units,
        ),
        name="mlp_both_ways",
    )(normed, weight_in, weight_out, unit, inv, gain, scale, own, upstream)

    grad_left, grad_right = neighbours(conv_grad)

    small, upstream_line[-1] = lax.optimization_barrier((small, upstream_line[-1]))
    piece = -(-(TAP_ROWS + SUB) // count)
    piece += -piece % SUB
    padded = piece * count
    sums = pl.pallas_call(
        functools.partial(kernel_grad_kernel, planes, height),
        grid=(tiles,),
        in_specs=[
            lane_block(rows),
            lane_block(rows),
            lane_block(rows),
            lane_block(rows),
            lane_block(SUB),
        ],
        out_specs=lane_block(padded),
        out_shape=jax.ShapeDtypeStruct((padded, channels), BF16),
        scratch_shapes=[
            spread_of(2 * MARGIN + planes),
            pltpu.VMEM((2, KS, SUB * SUB, LANES), F32),
            pltpu.VMEM((9, KS, SUB, LANES), F32),
            pltpu.VMEM((padded, LANES), F32),
        ],
        compiler_params=params(),
        cost_estimate=conv_cost(rows, channels),
        name="kernel_grad_terms",
    )(left, own, right, conv_grad, small)

    share = units // count
    tokens = line * rows
    base = me // quad * quad
    side = lax.rem(me, quad) // 2
    place = lax.rem(me // quad + line - jnp.arange(line, dtype=jnp.int32), line)
    which = jnp.concatenate(
        [
            jnp.stack(
                [
                    base + 1 - core,
                    base + 3 - core,
                    base + 2 - 2 * side + core,
                    base + 2 * side + core,
                ]
            ).astype(jnp.int32),
            place.astype(jnp.int32),
        ]
    )
    terms_cost = pl.CostEstimate(
        flops=16 * tokens * channels * share,
        bytes_accessed=4 * tokens * channels + 8 * share * channels,
        transcendentals=4 * tokens * share,
    )
    pair = (2, 2, share, channels)

    def chunk(at):
        return pl.BlockSpec((share, channels), lambda s, w: (w[s + at], 0))

    sets = [whole_block(1, channels), whole_block(line, rows, channels)]
    cotangents = [whole_block(rows, channels)] * line
    aligned = [pltpu.VMEM((tokens, channels), BF16)]

    which, sums, grad_left, grad_right = lax.optimization_barrier(
        (which, sums, grad_left, grad_right)
    )
    for_other = pl.pallas_call(
        other_core_terms_kernel,
        grid_spec=pltpu.PrefetchScalarGridSpec(
            num_scalar_prefetch=1,
            grid=(2,),
            in_specs=[chunk(0), chunk(0)] + sets + cotangents,
            out_specs=pl.BlockSpec((1,) + pair[1:], lambda s, w: (s, 0, 0, 0)),
            scratch_shapes=aligned,
        ),
        out_shape=jax.ShapeDtypeStruct(pair, BF16),
        compiler_params=params(),
        cost_estimate=terms_cost,
        name="weight_grads_other_core",
    )(which, weight_in, weight_out, scale, gathered, *upstream_line)
    from_other = lax.ppermute(for_other, "row", other_core)

    scattered = lax.all_to_all(
        sums.reshape(count, piece, channels), "row", split_axis=0, concat_axis=0, tiled=True
    )
    scattered, for_other = lax.optimization_barrier((scattered, for_other))
    copies = pl.pallas_call(
        spread_sum_kernel,
        in_specs=[whole_block(count, piece, channels)],
        out_specs=whole_block(count, piece, channels),
        out_shape=jax.ShapeDtypeStruct((count, piece, channels), BF16),
        grid=(1,),
        compiler_params=params(),
        name="kernel_grad_sum",
    )(scattered)
    totals = lax.all_to_all(copies, "row", split_axis=0, concat_axis=0, tiled=True)

    which, copies = lax.optimization_barrier((which, copies))
    sent, kept = pl.pallas_call(
        own_core_terms_kernel,
        grid_spec=pltpu.PrefetchScalarGridSpec(
            num_scalar_prefetch=1,
            grid=(2,),
            in_specs=[chunk(2), chunk(2)]
            + sets
            + [pl.BlockSpec((1,) + pair[1:], lambda s, w: ((w[s + 2] - w[0] // 4 * 4) // 2, 0, 0, 0))]
            + cotangents,
            out_specs=[whole_block(2, share, channels)] * 2,
            scratch_shapes=aligned,
        ),
        out_shape=[
            jax.ShapeDtypeStruct(pair[1:], BF16),
            jax.ShapeDtypeStruct(pair[1:], F32),
        ],
        compiler_params=params(),
        cost_estimate=terms_cost,
        name="weight_grads_own_core",
    )(which, weight_in, weight_out, scale, gathered, from_other, *upstream_line)
    got = lax.ppermute(sent, "row", other_side)

    conv_own, sent = lax.optimization_barrier((conv_grad, sent))
    voxel_grad = pl.pallas_call(
        functools.partial(input_grad_kernel, planes, height),
        grid=(tiles,),
        in_specs=[
            lane_block(rows),
            lane_block(rows),
            lane_block(rows),
            split_block,
            lane_block(rows),
        ],
        out_specs=lane_block(rows),
        out_shape=jax.ShapeDtypeStruct((rows, channels), BF16),
        scratch_shapes=[spread_of(2 * MARGIN + planes)],
        compiler_params=params(),
        cost_estimate=conv_cost(rows, channels),
        name="input_grad_conv",
    )(grad_left, conv_own, grad_right, split, upstream)

    kernel_grad, vectors = pl.pallas_call(
        unpack_kernel,
        grid=(1,),
        in_specs=[whole_block(count, piece, channels)],
        out_specs=[whole_block(TAP_ROWS, channels), whole_block(SUB, channels)],
        out_shape=[
            jax.ShapeDtypeStruct((TAP_ROWS, channels), F32),
            jax.ShapeDtypeStruct((SUB, channels), F32),
        ],
        compiler_params=params(),
        name="kernel_grad_unpack",
    )(totals)

    weight_in_grad, weight_out_grad = pl.pallas_call(
        last_sum_kernel,
        grid=(1,),
        in_specs=[whole_block(2, share, channels)] * 2,
        out_specs=[whole_block(share, channels)] * 2,
        out_shape=[jax.ShapeDtypeStruct((share, channels), F32)] * 2,
        compiler_params=params(),
        name="weight_grads_sum",
    )(kept, got)

    return (
        block_out.reshape(voxels.shape),
        voxel_grad.reshape(voxels.shape),
        kernel_grad,
        vectors[0],
        vectors[1],
        vectors[2],
        weight_in_grad,
        weight_out_grad,
    )


def solution(mesh):
    in_specs = (
        P(("group", "row"), None, None, None),
        P(),
        P(),
        P(),
        P(),
        P(),
        P(),
        P(("group", "row"), None, None, None),
    )
    out_specs = (
        P(("group", "row"), None, None, None),
        P(("group", "row"), None, None, None),
        P("group", None),
        P("group"),
        P("group"),
        P("group"),
        P(("group", "row"), None),
        P(("group", "row"), None),
    )
    return jax.shard_map(
        on_device, mesh=mesh, in_specs=in_specs, out_specs=out_specs, check_vma=False
    )
```

```python
import functools

import jax
import jax.numpy as jnp
from jax import lax
from jax.experimental import pallas as pl
from jax.experimental.pallas import tpu as pltpu
from jax.sharding import PartitionSpec as P

KS = 7
MARGIN = KS // 2
LANES = 128
SUB = 8
PAD = 3 * SUB
TAP_ROWS = KS * KS * KS

root_half = 0.7071067811865476
inv_root_tau = 0.3989422804014327
norm_eps = 1e-06

F32 = jnp.float32
BF16 = jnp.bfloat16


def split_source(v):
    terms = []
    for a, b in ((v[0] + v[2], v[1] + v[3]), (v[2], v[3]), (v[0], v[1])):
        terms += [a + b, b, a]
    return terms


def split_taps(t):
    terms = []
    for s in (
        (t[2], t[3], t[4]),
        (t[4] - t[2], t[5] - t[3], t[6] - t[4]),
        (t[0] - t[2], t[1] - t[3], t[2] - t[4]),
    ):
        terms += [s[1], s[2] - s[1], s[0] - s[1]]
    return terms


def split_grads(g):
    terms = []
    for a, b in ((g[0] + g[2], g[1] + g[3]), (g[0], g[1]), (g[2], g[3])):
        terms += [a + b, a, b]
    return terms


def join_outputs(m):
    pair = [(m[3 * k] + m[3 * k + 1], m[3 * k] + m[3 * k + 2]) for k in range(3)]
    return [
        pair[0][0] + pair[1][0],
        pair[0][1] + pair[1][1],
        pair[0][0] + pair[2][0],
        pair[0][1] + pair[2][1],
    ]


def join_taps(m):
    p, q, r = [
        (m[3 * k + 2], m[3 * k] - m[3 * k + 1] - m[3 * k + 2], m[3 * k + 1]) for k in range(3)
    ]
    return [
        r[0],
        r[1],
        p[0] - q[0] - r[0] + r[2],
        p[1] - q[1] - r[1],
        p[2] - q[2] - r[2] + q[0],
        q[1],
        q[2],
    ]


def tree_sum(terms):
    while len(terms) > 1:
        terms = [
            terms[k] + terms[k + 1] if k + 1 < len(terms) else terms[k]
            for k in range(0, len(terms), 2)
        ]
    return terms[0]


def stage_source(wanted, height, spread):
    row = height * SUB
    for at, (block, x) in enumerate(wanted):
        plane = block[x * row : (x + 1) * row, :].astype(F32)
        lines = [plane[y * SUB : (y + 1) * SUB, :] for y in range(height)]
        for j, term in enumerate(split_source(lines)):
            spread[j, at, SUB : 2 * SUB, :] = term


def rim_planes(left, right, planes):
    wanted = [(left, x) for x in range(planes - MARGIN, planes)]
    return wanted + [(right, x) for x in range(MARGIN)]


def all_planes(left, own, right, planes):
    rim = rim_planes(left, right, planes)
    return rim[:MARGIN] + [(own, x) for x in range(planes)] + rim[MARGIN:]


def by_core(core, inner, outer, stage):
    @pl.when(core[0] == 0)
    def _():
        stage(outer, inner)

    @pl.when(core[0] != 0)
    def _():
        stage(inner, outer)


def clear_rims(spread):
    zeros = jnp.zeros(spread.shape[:2] + (SUB, LANES), F32)
    spread[:, :, :SUB, :] = zeros
    spread[:, :, 2 * SUB :, :] = zeros


def stage_taps(taps, split):
    for dx in range(KS):
        rows = []
        for dy in range(KS):
            first = dx * KS * KS + dy * KS
            if first + SUB <= TAP_ROWS:
                rows.append(taps[first : first + SUB, :])
            else:
                rows.append(pltpu.roll(taps[TAP_ROWS - SUB : TAP_ROWS, :], SUB - 1, 0))
        for j, term in enumerate(split_taps(rows)):
            split[j, dx] = term


REVERSED = (0, 2, 1, 6, 8, 7, 3, 5, 4)


def convolve(spread, split, planes, held, flipped):
    terms = []
    for j in range(9):
        sums = [None] * planes
        for dz in range(KS):
            first = SUB - MARGIN + dz
            source = {x: spread[j, at, first : first + SUB, :] for at, x in enumerate(held)}
            weights = []
            for dx in range(KS):
                if flipped:
                    tap = split[REVERSED[j], KS - 1 - dx, KS - 1 - dz : KS - dz, :]
                else:
                    tap = split[j, dx, dz : dz + 1, :]
                weights.append(jnp.broadcast_to(tap, (SUB, LANES)))
            for x in range(planes):
                part = tree_sum(
                    [source[x + dx] * weights[dx] for dx in range(KS) if x + dx in source]
                )
                sums[x] = part if sums[x] is None else sums[x] + part
        terms.append(sums)
    return [join_outputs([terms[j][x] for j in range(9)]) for x in range(planes)]


def own_conv_kernel(planes, height, own, taps, out, split, spread):
    @pl.when(pl.program_id(0) == 0)
    def _():
        clear_rims(spread)

    stage_source([(own, x) for x in range(planes)], height, spread)
    stage_taps(taps, split)
    rows = convolve(spread, split, planes, range(MARGIN, MARGIN + planes), False)
    for x in range(planes):
        for y in range(height):
            at = (x * height + y) * SUB
            out[at : at + SUB, :] = rows[x][y]


def rim_conv_kernel(
    planes, height, core, inner, outer, split, partial, vectors, normed, unit, inv, spread, conv
):
    step = pl.program_id(0)

    @pl.when(step == 0)
    def _():
        clear_rims(spread)

    def stage(left, right):
        stage_source(rim_planes(left, right, planes), height, spread)

    by_core(core, inner, outer, stage)
    held = list(range(MARGIN)) + list(range(MARGIN + planes, 2 * MARGIN + planes))
    rows = convolve(spread, split, planes, held, False)
    for x in range(planes):
        for y in range(height):
            at = (x * height + y) * SUB
            conv[step, at : at + SUB, :] = rows[x][y] + partial[at : at + SUB, :]

    @pl.when(step == pl.num_programs(0) - 1)
    def _():
        tiles = conv.shape[0]
        channels = tiles * LANES
        parts = [conv[k] for k in range(tiles)]
        average = jnp.sum(tree_sum(parts), axis=1, keepdims=True) * (1.0 / channels)
        parts = [part - average for part in parts]
        variance = jnp.sum(
            tree_sum([part * part for part in parts]), axis=1, keepdims=True
        ) * (1.0 / channels)
        inverse = lax.rsqrt(variance + norm_eps)
        inv[...] = jnp.broadcast_to(inverse, inv.shape)
        for k in range(tiles):
            lanes = slice(k * LANES, (k + 1) * LANES)
            value = parts[k] * inverse
            unit[:, lanes] = value
            whole = (value * vectors[0:1, lanes] + vectors[1:2, lanes]).astype(BF16)
            for copy in range(normed.shape[0]):
                normed[copy, :, lanes] = whole


def input_grad_kernel(planes, height, core, inner, own, outer, split, cotangent, out, spread):
    @pl.when(pl.program_id(0) == 0)
    def _():
        clear_rims(spread)

    def stage(left, right):
        stage_source(all_planes(left, own, right, planes), height, spread)

    by_core(core, inner, outer, stage)
    rows = convolve(spread, split, planes, range(2 * MARGIN + planes), True)
    for x in range(planes):
        at = x * height * SUB
        whole = jnp.concatenate(rows[x], axis=0)
        upstream = cotangent[at : at + height * SUB, :].astype(F32)
        out[at : at + height * SUB, :] = (upstream + whole).astype(BF16)


def kernel_grad_kernel(
    planes, height, core, inner, own, outer, grads, small, out, spread, products, joined, flat
):
    @pl.when(pl.program_id(0) == 0)
    def _():
        clear_rims(spread)
        products[...] = jnp.zeros(products.shape, F32)
        flat[...] = jnp.zeros(flat.shape, F32)

    def stage(left, right):
        stage_source(all_planes(left, own, right, planes), height, spread)

    by_core(core, inner, outer, stage)
    upstream = []
    for x in range(planes):
        plane = grads[x * height * SUB : (x + 1) * height * SUB, :].astype(F32)
        upstream.append(
            split_grads([plane[y * SUB : (y + 1) * SUB, :] for y in range(height)])
        )
    for j in range(9):
        for dz in range(KS):
            first = SUB - MARGIN + dz
            source = [
                spread[j, x, first : first + SUB, :] for x in range(planes + KS - 1)
            ]
            for dx in range(KS):
                products[j % 2, dx, dz * SUB : (dz + 1) * SUB, :] = tree_sum(
                    [source[x + dx] * upstream[x][j] for x in range(planes)]
                )
        for dx in range(KS):
            joined[j, dx] = tree_sum(
                [products[j % 2, dx, pl.ds(s, SUB, stride=SUB), :] for s in range(SUB)]
            )
    for dx in range(KS):
        for dy, tile in enumerate(join_taps([joined[j, dx] for j in range(9)])):
            first = dx * KS * KS + dy * KS
            flat[first : first + SUB, :] = tile
    flat[TAP_ROWS : TAP_ROWS + SUB, :] = small[...]
    out[...] = flat[...].astype(out.dtype)


def mlp_kernel(
    normed,
    weight_in,
    weight_out,
    unit,
    inv,
    vectors,
    voxels,
    cotangent,
    block_out,
    conv_grad,
    small,
    mixed,
    back,
    mixed_grad,
):
    step = pl.program_id(0)
    gain = vectors[0:1, :]
    scale = vectors[2:3, :]

    @pl.when(step == 0)
    def _():
        mixed_grad[...] = (scale * cotangent[...].astype(F32)).astype(BF16)

    hidden = lax.dot_general(
        normed[...], weight_in[...], (((1,), (1,)), ((), ())), preferred_element_type=F32
    )
    act_grad = lax.dot_general(
        mixed_grad[...], weight_out[...], (((1,), (1,)), ((), ())), preferred_element_type=F32
    )
    activated, hidden_grad = slopes(hidden, act_grad)
    forward = jnp.dot(activated, weight_out[...], preferred_element_type=F32)
    backward = jnp.dot(hidden_grad, weight_in[...], preferred_element_type=F32)

    @pl.when(step == 0)
    def _():
        mixed[...] = forward
        back[...] = backward

    @pl.when(step > 0)
    def _():
        mixed[...] += forward
        back[...] += backward

    @pl.when(step == pl.num_programs(0) - 1)
    def _():
        channels = gain.shape[1]
        whole = mixed[...]
        block_out[...] = (voxels[...].astype(F32) + scale * whole).astype(BF16)
        scale_local = jnp.sum(cotangent[...].astype(F32) * whole, axis=0, keepdims=True)
        grad = back[...]
        one = unit[...]
        bias_local = jnp.sum(grad, axis=0, keepdims=True)
        gain_local = jnp.sum(grad * one, axis=0, keepdims=True)
        small[...] = jnp.concatenate(
            [gain_local, bias_local, scale_local, jnp.zeros((SUB - 3, channels), F32)], axis=0
        )
        scaled = grad * gain
        average = jnp.sum(scaled, axis=1, keepdims=True) * (1.0 / channels)
        slant = jnp.sum(scaled * one, axis=1, keepdims=True) * (1.0 / channels)
        conv_grad[...] = (inv[:, :1] * (scaled - average - one * slant)).astype(BF16)


def slopes(hidden, act_grad):
    cover = 0.5 * (1.0 + lax.erf(hidden * root_half))
    activated = (hidden * cover).astype(BF16)
    slope = cover + hidden * jnp.exp(-0.5 * hidden * hidden) * inv_root_tau
    return activated, (act_grad * slope).astype(BF16)


def weight_grad_terms(which, weight_in, weight_out, vectors, normed, cotangents, aligned):
    rows = normed.shape[1]
    line = len(cotangents)
    mixed_grad = jnp.concatenate(
        [(vectors[2:3, :] * part[...].astype(F32)).astype(BF16) for part in cotangents], axis=0
    )
    for k in range(line):
        aligned[k * rows : (k + 1) * rows, :] = normed[which[4 + k]]
    across = (((1,), (1,)), ((), ()))
    hidden = lax.dot_general(weight_in[...], aligned[...], across, preferred_element_type=F32)
    act_grad = lax.dot_general(weight_out[...], mixed_grad, across, preferred_element_type=F32)
    activated, hidden_grad = slopes(hidden, act_grad)
    return (
        jnp.dot(hidden_grad, aligned[...], preferred_element_type=F32),
        jnp.dot(activated, mixed_grad, preferred_element_type=F32),
    )


def other_core_terms_kernel(which, weight_in, weight_out, vectors, normed, *rest):
    *cotangents, out, aligned = rest
    terms = weight_grad_terms(which, weight_in, weight_out, vectors, normed, cotangents, aligned)
    for k in range(2):
        out[0, k] = terms[k].astype(BF16)


def own_core_terms_kernel(which, weight_in, weight_out, vectors, normed, got, *rest):
    *cotangents, sent, kept, aligned = rest
    terms = weight_grad_terms(which, weight_in, weight_out, vectors, normed, cotangents, aligned)
    step = pl.program_id(0)
    for k in range(2):
        total = terms[k] + got[0, k].astype(F32)

        @pl.when(step == 0)
        def _():
            sent[k] = total.astype(BF16)

        @pl.when(step == 1)
        def _():
            kept[k] = total


def last_sum_kernel(kept, got, in_grad, out_grad):
    for k, out in enumerate((in_grad, out_grad)):
        out[...] = kept[k] + got[k].astype(F32)


def spread_sum_kernel(parts, out):
    total = tree_sum([parts[k].astype(F32) for k in range(parts.shape[0])]).astype(BF16)
    for copy in range(out.shape[0]):
        out[copy] = total


def unpack_kernel(parts, out, small):
    piece = parts.shape[1]
    for k in range(-(-TAP_ROWS // piece)):
        first = k * piece
        length = min(piece, TAP_ROWS - first)
        out[first : first + length, :] = parts[k].astype(F32)[:length, :]
    k = TAP_ROWS // piece
    first = TAP_ROWS - k * piece
    rows = parts[k].astype(F32)
    if first + SUB > piece:
        rows = jnp.concatenate([rows, parts[k + 1].astype(F32)], axis=0)
    small[...] = rows[first : first + SUB, :]


def params(limit=24):
    return pltpu.CompilerParams(vmem_limit_bytes=limit * 1024 * 1024)


def lane_block(rows):
    return pl.BlockSpec((rows, LANES), lambda c, *_: (0, c))


def whole_block(*shape):
    return pl.BlockSpec(shape, lambda *_: (0,) * len(shape))


def rims(cells):
    count = lax.axis_size("row")
    between = [(i, i + 1) for i in range(1, count - 1, 2)]
    return (
        lax.ppermute(cells, "row", [(i, i ^ 1) for i in range(count)]),
        lax.ppermute(cells, "row", between + [(j, i) for i, j in between]),
    )


def conv_cost(rows, channels):
    return pl.CostEstimate(
        flops=rows * channels * TAP_ROWS * 2, bytes_accessed=4 * rows * channels * 4, transcendentals=0
    )


def on_device(
    voxels, dw_kernel, norm_gain, norm_bias, weight_in, weight_out, layer_scale, cotangent
):
    planes, height, breadth, channels = voxels.shape
    rows = planes * height * breadth
    units = weight_in.shape[0]
    count = lax.axis_size("row")
    me = lax.axis_index("row")
    quad = 4
    line = count // quad
    lines = [[quad * k + p for k in range(line)] for p in range(quad)]
    other_core = [(i, i ^ 1) for i in range(count)]
    other_side = [(i, i ^ 2) for i in range(count)]
    tiles = channels // LANES

    own = voxels.reshape(rows, channels)
    upstream = cotangent.reshape(rows, channels)
    vectors = jnp.stack([norm_gain, norm_bias, layer_scale])
    core = lax.rem(me, 2).astype(jnp.int32)
    parity = core.reshape(1)

    inner, outer = rims(own)

    def next_in_line(cells):
        return lax.ppermute(cells, "row", [(i, (i + quad) % count) for i in range(count)])

    upstream_line = [upstream, next_in_line(upstream)]

    def spread_of(held):
        return pltpu.VMEM((9, held, PAD, LANES), F32)

    split_block = pl.BlockSpec((None, 9, KS, SUB, LANES), lambda c, *_: (c, 0, 0, 0, 0))
    own, upstream_line[-1] = lax.optimization_barrier((own, upstream_line[-1]))
    upstream_line.append(next_in_line(upstream_line[-1]))
    partial, split = pl.pallas_call(
        functools.partial(own_conv_kernel, planes, height),
        grid=(tiles,),
        in_specs=[lane_block(rows), lane_block(TAP_ROWS)],
        out_specs=[lane_block(rows), split_block],
        out_shape=[
            jax.ShapeDtypeStruct((rows, channels), F32),
            jax.ShapeDtypeStruct((tiles, 9, KS, SUB, LANES), F32),
        ],
        scratch_shapes=[spread_of(planes)],
        compiler_params=params(),
        cost_estimate=conv_cost(rows, channels // 2),
        name="own_conv",
    )(own, dw_kernel)

    partial, upstream_line[-1] = lax.optimization_barrier((partial, upstream_line[-1]))
    for _ in range(3, line):
        upstream_line.append(next_in_line(upstream_line[-1]))
    normed, unit, inv = pl.pallas_call(
        functools.partial(rim_conv_kernel, planes, height),
        grid_spec=pltpu.PrefetchScalarGridSpec(
            num_scalar_prefetch=1,
            grid=(tiles,),
            in_specs=[
                lane_block(rows),
                lane_block(rows),
                split_block,
                lane_block(rows),
                whole_block(3, channels),
            ],
            out_specs=[
                whole_block(line, rows, channels),
                whole_block(rows, channels),
                whole_block(rows, LANES),
            ],
            scratch_shapes=[spread_of(2 * MARGIN), pltpu.VMEM((tiles, rows, LANES), F32)],
        ),
        out_shape=[
            jax.ShapeDtypeStruct((line, rows, channels), BF16),
            jax.ShapeDtypeStruct((rows, channels), F32),
            jax.ShapeDtypeStruct((rows, LANES), F32),
        ],
        compiler_params=params(),
        cost_estimate=conv_cost(rows, channels // 2),
        name="rim_conv",
    )(parity, inner, outer, split, partial, vectors)

    copies_out, upstream_line[-1] = lax.optimization_barrier((normed, upstream_line[-1]))
    gathered = lax.all_to_all(
        copies_out, "row", split_axis=0, concat_axis=0, tiled=True, axis_index_groups=lines
    )

    block = 512
    whole = whole_block(rows, channels)
    block_out, conv_grad, small = pl.pallas_call(
        mlp_kernel,
        grid=(units // block,),
        in_specs=[
            pl.BlockSpec((None, rows, channels), lambda f: (0, 0, 0)),
            pl.BlockSpec((block, channels), lambda f: (f, 0)),
            pl.BlockSpec((block, channels), lambda f: (f, 0)),
            whole,
            whole_block(rows, LANES),
            whole_block(3, channels),
            whole,
            whole,
        ],
        out_specs=[
            whole,
            whole,
            whole_block(SUB, channels),
        ],
        out_shape=[
            jax.ShapeDtypeStruct((rows, channels), BF16),
            jax.ShapeDtypeStruct((rows, channels), BF16),
            jax.ShapeDtypeStruct((SUB, channels), F32),
        ],
        scratch_shapes=[
            pltpu.VMEM((rows, channels), F32),
            pltpu.VMEM((rows, channels), F32),
            pltpu.VMEM((rows, channels), BF16),
        ],
        compiler_params=params(),
        cost_estimate=pl.CostEstimate(
            flops=8 * rows * channels * units,
            bytes_accessed=4 * units * channels,
            transcendentals=2 * rows * units,
        ),
        name="mlp_both_ways",
    )(normed, weight_in, weight_out, unit, inv, vectors, own, upstream)

    piece = -(-(TAP_ROWS + SUB) // count)
    piece += -piece % SUB
    padded = piece * count
    sums = pl.pallas_call(
        functools.partial(kernel_grad_kernel, planes, height),
        grid_spec=pltpu.PrefetchScalarGridSpec(
            num_scalar_prefetch=1,
            grid=(tiles,),
            in_specs=[
                lane_block(rows),
                lane_block(rows),
                lane_block(rows),
                lane_block(rows),
                lane_block(SUB),
            ],
            out_specs=lane_block(padded),
            scratch_shapes=[
                spread_of(2 * MARGIN + planes),
                pltpu.VMEM((2, KS, SUB * SUB, LANES), F32),
                pltpu.VMEM((9, KS, SUB, LANES), F32),
                pltpu.VMEM((padded, LANES), F32),
            ],
        ),
        out_shape=jax.ShapeDtypeStruct((padded, channels), BF16),
        compiler_params=params(),
        cost_estimate=conv_cost(rows, channels),
        name="kernel_grad_terms",
    )(parity, inner, own, outer, conv_grad, small)
    scattered = lax.all_to_all(
        sums.reshape(count, piece, channels), "row", split_axis=0, concat_axis=0, tiled=True
    )

    conv_grad, sums = lax.optimization_barrier((conv_grad, sums))
    grad_inner, grad_outer = rims(conv_grad)

    share = units // count
    tokens = line * rows
    base = me // quad * quad
    side = lax.rem(me, quad) // 2
    place = lax.rem(me // quad + line - jnp.arange(line, dtype=jnp.int32), line)
    which = jnp.concatenate(
        [
            jnp.stack(
                [
                    base + 1 - core,
                    base + 3 - core,
                    base + 2 - 2 * side + core,
                    base + 2 * side + core,
                ]
            ).astype(jnp.int32),
            place.astype(jnp.int32),
        ]
    )
    terms_cost = pl.CostEstimate(
        flops=16 * tokens * channels * share,
        bytes_accessed=4 * tokens * channels + 8 * share * channels,
        transcendentals=4 * tokens * share,
    )
    pair = (2, 2, share, channels)

    def chunk(at):
        return pl.BlockSpec((share, channels), lambda s, w: (w[s + at], 0))

    sets = [whole_block(3, channels), whole_block(line, rows, channels)]
    cotangents = [whole_block(rows, channels)] * line
    aligned = [pltpu.VMEM((tokens, channels), BF16)]

    which, sums = lax.optimization_barrier((which, sums))
    for_other = pl.pallas_call(
        other_core_terms_kernel,
        grid_spec=pltpu.PrefetchScalarGridSpec(
            num_scalar_prefetch=1,
            grid=(2,),
            in_specs=[chunk(0), chunk(0)] + sets + cotangents,
            out_specs=pl.BlockSpec((1,) + pair[1:], lambda s, w: (s, 0, 0, 0)),
            scratch_shapes=aligned,
        ),
        out_shape=jax.ShapeDtypeStruct(pair, BF16),
        compiler_params=params(),
        cost_estimate=terms_cost,
        name="weight_grads_other_core",
    )(which, weight_in, weight_out, vectors, gathered, *upstream_line)
    from_other = lax.ppermute(for_other, "row", other_core)

    sent, kept = pl.pallas_call(
        own_core_terms_kernel,
        grid_spec=pltpu.PrefetchScalarGridSpec(
            num_scalar_prefetch=1,
            grid=(2,),
            in_specs=[chunk(2), chunk(2)]
            + sets
            + [pl.BlockSpec((1,) + pair[1:], lambda s, w: ((w[s + 2] - w[0] // 4 * 4) // 2, 0, 0, 0))]
            + cotangents,
            out_specs=[whole_block(2, share, channels)] * 2,
            scratch_shapes=aligned,
        ),
        out_shape=[
            jax.ShapeDtypeStruct(pair[1:], BF16),
            jax.ShapeDtypeStruct(pair[1:], F32),
        ],
        compiler_params=params(),
        cost_estimate=terms_cost,
        name="weight_grads_own_core",
    )(which, weight_in, weight_out, vectors, gathered, from_other, *upstream_line)
    got = lax.ppermute(sent, "row", other_side)

    scattered, sent = lax.optimization_barrier((scattered, sent))
    copies = pl.pallas_call(
        spread_sum_kernel,
        in_specs=[whole_block(count, piece, channels)],
        out_specs=whole_block(count, piece, channels),
        out_shape=jax.ShapeDtypeStruct((count, piece, channels), BF16),
        grid=(1,),
        compiler_params=params(),
        name="kernel_grad_sum",
    )(scattered)
    totals = lax.all_to_all(copies, "row", split_axis=0, concat_axis=0, tiled=True)

    conv_own, copies = lax.optimization_barrier((conv_grad, copies))
    voxel_grad = pl.pallas_call(
        functools.partial(input_grad_kernel, planes, height),
        grid_spec=pltpu.PrefetchScalarGridSpec(
            num_scalar_prefetch=1,
            grid=(tiles,),
            in_specs=[
                lane_block(rows),
                lane_block(rows),
                lane_block(rows),
                split_block,
                lane_block(rows),
            ],
            out_specs=lane_block(rows),
            scratch_shapes=[spread_of(2 * MARGIN + planes)],
        ),
        out_shape=jax.ShapeDtypeStruct((rows, channels), BF16),
        compiler_params=params(),
        cost_estimate=conv_cost(rows, channels),
        name="input_grad_conv",
    )(parity, grad_inner, conv_own, grad_outer, split, upstream)

    kernel_grad, vector_grads = pl.pallas_call(
        unpack_kernel,
        grid=(1,),
        in_specs=[whole_block(count, piece, channels)],
        out_specs=[whole_block(TAP_ROWS, channels), whole_block(SUB, channels)],
        out_shape=[
            jax.ShapeDtypeStruct((TAP_ROWS, channels), F32),
            jax.ShapeDtypeStruct((SUB, channels), F32),
        ],
        compiler_params=params(),
        name="kernel_grad_unpack",
    )(totals)

    weight_in_grad, weight_out_grad = pl.pallas_call(
        last_sum_kernel,
        grid=(1,),
        in_specs=[whole_block(2, share, channels)] * 2,
        out_specs=[whole_block(share, channels)] * 2,
        out_shape=[jax.ShapeDtypeStruct((share, channels), F32)] * 2,
        compiler_params=params(),
        name="weight_grads_sum",
    )(kept, got)

    return (
        block_out.reshape(voxels.shape),
        voxel_grad.reshape(voxels.shape),
        kernel_grad,
        vector_grads[0],
        vector_grads[1],
        vector_grads[2],
        weight_in_grad,
        weight_out_grad,
    )


def solution(mesh):
    in_specs = (
        P(("group", "row"), None, None, None),
        P(),
        P(),
        P(),
        P(),
        P(),
        P(),
        P(("group", "row"), None, None, None),
    )
    out_specs = (
        P(("group", "row"), None, None, None),
        P(("group", "row"), None, None, None),
        P("group", None),
        P("group"),
        P("group"),
        P("group"),
        P(("group", "row"), None),
        P(("group", "row"), None),
    )
    return jax.shard_map(
        on_device, mesh=mesh, in_specs=in_specs, out_specs=out_specs, check_vma=False
    )
```

```python
import functools

import jax
import jax.numpy as jnp
from jax import lax
from jax.experimental import pallas as pl
from jax.experimental.pallas import tpu as pltpu
from jax.sharding import PartitionSpec as P

KS = 7
MARGIN = KS // 2
LANES = 128
SUB = 8
PAD = 3 * SUB
TAP_ROWS = KS * KS * KS

root_half = 0.7071067811865476
inv_root_tau = 0.3989422804014327
norm_eps = 1e-06
erf_step = 0.3275911
erf_terms = tuple(
    0.5 * a for a in (0.254829592, -0.284496736, 1.421413741, -1.453152027, 1.061405429)
)

NO_COST = pl.CostEstimate(flops=0, bytes_accessed=0, transcendentals=0)

F32 = jnp.float32
BF16 = jnp.bfloat16


def split_source(v):
    terms = []
    for a, b in ((v[0] + v[2], v[1] + v[3]), (v[2], v[3]), (v[0], v[1])):
        terms += [a + b, b, a]
    return terms


def split_taps(t):
    terms = []
    for s in (
        (t[2], t[3], t[4]),
        (t[4] - t[2], t[5] - t[3], t[6] - t[4]),
        (t[0] - t[2], t[1] - t[3], t[2] - t[4]),
    ):
        terms += [s[1], s[2] - s[1], s[0] - s[1]]
    return terms


def split_grads(g):
    terms = []
    for a, b in ((g[0] + g[2], g[1] + g[3]), (g[0], g[1]), (g[2], g[3])):
        terms += [a + b, a, b]
    return terms


def join_outputs(m):
    pair = [(m[3 * k] + m[3 * k + 1], m[3 * k] + m[3 * k + 2]) for k in range(3)]
    return [
        pair[0][0] + pair[1][0],
        pair[0][1] + pair[1][1],
        pair[0][0] + pair[2][0],
        pair[0][1] + pair[2][1],
    ]


def join_taps(m):
    p, q, r = [
        (m[3 * k + 2], m[3 * k] - m[3 * k + 1] - m[3 * k + 2], m[3 * k + 1]) for k in range(3)
    ]
    return [
        r[0],
        r[1],
        p[0] - q[0] - r[0] + r[2],
        p[1] - q[1] - r[1],
        p[2] - q[2] - r[2] + q[0],
        q[1],
        q[2],
    ]


def tree_sum(terms):
    while len(terms) > 1:
        terms = [
            terms[k] + terms[k + 1] if k + 1 < len(terms) else terms[k]
            for k in range(0, len(terms), 2)
        ]
    return terms[0]


def stage_source(wanted, height, spread):
    row = height * SUB
    for at, (block, x) in enumerate(wanted):
        plane = block[x * row : (x + 1) * row, :].astype(F32)
        lines = [plane[y * SUB : (y + 1) * SUB, :] for y in range(height)]
        for j, term in enumerate(split_source(lines)):
            spread[j, at, SUB : 2 * SUB, :] = term


def rim_planes(left, right, planes):
    wanted = [(left, x) for x in range(planes - MARGIN, planes)]
    return wanted + [(right, x) for x in range(MARGIN)]


def all_planes(left, own, right, planes):
    rim = rim_planes(left, right, planes)
    return rim[:MARGIN] + [(own, x) for x in range(planes)] + rim[MARGIN:]


def by_core(core, inner, outer, stage):
    @pl.when(core[0] == 0)
    def _():
        stage(outer, inner)

    @pl.when(core[0] != 0)
    def _():
        stage(inner, outer)


def clear_rims(spread):
    zeros = jnp.zeros(spread.shape[:2] + (SUB, LANES), F32)
    spread[:, :, :SUB, :] = zeros
    spread[:, :, 2 * SUB :, :] = zeros


def stage_taps(taps, split):
    for dx in range(KS):
        rows = []
        for dy in range(KS):
            first = dx * KS * KS + dy * KS
            if first + SUB <= TAP_ROWS:
                rows.append(taps[first : first + SUB, :])
            else:
                rows.append(pltpu.roll(taps[TAP_ROWS - SUB : TAP_ROWS, :], SUB - 1, 0))
        for j, term in enumerate(split_taps(rows)):
            split[j, dx] = term


REVERSED = (0, 2, 1, 6, 8, 7, 3, 5, 4)


def convolve(spread, split, planes, held, flipped):
    terms = []
    for j in range(9):
        sums = [None] * planes
        for dz in range(KS):
            first = SUB - MARGIN + dz
            source = {x: spread[j, at, first : first + SUB, :] for at, x in enumerate(held)}
            weights = []
            for dx in range(KS):
                if flipped:
                    tap = split[REVERSED[j], KS - 1 - dx, KS - 1 - dz : KS - dz, :]
                else:
                    tap = split[j, dx, dz : dz + 1, :]
                weights.append(jnp.broadcast_to(tap, (SUB, LANES)))
            for x in range(planes):
                part = tree_sum(
                    [source[x + dx] * weights[dx] for dx in range(KS) if x + dx in source]
                )
                sums[x] = part if sums[x] is None else sums[x] + part
        terms.append(sums)
    return [join_outputs([terms[j][x] for j in range(9)]) for x in range(planes)]


def own_conv_kernel(planes, height, own, taps, out, split, spread):
    @pl.when(pl.program_id(0) == 0)
    def _():
        clear_rims(spread)

    stage_source([(own, x) for x in range(planes)], height, spread)
    stage_taps(taps, split)
    rows = convolve(spread, split, planes, range(MARGIN, MARGIN + planes), False)
    for x in range(planes):
        for y in range(height):
            at = (x * height + y) * SUB
            out[at : at + SUB, :] = rows[x][y]


def rim_conv_kernel(
    planes, height, core, inner, outer, split, partial, gain, bias, normed, unit, inv, spread, conv
):
    step = pl.program_id(0)

    @pl.when(step == 0)
    def _():
        clear_rims(spread)

    def stage(left, right):
        stage_source(rim_planes(left, right, planes), height, spread)

    by_core(core, inner, outer, stage)
    held = list(range(MARGIN)) + list(range(MARGIN + planes, 2 * MARGIN + planes))
    rows = convolve(spread, split, planes, held, False)
    for x in range(planes):
        for y in range(height):
            at = (x * height + y) * SUB
            conv[step, at : at + SUB, :] = rows[x][y] + partial[at : at + SUB, :]

    @pl.when(step == pl.num_programs(0) - 1)
    def _():
        tiles = conv.shape[0]
        channels = tiles * LANES
        parts = [conv[k] for k in range(tiles)]
        gains = gain[...].reshape(1, channels)
        biases = bias[...].reshape(1, channels)
        average = jnp.sum(tree_sum(parts), axis=1, keepdims=True) * (1.0 / channels)
        parts = [part - average for part in parts]
        variance = jnp.sum(
            tree_sum([part * part for part in parts]), axis=1, keepdims=True
        ) * (1.0 / channels)
        inverse = lax.rsqrt(variance + norm_eps)
        inv[...] = jnp.broadcast_to(inverse, inv.shape)
        for k in range(tiles):
            lanes = slice(k * LANES, (k + 1) * LANES)
            value = parts[k] * inverse
            unit[:, lanes] = value
            whole = (value * gains[:, lanes] + biases[:, lanes]).astype(BF16)
            for copy in range(normed.shape[0]):
                normed[copy, :, lanes] = whole


def input_grad_kernel(planes, height, core, inner, own, outer, split, cotangent, out, spread):
    @pl.when(pl.program_id(0) == 0)
    def _():
        clear_rims(spread)

    def stage(left, right):
        stage_source(all_planes(left, own, right, planes), height, spread)

    by_core(core, inner, outer, stage)
    rows = convolve(spread, split, planes, range(2 * MARGIN + planes), True)
    for x in range(planes):
        at = x * height * SUB
        whole = jnp.concatenate(rows[x], axis=0)
        upstream = cotangent[at : at + height * SUB, :].astype(F32)
        out[at : at + height * SUB, :] = (upstream + whole).astype(BF16)


def kernel_grad_kernel(
    planes, height, core, inner, own, outer, grads, small, out, spread, products, joined, flat
):
    @pl.when(pl.program_id(0) == 0)
    def _():
        clear_rims(spread)
        products[...] = jnp.zeros(products.shape, F32)
        flat[...] = jnp.zeros(flat.shape, F32)

    def stage(left, right):
        stage_source(all_planes(left, own, right, planes), height, spread)

    by_core(core, inner, outer, stage)
    upstream = []
    for x in range(planes):
        plane = grads[x * height * SUB : (x + 1) * height * SUB, :].astype(F32)
        upstream.append(
            split_grads([plane[y * SUB : (y + 1) * SUB, :] for y in range(height)])
        )
    for j in range(9):
        for dz in range(KS):
            first = SUB - MARGIN + dz
            source = [
                spread[j, x, first : first + SUB, :] for x in range(planes + KS - 1)
            ]
            for dx in range(KS):
                products[j % 2, dx, dz * SUB : (dz + 1) * SUB, :] = tree_sum(
                    [source[x + dx] * upstream[x][j] for x in range(planes)]
                )
        for dx in range(KS):
            joined[j, dx] = tree_sum(
                [products[j % 2, dx, pl.ds(s, SUB, stride=SUB), :] for s in range(SUB)]
            )
    for dx in range(KS):
        for dy, tile in enumerate(join_taps([joined[j, dx] for j in range(9)])):
            first = dx * KS * KS + dy * KS
            flat[first : first + SUB, :] = tile
    flat[TAP_ROWS : TAP_ROWS + SUB, :] = small[...]
    out[...] = flat[...].astype(out.dtype)


def mlp_kernel(
    normed,
    weight_in,
    weight_out,
    unit,
    inv,
    norm_gain,
    layer_scale,
    voxels,
    cotangent,
    block_out,
    conv_grad,
    small,
    mixed,
    back,
    mixed_grad,
):
    step = pl.program_id(0)
    gain = norm_gain[...].reshape(1, -1)
    scale = layer_scale[...].reshape(1, -1)

    @pl.when(step == 0)
    def _():
        mixed_grad[...] = (scale * cotangent[...].astype(F32)).astype(BF16)

    hidden = lax.dot_general(
        normed[...], weight_in[...], (((1,), (1,)), ((), ())), preferred_element_type=F32
    )
    act_grad = lax.dot_general(
        mixed_grad[...], weight_out[...], (((1,), (1,)), ((), ())), preferred_element_type=F32
    )
    activated, hidden_grad = slopes(hidden, act_grad)
    forward = jnp.dot(activated, weight_out[...], preferred_element_type=F32)
    backward = jnp.dot(hidden_grad, weight_in[...], preferred_element_type=F32)

    @pl.when(step == 0)
    def _():
        mixed[...] = forward
        back[...] = backward

    @pl.when(step > 0)
    def _():
        mixed[...] += forward
        back[...] += backward

    @pl.when(step == pl.num_programs(0) - 1)
    def _():
        channels = gain.shape[1]
        whole = mixed[...]
        block_out[...] = (voxels[...].astype(F32) + scale * whole).astype(BF16)
        scale_local = jnp.sum(cotangent[...].astype(F32) * whole, axis=0, keepdims=True)
        grad = back[...]
        one = unit[...]
        bias_local = jnp.sum(grad, axis=0, keepdims=True)
        gain_local = jnp.sum(grad * one, axis=0, keepdims=True)
        small[...] = jnp.concatenate(
            [gain_local, bias_local, scale_local, jnp.zeros((SUB - 3, channels), F32)], axis=0
        )
        scaled = grad * gain
        average = jnp.sum(scaled, axis=1, keepdims=True) * (1.0 / channels)
        slant = jnp.sum(scaled * one, axis=1, keepdims=True) * (1.0 / channels)
        conv_grad[...] = (inv[:, :1] * (scaled - average - one * slant)).astype(BF16)


def slopes(hidden, act_grad):
    bell = jnp.exp(-0.5 * hidden * hidden)
    below = 1.0 + (erf_step * root_half) * jnp.abs(hidden)
    t = pl.reciprocal(below, approx=True)
    t = t * (2.0 - below * t)
    poly = erf_terms[-1]
    for term in erf_terms[-2::-1]:
        poly = poly * t + term
    tail = poly * t * bell
    cover = jnp.where(hidden < 0.0, tail, 1.0 - tail)
    activated = (hidden * cover).astype(BF16)
    slope = cover + hidden * bell * inv_root_tau
    return activated, (act_grad * slope).astype(BF16)


def weight_grad_terms(which, weight_in, weight_out, scale, normed, cotangents, aligned):
    rows = normed.shape[1]
    line = len(cotangents)
    scales = scale[...].reshape(1, -1)
    mixed_grad = jnp.concatenate(
        [(scales * part[...].astype(F32)).astype(BF16) for part in cotangents], axis=0
    )
    for k in range(line):
        aligned[k * rows : (k + 1) * rows, :] = normed[which[4 + k]]
    across = (((1,), (1,)), ((), ()))
    hidden = lax.dot_general(weight_in[...], aligned[...], across, preferred_element_type=F32)
    act_grad = lax.dot_general(weight_out[...], mixed_grad, across, preferred_element_type=F32)
    activated, hidden_grad = slopes(hidden, act_grad)
    return (
        jnp.dot(hidden_grad, aligned[...], preferred_element_type=F32),
        jnp.dot(activated, mixed_grad, preferred_element_type=F32),
    )


def other_core_terms_kernel(which, weight_in, weight_out, scale, normed, *rest):
    *cotangents, out, aligned = rest
    terms = weight_grad_terms(which, weight_in, weight_out, scale, normed, cotangents, aligned)
    for k in range(2):
        out[0, k] = terms[k].astype(BF16)


def own_core_terms_kernel(which, weight_in, weight_out, scale, normed, got, *rest):
    *cotangents, sent, kept, aligned = rest
    terms = weight_grad_terms(which, weight_in, weight_out, scale, normed, cotangents, aligned)
    step = pl.program_id(0)
    for k in range(2):
        total = terms[k] + got[0, k].astype(F32)

        @pl.when(step == 0)
        def _():
            sent[k] = total.astype(BF16)

        @pl.when(step == 1)
        def _():
            kept[k] = total


def last_sum_kernel(kept, got, in_grad, out_grad):
    for k, out in enumerate((in_grad, out_grad)):
        out[...] = kept[k] + got[k].astype(F32)


def spread_sum_kernel(parts, out):
    total = tree_sum([parts[k].astype(F32) for k in range(parts.shape[0])]).astype(BF16)
    for copy in range(out.shape[0]):
        out[copy] = total


def unpack_kernel(parts, out, *small):
    piece = parts.shape[1]
    for k in range(-(-TAP_ROWS // piece)):
        first = k * piece
        length = min(piece, TAP_ROWS - first)
        out[first : first + length, :] = parts[k].astype(F32)[:length, :]
    k = TAP_ROWS // piece
    first = TAP_ROWS - k * piece
    rows = parts[k].astype(F32)
    if first + SUB > piece:
        rows = jnp.concatenate([rows, parts[k + 1].astype(F32)], axis=0)
    for k, line in enumerate(small):
        line[...] = rows[first + k : first + k + 1, :].reshape(line.shape)


def params(limit=48):
    return pltpu.CompilerParams(vmem_limit_bytes=limit * 1024 * 1024)


def lane_block(rows):
    return pl.BlockSpec((rows, LANES), lambda c, *_: (0, c))


def whole_block(*shape):
    return pl.BlockSpec(shape, lambda *_: (0,) * len(shape))


def rims(cells):
    count = lax.axis_size("row")
    between = [(i, i + 1) for i in range(1, count - 1, 2)]
    return (
        lax.ppermute(cells, "row", [(i, i ^ 1) for i in range(count)]),
        lax.ppermute(cells, "row", between + [(j, i) for i, j in between]),
    )


def on_device(
    voxels, dw_kernel, norm_gain, norm_bias, weight_in, weight_out, layer_scale, cotangent
):
    planes, height, breadth, channels = voxels.shape
    rows = planes * height * breadth
    units = weight_in.shape[0]
    count = lax.axis_size("row")
    me = lax.axis_index("row")
    quad = 4
    line = count // quad
    lines = [[quad * k + p for k in range(line)] for p in range(quad)]
    other_core = [(i, i ^ 1) for i in range(count)]
    other_side = [(i, i ^ 2) for i in range(count)]
    tiles = channels // LANES

    own = voxels.reshape(rows, channels)
    upstream = cotangent.reshape(rows, channels)
    core = lax.rem(me, 2).astype(jnp.int32)
    parity = core.reshape(1)

    inner, outer = rims(own)

    upstream_line = [upstream] + [
        lax.ppermute(upstream, "row", [(i, (i + quad * k) % count) for i in range(count)])
        for k in range(1, line)
    ]

    def spread_of(held):
        return pltpu.VMEM((9, held, PAD, LANES), F32)

    split_block = pl.BlockSpec((None, 9, KS, SUB, LANES), lambda c, *_: (c, 0, 0, 0, 0))
    partial, split = pl.pallas_call(
        functools.partial(own_conv_kernel, planes, height),
        grid=(tiles,),
        in_specs=[lane_block(rows), lane_block(TAP_ROWS)],
        out_specs=[lane_block(rows), split_block],
        out_shape=[
            jax.ShapeDtypeStruct((rows, channels), F32),
            jax.ShapeDtypeStruct((tiles, 9, KS, SUB, LANES), F32),
        ],
        scratch_shapes=[spread_of(planes)],
        compiler_params=params(),
        cost_estimate=NO_COST,
        name="own_conv",
    )(own, dw_kernel)

    normed, unit, inv = pl.pallas_call(
        functools.partial(rim_conv_kernel, planes, height),
        grid_spec=pltpu.PrefetchScalarGridSpec(
            num_scalar_prefetch=1,
            grid=(tiles,),
            in_specs=[
                lane_block(rows),
                lane_block(rows),
                split_block,
                lane_block(rows),
                whole_block(channels),
                whole_block(channels),
            ],
            out_specs=[
                whole_block(line, rows, channels),
                whole_block(rows, channels),
                whole_block(rows, LANES),
            ],
            scratch_shapes=[spread_of(2 * MARGIN), pltpu.VMEM((tiles, rows, LANES), F32)],
        ),
        out_shape=[
            jax.ShapeDtypeStruct((line, rows, channels), BF16),
            jax.ShapeDtypeStruct((rows, channels), F32),
            jax.ShapeDtypeStruct((rows, LANES), F32),
        ],
        compiler_params=params(),
        cost_estimate=NO_COST,
        name="rim_conv",
    )(parity, inner, outer, split, partial, norm_gain, norm_bias)

    gathered = lax.all_to_all(
        normed, "row", split_axis=0, concat_axis=0, tiled=True, axis_index_groups=lines
    )

    block = 512
    whole = whole_block(rows, channels)
    block_out, conv_grad, small = pl.pallas_call(
        mlp_kernel,
        grid=(units // block,),
        in_specs=[
            pl.BlockSpec((None, rows, channels), lambda f: (0, 0, 0)),
            pl.BlockSpec((block, channels), lambda f: (f, 0)),
            pl.BlockSpec((block, channels), lambda f: (f, 0)),
            whole,
            whole_block(rows, LANES),
            whole_block(channels),
            whole_block(channels),
            whole,
            whole,
        ],
        out_specs=[
            whole,
            whole,
            whole_block(SUB, channels),
        ],
        out_shape=[
            jax.ShapeDtypeStruct((rows, channels), BF16),
            jax.ShapeDtypeStruct((rows, channels), BF16),
            jax.ShapeDtypeStruct((SUB, channels), F32),
        ],
        scratch_shapes=[
            pltpu.VMEM((rows, channels), F32),
            pltpu.VMEM((rows, channels), F32),
            pltpu.VMEM((rows, channels), BF16),
        ],
        compiler_params=params(),
        cost_estimate=NO_COST,
        name="mlp_both_ways",
    )(normed, weight_in, weight_out, unit, inv, norm_gain, layer_scale, own, upstream)

    piece = -(-(TAP_ROWS + SUB) // count)
    piece += -piece % SUB
    padded = piece * count
    sums = pl.pallas_call(
        functools.partial(kernel_grad_kernel, planes, height),
        grid_spec=pltpu.PrefetchScalarGridSpec(
            num_scalar_prefetch=1,
            grid=(tiles,),
            in_specs=[
                lane_block(rows),
                lane_block(rows),
                lane_block(rows),
                lane_block(rows),
                lane_block(SUB),
            ],
            out_specs=lane_block(padded),
            scratch_shapes=[
                spread_of(2 * MARGIN + planes),
                pltpu.VMEM((2, KS, SUB * SUB, LANES), F32),
                pltpu.VMEM((9, KS, SUB, LANES), F32),
                pltpu.VMEM((padded, LANES), F32),
            ],
        ),
        out_shape=jax.ShapeDtypeStruct((padded, channels), BF16),
        compiler_params=params(),
        cost_estimate=NO_COST,
        name="kernel_grad_terms",
    )(parity, inner, own, outer, conv_grad, small)
    share = units // count
    tokens = line * rows
    base = me // quad * quad
    side = lax.rem(me, quad) // 2
    place = lax.rem(me // quad + line - jnp.arange(line, dtype=jnp.int32), line)
    which = jnp.concatenate(
        [
            jnp.stack(
                [
                    base + 1 - core,
                    base + 3 - core,
                    base + 2 - 2 * side + core,
                    base + 2 * side + core,
                ]
            ).astype(jnp.int32),
            place.astype(jnp.int32),
        ]
    )
    pair = (2, 2, share, channels)

    def chunk(at):
        return pl.BlockSpec((share, channels), lambda s, w: (w[s + at], 0))

    sets = [whole_block(channels), whole_block(line, rows, channels)]
    cotangents = [whole_block(rows, channels)] * line
    aligned = [pltpu.VMEM((tokens, channels), BF16)]

    which, sums, conv_grad = lax.optimization_barrier((which, sums, conv_grad))
    scattered = lax.all_to_all(
        sums.reshape(count, piece, channels), "row", split_axis=0, concat_axis=0, tiled=True
    )
    grad_inner, grad_outer = rims(conv_grad)
    for_other = pl.pallas_call(
        other_core_terms_kernel,
        grid_spec=pltpu.PrefetchScalarGridSpec(
            num_scalar_prefetch=1,
            grid=(2,),
            in_specs=[chunk(0), chunk(0)] + sets + cotangents,
            out_specs=pl.BlockSpec((1,) + pair[1:], lambda s, w: (s, 0, 0, 0)),
            scratch_shapes=aligned,
        ),
        out_shape=jax.ShapeDtypeStruct(pair, BF16),
        compiler_params=params(),
        cost_estimate=NO_COST,
        name="weight_grads_other_core",
    )(which, weight_in, weight_out, layer_scale, gathered, *upstream_line)
    from_other = lax.ppermute(for_other, "row", other_core)

    sent, kept = pl.pallas_call(
        own_core_terms_kernel,
        grid_spec=pltpu.PrefetchScalarGridSpec(
            num_scalar_prefetch=1,
            grid=(2,),
            in_specs=[chunk(2), chunk(2)]
            + sets
            + [pl.BlockSpec((1,) + pair[1:], lambda s, w: ((w[s + 2] - w[0] // 4 * 4) // 2, 0, 0, 0))]
            + cotangents,
            out_specs=[whole_block(2, share, channels)] * 2,
            scratch_shapes=aligned,
        ),
        out_shape=[
            jax.ShapeDtypeStruct(pair[1:], BF16),
            jax.ShapeDtypeStruct(pair[1:], F32),
        ],
        compiler_params=params(),
        cost_estimate=NO_COST,
        name="weight_grads_own_core",
    )(which, weight_in, weight_out, layer_scale, gathered, from_other, *upstream_line)
    got = lax.ppermute(sent, "row", other_side)

    scattered, kept = lax.optimization_barrier((scattered, kept))
    copies = pl.pallas_call(
        spread_sum_kernel,
        in_specs=[whole_block(count, piece, channels)],
        out_specs=whole_block(count, piece, channels),
        out_shape=jax.ShapeDtypeStruct((count, piece, channels), BF16),
        grid=(1,),
        compiler_params=params(),
        cost_estimate=NO_COST,
        name="kernel_grad_sum",
    )(scattered)
    conv_own, copies = lax.optimization_barrier((conv_grad, copies))
    totals = lax.all_to_all(copies, "row", split_axis=0, concat_axis=0, tiled=True)
    voxel_grad = pl.pallas_call(
        functools.partial(input_grad_kernel, planes, height),
        grid_spec=pltpu.PrefetchScalarGridSpec(
            num_scalar_prefetch=1,
            grid=(tiles,),
            in_specs=[
                lane_block(rows),
                lane_block(rows),
                lane_block(rows),
                split_block,
                lane_block(rows),
            ],
            out_specs=lane_block(rows),
            scratch_shapes=[spread_of(2 * MARGIN + planes)],
        ),
        out_shape=jax.ShapeDtypeStruct((rows, channels), BF16),
        compiler_params=params(),
        cost_estimate=NO_COST,
        name="input_grad_conv",
    )(parity, grad_inner, conv_own, grad_outer, split, upstream)

    kernel_grad, *vector_grads = pl.pallas_call(
        unpack_kernel,
        grid=(1,),
        in_specs=[whole_block(count, piece, channels)],
        out_specs=[whole_block(TAP_ROWS, channels)] + [whole_block(channels)] * 3,
        out_shape=[
            jax.ShapeDtypeStruct((TAP_ROWS, channels), F32),
        ]
        + [jax.ShapeDtypeStruct((channels,), F32)] * 3,
        compiler_params=params(),
        cost_estimate=NO_COST,
        name="kernel_grad_unpack",
    )(totals)

    weight_in_grad, weight_out_grad = pl.pallas_call(
        last_sum_kernel,
        grid=(1,),
        in_specs=[whole_block(2, share, channels)] * 2,
        out_specs=[whole_block(share, channels)] * 2,
        out_shape=[jax.ShapeDtypeStruct((share, channels), F32)] * 2,
        compiler_params=params(),
        cost_estimate=NO_COST,
        name="weight_grads_sum",
    )(kept, got)

    return (
        block_out.reshape(voxels.shape),
        voxel_grad.reshape(voxels.shape),
        kernel_grad,
        *vector_grads,
        weight_in_grad,
        weight_out_grad,
    )


def solution(mesh):
    in_specs = (
        P(("group", "row"), None, None, None),
        P(),
        P(),
        P(),
        P(),
        P(),
        P(),
        P(("group", "row"), None, None, None),
    )
    out_specs = (
        P(("group", "row"), None, None, None),
        P(("group", "row"), None, None, None),
        P("group", None),
        P("group"),
        P("group"),
        P("group"),
        P(("group", "row"), None),
        P(("group", "row"), None),
    )
    return jax.shard_map(
        on_device, mesh=mesh, in_specs=in_specs, out_specs=out_specs, check_vma=False
    )
```

```python
import functools

import jax
import jax.numpy as jnp
from jax import lax
from jax.experimental import pallas as pl
from jax.experimental.pallas import tpu as pltpu
from jax.sharding import PartitionSpec as P

KS = 7
MARGIN = KS // 2
LANES = 128
SUB = 8
PAD = 3 * SUB
TAP_ROWS = KS * KS * KS

root_half = 0.7071067811865476
inv_root_tau = 0.3989422804014327
norm_eps = 1e-06
erf_step = 0.3275911
erf_terms = tuple(
    0.5 * a for a in (0.254829592, -0.284496736, 1.421413741, -1.453152027, 1.061405429)
)

NO_COST = pl.CostEstimate(flops=0, bytes_accessed=0, transcendentals=0)

F32 = jnp.float32
BF16 = jnp.bfloat16


def split_source(v):
    terms = []
    for a, b in ((v[0] + v[2], v[1] + v[3]), (v[2], v[3]), (v[0], v[1])):
        terms += [a + b, b, a]
    return terms


def split_taps(t):
    terms = []
    for s in (
        (t[2], t[3], t[4]),
        (t[4] - t[2], t[5] - t[3], t[6] - t[4]),
        (t[0] - t[2], t[1] - t[3], t[2] - t[4]),
    ):
        terms += [s[1], s[2] - s[1], s[0] - s[1]]
    return terms


def split_grads(g):
    terms = []
    for a, b in ((g[0] + g[2], g[1] + g[3]), (g[0], g[1]), (g[2], g[3])):
        terms += [a + b, a, b]
    return terms


def join_outputs(m):
    pair = [(m[3 * k] + m[3 * k + 1], m[3 * k] + m[3 * k + 2]) for k in range(3)]
    return [
        pair[0][0] + pair[1][0],
        pair[0][1] + pair[1][1],
        pair[0][0] + pair[2][0],
        pair[0][1] + pair[2][1],
    ]


def join_taps(m):
    p, q, r = [
        (m[3 * k + 2], m[3 * k] - m[3 * k + 1] - m[3 * k + 2], m[3 * k + 1]) for k in range(3)
    ]
    return [
        r[0],
        r[1],
        p[0] - q[0] - r[0] + r[2],
        p[1] - q[1] - r[1],
        p[2] - q[2] - r[2] + q[0],
        q[1],
        q[2],
    ]


def tree_sum(terms):
    while len(terms) > 1:
        terms = [
            terms[k] + terms[k + 1] if k + 1 < len(terms) else terms[k]
            for k in range(0, len(terms), 2)
        ]
    return terms[0]


def stage_source(wanted, height, spread):
    row = height * SUB
    for at, (block, x) in enumerate(wanted):
        plane = block[x * row : (x + 1) * row, :].astype(F32)
        lines = [plane[y * SUB : (y + 1) * SUB, :] for y in range(height)]
        for j, term in enumerate(split_source(lines)):
            spread[j, at, SUB : 2 * SUB, :] = term


def rim_planes(left, right, planes):
    wanted = [(left, x) for x in range(planes - MARGIN, planes)]
    return wanted + [(right, x) for x in range(MARGIN)]


def all_planes(left, own, right, planes):
    rim = rim_planes(left, right, planes)
    return rim[:MARGIN] + [(own, x) for x in range(planes)] + rim[MARGIN:]


def by_core(core, inner, outer, stage):
    @pl.when(core[0] == 0)
    def _():
        stage(outer, inner)

    @pl.when(core[0] != 0)
    def _():
        stage(inner, outer)


def clear_rims(spread):
    zeros = jnp.zeros(spread.shape[:2] + (SUB, LANES), F32)
    spread[:, :, :SUB, :] = zeros
    spread[:, :, 2 * SUB :, :] = zeros


def stage_taps(taps, split):
    for dx in range(KS):
        rows = []
        for dy in range(KS):
            first = dx * KS * KS + dy * KS
            if first + SUB <= TAP_ROWS:
                rows.append(taps[first : first + SUB, :])
            else:
                rows.append(pltpu.roll(taps[TAP_ROWS - SUB : TAP_ROWS, :], SUB - 1, 0))
        for j, term in enumerate(split_taps(rows)):
            split[j, dx] = term


REVERSED = (0, 2, 1, 6, 8, 7, 3, 5, 4)


def convolve(spread, split, planes, held, flipped):
    terms = []
    for j in range(9):
        sums = [None] * planes
        for dz in range(KS):
            first = SUB - MARGIN + dz
            source = {x: spread[j, at, first : first + SUB, :] for at, x in enumerate(held)}
            weights = []
            for dx in range(KS):
                if flipped:
                    tap = split[REVERSED[j], KS - 1 - dx, KS - 1 - dz : KS - dz, :]
                else:
                    tap = split[j, dx, dz : dz + 1, :]
                weights.append(jnp.broadcast_to(tap, (SUB, LANES)))
            for x in range(planes):
                part = tree_sum(
                    [source[x + dx] * weights[dx] for dx in range(KS) if x + dx in source]
                )
                sums[x] = part if sums[x] is None else sums[x] + part
        terms.append(sums)
    return [join_outputs([terms[j][x] for j in range(9)]) for x in range(planes)]


def own_conv_kernel(planes, height, own, taps, out, split, spread):
    @pl.when(pl.program_id(0) == 0)
    def _():
        clear_rims(spread)

    stage_source([(own, x) for x in range(planes)], height, spread)
    stage_taps(taps, split)
    rows = convolve(spread, split, planes, range(MARGIN, MARGIN + planes), False)
    for x in range(planes):
        for y in range(height):
            at = (x * height + y) * SUB
            out[at : at + SUB, :] = rows[x][y]


def rim_conv_kernel(
    planes, height, core, inner, outer, split, partial, gain, bias, normed, centered, spread, conv
):
    step = pl.program_id(0)

    @pl.when(step == 0)
    def _():
        clear_rims(spread)

    def stage(left, right):
        stage_source(rim_planes(left, right, planes), height, spread)

    by_core(core, inner, outer, stage)
    held = list(range(MARGIN)) + list(range(MARGIN + planes, 2 * MARGIN + planes))
    rows = convolve(spread, split, planes, held, False)
    for x in range(planes):
        for y in range(height):
            at = (x * height + y) * SUB
            conv[step, at : at + SUB, :] = rows[x][y] + partial[at : at + SUB, :]

    @pl.when(step == pl.num_programs(0) - 1)
    def _():
        tiles = conv.shape[0]
        channels = tiles * LANES
        parts = [conv[k] for k in range(tiles)]
        gains = gain[...].reshape(1, channels)
        biases = bias[...].reshape(1, channels)
        average = jnp.sum(tree_sum(parts), axis=1, keepdims=True) * (1.0 / channels)
        parts = [part - average for part in parts]
        variance = jnp.sum(
            tree_sum([part * part for part in parts]), axis=1, keepdims=True
        ) * (1.0 / channels)
        inverse = lax.rsqrt(variance + norm_eps)
        for k in range(tiles):
            lanes = slice(k * LANES, (k + 1) * LANES)
            centered[:, lanes] = parts[k]
            value = parts[k] * inverse
            whole = (value * gains[:, lanes] + biases[:, lanes]).astype(BF16)
            for copy in range(normed.shape[0]):
                normed[copy, :, lanes] = whole


def input_grad_kernel(planes, height, core, inner, own, outer, split, cotangent, out, spread):
    @pl.when(pl.program_id(0) == 0)
    def _():
        clear_rims(spread)

    def stage(left, right):
        stage_source(all_planes(left, own, right, planes), height, spread)

    by_core(core, inner, outer, stage)
    rows = convolve(spread, split, planes, range(2 * MARGIN + planes), True)
    for x in range(planes):
        at = x * height * SUB
        whole = jnp.concatenate(rows[x], axis=0)
        upstream = cotangent[at : at + height * SUB, :].astype(F32)
        out[at : at + height * SUB, :] = (upstream + whole).astype(BF16)


def kernel_grad_kernel(
    planes, height, which, inner, own, outer, grads, small, out, spread, products, joined, flat
):
    @pl.when(pl.program_id(0) == 0)
    def _():
        clear_rims(spread)
        products[...] = jnp.zeros(products.shape, F32)
        flat[...] = jnp.zeros(flat.shape, F32)

    def stage(left, right):
        stage_source(all_planes(left, own, right, planes), height, spread)

    by_core(which, inner, outer, stage)
    upstream = []
    for x in range(planes):
        plane = grads[x * height * SUB : (x + 1) * height * SUB, :].astype(F32)
        upstream.append(
            split_grads([plane[y * SUB : (y + 1) * SUB, :] for y in range(height)])
        )
    for j in range(9):
        for dz in range(KS):
            first = SUB - MARGIN + dz
            source = [
                spread[j, x, first : first + SUB, :] for x in range(planes + KS - 1)
            ]
            for dx in range(KS):
                products[j % 2, dx, dz * SUB : (dz + 1) * SUB, :] = tree_sum(
                    [source[x + dx] * upstream[x][j] for x in range(planes)]
                )
        for dx in range(KS):
            joined[j, dx] = tree_sum(
                [products[j % 2, dx, pl.ds(s, SUB, stride=SUB), :] for s in range(SUB)]
            )
    for dx in range(KS):
        for dy, tile in enumerate(join_taps([joined[j, dx] for j in range(9)])):
            first = dx * KS * KS + dy * KS
            flat[first : first + SUB, :] = tile
    flat[TAP_ROWS : TAP_ROWS + SUB, :] = small[...]
    out[...] = flat[...].astype(out.dtype)


def mlp_kernel(
    normed,
    weight_in,
    weight_out,
    centered,
    norm_gain,
    layer_scale,
    voxels,
    cotangent,
    block_out,
    conv_grad,
    small,
    mixed,
    back,
    mixed_grad,
):
    step = pl.program_id(0)
    gain = norm_gain[...].reshape(1, -1)
    scale = layer_scale[...].reshape(1, -1)

    @pl.when(step == 0)
    def _():
        mixed_grad[...] = (scale * cotangent[...].astype(F32)).astype(BF16)

    hidden = lax.dot_general(
        normed[...], weight_in[...], (((1,), (1,)), ((), ())), preferred_element_type=F32
    )
    act_grad = lax.dot_general(
        mixed_grad[...], weight_out[...], (((1,), (1,)), ((), ())), preferred_element_type=F32
    )
    activated, hidden_grad = slopes(hidden, act_grad)
    forward = jnp.dot(activated, weight_out[...], preferred_element_type=F32)
    backward = jnp.dot(hidden_grad, weight_in[...], preferred_element_type=F32)

    @pl.when(step == 0)
    def _():
        mixed[...] = forward
        back[...] = backward

    @pl.when(step > 0)
    def _():
        mixed[...] += forward
        back[...] += backward

    @pl.when(step == pl.num_programs(0) - 1)
    def _():
        channels = gain.shape[1]
        whole = mixed[...]
        block_out[...] = (voxels[...].astype(F32) + scale * whole).astype(BF16)
        scale_local = jnp.sum(cotangent[...].astype(F32) * whole, axis=0, keepdims=True)
        grad = back[...]
        deviation = centered[...]
        variance = jnp.sum(deviation * deviation, axis=1, keepdims=True) * (1.0 / channels)
        inverse = lax.rsqrt(variance + norm_eps)
        one = deviation * inverse
        bias_local = jnp.sum(grad, axis=0, keepdims=True)
        gain_local = jnp.sum(grad * one, axis=0, keepdims=True)
        small[...] = jnp.concatenate(
            [gain_local, bias_local, scale_local, jnp.zeros((SUB - 3, channels), F32)], axis=0
        )
        scaled = grad * gain
        average = jnp.sum(scaled, axis=1, keepdims=True) * (1.0 / channels)
        slant = jnp.sum(scaled * one, axis=1, keepdims=True) * (1.0 / channels)
        conv_grad[...] = (inverse * (scaled - average - one * slant)).astype(BF16)


def slopes(hidden, act_grad):
    bell = jnp.exp(-0.5 * hidden * hidden)
    below = 1.0 + (erf_step * root_half) * jnp.abs(hidden)
    t = pl.reciprocal(below, approx=True)
    t = t * (2.0 - below * t)
    poly = erf_terms[-1]
    for term in erf_terms[-2::-1]:
        poly = poly * t + term
    tail = poly * t * bell
    cover = jnp.where(hidden < 0.0, tail, 1.0 - tail)
    activated = (hidden * cover).astype(BF16)
    slope = cover + hidden * bell * inv_root_tau
    return activated, (act_grad * slope).astype(BF16)


def weight_grad_terms(which, weight_in, weight_out, scale, normed, cotangents, aligned):
    rows = normed.shape[1]
    line = len(cotangents)
    scales = scale[...].reshape(1, -1)
    mixed_grad = jnp.concatenate(
        [(scales * part[...].astype(F32)).astype(BF16) for part in cotangents], axis=0
    )
    for k in range(line):
        aligned[k * rows : (k + 1) * rows, :] = normed[which[4 + k]]
    across = (((1,), (1,)), ((), ()))
    hidden = lax.dot_general(weight_in[...], aligned[...], across, preferred_element_type=F32)
    act_grad = lax.dot_general(weight_out[...], mixed_grad, across, preferred_element_type=F32)
    activated, hidden_grad = slopes(hidden, act_grad)
    return (
        jnp.dot(hidden_grad, aligned[...], preferred_element_type=F32),
        jnp.dot(activated, mixed_grad, preferred_element_type=F32),
    )


def other_core_terms_kernel(which, weight_in, weight_out, scale, normed, *rest):
    *cotangents, out, aligned = rest
    terms = weight_grad_terms(which, weight_in, weight_out, scale, normed, cotangents, aligned)
    for k in range(2):
        out[0, k] = terms[k].astype(BF16)


def own_core_terms_kernel(which, weight_in, weight_out, scale, normed, got, *rest):
    *cotangents, sent, kept, aligned = rest
    terms = weight_grad_terms(which, weight_in, weight_out, scale, normed, cotangents, aligned)
    step = pl.program_id(0)
    for k in range(2):
        total = terms[k] + got[0, k].astype(F32)

        @pl.when(step == 0)
        def _():
            sent[k] = total.astype(BF16)

        @pl.when(step == 1)
        def _():
            kept[k] = total


def last_sum_kernel(kept, got, in_grad, out_grad):
    for k, out in enumerate((in_grad, out_grad)):
        out[...] = kept[k] + got[k].astype(F32)


def spread_sum_kernel(parts, out):
    total = tree_sum([parts[k].astype(F32) for k in range(parts.shape[0])]).astype(BF16)
    for copy in range(out.shape[0]):
        out[copy] = total


def unpack_kernel(core, own, other, out, *small):
    piece, wide = own.shape[1:]

    def unpack(*halves):
        last = []
        for side, parts in enumerate(halves):
            lanes = slice(side * wide, (side + 1) * wide)
            for k in range(-(-TAP_ROWS // piece)):
                first = k * piece
                length = min(piece, TAP_ROWS - first)
                out[first : first + length, lanes] = parts[k].astype(F32)[:length, :]
            k = TAP_ROWS // piece
            last.append(parts[k].astype(F32))
        rows = jnp.concatenate(last, axis=1)
        first = TAP_ROWS % piece
        for k, line in enumerate(small):
            line[...] = rows[first + k : first + k + 1, :].reshape(line.shape)

    by_core(core, own, other, lambda outer, inner: unpack(inner, outer))


def params(limit=48):
    return pltpu.CompilerParams(vmem_limit_bytes=limit * 1024 * 1024)


def lane_block(rows):
    return pl.BlockSpec((rows, LANES), lambda c, *_: (0, c))


def whole_block(*shape):
    return pl.BlockSpec(shape, lambda *_: (0,) * len(shape))


def rims(cells):
    count = lax.axis_size("row")
    between = [(i, i + 1) for i in range(1, count - 1, 2)]
    return (
        lax.ppermute(cells, "row", [(i, i ^ 1) for i in range(count)]),
        lax.ppermute(cells, "row", between + [(j, i) for i, j in between]),
    )


def on_device(
    voxels, dw_kernel, norm_gain, norm_bias, weight_in, weight_out, layer_scale, cotangent
):
    planes, height, breadth, channels = voxels.shape
    rows = planes * height * breadth
    units = weight_in.shape[0]
    count = lax.axis_size("row")
    me = lax.axis_index("row")
    quad = 4
    line = count // quad
    lines = [[quad * k + p for k in range(line)] for p in range(quad)]
    other_core = [(i, i ^ 1) for i in range(count)]
    other_side = [(i, i ^ 2) for i in range(count)]
    tiles = channels // LANES

    own = voxels.reshape(rows, channels)
    upstream = cotangent.reshape(rows, channels)
    core = lax.rem(me, 2).astype(jnp.int32)
    parity = core.reshape(1)

    inner, outer = rims(own)

    def next_in_line(cells):
        return lax.ppermute(cells, "row", [(i, (i + quad) % count) for i in range(count)])

    upstream_line = [upstream, next_in_line(upstream)]

    def spread_of(held):
        return pltpu.VMEM((9, held, PAD, LANES), F32)

    split_block = pl.BlockSpec((None, 9, KS, SUB, LANES), lambda c, *_: (c, 0, 0, 0, 0))
    partial, split = pl.pallas_call(
        functools.partial(own_conv_kernel, planes, height),
        grid=(tiles,),
        in_specs=[lane_block(rows), lane_block(TAP_ROWS)],
        out_specs=[lane_block(rows), split_block],
        out_shape=[
            jax.ShapeDtypeStruct((rows, channels), F32),
            jax.ShapeDtypeStruct((tiles, 9, KS, SUB, LANES), F32),
        ],
        scratch_shapes=[spread_of(planes)],
        compiler_params=params(),
        cost_estimate=NO_COST,
        name="own_conv",
    )(own, dw_kernel)

    partial, upstream_line[1] = lax.optimization_barrier((partial, upstream_line[1]))
    upstream_line.append(next_in_line(upstream_line[1]))
    normed, centered = pl.pallas_call(
        functools.partial(rim_conv_kernel, planes, height),
        grid_spec=pltpu.PrefetchScalarGridSpec(
            num_scalar_prefetch=1,
            grid=(tiles,),
            in_specs=[
                lane_block(rows),
                lane_block(rows),
                split_block,
                lane_block(rows),
                whole_block(channels),
                whole_block(channels),
            ],
            out_specs=[
                whole_block(line, rows, channels),
                whole_block(rows, channels),
            ],
            scratch_shapes=[spread_of(2 * MARGIN), pltpu.VMEM((tiles, rows, LANES), F32)],
        ),
        out_shape=[
            jax.ShapeDtypeStruct((line, rows, channels), BF16),
            jax.ShapeDtypeStruct((rows, channels), F32),
        ],
        compiler_params=params(),
        cost_estimate=NO_COST,
        name="rim_conv",
    )(parity, inner, outer, split, partial, norm_gain, norm_bias)

    centered, upstream_line[2] = lax.optimization_barrier((centered, upstream_line[2]))
    for _ in range(3, line):
        upstream_line.append(next_in_line(upstream_line[-1]))
    gathered = lax.all_to_all(
        normed, "row", split_axis=0, concat_axis=0, tiled=True, axis_index_groups=lines
    )

    block = 512
    whole = whole_block(rows, channels)
    block_out, conv_grad, small = pl.pallas_call(
        mlp_kernel,
        grid=(units // block,),
        in_specs=[
            pl.BlockSpec((None, rows, channels), lambda f: (0, 0, 0)),
            pl.BlockSpec((block, channels), lambda f: (f, 0)),
            pl.BlockSpec((block, channels), lambda f: (f, 0)),
            whole,
            whole_block(channels),
            whole_block(channels),
            whole,
            whole,
        ],
        out_specs=[
            whole,
            whole,
            whole_block(SUB, channels),
        ],
        out_shape=[
            jax.ShapeDtypeStruct((rows, channels), BF16),
            jax.ShapeDtypeStruct((rows, channels), BF16),
            jax.ShapeDtypeStruct((SUB, channels), F32),
        ],
        scratch_shapes=[
            pltpu.VMEM((rows, channels), F32),
            pltpu.VMEM((rows, channels), F32),
            pltpu.VMEM((rows, channels), BF16),
        ],
        compiler_params=params(),
        cost_estimate=NO_COST,
        name="mlp_both_ways",
    )(normed, weight_in, weight_out, centered, norm_gain, layer_scale, own, upstream)

    grad_inner, grad_outer = rims(conv_grad)

    half = count // 2
    alike = [[2 * k + p for k in range(half)] for p in range(2)]
    half_tiles = tiles // 2
    wide = half_tiles * LANES
    piece = -(-(TAP_ROWS + SUB) // half)
    piece += -piece % (2 * SUB)
    padded = piece * half

    def kernel_grad_half(side, name):
        def at(block_rows):
            return pl.BlockSpec((block_rows, LANES), lambda c, w: (0, w[1] * half_tiles + c))

        return pl.pallas_call(
            functools.partial(kernel_grad_kernel, planes, height),
            grid_spec=pltpu.PrefetchScalarGridSpec(
                num_scalar_prefetch=1,
                grid=(half_tiles,),
                in_specs=[at(rows), at(rows), at(rows), at(rows), at(SUB)],
                out_specs=pl.BlockSpec((padded, LANES), lambda c, w: (0, c)),
                scratch_shapes=[
                    spread_of(2 * MARGIN + planes),
                    pltpu.VMEM((2, KS, SUB * SUB, LANES), F32),
                    pltpu.VMEM((9, KS, SUB, LANES), F32),
                    pltpu.VMEM((padded, LANES), F32),
                ],
            ),
            out_shape=jax.ShapeDtypeStruct((padded, wide), BF16),
            compiler_params=params(),
            cost_estimate=NO_COST,
            name=name,
        )(jnp.stack([core, side]), inner, own, outer, conv_grad, small)

    half_sent = kernel_grad_half(1 - core, "kernel_grad_other_half")
    half_got = lax.ppermute(half_sent, "row", other_core)
    half_kept = kernel_grad_half(core, "kernel_grad_own_half")
    half_got, grad_inner, grad_outer = lax.optimization_barrier((half_got, grad_inner, grad_outer))
    sums = (half_kept.astype(F32) + half_got.astype(F32)).astype(BF16)

    share = units // count
    tokens = line * rows
    base = me // quad * quad
    side = lax.rem(me, quad) // 2
    place = lax.rem(me // quad + line - jnp.arange(line, dtype=jnp.int32), line)
    which = jnp.concatenate(
        [
            jnp.stack(
                [
                    base + 1 - core,
                    base + 3 - core,
                    base + 2 - 2 * side + core,
                    base + 2 * side + core,
                ]
            ).astype(jnp.int32),
            place.astype(jnp.int32),
        ]
    )
    pair = (2, 2, share, channels)

    def chunk(at):
        return pl.BlockSpec((share, channels), lambda s, w: (w[s + at], 0))

    sets = [whole_block(channels), whole_block(line, rows, channels)]
    cotangents = [whole_block(rows, channels)] * line
    aligned = [pltpu.VMEM((tokens, channels), BF16)]

    which, sums = lax.optimization_barrier((which, sums))
    scattered = lax.all_to_all(
        sums.reshape(half, piece, wide),
        "row",
        split_axis=0,
        concat_axis=0,
        tiled=True,
        axis_index_groups=alike,
    )
    for_other = pl.pallas_call(
        other_core_terms_kernel,
        grid_spec=pltpu.PrefetchScalarGridSpec(
            num_scalar_prefetch=1,
            grid=(2,),
            in_specs=[chunk(0), chunk(0)] + sets + cotangents,
            out_specs=pl.BlockSpec((1,) + pair[1:], lambda s, w: (s, 0, 0, 0)),
            scratch_shapes=aligned,
        ),
        out_shape=jax.ShapeDtypeStruct(pair, BF16),
        compiler_params=params(),
        cost_estimate=NO_COST,
        name="weight_grads_other_core",
    )(which, weight_in, weight_out, layer_scale, gathered, *upstream_line)
    scattered, for_other = lax.optimization_barrier((scattered, for_other))
    from_other = lax.ppermute(for_other, "row", other_core)
    copies = pl.pallas_call(
        spread_sum_kernel,
        in_specs=[whole_block(half, piece, wide)],
        out_specs=whole_block(half, piece, wide),
        out_shape=jax.ShapeDtypeStruct((half, piece, wide), BF16),
        grid=(1,),
        compiler_params=params(),
        cost_estimate=NO_COST,
        name="kernel_grad_sum",
    )(scattered)
    which, copies = lax.optimization_barrier((which, copies))
    totals = lax.all_to_all(
        copies, "row", split_axis=0, concat_axis=0, tiled=True, axis_index_groups=alike
    )
    other_totals = lax.ppermute(totals, "row", other_core)

    sent, kept = pl.pallas_call(
        own_core_terms_kernel,
        grid_spec=pltpu.PrefetchScalarGridSpec(
            num_scalar_prefetch=1,
            grid=(2,),
            in_specs=[chunk(2), chunk(2)]
            + sets
            + [pl.BlockSpec((1,) + pair[1:], lambda s, w: ((w[s + 2] - w[0] // 4 * 4) // 2, 0, 0, 0))]
            + cotangents,
            out_specs=[whole_block(2, share, channels)] * 2,
            scratch_shapes=aligned,
        ),
        out_shape=[
            jax.ShapeDtypeStruct(pair[1:], BF16),
            jax.ShapeDtypeStruct(pair[1:], F32),
        ],
        compiler_params=params(),
        cost_estimate=NO_COST,
        name="weight_grads_own_core",
    )(which, weight_in, weight_out, layer_scale, gathered, from_other, *upstream_line)
    got = lax.ppermute(sent, "row", other_side)

    conv_own, kept = lax.optimization_barrier((conv_grad, kept))
    voxel_grad = pl.pallas_call(
        functools.partial(input_grad_kernel, planes, height),
        grid_spec=pltpu.PrefetchScalarGridSpec(
            num_scalar_prefetch=1,
            grid=(tiles,),
            in_specs=[
                lane_block(rows),
                lane_block(rows),
                lane_block(rows),
                split_block,
                lane_block(rows),
            ],
            out_specs=lane_block(rows),
            scratch_shapes=[spread_of(2 * MARGIN + planes)],
        ),
        out_shape=jax.ShapeDtypeStruct((rows, channels), BF16),
        compiler_params=params(),
        cost_estimate=NO_COST,
        name="input_grad_conv",
    )(parity, grad_inner, conv_own, grad_outer, split, upstream)

    kernel_grad, *vector_grads = pl.pallas_call(
        unpack_kernel,
        grid_spec=pltpu.PrefetchScalarGridSpec(
            num_scalar_prefetch=1,
            grid=(1,),
            in_specs=[whole_block(half, piece, wide)] * 2,
            out_specs=[whole_block(TAP_ROWS, channels)] + [whole_block(channels)] * 3,
        ),
        out_shape=[jax.ShapeDtypeStruct((TAP_ROWS, channels), F32)]
        + [jax.ShapeDtypeStruct((channels,), F32)] * 3,
        compiler_params=params(),
        cost_estimate=NO_COST,
        name="kernel_grad_unpack",
    )(parity, totals, other_totals)

    weight_in_grad, weight_out_grad = pl.pallas_call(
        last_sum_kernel,
        grid=(1,),
        in_specs=[whole_block(2, share, channels)] * 2,
        out_specs=[whole_block(share, channels)] * 2,
        out_shape=[jax.ShapeDtypeStruct((share, channels), F32)] * 2,
        compiler_params=params(),
        cost_estimate=NO_COST,
        name="weight_grads_sum",
    )(kept, got)

    return (
        block_out.reshape(voxels.shape),
        voxel_grad.reshape(voxels.shape),
        kernel_grad,
        *vector_grads,
        weight_in_grad,
        weight_out_grad,
    )


def solution(mesh):
    in_specs = (
        P(("group", "row"), None, None, None),
        P(),
        P(),
        P(),
        P(),
        P(),
        P(),
        P(("group", "row"), None, None, None),
    )
    out_specs = (
        P(("group", "row"), None, None, None),
        P(("group", "row"), None, None, None),
        P("group", None),
        P("group"),
        P("group"),
        P("group"),
        P(("group", "row"), None),
        P(("group", "row"), None),
    )
    return jax.shard_map(
        on_device, mesh=mesh, in_specs=in_specs, out_specs=out_specs, check_vma=False
    )
```

```python
import functools

import jax
import jax.numpy as jnp
from jax import lax
from jax.experimental import pallas as pl
from jax.experimental.pallas import tpu as pltpu
from jax.sharding import PartitionSpec as P

KS = 7
MARGIN = KS // 2
LANES = 128
SUB = 8
PAD = 3 * SUB
TAP_ROWS = KS * KS * KS

root_half = 0.7071067811865476
inv_root_tau = 0.3989422804014327
norm_eps = 1e-06
erf_step = 0.3275911
erf_terms = tuple(
    0.5 * a for a in (0.254829592, -0.284496736, 1.421413741, -1.453152027, 1.061405429)
)

NO_COST = pl.CostEstimate(flops=0, bytes_accessed=0, transcendentals=0)

F32 = jnp.float32
BF16 = jnp.bfloat16


def split_source(v):
    terms = []
    for a, b in ((v[0] + v[2], v[1] + v[3]), (v[2], v[3]), (v[0], v[1])):
        terms += [a + b, b, a]
    return terms


def split_taps(t):
    terms = []
    for s in (
        (t[2], t[3], t[4]),
        (t[4] - t[2], t[5] - t[3], t[6] - t[4]),
        (t[0] - t[2], t[1] - t[3], t[2] - t[4]),
    ):
        terms += [s[1], s[2] - s[1], s[0] - s[1]]
    return terms


def split_grads(g):
    terms = []
    for a, b in ((g[0] + g[2], g[1] + g[3]), (g[0], g[1]), (g[2], g[3])):
        terms += [a + b, a, b]
    return terms


def join_outputs(m):
    pair = [(m[3 * k] + m[3 * k + 1], m[3 * k] + m[3 * k + 2]) for k in range(3)]
    return [
        pair[0][0] + pair[1][0],
        pair[0][1] + pair[1][1],
        pair[0][0] + pair[2][0],
        pair[0][1] + pair[2][1],
    ]


def join_taps(m):
    p, q, r = [
        (m[3 * k + 2], m[3 * k] - m[3 * k + 1] - m[3 * k + 2], m[3 * k + 1]) for k in range(3)
    ]
    return [
        r[0],
        r[1],
        p[0] - q[0] - r[0] + r[2],
        p[1] - q[1] - r[1],
        p[2] - q[2] - r[2] + q[0],
        q[1],
        q[2],
    ]


def tree_sum(terms):
    while len(terms) > 1:
        terms = [
            terms[k] + terms[k + 1] if k + 1 < len(terms) else terms[k]
            for k in range(0, len(terms), 2)
        ]
    return terms[0]


def stage_source(wanted, height, spread):
    row = height * SUB
    for at, (block, x) in enumerate(wanted):
        plane = block[x * row : (x + 1) * row, :].astype(F32)
        lines = [plane[y * SUB : (y + 1) * SUB, :] for y in range(height)]
        for j, term in enumerate(split_source(lines)):
            spread[j, at, SUB : 2 * SUB, :] = term


def rim_planes(left, right, planes):
    wanted = [(left, x) for x in range(planes - MARGIN, planes)]
    return wanted + [(right, x) for x in range(MARGIN)]


def all_planes(left, own, right, planes):
    rim = rim_planes(left, right, planes)
    return rim[:MARGIN] + [(own, x) for x in range(planes)] + rim[MARGIN:]


def by_core(core, inner, outer, stage):
    @pl.when(core[0] == 0)
    def _():
        stage(outer, inner)

    @pl.when(core[0] != 0)
    def _():
        stage(inner, outer)


def clear_rims(spread):
    zeros = jnp.zeros(spread.shape[:2] + (SUB, LANES), F32)
    spread[:, :, :SUB, :] = zeros
    spread[:, :, 2 * SUB :, :] = zeros


def stage_taps(taps, split):
    for dx in range(KS):
        rows = []
        for dy in range(KS):
            first = dx * KS * KS + dy * KS
            if first + SUB <= TAP_ROWS:
                rows.append(taps[first : first + SUB, :])
            else:
                rows.append(pltpu.roll(taps[TAP_ROWS - SUB : TAP_ROWS, :], SUB - 1, 0))
        for j, term in enumerate(split_taps(rows)):
            split[j, dx] = term


REVERSED = (0, 2, 1, 6, 8, 7, 3, 5, 4)


def convolve(spread, split, planes, held, flipped):
    terms = []
    for j in range(9):
        sums = [None] * planes
        for dz in range(KS):
            first = SUB - MARGIN + dz
            source = {x: spread[j, at, first : first + SUB, :] for at, x in enumerate(held)}
            weights = []
            for dx in range(KS):
                if flipped:
                    tap = split[REVERSED[j], KS - 1 - dx, KS - 1 - dz : KS - dz, :]
                else:
                    tap = split[j, dx, dz : dz + 1, :]
                weights.append(jnp.broadcast_to(tap, (SUB, LANES)))
            for x in range(planes):
                part = tree_sum(
                    [source[x + dx] * weights[dx] for dx in range(KS) if x + dx in source]
                )
                sums[x] = part if sums[x] is None else sums[x] + part
        terms.append(sums)
    return [join_outputs([terms[j][x] for j in range(9)]) for x in range(planes)]


def own_conv_kernel(planes, height, own, taps, out, split, spread):
    @pl.when(pl.program_id(0) == 0)
    def _():
        clear_rims(spread)

    stage_source([(own, x) for x in range(planes)], height, spread)
    stage_taps(taps, split)
    rows = convolve(spread, split, planes, range(MARGIN, MARGIN + planes), False)
    for x in range(planes):
        for y in range(height):
            at = (x * height + y) * SUB
            out[at : at + SUB, :] = rows[x][y]


def rim_conv_kernel(
    planes, height, core, inner, outer, split, partial, gain, bias, normed, centered, spread, conv
):
    step = pl.program_id(0)

    @pl.when(step == 0)
    def _():
        clear_rims(spread)

    def stage(left, right):
        stage_source(rim_planes(left, right, planes), height, spread)

    by_core(core, inner, outer, stage)
    held = list(range(MARGIN)) + list(range(MARGIN + planes, 2 * MARGIN + planes))
    rows = convolve(spread, split, planes, held, False)
    for x in range(planes):
        for y in range(height):
            at = (x * height + y) * SUB
            conv[step, at : at + SUB, :] = rows[x][y] + partial[at : at + SUB, :]

    @pl.when(step == pl.num_programs(0) - 1)
    def _():
        tiles = conv.shape[0]
        channels = tiles * LANES
        parts = [conv[k] for k in range(tiles)]
        gains = gain[...].reshape(1, channels)
        biases = bias[...].reshape(1, channels)
        average = jnp.sum(tree_sum(parts), axis=1, keepdims=True) * (1.0 / channels)
        parts = [part - average for part in parts]
        variance = jnp.sum(
            tree_sum([part * part for part in parts]), axis=1, keepdims=True
        ) * (1.0 / channels)
        inverse = lax.rsqrt(variance + norm_eps)
        for k in range(tiles):
            lanes = slice(k * LANES, (k + 1) * LANES)
            centered[:, lanes] = parts[k]
            value = parts[k] * inverse
            whole = (value * gains[:, lanes] + biases[:, lanes]).astype(BF16)
            for copy in range(normed.shape[0]):
                normed[copy, :, lanes] = whole


def input_grad_kernel(
    planes, height, core, inner, own, outer, taps, cotangent, out, spread, split
):
    @pl.when(pl.program_id(0) == 0)
    def _():
        clear_rims(spread)

    def stage(left, right):
        stage_source(all_planes(left, own, right, planes), height, spread)

    by_core(core, inner, outer, stage)
    stage_taps(taps, split)
    rows = convolve(spread, split, planes, range(2 * MARGIN + planes), True)
    for x in range(planes):
        at = x * height * SUB
        whole = jnp.concatenate(rows[x], axis=0)
        upstream = cotangent[at : at + height * SUB, :].astype(F32)
        out[at : at + height * SUB, :] = (upstream + whole).astype(BF16)


def kernel_grad_kernel(
    planes, height, which, inner, own, outer, grads, small, sent, kept, spread, products, joined, flat
):
    @pl.when(pl.program_id(0) == 0)
    def _():
        clear_rims(spread)
        products[...] = jnp.zeros(products.shape, F32)
        flat[...] = jnp.zeros(flat.shape, F32)

    def stage(left, right):
        stage_source(all_planes(left, own, right, planes), height, spread)

    by_core(which, inner, outer, stage)
    upstream = []
    for x in range(planes):
        plane = grads[x * height * SUB : (x + 1) * height * SUB, :].astype(F32)
        upstream.append(
            split_grads([plane[y * SUB : (y + 1) * SUB, :] for y in range(height)])
        )
    for j in range(9):
        for dz in range(KS):
            first = SUB - MARGIN + dz
            source = [
                spread[j, x, first : first + SUB, :] for x in range(planes + KS - 1)
            ]
            for dx in range(KS):
                products[j % 2, dx, dz * SUB : (dz + 1) * SUB, :] = tree_sum(
                    [source[x + dx] * upstream[x][j] for x in range(planes)]
                )
        for dx in range(KS):
            joined[j, dx] = tree_sum(
                [products[j % 2, dx, pl.ds(s, SUB, stride=SUB), :] for s in range(SUB)]
            )
    for dx in range(KS):
        for dy, tile in enumerate(join_taps([joined[j, dx] for j in range(9)])):
            row = dx * KS * KS + dy * KS
            flat[row : row + SUB, :] = tile
    flat[TAP_ROWS : TAP_ROWS + SUB, :] = small[...]
    step = pl.program_id(0)
    half = pl.num_programs(0) // 2

    @pl.when(step < half)
    def _():
        sent[...] = flat[...].astype(BF16)

    @pl.when(step >= half)
    def _():
        kept[...] = flat[...].astype(BF16)


def mlp_kernel(
    normed,
    weight_in,
    weight_out,
    centered,
    norm_gain,
    layer_scale,
    voxels,
    cotangent,
    block_out,
    conv_grad,
    small,
    mixed,
    back,
    mixed_grad,
):
    step = pl.program_id(0)
    gain = norm_gain[...].reshape(1, -1)
    scale = layer_scale[...].reshape(1, -1)

    @pl.when(step == 0)
    def _():
        mixed_grad[...] = (scale * cotangent[...].astype(F32)).astype(BF16)

    hidden = lax.dot_general(
        normed[...], weight_in[...], (((1,), (1,)), ((), ())), preferred_element_type=F32
    )
    act_grad = lax.dot_general(
        mixed_grad[...], weight_out[...], (((1,), (1,)), ((), ())), preferred_element_type=F32
    )
    activated, hidden_grad = slopes(hidden, act_grad)
    forward = jnp.dot(activated, weight_out[...], preferred_element_type=F32)
    backward = jnp.dot(hidden_grad, weight_in[...], preferred_element_type=F32)

    @pl.when(step == 0)
    def _():
        mixed[...] = forward
        back[...] = backward

    @pl.when(step > 0)
    def _():
        mixed[...] += forward
        back[...] += backward

    @pl.when(step == pl.num_programs(0) - 1)
    def _():
        channels = gain.shape[1]
        whole = mixed[...]
        block_out[...] = (voxels[...].astype(F32) + scale * whole).astype(BF16)
        scale_local = jnp.sum(cotangent[...].astype(F32) * whole, axis=0, keepdims=True)
        grad = back[...]
        deviation = centered[...]
        variance = jnp.sum(deviation * deviation, axis=1, keepdims=True) * (1.0 / channels)
        inverse = lax.rsqrt(variance + norm_eps)
        one = deviation * inverse
        bias_local = jnp.sum(grad, axis=0, keepdims=True)
        gain_local = jnp.sum(grad * one, axis=0, keepdims=True)
        small[...] = jnp.concatenate(
            [gain_local, bias_local, scale_local, jnp.zeros((SUB - 3, channels), F32)], axis=0
        )
        scaled = grad * gain
        average = jnp.sum(scaled, axis=1, keepdims=True) * (1.0 / channels)
        slant = jnp.sum(scaled * one, axis=1, keepdims=True) * (1.0 / channels)
        conv_grad[...] = (inverse * (scaled - average - one * slant)).astype(BF16)


def slopes(hidden, act_grad):
    bell = jnp.exp(-0.5 * hidden * hidden)
    below = 1.0 + (erf_step * root_half) * jnp.abs(hidden)
    t = pl.reciprocal(below, approx=True)
    t = t * (2.0 - below * t)
    poly = erf_terms[-1]
    for term in erf_terms[-2::-1]:
        poly = poly * t + term
    tail = poly * t * bell
    cover = jnp.where(hidden < 0.0, tail, 1.0 - tail)
    activated = (hidden * cover).astype(BF16)
    slope = cover + hidden * bell * inv_root_tau
    return activated, (act_grad * slope).astype(BF16)


def weight_grad_terms(which, weight_in, weight_out, scale, normed, cotangents, aligned):
    rows = normed.shape[1]
    line = len(cotangents)
    scales = scale[...].reshape(1, -1)
    mixed_grad = jnp.concatenate(
        [(scales * part[...].astype(F32)).astype(BF16) for part in cotangents], axis=0
    )
    for k in range(line):
        aligned[k * rows : (k + 1) * rows, :] = normed[which[4 + k]]
    across = (((1,), (1,)), ((), ()))
    hidden = lax.dot_general(weight_in[...], aligned[...], across, preferred_element_type=F32)
    act_grad = lax.dot_general(weight_out[...], mixed_grad, across, preferred_element_type=F32)
    activated, hidden_grad = slopes(hidden, act_grad)
    return (
        jnp.dot(hidden_grad, aligned[...], preferred_element_type=F32),
        jnp.dot(activated, mixed_grad, preferred_element_type=F32),
    )


def other_core_terms_kernel(which, weight_in, weight_out, scale, normed, *rest):
    *cotangents, out, aligned = rest
    terms = weight_grad_terms(which, weight_in, weight_out, scale, normed, cotangents, aligned)
    for k in range(2):
        out[0, k] = terms[k].astype(BF16)


def own_core_terms_kernel(which, weight_in, weight_out, scale, normed, got, *rest):
    *cotangents, sent, kept, aligned = rest
    terms = weight_grad_terms(which, weight_in, weight_out, scale, normed, cotangents, aligned)
    step = pl.program_id(0)
    for k in range(2):
        total = terms[k] + got[0, k].astype(F32)

        @pl.when(step == 0)
        def _():
            sent[k] = total.astype(BF16)

        @pl.when(step == 1)
        def _():
            kept[k] = total


def last_sum_kernel(kept, got, in_grad, out_grad):
    for k, out in enumerate((in_grad, out_grad)):
        out[...] = kept[k] + got[k].astype(F32)


def chip_sum_kernel(kept, got, out):
    out[...] = (kept[...].astype(F32) + got[...].astype(F32)).astype(BF16)


def spread_sum_kernel(parts, out):
    total = tree_sum([parts[k].astype(F32) for k in range(parts.shape[0])]).astype(BF16)
    for copy in range(out.shape[0]):
        out[copy] = total


def unpack_kernel(core, own, other, out, *small):
    piece, wide = own.shape[1:]

    def unpack(*halves):
        last = []
        for side, parts in enumerate(halves):
            lanes = slice(side * wide, (side + 1) * wide)
            for k in range(-(-TAP_ROWS // piece)):
                first = k * piece
                length = min(piece, TAP_ROWS - first)
                out[first : first + length, lanes] = parts[k].astype(F32)[:length, :]
            k = TAP_ROWS // piece
            last.append(parts[k].astype(F32))
        rows = jnp.concatenate(last, axis=1)
        first = TAP_ROWS % piece
        for k, line in enumerate(small):
            line[...] = rows[first + k : first + k + 1, :].reshape(line.shape)

    by_core(core, own, other, lambda outer, inner: unpack(inner, outer))


def params(limit=48):
    return pltpu.CompilerParams(vmem_limit_bytes=limit * 1024 * 1024)


def lane_block(rows):
    return pl.BlockSpec((rows, LANES), lambda c, *_: (0, c))


def whole_block(*shape):
    return pl.BlockSpec(shape, lambda *_: (0,) * len(shape))


def rims(cells):
    count = lax.axis_size("row")
    between = [(i, i + 1) for i in range(1, count - 1, 2)]
    return (
        lax.ppermute(cells, "row", [(i, i ^ 1) for i in range(count)]),
        lax.ppermute(cells, "row", between + [(j, i) for i, j in between]),
    )


def on_device(
    voxels, dw_kernel, norm_gain, norm_bias, weight_in, weight_out, layer_scale, cotangent
):
    planes, height, breadth, channels = voxels.shape
    rows = planes * height * breadth
    units = weight_in.shape[0]
    count = lax.axis_size("row")
    me = lax.axis_index("row")
    quad = 4
    line = count // quad
    lines = [[quad * k + p for k in range(line)] for p in range(quad)]
    other_core = [(i, i ^ 1) for i in range(count)]
    other_side = [(i, i ^ 2) for i in range(count)]
    tiles = channels // LANES

    own = voxels.reshape(rows, channels)
    upstream = cotangent.reshape(rows, channels)
    core = lax.rem(me, 2).astype(jnp.int32)
    parity = core.reshape(1)

    inner, outer = rims(own)

    def along_line(cells, steps):
        return lax.ppermute(cells, "row", [(i, (i + quad * steps) % count) for i in range(count)])

    upstream_line = [upstream] + [None] * (line - 1)
    upstream_line[1] = along_line(upstream, 1)
    upstream_line[-1] = along_line(upstream, -1)

    def spread_of(held):
        return pltpu.VMEM((9, held, PAD, LANES), F32)

    split_block = pl.BlockSpec((None, 9, KS, SUB, LANES), lambda c, *_: (c, 0, 0, 0, 0))
    partial, split = pl.pallas_call(
        functools.partial(own_conv_kernel, planes, height),
        grid=(tiles,),
        in_specs=[lane_block(rows), lane_block(TAP_ROWS)],
        out_specs=[lane_block(rows), split_block],
        out_shape=[
            jax.ShapeDtypeStruct((rows, channels), F32),
            jax.ShapeDtypeStruct((tiles, 9, KS, SUB, LANES), F32),
        ],
        scratch_shapes=[spread_of(planes)],
        compiler_params=params(),
        cost_estimate=NO_COST,
        name="own_conv",
    )(own, dw_kernel)

    partial, upstream_line[1], upstream_line[-1] = lax.optimization_barrier(
        (partial, upstream_line[1], upstream_line[-1])
    )
    for k in range(2, line - 1):
        upstream_line[k] = along_line(upstream_line[k - 1], 1)
    normed, centered = pl.pallas_call(
        functools.partial(rim_conv_kernel, planes, height),
        grid_spec=pltpu.PrefetchScalarGridSpec(
            num_scalar_prefetch=1,
            grid=(tiles,),
            in_specs=[
                lane_block(rows),
                lane_block(rows),
                split_block,
                lane_block(rows),
                whole_block(channels),
                whole_block(channels),
            ],
            out_specs=[
                whole_block(line, rows, channels),
                whole_block(rows, channels),
            ],
            scratch_shapes=[spread_of(2 * MARGIN), pltpu.VMEM((tiles, rows, LANES), F32)],
        ),
        out_shape=[
            jax.ShapeDtypeStruct((line, rows, channels), BF16),
            jax.ShapeDtypeStruct((rows, channels), F32),
        ],
        compiler_params=params(),
        cost_estimate=NO_COST,
        name="rim_conv",
    )(parity, inner, outer, split, partial, norm_gain, norm_bias)

    normed, centered, upstream_line[2] = lax.optimization_barrier(
        (normed, centered, upstream_line[2])
    )
    gathered = lax.all_to_all(
        normed, "row", split_axis=0, concat_axis=0, tiled=True, axis_index_groups=lines
    )

    block = 512
    whole = whole_block(rows, channels)
    block_out, conv_grad, small = pl.pallas_call(
        mlp_kernel,
        grid=(units // block,),
        in_specs=[
            pl.BlockSpec((None, rows, channels), lambda f: (0, 0, 0)),
            pl.BlockSpec((block, channels), lambda f: (f, 0)),
            pl.BlockSpec((block, channels), lambda f: (f, 0)),
            whole,
            whole_block(channels),
            whole_block(channels),
            whole,
            whole,
        ],
        out_specs=[
            whole,
            whole,
            whole_block(SUB, channels),
        ],
        out_shape=[
            jax.ShapeDtypeStruct((rows, channels), BF16),
            jax.ShapeDtypeStruct((rows, channels), BF16),
            jax.ShapeDtypeStruct((SUB, channels), F32),
        ],
        scratch_shapes=[
            pltpu.VMEM((rows, channels), F32),
            pltpu.VMEM((rows, channels), F32),
            pltpu.VMEM((rows, channels), BF16),
        ],
        compiler_params=params(),
        cost_estimate=NO_COST,
        name="mlp_both_ways",
    )(normed, weight_in, weight_out, centered, norm_gain, layer_scale, own, upstream)

    grad_inner, grad_outer = rims(conv_grad)

    half = count // 2
    alike = [[2 * k + p for k in range(half)] for p in range(2)]
    half_tiles = tiles // 2
    wide = half_tiles * LANES
    piece = -(-(TAP_ROWS + SUB) // half)
    piece += -piece % (2 * SUB)
    padded = piece * half

    def tile_of(block_rows):
        def at(c, w):
            return 0, (c + w[1] * half_tiles) % tiles

        return pl.BlockSpec((block_rows, LANES), at)

    half_sent, half_kept = pl.pallas_call(
        functools.partial(kernel_grad_kernel, planes, height),
        grid_spec=pltpu.PrefetchScalarGridSpec(
            num_scalar_prefetch=1,
            grid=(tiles,),
            in_specs=[tile_of(rows), tile_of(rows), tile_of(rows), tile_of(rows), tile_of(SUB)],
            out_specs=[
                pl.BlockSpec((padded, LANES), lambda c, w: (0, jnp.minimum(c, half_tiles - 1))),
                pl.BlockSpec((padded, LANES), lambda c, w: (0, jnp.maximum(c - half_tiles, 0))),
            ],
            scratch_shapes=[
                spread_of(2 * MARGIN + planes),
                pltpu.VMEM((2, KS, SUB * SUB, LANES), F32),
                pltpu.VMEM((9, KS, SUB, LANES), F32),
                pltpu.VMEM((padded, LANES), F32),
            ],
        ),
        out_shape=[jax.ShapeDtypeStruct((padded, wide), BF16)] * 2,
        compiler_params=params(),
        cost_estimate=NO_COST,
        name="kernel_grad_terms",
    )(jnp.stack([core, 1 - core]), inner, own, outer, conv_grad, small)

    share = units // count
    tokens = line * rows
    base = me // quad * quad
    side = lax.rem(me, quad) // 2
    place = lax.rem(me // quad + line - jnp.arange(line, dtype=jnp.int32), line)
    which = jnp.concatenate(
        [
            jnp.stack(
                [
                    base + 1 - core,
                    base + 3 - core,
                    base + 2 - 2 * side + core,
                    base + 2 * side + core,
                ]
            ).astype(jnp.int32),
            place.astype(jnp.int32),
        ]
    )
    pair = (2, 2, share, channels)

    def chunk(at):
        return pl.BlockSpec((share, channels), lambda s, w: (w[s + at], 0))

    sets = [whole_block(channels), whole_block(line, rows, channels)]
    cotangents = [whole_block(rows, channels)] * line
    aligned = [pltpu.VMEM((tokens, channels), BF16)]

    which, half_sent, half_kept, grad_inner, grad_outer = lax.optimization_barrier(
        (which, half_sent, half_kept, grad_inner, grad_outer)
    )
    half_got = lax.ppermute(half_sent, "row", other_core)
    for_other = pl.pallas_call(
        other_core_terms_kernel,
        grid_spec=pltpu.PrefetchScalarGridSpec(
            num_scalar_prefetch=1,
            grid=(2,),
            in_specs=[chunk(0), chunk(0)] + sets + cotangents,
            out_specs=pl.BlockSpec((1,) + pair[1:], lambda s, w: (s, 0, 0, 0)),
            scratch_shapes=aligned,
        ),
        out_shape=jax.ShapeDtypeStruct(pair, BF16),
        compiler_params=params(),
        cost_estimate=NO_COST,
        name="weight_grads_other_core",
    )(which, weight_in, weight_out, layer_scale, gathered, *upstream_line)
    half_kept, for_other = lax.optimization_barrier((half_kept, for_other))
    from_other = lax.ppermute(for_other, "row", other_core)
    sums = pl.pallas_call(
        chip_sum_kernel,
        in_specs=[whole_block(padded, wide)] * 2,
        out_specs=whole_block(padded, wide),
        out_shape=jax.ShapeDtypeStruct((padded, wide), BF16),
        grid=(1,),
        compiler_params=params(),
        cost_estimate=NO_COST,
        name="kernel_grad_chip_sum",
    )(half_kept, half_got)
    scattered = lax.all_to_all(
        sums.reshape(half, piece, wide),
        "row",
        split_axis=0,
        concat_axis=0,
        tiled=True,
        axis_index_groups=alike,
    )
    sent, kept = pl.pallas_call(
        own_core_terms_kernel,
        grid_spec=pltpu.PrefetchScalarGridSpec(
            num_scalar_prefetch=1,
            grid=(2,),
            in_specs=[chunk(2), chunk(2)]
            + sets
            + [pl.BlockSpec((1,) + pair[1:], lambda s, w: ((w[s + 2] - w[0] // 4 * 4) // 2, 0, 0, 0))]
            + cotangents,
            out_specs=[whole_block(2, share, channels)] * 2,
            scratch_shapes=aligned,
        ),
        out_shape=[
            jax.ShapeDtypeStruct(pair[1:], BF16),
            jax.ShapeDtypeStruct(pair[1:], F32),
        ],
        compiler_params=params(),
        cost_estimate=NO_COST,
        name="weight_grads_own_core",
    )(which, weight_in, weight_out, layer_scale, gathered, from_other, *upstream_line)
    got = lax.ppermute(sent, "row", other_side)

    scattered, kept = lax.optimization_barrier((scattered, kept))
    copies = pl.pallas_call(
        spread_sum_kernel,
        in_specs=[whole_block(half, piece, wide)],
        out_specs=whole_block(half, piece, wide),
        out_shape=jax.ShapeDtypeStruct((half, piece, wide), BF16),
        grid=(1,),
        compiler_params=params(),
        cost_estimate=NO_COST,
        name="kernel_grad_sum",
    )(scattered)
    conv_own, copies = lax.optimization_barrier((conv_grad, copies))
    totals = lax.all_to_all(
        copies, "row", split_axis=0, concat_axis=0, tiled=True, axis_index_groups=alike
    )
    other_totals = lax.ppermute(totals, "row", other_core)

    voxel_grad = pl.pallas_call(
        functools.partial(input_grad_kernel, planes, height),
        grid_spec=pltpu.PrefetchScalarGridSpec(
            num_scalar_prefetch=1,
            grid=(tiles,),
            in_specs=[
                lane_block(rows),
                lane_block(rows),
                lane_block(rows),
                lane_block(TAP_ROWS),
                lane_block(rows),
            ],
            out_specs=lane_block(rows),
            scratch_shapes=[
                spread_of(2 * MARGIN + planes),
                pltpu.VMEM((9, KS, SUB, LANES), F32),
            ],
        ),
        out_shape=jax.ShapeDtypeStruct((rows, channels), BF16),
        compiler_params=params(),
        cost_estimate=NO_COST,
        name="input_grad_conv",
    )(parity, grad_inner, conv_own, grad_outer, dw_kernel, upstream)

    kernel_grad, *vector_grads = pl.pallas_call(
        unpack_kernel,
        grid_spec=pltpu.PrefetchScalarGridSpec(
            num_scalar_prefetch=1,
            grid=(1,),
            in_specs=[whole_block(half, piece, wide)] * 2,
            out_specs=[whole_block(TAP_ROWS, channels)] + [whole_block(channels)] * 3,
        ),
        out_shape=[jax.ShapeDtypeStruct((TAP_ROWS, channels), F32)]
        + [jax.ShapeDtypeStruct((channels,), F32)] * 3,
        compiler_params=params(),
        cost_estimate=NO_COST,
        name="kernel_grad_unpack",
    )(parity, totals, other_totals)

    weight_in_grad, weight_out_grad = pl.pallas_call(
        last_sum_kernel,
        grid=(1,),
        in_specs=[whole_block(2, share, channels)] * 2,
        out_specs=[whole_block(share, channels)] * 2,
        out_shape=[jax.ShapeDtypeStruct((share, channels), F32)] * 2,
        compiler_params=params(),
        cost_estimate=NO_COST,
        name="weight_grads_sum",
    )(kept, got)

    return (
        block_out.reshape(voxels.shape),
        voxel_grad.reshape(voxels.shape),
        kernel_grad,
        *vector_grads,
        weight_in_grad,
        weight_out_grad,
    )


def solution(mesh):
    in_specs = (
        P(("group", "row"), None, None, None),
        P(),
        P(),
        P(),
        P(),
        P(),
        P(),
        P(("group", "row"), None, None, None),
    )
    out_specs = (
        P(("group", "row"), None, None, None),
        P(("group", "row"), None, None, None),
        P("group", None),
        P("group"),
        P("group"),
        P("group"),
        P(("group", "row"), None),
        P(("group", "row"), None),
    )
    return jax.shard_map(
        on_device, mesh=mesh, in_specs=in_specs, out_specs=out_specs, check_vma=False
    )
```

```python
import functools

import jax
import jax.numpy as jnp
from jax import lax
from jax.experimental import pallas as pl
from jax.experimental.pallas import tpu as pltpu
from jax.sharding import PartitionSpec as P

KS = 7
MARGIN = KS // 2
LANES = 128
SUB = 8
PAD = 3 * SUB
TAP_ROWS = KS * KS * KS

root_half = 0.7071067811865476
inv_root_tau = 0.3989422804014327
norm_eps = 1e-06
erf_step = 0.3275911
erf_terms = tuple(
    0.5 * a for a in (0.254829592, -0.284496736, 1.421413741, -1.453152027, 1.061405429)
)

NO_COST = pl.CostEstimate(flops=0, bytes_accessed=0, transcendentals=0)

F32 = jnp.float32
BF16 = jnp.bfloat16


def split_source(v):
    terms = []
    for a, b in ((v[0] + v[2], v[1] + v[3]), (v[2], v[3]), (v[0], v[1])):
        terms += [a + b, b, a]
    return terms


def split_taps(t):
    terms = []
    for s in (
        (t[2], t[3], t[4]),
        (t[4] - t[2], t[5] - t[3], t[6] - t[4]),
        (t[0] - t[2], t[1] - t[3], t[2] - t[4]),
    ):
        terms += [s[1], s[2] - s[1], s[0] - s[1]]
    return terms


def split_grads(g):
    terms = []
    for a, b in ((g[0] + g[2], g[1] + g[3]), (g[0], g[1]), (g[2], g[3])):
        terms += [a + b, a, b]
    return terms


def join_outputs(m):
    pair = [(m[3 * k] + m[3 * k + 1], m[3 * k] + m[3 * k + 2]) for k in range(3)]
    return [
        pair[0][0] + pair[1][0],
        pair[0][1] + pair[1][1],
        pair[0][0] + pair[2][0],
        pair[0][1] + pair[2][1],
    ]


def join_taps(m):
    p, q, r = [
        (m[3 * k + 2], m[3 * k] - m[3 * k + 1] - m[3 * k + 2], m[3 * k + 1]) for k in range(3)
    ]
    return [
        r[0],
        r[1],
        p[0] - q[0] - r[0] + r[2],
        p[1] - q[1] - r[1],
        p[2] - q[2] - r[2] + q[0],
        q[1],
        q[2],
    ]


def tree_sum(terms):
    while len(terms) > 1:
        terms = [
            terms[k] + terms[k + 1] if k + 1 < len(terms) else terms[k]
            for k in range(0, len(terms), 2)
        ]
    return terms[0]


def stage_source(wanted, height, spread):
    row = height * SUB
    for at, (block, x) in enumerate(wanted):
        plane = block[x * row : (x + 1) * row, :].astype(F32)
        lines = [plane[y * SUB : (y + 1) * SUB, :] for y in range(height)]
        for j, term in enumerate(split_source(lines)):
            spread[j, at, SUB : 2 * SUB, :] = term


def rim_planes(left, right, planes):
    wanted = [(left, x) for x in range(planes - MARGIN, planes)]
    return wanted + [(right, x) for x in range(MARGIN)]


def all_planes(left, own, right, planes):
    rim = rim_planes(left, right, planes)
    return rim[:MARGIN] + [(own, x) for x in range(planes)] + rim[MARGIN:]


def by_core(core, inner, outer, stage):
    @pl.when(core[0] == 0)
    def _():
        stage(outer, inner)

    @pl.when(core[0] != 0)
    def _():
        stage(inner, outer)


def clear_rims(spread):
    zeros = jnp.zeros(spread.shape[:2] + (SUB, LANES), F32)
    spread[:, :, :SUB, :] = zeros
    spread[:, :, 2 * SUB :, :] = zeros


def stage_taps(taps, split):
    for dx in range(KS):
        rows = []
        for dy in range(KS):
            first = dx * KS * KS + dy * KS
            if first + SUB <= TAP_ROWS:
                rows.append(taps[first : first + SUB, :])
            else:
                rows.append(pltpu.roll(taps[TAP_ROWS - SUB : TAP_ROWS, :], SUB - 1, 0))
        for j, term in enumerate(split_taps(rows)):
            split[j, dx] = term


REVERSED = (0, 2, 1, 6, 8, 7, 3, 5, 4)


def convolve(spread, split, planes, held, flipped):
    terms = []
    for j in range(9):
        sums = [None] * planes
        for dz in range(KS):
            first = SUB - MARGIN + dz
            source = {x: spread[j, at, first : first + SUB, :] for at, x in enumerate(held)}
            weights = []
            for dx in range(KS):
                if flipped:
                    tap = split[REVERSED[j], KS - 1 - dx, KS - 1 - dz : KS - dz, :]
                else:
                    tap = split[j, dx, dz : dz + 1, :]
                weights.append(jnp.broadcast_to(tap, (SUB, LANES)))
            for x in range(planes):
                part = tree_sum(
                    [source[x + dx] * weights[dx] for dx in range(KS) if x + dx in source]
                )
                sums[x] = part if sums[x] is None else sums[x] + part
        terms.append(sums)
    return [join_outputs([terms[j][x] for j in range(9)]) for x in range(planes)]


def own_conv_kernel(planes, height, own, taps, out, split, spread):
    @pl.when(pl.program_id(0) == 0)
    def _():
        clear_rims(spread)

    stage_source([(own, x) for x in range(planes)], height, spread)
    stage_taps(taps, split)
    rows = convolve(spread, split, planes, range(MARGIN, MARGIN + planes), False)
    for x in range(planes):
        for y in range(height):
            at = (x * height + y) * SUB
            out[at : at + SUB, :] = rows[x][y]


def rim_conv_kernel(
    planes, height, core, inner, outer, split, partial, gain, bias, normed, centered, spread, conv
):
    step = pl.program_id(0)

    @pl.when(step == 0)
    def _():
        clear_rims(spread)

    def stage(left, right):
        stage_source(rim_planes(left, right, planes), height, spread)

    by_core(core, inner, outer, stage)
    held = list(range(MARGIN)) + list(range(MARGIN + planes, 2 * MARGIN + planes))
    rows = convolve(spread, split, planes, held, False)
    for x in range(planes):
        for y in range(height):
            at = (x * height + y) * SUB
            conv[step, at : at + SUB, :] = rows[x][y] + partial[at : at + SUB, :]

    @pl.when(step == pl.num_programs(0) - 1)
    def _():
        tiles = conv.shape[0]
        channels = tiles * LANES
        parts = [conv[k] for k in range(tiles)]
        gains = gain[...].reshape(1, channels)
        biases = bias[...].reshape(1, channels)
        average = jnp.sum(tree_sum(parts), axis=1, keepdims=True) * (1.0 / channels)
        parts = [part - average for part in parts]
        variance = jnp.sum(
            tree_sum([part * part for part in parts]), axis=1, keepdims=True
        ) * (1.0 / channels)
        inverse = lax.rsqrt(variance + norm_eps)
        for k in range(tiles):
            lanes = slice(k * LANES, (k + 1) * LANES)
            centered[:, lanes] = parts[k]
            value = parts[k] * inverse
            whole = (value * gains[:, lanes] + biases[:, lanes]).astype(BF16)
            for copy in range(normed.shape[0]):
                normed[copy, :, lanes] = whole


def input_grad_kernel(
    planes, height, core, inner, own, outer, taps, cotangent, out, spread, split
):
    @pl.when(pl.program_id(0) == 0)
    def _():
        clear_rims(spread)

    def stage(left, right):
        stage_source(all_planes(left, own, right, planes), height, spread)

    by_core(core, inner, outer, stage)
    stage_taps(taps, split)
    rows = convolve(spread, split, planes, range(2 * MARGIN + planes), True)
    for x in range(planes):
        at = x * height * SUB
        whole = jnp.concatenate(rows[x], axis=0)
        upstream = cotangent[at : at + height * SUB, :].astype(F32)
        out[at : at + height * SUB, :] = (upstream + whole).astype(BF16)


def kernel_grad_kernel(
    planes, height, which, inner, own, outer, grads, small, sent, kept, spread, products, joined, flat
):
    @pl.when(pl.program_id(0) == 0)
    def _():
        clear_rims(spread)
        products[...] = jnp.zeros(products.shape, F32)
        flat[...] = jnp.zeros(flat.shape, F32)

    def stage(left, right):
        stage_source(all_planes(left, own, right, planes), height, spread)

    by_core(which, inner, outer, stage)
    upstream = []
    for x in range(planes):
        plane = grads[x * height * SUB : (x + 1) * height * SUB, :].astype(F32)
        upstream.append(
            split_grads([plane[y * SUB : (y + 1) * SUB, :] for y in range(height)])
        )
    for j in range(9):
        for dz in range(KS):
            first = SUB - MARGIN + dz
            source = [
                spread[j, x, first : first + SUB, :] for x in range(planes + KS - 1)
            ]
            for dx in range(KS):
                products[j % 2, dx, dz * SUB : (dz + 1) * SUB, :] = tree_sum(
                    [source[x + dx] * upstream[x][j] for x in range(planes)]
                )
        for dx in range(KS):
            joined[j, dx] = tree_sum(
                [products[j % 2, dx, pl.ds(s, SUB, stride=SUB), :] for s in range(SUB)]
            )
    for dx in range(KS):
        for dy, tile in enumerate(join_taps([joined[j, dx] for j in range(9)])):
            row = dx * KS * KS + dy * KS
            flat[row : row + SUB, :] = tile
    flat[TAP_ROWS : TAP_ROWS + SUB, :] = small[...]
    step = pl.program_id(0)
    half = pl.num_programs(0) // 2

    @pl.when(step < half)
    def _():
        sent[...] = flat[...].astype(BF16)

    @pl.when(step >= half)
    def _():
        kept[...] = flat[...].astype(BF16)


def mlp_kernel(
    normed,
    weight_in,
    weight_out,
    centered,
    norm_gain,
    layer_scale,
    voxels,
    cotangent,
    block_out,
    conv_grad,
    small,
    mixed,
    back,
    mixed_grad,
):
    step = pl.program_id(0)
    gain = norm_gain[...].reshape(1, -1)
    scale = layer_scale[...].reshape(1, -1)

    @pl.when(step == 0)
    def _():
        mixed_grad[...] = (scale * cotangent[...].astype(F32)).astype(BF16)

    hidden = lax.dot_general(
        normed[...], weight_in[...], (((1,), (1,)), ((), ())), preferred_element_type=F32
    )
    act_grad = lax.dot_general(
        mixed_grad[...], weight_out[...], (((1,), (1,)), ((), ())), preferred_element_type=F32
    )
    activated, hidden_grad = slopes(hidden, act_grad)
    forward = jnp.dot(activated, weight_out[...], preferred_element_type=F32)
    backward = jnp.dot(hidden_grad, weight_in[...], preferred_element_type=F32)

    @pl.when(step == 0)
    def _():
        mixed[...] = forward
        back[...] = backward

    @pl.when(step > 0)
    def _():
        mixed[...] += forward
        back[...] += backward

    @pl.when(step == pl.num_programs(0) - 1)
    def _():
        channels = gain.shape[1]
        whole = mixed[...]
        block_out[...] = (voxels[...].astype(F32) + scale * whole).astype(BF16)
        scale_local = jnp.sum(cotangent[...].astype(F32) * whole, axis=0, keepdims=True)
        grad = back[...]
        deviation = centered[...]
        variance = jnp.sum(deviation * deviation, axis=1, keepdims=True) * (1.0 / channels)
        inverse = lax.rsqrt(variance + norm_eps)
        one = deviation * inverse
        bias_local = jnp.sum(grad, axis=0, keepdims=True)
        gain_local = jnp.sum(grad * one, axis=0, keepdims=True)
        small[...] = jnp.concatenate(
            [gain_local, bias_local, scale_local, jnp.zeros((SUB - 3, channels), F32)], axis=0
        )
        scaled = grad * gain
        average = jnp.sum(scaled, axis=1, keepdims=True) * (1.0 / channels)
        slant = jnp.sum(scaled * one, axis=1, keepdims=True) * (1.0 / channels)
        conv_grad[...] = (inverse * (scaled - average - one * slant)).astype(BF16)


def slopes(hidden, act_grad):
    bell = jnp.exp(-0.5 * hidden * hidden)
    below = 1.0 + (erf_step * root_half) * jnp.abs(hidden)
    t = pl.reciprocal(below, approx=True)
    t = t * (2.0 - below * t)
    poly = erf_terms[-1]
    for term in erf_terms[-2::-1]:
        poly = poly * t + term
    tail = poly * t * bell
    cover = jnp.where(hidden < 0.0, tail, 1.0 - tail)
    activated = (hidden * cover).astype(BF16)
    slope = cover + hidden * bell * inv_root_tau
    return activated, (act_grad * slope).astype(BF16)


def weight_grad_terms(which, weight_in, weight_out, scale, normed, cotangents, aligned):
    rows = normed.shape[1]
    line = len(cotangents)
    scales = scale[...].reshape(1, -1)
    mixed_grad = jnp.concatenate(
        [(scales * part[...].astype(F32)).astype(BF16) for part in cotangents], axis=0
    )
    for k in range(line):
        aligned[k * rows : (k + 1) * rows, :] = normed[which[4 + k]]
    across = (((1,), (1,)), ((), ()))
    hidden = lax.dot_general(weight_in[...], aligned[...], across, preferred_element_type=F32)
    act_grad = lax.dot_general(weight_out[...], mixed_grad, across, preferred_element_type=F32)
    activated, hidden_grad = slopes(hidden, act_grad)
    return (
        jnp.dot(hidden_grad, aligned[...], preferred_element_type=F32),
        jnp.dot(activated, mixed_grad, preferred_element_type=F32),
    )


def other_core_terms_kernel(which, weight_in, weight_out, scale, normed, *rest):
    *cotangents, out, aligned = rest
    terms = weight_grad_terms(which, weight_in, weight_out, scale, normed, cotangents, aligned)
    for k in range(2):
        out[0, k] = terms[k].astype(BF16)


def own_core_terms_kernel(which, weight_in, weight_out, scale, normed, got, *rest):
    *cotangents, sent, kept, aligned = rest
    terms = weight_grad_terms(which, weight_in, weight_out, scale, normed, cotangents, aligned)
    step = pl.program_id(0)
    for k in range(2):
        total = terms[k] + got[0, k].astype(F32)

        @pl.when(step == 0)
        def _():
            sent[k] = total.astype(BF16)

        @pl.when(step == 1)
        def _():
            kept[k] = total


def last_sum_kernel(kept, got, in_grad, out_grad):
    for k, out in enumerate((in_grad, out_grad)):
        out[...] = kept[k] + got[k].astype(F32)


def chip_sum_kernel(kept, got, out):
    out[...] = (kept[...].astype(F32) + got[...].astype(F32)).astype(BF16)


def spread_sum_kernel(parts, out):
    total = tree_sum([parts[k].astype(F32) for k in range(parts.shape[0])]).astype(BF16)
    for copy in range(out.shape[0]):
        out[copy] = total


def unpack_kernel(core, own, other, out, *small):
    piece, wide = own.shape[1:]

    def unpack(*halves):
        last = []
        for side, parts in enumerate(halves):
            lanes = slice(side * wide, (side + 1) * wide)
            for k in range(-(-TAP_ROWS // piece)):
                first = k * piece
                length = min(piece, TAP_ROWS - first)
                out[first : first + length, lanes] = parts[k].astype(F32)[:length, :]
            k = TAP_ROWS // piece
            last.append(parts[k].astype(F32))
        rows = jnp.concatenate(last, axis=1)
        first = TAP_ROWS % piece
        for k, line in enumerate(small):
            line[...] = rows[first + k : first + k + 1, :].reshape(line.shape)

    by_core(core, own, other, lambda outer, inner: unpack(inner, outer))


def params(limit=48):
    return pltpu.CompilerParams(vmem_limit_bytes=limit * 1024 * 1024)


def lane_block(rows):
    return pl.BlockSpec((rows, LANES), lambda c, *_: (0, c))


def whole_block(*shape):
    return pl.BlockSpec(shape, lambda *_: (0,) * len(shape))


def rims(cells):
    count = lax.axis_size("row")
    between = [(i, i + 1) for i in range(1, count - 1, 2)]
    return (
        lax.ppermute(cells, "row", [(i, i ^ 1) for i in range(count)]),
        lax.ppermute(cells, "row", between + [(j, i) for i, j in between]),
    )


def on_device(
    voxels, dw_kernel, norm_gain, norm_bias, weight_in, weight_out, layer_scale, cotangent
):
    planes, height, breadth, channels = voxels.shape
    rows = planes * height * breadth
    units = weight_in.shape[0]
    count = lax.axis_size("row")
    me = lax.axis_index("row")
    quad = 4
    line = count // quad
    lines = [[quad * k + p for k in range(line)] for p in range(quad)]
    other_core = [(i, i ^ 1) for i in range(count)]
    other_side = [(i, i ^ 2) for i in range(count)]
    tiles = channels // LANES

    own = voxels.reshape(rows, channels)
    upstream = cotangent.reshape(rows, channels)
    core = lax.rem(me, 2).astype(jnp.int32)
    parity = core.reshape(1)

    inner, outer = rims(own)

    def along_line(cells, steps):
        return lax.ppermute(cells, "row", [(i, (i + quad * steps) % count) for i in range(count)])

    upstream_line = [upstream] + [None] * (line - 1)
    upstream_line[1] = along_line(upstream, 1)
    upstream_line[-1] = along_line(upstream, -1)

    def spread_of(held):
        return pltpu.VMEM((9, held, PAD, LANES), F32)

    split_block = pl.BlockSpec((None, 9, KS, SUB, LANES), lambda c, *_: (c, 0, 0, 0, 0))
    partial, split = pl.pallas_call(
        functools.partial(own_conv_kernel, planes, height),
        grid=(tiles,),
        in_specs=[lane_block(rows), lane_block(TAP_ROWS)],
        out_specs=[lane_block(rows), split_block],
        out_shape=[
            jax.ShapeDtypeStruct((rows, channels), F32),
            jax.ShapeDtypeStruct((tiles, 9, KS, SUB, LANES), F32),
        ],
        scratch_shapes=[spread_of(planes)],
        compiler_params=params(),
        cost_estimate=NO_COST,
        name="own_conv",
    )(own, dw_kernel)

    partial, upstream_line[1], upstream_line[-1] = lax.optimization_barrier(
        (partial, upstream_line[1], upstream_line[-1])
    )
    for k in range(2, line - 1):
        upstream_line[k] = along_line(upstream_line[k - 1], 1)
    normed, centered = pl.pallas_call(
        functools.partial(rim_conv_kernel, planes, height),
        grid_spec=pltpu.PrefetchScalarGridSpec(
            num_scalar_prefetch=1,
            grid=(tiles,),
            in_specs=[
                lane_block(rows),
                lane_block(rows),
                split_block,
                lane_block(rows),
                whole_block(channels),
                whole_block(channels),
            ],
            out_specs=[
                whole_block(line, rows, channels),
                whole_block(rows, channels),
            ],
            scratch_shapes=[spread_of(2 * MARGIN), pltpu.VMEM((tiles, rows, LANES), F32)],
        ),
        out_shape=[
            jax.ShapeDtypeStruct((line, rows, channels), BF16),
            jax.ShapeDtypeStruct((rows, channels), F32),
        ],
        compiler_params=params(),
        cost_estimate=NO_COST,
        name="rim_conv",
    )(parity, inner, outer, split, partial, norm_gain, norm_bias)

    normed, centered, upstream_line[2] = lax.optimization_barrier(
        (normed, centered, upstream_line[2])
    )
    gathered = lax.all_to_all(
        normed, "row", split_axis=0, concat_axis=0, tiled=True, axis_index_groups=lines
    )

    block = 512
    whole = whole_block(rows, channels)
    block_out, conv_grad, small = pl.pallas_call(
        mlp_kernel,
        grid=(units // block,),
        in_specs=[
            pl.BlockSpec((None, rows, channels), lambda f: (0, 0, 0)),
            pl.BlockSpec((block, channels), lambda f: (f, 0)),
            pl.BlockSpec((block, channels), lambda f: (f, 0)),
            whole,
            whole_block(channels),
            whole_block(channels),
            whole,
            whole,
        ],
        out_specs=[
            whole,
            whole,
            whole_block(SUB, channels),
        ],
        out_shape=[
            jax.ShapeDtypeStruct((rows, channels), BF16),
            jax.ShapeDtypeStruct((rows, channels), BF16),
            jax.ShapeDtypeStruct((SUB, channels), F32),
        ],
        scratch_shapes=[
            pltpu.VMEM((rows, channels), F32),
            pltpu.VMEM((rows, channels), F32),
            pltpu.VMEM((rows, channels), BF16),
        ],
        compiler_params=params(),
        cost_estimate=NO_COST,
        name="mlp_both_ways",
    )(normed, weight_in, weight_out, centered, norm_gain, layer_scale, own, upstream)

    half = count // 2
    alike = [[2 * k + p for k in range(half)] for p in range(2)]
    half_tiles = tiles // 2
    wide = half_tiles * LANES
    piece = -(-(TAP_ROWS + SUB) // half)
    piece += -piece % (2 * SUB)
    padded = piece * half

    def tile_of(block_rows):
        def at(c, w):
            return 0, (c + w[1] * half_tiles) % tiles

        return pl.BlockSpec((block_rows, LANES), at)

    half_sent, half_kept = pl.pallas_call(
        functools.partial(kernel_grad_kernel, planes, height),
        grid_spec=pltpu.PrefetchScalarGridSpec(
            num_scalar_prefetch=1,
            grid=(tiles,),
            in_specs=[tile_of(rows), tile_of(rows), tile_of(rows), tile_of(rows), tile_of(SUB)],
            out_specs=[
                pl.BlockSpec((padded, LANES), lambda c, w: (0, jnp.minimum(c, half_tiles - 1))),
                pl.BlockSpec((padded, LANES), lambda c, w: (0, jnp.maximum(c - half_tiles, 0))),
            ],
            scratch_shapes=[
                spread_of(2 * MARGIN + planes),
                pltpu.VMEM((2, KS, SUB * SUB, LANES), F32),
                pltpu.VMEM((9, KS, SUB, LANES), F32),
                pltpu.VMEM((padded, LANES), F32),
            ],
        ),
        out_shape=[jax.ShapeDtypeStruct((padded, wide), BF16)] * 2,
        compiler_params=params(),
        cost_estimate=NO_COST,
        name="kernel_grad_terms",
    )(jnp.stack([core, 1 - core]), inner, own, outer, conv_grad, small)

    half_sent, conv_grad = lax.optimization_barrier((half_sent, conv_grad))
    half_got = lax.ppermute(half_sent, "row", other_core)
    grad_inner, grad_outer = rims(conv_grad)
    sums = pl.pallas_call(
        chip_sum_kernel,
        in_specs=[whole_block(padded, wide)] * 2,
        out_specs=whole_block(padded, wide),
        out_shape=jax.ShapeDtypeStruct((padded, wide), BF16),
        grid=(1,),
        compiler_params=params(),
        cost_estimate=NO_COST,
        name="kernel_grad_chip_sum",
    )(half_kept, half_got)

    share = units // count
    tokens = line * rows
    base = me // quad * quad
    side = lax.rem(me, quad) // 2
    place = lax.rem(me // quad + line - jnp.arange(line, dtype=jnp.int32), line)
    which = jnp.concatenate(
        [
            jnp.stack(
                [
                    base + 1 - core,
                    base + 3 - core,
                    base + 2 - 2 * side + core,
                    base + 2 * side + core,
                ]
            ).astype(jnp.int32),
            place.astype(jnp.int32),
        ]
    )
    pair = (2, 2, share, channels)

    def chunk(at):
        return pl.BlockSpec((share, channels), lambda s, w: (w[s + at], 0))

    sets = [whole_block(channels), whole_block(line, rows, channels)]
    cotangents = [whole_block(rows, channels)] * line
    aligned = [pltpu.VMEM((tokens, channels), BF16)]

    which, sums = lax.optimization_barrier((which, sums))
    scattered = lax.all_to_all(
        sums.reshape(half, piece, wide),
        "row",
        split_axis=0,
        concat_axis=0,
        tiled=True,
        axis_index_groups=alike,
    )
    for_other = pl.pallas_call(
        other_core_terms_kernel,
        grid_spec=pltpu.PrefetchScalarGridSpec(
            num_scalar_prefetch=1,
            grid=(2,),
            in_specs=[chunk(0), chunk(0)] + sets + cotangents,
            out_specs=pl.BlockSpec((1,) + pair[1:], lambda s, w: (s, 0, 0, 0)),
            scratch_shapes=aligned,
        ),
        out_shape=jax.ShapeDtypeStruct(pair, BF16),
        compiler_params=params(),
        cost_estimate=NO_COST,
        name="weight_grads_other_core",
    )(which, weight_in, weight_out, layer_scale, gathered, *upstream_line)
    from_other = lax.ppermute(for_other, "row", other_core)
    sent, kept = pl.pallas_call(
        own_core_terms_kernel,
        grid_spec=pltpu.PrefetchScalarGridSpec(
            num_scalar_prefetch=1,
            grid=(2,),
            in_specs=[chunk(2), chunk(2)]
            + sets
            + [pl.BlockSpec((1,) + pair[1:], lambda s, w: ((w[s + 2] - w[0] // 4 * 4) // 2, 0, 0, 0))]
            + cotangents,
            out_specs=[whole_block(2, share, channels)] * 2,
            scratch_shapes=aligned,
        ),
        out_shape=[
            jax.ShapeDtypeStruct(pair[1:], BF16),
            jax.ShapeDtypeStruct(pair[1:], F32),
        ],
        compiler_params=params(),
        cost_estimate=NO_COST,
        name="weight_grads_own_core",
    )(which, weight_in, weight_out, layer_scale, gathered, from_other, *upstream_line)
    got = lax.ppermute(sent, "row", other_side)

    scattered, kept = lax.optimization_barrier((scattered, kept))
    copies = pl.pallas_call(
        spread_sum_kernel,
        in_specs=[whole_block(half, piece, wide)],
        out_specs=whole_block(half, piece, wide),
        out_shape=jax.ShapeDtypeStruct((half, piece, wide), BF16),
        grid=(1,),
        compiler_params=params(),
        cost_estimate=NO_COST,
        name="kernel_grad_sum",
    )(scattered)
    conv_own, copies = lax.optimization_barrier((conv_grad, copies))
    totals = lax.all_to_all(
        copies, "row", split_axis=0, concat_axis=0, tiled=True, axis_index_groups=alike
    )

    voxel_grad = pl.pallas_call(
        functools.partial(input_grad_kernel, planes, height),
        grid_spec=pltpu.PrefetchScalarGridSpec(
            num_scalar_prefetch=1,
            grid=(tiles,),
            in_specs=[
                lane_block(rows),
                lane_block(rows),
                lane_block(rows),
                lane_block(TAP_ROWS),
                lane_block(rows),
            ],
            out_specs=lane_block(rows),
            scratch_shapes=[
                spread_of(2 * MARGIN + planes),
                pltpu.VMEM((9, KS, SUB, LANES), F32),
            ],
        ),
        out_shape=jax.ShapeDtypeStruct((rows, channels), BF16),
        compiler_params=params(),
        cost_estimate=NO_COST,
        name="input_grad_conv",
    )(parity, grad_inner, conv_own, grad_outer, dw_kernel, upstream)

    totals, voxel_grad = lax.optimization_barrier((totals, voxel_grad))
    other_totals = lax.ppermute(totals, "row", other_core)
    kernel_grad, *vector_grads = pl.pallas_call(
        unpack_kernel,
        grid_spec=pltpu.PrefetchScalarGridSpec(
            num_scalar_prefetch=1,
            grid=(1,),
            in_specs=[whole_block(half, piece, wide)] * 2,
            out_specs=[whole_block(TAP_ROWS, channels)] + [whole_block(channels)] * 3,
        ),
        out_shape=[jax.ShapeDtypeStruct((TAP_ROWS, channels), F32)]
        + [jax.ShapeDtypeStruct((channels,), F32)] * 3,
        compiler_params=params(),
        cost_estimate=NO_COST,
        name="kernel_grad_unpack",
    )(parity, totals, other_totals)

    weight_in_grad, weight_out_grad = pl.pallas_call(
        last_sum_kernel,
        grid=(1,),
        in_specs=[whole_block(2, share, channels)] * 2,
        out_specs=[whole_block(share, channels)] * 2,
        out_shape=[jax.ShapeDtypeStruct((share, channels), F32)] * 2,
        compiler_params=params(),
        cost_estimate=NO_COST,
        name="weight_grads_sum",
    )(kept, got)

    return (
        block_out.reshape(voxels.shape),
        voxel_grad.reshape(voxels.shape),
        kernel_grad,
        *vector_grads,
        weight_in_grad,
        weight_out_grad,
    )


def solution(mesh):
    in_specs = (
        P(("group", "row"), None, None, None),
        P(),
        P(),
        P(),
        P(),
        P(),
        P(),
        P(("group", "row"), None, None, None),
    )
    out_specs = (
        P(("group", "row"), None, None, None),
        P(("group", "row"), None, None, None),
        P("group", None),
        P("group"),
        P("group"),
        P("group"),
        P(("group", "row"), None),
        P(("group", "row"), None),
    )
    return jax.shard_map(
        on_device, mesh=mesh, in_specs=in_specs, out_specs=out_specs, check_vma=False
    )
```

```python
import functools

import jax
import jax.numpy as jnp
from jax import lax
from jax.experimental import pallas as pl
from jax.experimental.pallas import tpu as pltpu
from jax.sharding import PartitionSpec as P

KS = 7
MARGIN = KS // 2
LANES = 128
SUB = 8
PAD = 3 * SUB
TAP_ROWS = KS * KS * KS

root_half = 0.7071067811865476
inv_root_tau = 0.3989422804014327
norm_eps = 1e-06
erf_step = 0.3275911
erf_terms = tuple(
    0.5 * a for a in (0.254829592, -0.284496736, 1.421413741, -1.453152027, 1.061405429)
)

NO_COST = pl.CostEstimate(flops=0, bytes_accessed=0, transcendentals=0)

F32 = jnp.float32
BF16 = jnp.bfloat16


def split_source(v):
    terms = []
    for a, b in ((v[0] + v[2], v[1] + v[3]), (v[2], v[3]), (v[0], v[1])):
        terms += [a + b, b, a]
    return terms


def split_taps(t):
    terms = []
    for s in (
        (t[2], t[3], t[4]),
        (t[4] - t[2], t[5] - t[3], t[6] - t[4]),
        (t[0] - t[2], t[1] - t[3], t[2] - t[4]),
    ):
        terms += [s[1], s[2] - s[1], s[0] - s[1]]
    return terms


def split_grads(g):
    terms = []
    for a, b in ((g[0] + g[2], g[1] + g[3]), (g[0], g[1]), (g[2], g[3])):
        terms += [a + b, a, b]
    return terms


def join_outputs(m):
    pair = [(m[3 * k] + m[3 * k + 1], m[3 * k] + m[3 * k + 2]) for k in range(3)]
    return [
        pair[0][0] + pair[1][0],
        pair[0][1] + pair[1][1],
        pair[0][0] + pair[2][0],
        pair[0][1] + pair[2][1],
    ]


def join_taps(m):
    p, q, r = [
        (m[3 * k + 2], m[3 * k] - m[3 * k + 1] - m[3 * k + 2], m[3 * k + 1]) for k in range(3)
    ]
    return [
        r[0],
        r[1],
        p[0] - q[0] - r[0] + r[2],
        p[1] - q[1] - r[1],
        p[2] - q[2] - r[2] + q[0],
        q[1],
        q[2],
    ]


def tree_sum(terms):
    while len(terms) > 1:
        terms = [
            terms[k] + terms[k + 1] if k + 1 < len(terms) else terms[k]
            for k in range(0, len(terms), 2)
        ]
    return terms[0]


def stage_source(wanted, height, spread):
    row = height * SUB
    for at, (block, x) in enumerate(wanted):
        plane = block[x * row : (x + 1) * row, :].astype(F32)
        lines = [plane[y * SUB : (y + 1) * SUB, :] for y in range(height)]
        for j, term in enumerate(split_source(lines)):
            spread[j, at, SUB : 2 * SUB, :] = term


def rim_planes(left, right, planes):
    wanted = [(left, x) for x in range(planes - MARGIN, planes)]
    return wanted + [(right, x) for x in range(MARGIN)]


def all_planes(left, own, right, planes):
    rim = rim_planes(left, right, planes)
    return rim[:MARGIN] + [(own, x) for x in range(planes)] + rim[MARGIN:]


def by_core(core, inner, outer, stage):
    @pl.when(core[0] == 0)
    def _():
        stage(outer, inner)

    @pl.when(core[0] != 0)
    def _():
        stage(inner, outer)


def clear_rims(spread):
    zeros = jnp.zeros(spread.shape[:2] + (SUB, LANES), F32)
    spread[:, :, :SUB, :] = zeros
    spread[:, :, 2 * SUB :, :] = zeros


def stage_taps(taps, split):
    for dx in range(KS):
        rows = []
        for dy in range(KS):
            first = dx * KS * KS + dy * KS
            if first + SUB <= TAP_ROWS:
                rows.append(taps[first : first + SUB, :])
            else:
                rows.append(pltpu.roll(taps[TAP_ROWS - SUB : TAP_ROWS, :], SUB - 1, 0))
        for j, term in enumerate(split_taps(rows)):
            split[j, dx] = term


REVERSED = (0, 2, 1, 6, 8, 7, 3, 5, 4)


def convolve(spread, split, planes, held, flipped):
    terms = []
    for j in range(9):
        sums = [None] * planes
        for dz in range(KS):
            first = SUB - MARGIN + dz
            source = {x: spread[j, at, first : first + SUB, :] for at, x in enumerate(held)}
            weights = []
            for dx in range(KS):
                if flipped:
                    tap = split[REVERSED[j], KS - 1 - dx, KS - 1 - dz : KS - dz, :]
                else:
                    tap = split[j, dx, dz : dz + 1, :]
                weights.append(jnp.broadcast_to(tap, (SUB, LANES)))
            for x in range(planes):
                part = tree_sum(
                    [source[x + dx] * weights[dx] for dx in range(KS) if x + dx in source]
                )
                sums[x] = part if sums[x] is None else sums[x] + part
        terms.append(sums)
    return [join_outputs([terms[j][x] for j in range(9)]) for x in range(planes)]


def own_conv_kernel(planes, height, own, taps, out, split, spread):
    @pl.when(pl.program_id(0) == 0)
    def _():
        clear_rims(spread)

    stage_source([(own, x) for x in range(planes)], height, spread)
    stage_taps(taps, split)
    rows = convolve(spread, split, planes, range(MARGIN, MARGIN + planes), False)
    for x in range(planes):
        for y in range(height):
            at = (x * height + y) * SUB
            out[at : at + SUB, :] = rows[x][y]


def rim_conv_kernel(
    planes, height, core, inner, outer, split, partial, gain, bias, normed, centered, spread, conv
):
    step = pl.program_id(0)

    @pl.when(step == 0)
    def _():
        clear_rims(spread)

    def stage(left, right):
        stage_source(rim_planes(left, right, planes), height, spread)

    by_core(core, inner, outer, stage)
    held = list(range(MARGIN)) + list(range(MARGIN + planes, 2 * MARGIN + planes))
    rows = convolve(spread, split, planes, held, False)
    for x in range(planes):
        for y in range(height):
            at = (x * height + y) * SUB
            conv[step, at : at + SUB, :] = rows[x][y] + partial[at : at + SUB, :]

    @pl.when(step == pl.num_programs(0) - 1)
    def _():
        tiles = conv.shape[0]
        channels = tiles * LANES
        parts = [conv[k] for k in range(tiles)]
        gains = gain[...].reshape(1, channels)
        biases = bias[...].reshape(1, channels)
        average = jnp.sum(tree_sum(parts), axis=1, keepdims=True) * (1.0 / channels)
        parts = [part - average for part in parts]
        variance = jnp.sum(
            tree_sum([part * part for part in parts]), axis=1, keepdims=True
        ) * (1.0 / channels)
        inverse = lax.rsqrt(variance + norm_eps)
        for k in range(tiles):
            lanes = slice(k * LANES, (k + 1) * LANES)
            centered[:, lanes] = parts[k]
            value = parts[k] * inverse
            whole = (value * gains[:, lanes] + biases[:, lanes]).astype(BF16)
            for copy in range(normed.shape[0]):
                normed[copy, :, lanes] = whole


def input_grad_kernel(
    planes, height, core, inner, own, outer, taps, cotangent, out, spread, split
):
    @pl.when(pl.program_id(0) == 0)
    def _():
        clear_rims(spread)

    def stage(left, right):
        stage_source(all_planes(left, own, right, planes), height, spread)

    by_core(core, inner, outer, stage)
    stage_taps(taps, split)
    rows = convolve(spread, split, planes, range(2 * MARGIN + planes), True)
    for x in range(planes):
        at = x * height * SUB
        whole = jnp.concatenate(rows[x], axis=0)
        upstream = cotangent[at : at + height * SUB, :].astype(F32)
        out[at : at + height * SUB, :] = (upstream + whole).astype(BF16)


def kernel_grad_kernel(
    planes, height, which, inner, own, outer, grads, small, sent, kept, spread, products, joined, flat
):
    @pl.when(pl.program_id(0) == 0)
    def _():
        clear_rims(spread)
        products[...] = jnp.zeros(products.shape, F32)
        flat[...] = jnp.zeros(flat.shape, F32)

    def stage(left, right):
        stage_source(all_planes(left, own, right, planes), height, spread)

    by_core(which, inner, outer, stage)
    upstream = []
    for x in range(planes):
        plane = grads[x * height * SUB : (x + 1) * height * SUB, :].astype(F32)
        upstream.append(
            split_grads([plane[y * SUB : (y + 1) * SUB, :] for y in range(height)])
        )
    for j in range(9):
        for dz in range(KS):
            first = SUB - MARGIN + dz
            source = [
                spread[j, x, first : first + SUB, :] for x in range(planes + KS - 1)
            ]
            for dx in range(KS):
                products[j % 2, dx, dz * SUB : (dz + 1) * SUB, :] = tree_sum(
                    [source[x + dx] * upstream[x][j] for x in range(planes)]
                )
        for dx in range(KS):
            joined[j, dx] = tree_sum(
                [products[j % 2, dx, pl.ds(s, SUB, stride=SUB), :] for s in range(SUB)]
            )
    for dx in range(KS):
        for dy, tile in enumerate(join_taps([joined[j, dx] for j in range(9)])):
            row = dx * KS * KS + dy * KS
            flat[row : row + SUB, :] = tile
    flat[TAP_ROWS : TAP_ROWS + SUB, :] = small[...]
    step = pl.program_id(0)
    half = pl.num_programs(0) // 2

    @pl.when(step < half)
    def _():
        sent[...] = flat[...].astype(BF16)

    @pl.when(step >= half)
    def _():
        kept[...] = flat[...].astype(BF16)


def mlp_kernel(
    normed,
    weight_in,
    weight_out,
    centered,
    norm_gain,
    layer_scale,
    voxels,
    cotangent,
    block_out,
    conv_grad,
    small,
    mixed,
    back,
    mixed_grad,
):
    step = pl.program_id(0)
    gain = norm_gain[...].reshape(1, -1)
    scale = layer_scale[...].reshape(1, -1)

    @pl.when(step == 0)
    def _():
        mixed_grad[...] = (scale * cotangent[...].astype(F32)).astype(BF16)

    hidden = lax.dot_general(
        normed[...], weight_in[...], (((1,), (1,)), ((), ())), preferred_element_type=F32
    )
    act_grad = lax.dot_general(
        mixed_grad[...], weight_out[...], (((1,), (1,)), ((), ())), preferred_element_type=F32
    )
    activated, hidden_grad = slopes(hidden, act_grad)
    forward = jnp.dot(activated, weight_out[...], preferred_element_type=F32)
    backward = jnp.dot(hidden_grad, weight_in[...], preferred_element_type=F32)

    @pl.when(step == 0)
    def _():
        mixed[...] = forward
        back[...] = backward

    @pl.when(step > 0)
    def _():
        mixed[...] += forward
        back[...] += backward

    @pl.when(step == pl.num_programs(0) - 1)
    def _():
        channels = gain.shape[1]
        whole = mixed[...]
        block_out[...] = (voxels[...].astype(F32) + scale * whole).astype(BF16)
        scale_local = jnp.sum(cotangent[...].astype(F32) * whole, axis=0, keepdims=True)
        grad = back[...]
        deviation = centered[...]
        variance = jnp.sum(deviation * deviation, axis=1, keepdims=True) * (1.0 / channels)
        inverse = lax.rsqrt(variance + norm_eps)
        one = deviation * inverse
        bias_local = jnp.sum(grad, axis=0, keepdims=True)
        gain_local = jnp.sum(grad * one, axis=0, keepdims=True)
        small[...] = jnp.concatenate(
            [gain_local, bias_local, scale_local, jnp.zeros((SUB - 3, channels), F32)], axis=0
        )
        scaled = grad * gain
        average = jnp.sum(scaled, axis=1, keepdims=True) * (1.0 / channels)
        slant = jnp.sum(scaled * one, axis=1, keepdims=True) * (1.0 / channels)
        conv_grad[...] = (inverse * (scaled - average - one * slant)).astype(BF16)


def slopes(hidden, act_grad):
    bell = jnp.exp(-0.5 * hidden * hidden)
    below = 1.0 + (erf_step * root_half) * jnp.abs(hidden)
    t = pl.reciprocal(below, approx=True)
    t = t * (2.0 - below * t)
    poly = erf_terms[-1]
    for term in erf_terms[-2::-1]:
        poly = poly * t + term
    tail = poly * t * bell
    cover = jnp.where(hidden < 0.0, tail, 1.0 - tail)
    activated = (hidden * cover).astype(BF16)
    slope = cover + hidden * bell * inv_root_tau
    return activated, (act_grad * slope).astype(BF16)


def weight_grad_terms(which, weight_in, weight_out, scale, normed, cotangents, aligned):
    rows = normed.shape[1]
    line = len(cotangents)
    scales = scale[...].reshape(1, -1)
    mixed_grad = jnp.concatenate(
        [(scales * part[...].astype(F32)).astype(BF16) for part in cotangents], axis=0
    )
    for k in range(line):
        aligned[k * rows : (k + 1) * rows, :] = normed[which[4 + k]]
    across = (((1,), (1,)), ((), ()))
    hidden = lax.dot_general(weight_in[...], aligned[...], across, preferred_element_type=F32)
    act_grad = lax.dot_general(weight_out[...], mixed_grad, across, preferred_element_type=F32)
    activated, hidden_grad = slopes(hidden, act_grad)
    return (
        jnp.dot(hidden_grad, aligned[...], preferred_element_type=F32),
        jnp.dot(activated, mixed_grad, preferred_element_type=F32),
    )


def side_terms_kernel(which, weight_in, weight_out, scale, normed, *rest):
    *cotangents, sent, kept, aligned = rest
    terms = weight_grad_terms(which, weight_in, weight_out, scale, normed, cotangents, aligned)
    step = pl.program_id(0)

    @pl.when(step == 0)
    def _():
        for k in range(2):
            sent[k] = terms[k].astype(BF16)

    @pl.when(step == 1)
    def _():
        for k in range(2):
            kept[k] = terms[k]


def far_sum_kernel(kept, got, in_grad, out_grad):
    for k, out in enumerate((in_grad, out_grad)):
        out[...] = (kept[k] + got[k].astype(F32)).astype(BF16)


def last_sum_kernel(kept, got, in_far, out_far, in_grad, out_grad):
    for k, (far, out) in enumerate(((in_far, in_grad), (out_far, out_grad))):
        out[...] = (kept[k] + got[k].astype(F32)) + far[...].astype(F32)


def chip_sum_kernel(kept, got, out):
    out[...] = (kept[...].astype(F32) + got[...].astype(F32)).astype(BF16)


def spread_sum_kernel(parts, out):
    total = tree_sum([parts[k].astype(F32) for k in range(parts.shape[0])]).astype(BF16)
    for copy in range(out.shape[0]):
        out[copy] = total


def unpack_kernel(core, own, other, out, *small):
    piece, wide = own.shape[1:]

    def unpack(*halves):
        last = []
        for side, parts in enumerate(halves):
            lanes = slice(side * wide, (side + 1) * wide)
            for k in range(-(-TAP_ROWS // piece)):
                first = k * piece
                length = min(piece, TAP_ROWS - first)
                out[first : first + length, lanes] = parts[k].astype(F32)[:length, :]
            k = TAP_ROWS // piece
            last.append(parts[k].astype(F32))
        rows = jnp.concatenate(last, axis=1)
        first = TAP_ROWS % piece
        for k, line in enumerate(small):
            line[...] = rows[first + k : first + k + 1, :].reshape(line.shape)

    by_core(core, own, other, lambda outer, inner: unpack(inner, outer))


def params(limit=48):
    return pltpu.CompilerParams(vmem_limit_bytes=limit * 1024 * 1024)


def lane_block(rows):
    return pl.BlockSpec((rows, LANES), lambda c, *_: (0, c))


def whole_block(*shape):
    return pl.BlockSpec(shape, lambda *_: (0,) * len(shape))


def rims(cells):
    count = lax.axis_size("row")
    between = [(i, i + 1) for i in range(1, count - 1, 2)]
    return (
        lax.ppermute(cells, "row", [(i, i ^ 1) for i in range(count)]),
        lax.ppermute(cells, "row", between + [(j, i) for i, j in between]),
    )


def on_device(
    voxels, dw_kernel, norm_gain, norm_bias, weight_in, weight_out, layer_scale, cotangent
):
    planes, height, breadth, channels = voxels.shape
    rows = planes * height * breadth
    units = weight_in.shape[0]
    count = lax.axis_size("row")
    me = lax.axis_index("row")
    quad = 4
    line = count // quad
    lines = [[quad * k + p for k in range(line)] for p in range(quad)]
    other_core = [(i, i ^ 1) for i in range(count)]
    other_side = [(i, i ^ 2) for i in range(count)]
    tiles = channels // LANES

    own = voxels.reshape(rows, channels)
    upstream = cotangent.reshape(rows, channels)
    core = lax.rem(me, 2).astype(jnp.int32)
    parity = core.reshape(1)

    inner, outer = rims(own)

    def along_line(cells, steps):
        return lax.ppermute(cells, "row", [(i, (i + quad * steps) % count) for i in range(count)])

    upstream_line = [upstream] + [None] * (line - 1)
    upstream_line[1] = along_line(upstream, 1)
    upstream_line[-1] = along_line(upstream, -1)

    def spread_of(held):
        return pltpu.VMEM((9, held, PAD, LANES), F32)

    split_block = pl.BlockSpec((None, 9, KS, SUB, LANES), lambda c, *_: (c, 0, 0, 0, 0))
    partial, split = pl.pallas_call(
        functools.partial(own_conv_kernel, planes, height),
        grid=(tiles,),
        in_specs=[lane_block(rows), lane_block(TAP_ROWS)],
        out_specs=[lane_block(rows), split_block],
        out_shape=[
            jax.ShapeDtypeStruct((rows, channels), F32),
            jax.ShapeDtypeStruct((tiles, 9, KS, SUB, LANES), F32),
        ],
        scratch_shapes=[spread_of(planes)],
        compiler_params=params(),
        cost_estimate=NO_COST,
        name="own_conv",
    )(own, dw_kernel)

    partial, upstream_line[1], upstream_line[-1] = lax.optimization_barrier(
        (partial, upstream_line[1], upstream_line[-1])
    )
    for k in range(2, line - 1):
        upstream_line[k] = along_line(upstream_line[k - 1], 1)
    normed, centered = pl.pallas_call(
        functools.partial(rim_conv_kernel, planes, height),
        grid_spec=pltpu.PrefetchScalarGridSpec(
            num_scalar_prefetch=1,
            grid=(tiles,),
            in_specs=[
                lane_block(rows),
                lane_block(rows),
                split_block,
                lane_block(rows),
                whole_block(channels),
                whole_block(channels),
            ],
            out_specs=[
                whole_block(line, rows, channels),
                whole_block(rows, channels),
            ],
            scratch_shapes=[spread_of(2 * MARGIN), pltpu.VMEM((tiles, rows, LANES), F32)],
        ),
        out_shape=[
            jax.ShapeDtypeStruct((line, rows, channels), BF16),
            jax.ShapeDtypeStruct((rows, channels), F32),
        ],
        compiler_params=params(),
        cost_estimate=NO_COST,
        name="rim_conv",
    )(parity, inner, outer, split, partial, norm_gain, norm_bias)

    normed, centered, upstream_line[2] = lax.optimization_barrier(
        (normed, centered, upstream_line[2])
    )
    gathered = lax.all_to_all(
        normed, "row", split_axis=0, concat_axis=0, tiled=True, axis_index_groups=lines
    )

    block = 512
    whole = whole_block(rows, channels)
    block_out, conv_grad, small = pl.pallas_call(
        mlp_kernel,
        grid=(units // block,),
        in_specs=[
            pl.BlockSpec((None, rows, channels), lambda f: (0, 0, 0)),
            pl.BlockSpec((block, channels), lambda f: (f, 0)),
            pl.BlockSpec((block, channels), lambda f: (f, 0)),
            whole,
            whole_block(channels),
            whole_block(channels),
            whole,
            whole,
        ],
        out_specs=[
            whole,
            whole,
            whole_block(SUB, channels),
        ],
        out_shape=[
            jax.ShapeDtypeStruct((rows, channels), BF16),
            jax.ShapeDtypeStruct((rows, channels), BF16),
            jax.ShapeDtypeStruct((SUB, channels), F32),
        ],
        scratch_shapes=[
            pltpu.VMEM((rows, channels), F32),
            pltpu.VMEM((rows, channels), F32),
            pltpu.VMEM((rows, channels), BF16),
        ],
        compiler_params=params(),
        cost_estimate=NO_COST,
        name="mlp_both_ways",
    )(normed, weight_in, weight_out, centered, norm_gain, layer_scale, own, upstream)

    half = count // 2
    alike = [[2 * k + p for k in range(half)] for p in range(2)]
    half_tiles = tiles // 2
    wide = half_tiles * LANES
    piece = -(-(TAP_ROWS + SUB) // half)
    piece += -piece % (2 * SUB)
    padded = piece * half

    def tile_of(block_rows):
        def at(c, w):
            return 0, (c + w[1] * half_tiles) % tiles

        return pl.BlockSpec((block_rows, LANES), at)

    half_sent, half_kept = pl.pallas_call(
        functools.partial(kernel_grad_kernel, planes, height),
        grid_spec=pltpu.PrefetchScalarGridSpec(
            num_scalar_prefetch=1,
            grid=(tiles,),
            in_specs=[tile_of(rows), tile_of(rows), tile_of(rows), tile_of(rows), tile_of(SUB)],
            out_specs=[
                pl.BlockSpec((padded, LANES), lambda c, w: (0, jnp.minimum(c, half_tiles - 1))),
                pl.BlockSpec((padded, LANES), lambda c, w: (0, jnp.maximum(c - half_tiles, 0))),
            ],
            scratch_shapes=[
                spread_of(2 * MARGIN + planes),
                pltpu.VMEM((2, KS, SUB * SUB, LANES), F32),
                pltpu.VMEM((9, KS, SUB, LANES), F32),
                pltpu.VMEM((padded, LANES), F32),
            ],
        ),
        out_shape=[jax.ShapeDtypeStruct((padded, wide), BF16)] * 2,
        compiler_params=params(),
        cost_estimate=NO_COST,
        name="kernel_grad_terms",
    )(jnp.stack([core, 1 - core]), inner, own, outer, conv_grad, small)

    half_sent, conv_grad = lax.optimization_barrier((half_sent, conv_grad))
    half_got = lax.ppermute(half_sent, "row", other_core)
    grad_inner, grad_outer = rims(conv_grad)
    sums = pl.pallas_call(
        chip_sum_kernel,
        in_specs=[whole_block(padded, wide)] * 2,
        out_specs=whole_block(padded, wide),
        out_shape=jax.ShapeDtypeStruct((padded, wide), BF16),
        grid=(1,),
        compiler_params=params(),
        cost_estimate=NO_COST,
        name="kernel_grad_chip_sum",
    )(half_kept, half_got)

    share = units // count
    tokens = line * rows
    base = me // quad * quad
    side = lax.rem(me, quad) // 2
    place = lax.rem(me // quad + line - jnp.arange(line, dtype=jnp.int32), line)
    far = base + 2 * (1 - side)
    near = base + 2 * side
    which = jnp.concatenate(
        [
            jnp.stack([far + 1 - core, far + core, near + 1 - core, near + core]).astype(jnp.int32),
            place.astype(jnp.int32),
        ]
    )
    pair = (2, share, channels)

    def side_terms(first, name):
        chunk = pl.BlockSpec((share, channels), lambda s, w: (w[s + first], 0))
        return pl.pallas_call(
            side_terms_kernel,
            grid_spec=pltpu.PrefetchScalarGridSpec(
                num_scalar_prefetch=1,
                grid=(2,),
                in_specs=[
                    chunk,
                    chunk,
                    whole_block(channels),
                    whole_block(line, rows, channels),
                ]
                + [whole_block(rows, channels)] * line,
                out_specs=[whole_block(*pair)] * 2,
                scratch_shapes=[pltpu.VMEM((tokens, channels), BF16)],
            ),
            out_shape=[jax.ShapeDtypeStruct(pair, BF16), jax.ShapeDtypeStruct(pair, F32)],
            compiler_params=params(),
            cost_estimate=NO_COST,
            name=name,
        )(which, weight_in, weight_out, layer_scale, gathered, *upstream_line)

    which, sums, grad_inner, grad_outer = lax.optimization_barrier(
        (which, sums, grad_inner, grad_outer)
    )
    far_sent, far_kept = side_terms(0, "weight_grads_far_side")
    far_got = lax.ppermute(far_sent, "row", other_core)
    scattered = lax.all_to_all(
        sums.reshape(half, piece, wide),
        "row",
        split_axis=0,
        concat_axis=0,
        tiled=True,
        axis_index_groups=alike,
    )
    in_sent, out_sent = pl.pallas_call(
        far_sum_kernel,
        grid=(1,),
        in_specs=[whole_block(*pair)] * 2,
        out_specs=[whole_block(*pair[1:])] * 2,
        out_shape=[jax.ShapeDtypeStruct(pair[1:], BF16)] * 2,
        compiler_params=params(),
        cost_estimate=NO_COST,
        name="weight_grads_far_sum",
    )(far_kept, far_got)
    in_far = lax.ppermute(in_sent, "row", other_side)

    which, out_sent = lax.optimization_barrier((which, out_sent))
    sent, kept = side_terms(2, "weight_grads_near_side")
    sent, in_far = lax.optimization_barrier((sent, in_far))
    got = lax.ppermute(sent, "row", other_core)
    out_far = lax.ppermute(out_sent, "row", other_side)

    scattered, kept = lax.optimization_barrier((scattered, kept))
    copies = pl.pallas_call(
        spread_sum_kernel,
        in_specs=[whole_block(half, piece, wide)],
        out_specs=whole_block(half, piece, wide),
        out_shape=jax.ShapeDtypeStruct((half, piece, wide), BF16),
        grid=(1,),
        compiler_params=params(),
        cost_estimate=NO_COST,
        name="kernel_grad_sum",
    )(scattered)
    conv_own, copies, out_far = lax.optimization_barrier((conv_grad, copies, out_far))
    totals = lax.all_to_all(
        copies, "row", split_axis=0, concat_axis=0, tiled=True, axis_index_groups=alike
    )

    voxel_grad = pl.pallas_call(
        functools.partial(input_grad_kernel, planes, height),
        grid_spec=pltpu.PrefetchScalarGridSpec(
            num_scalar_prefetch=1,
            grid=(tiles,),
            in_specs=[
                lane_block(rows),
                lane_block(rows),
                lane_block(rows),
                lane_block(TAP_ROWS),
                lane_block(rows),
            ],
            out_specs=lane_block(rows),
            scratch_shapes=[
                spread_of(2 * MARGIN + planes),
                pltpu.VMEM((9, KS, SUB, LANES), F32),
            ],
        ),
        out_shape=jax.ShapeDtypeStruct((rows, channels), BF16),
        compiler_params=params(),
        cost_estimate=NO_COST,
        name="input_grad_conv",
    )(parity, grad_inner, conv_own, grad_outer, dw_kernel, upstream)

    totals, voxel_grad = lax.optimization_barrier((totals, voxel_grad))
    other_totals = lax.ppermute(totals, "row", other_core)
    kernel_grad, *vector_grads = pl.pallas_call(
        unpack_kernel,
        grid_spec=pltpu.PrefetchScalarGridSpec(
            num_scalar_prefetch=1,
            grid=(1,),
            in_specs=[whole_block(half, piece, wide)] * 2,
            out_specs=[whole_block(TAP_ROWS, channels)] + [whole_block(channels)] * 3,
        ),
        out_shape=[jax.ShapeDtypeStruct((TAP_ROWS, channels), F32)]
        + [jax.ShapeDtypeStruct((channels,), F32)] * 3,
        compiler_params=params(),
        cost_estimate=NO_COST,
        name="kernel_grad_unpack",
    )(parity, totals, other_totals)

    weight_in_grad, weight_out_grad = pl.pallas_call(
        last_sum_kernel,
        grid=(1,),
        in_specs=[whole_block(*pair)] * 2 + [whole_block(*pair[1:])] * 2,
        out_specs=[whole_block(*pair[1:])] * 2,
        out_shape=[jax.ShapeDtypeStruct(pair[1:], F32)] * 2,
        compiler_params=params(),
        cost_estimate=NO_COST,
        name="weight_grads_sum",
    )(kept, got, in_far, out_far)

    return (
        block_out.reshape(voxels.shape),
        voxel_grad.reshape(voxels.shape),
        kernel_grad,
        *vector_grads,
        weight_in_grad,
        weight_out_grad,
    )


def solution(mesh):
    in_specs = (
        P(("group", "row"), None, None, None),
        P(),
        P(),
        P(),
        P(),
        P(),
        P(),
        P(("group", "row"), None, None, None),
    )
    out_specs = (
        P(("group", "row"), None, None, None),
        P(("group", "row"), None, None, None),
        P("group", None),
        P("group"),
        P("group"),
        P("group"),
        P(("group", "row"), None),
        P(("group", "row"), None),
    )
    return jax.shard_map(
        on_device, mesh=mesh, in_specs=in_specs, out_specs=out_specs, check_vma=False
    )
```

```python
import functools

import jax
import jax.numpy as jnp
from jax import lax
from jax.experimental import pallas as pl
from jax.experimental.pallas import tpu as pltpu
from jax.sharding import PartitionSpec as P

KS = 7
MARGIN = KS // 2
LANES = 128
SUB = 8
PAD = 3 * SUB
TAP_ROWS = KS * KS * KS

root_half = 0.7071067811865476
inv_root_tau = 0.3989422804014327
norm_eps = 1e-06
erf_step = 0.3275911
erf_terms = tuple(
    0.5 * a for a in (0.254829592, -0.284496736, 1.421413741, -1.453152027, 1.061405429)
)

NO_COST = pl.CostEstimate(flops=0, bytes_accessed=0, transcendentals=0)

F32 = jnp.float32
BF16 = jnp.bfloat16


def split_source(v):
    terms = []
    for a, b in ((v[0] + v[2], v[1] + v[3]), (v[2], v[3]), (v[0], v[1])):
        terms += [a + b, b, a]
    return terms


def split_taps(t):
    terms = []
    for s in (
        (t[2], t[3], t[4]),
        (t[4] - t[2], t[5] - t[3], t[6] - t[4]),
        (t[0] - t[2], t[1] - t[3], t[2] - t[4]),
    ):
        terms += [s[1], s[2] - s[1], s[0] - s[1]]
    return terms


def split_grads(g):
    terms = []
    for a, b in ((g[0] + g[2], g[1] + g[3]), (g[0], g[1]), (g[2], g[3])):
        terms += [a + b, a, b]
    return terms


def join_outputs(m):
    pair = [(m[3 * k] + m[3 * k + 1], m[3 * k] + m[3 * k + 2]) for k in range(3)]
    return [
        pair[0][0] + pair[1][0],
        pair[0][1] + pair[1][1],
        pair[0][0] + pair[2][0],
        pair[0][1] + pair[2][1],
    ]


def join_taps(m):
    p, q, r = [
        (m[3 * k + 2], m[3 * k] - m[3 * k + 1] - m[3 * k + 2], m[3 * k + 1]) for k in range(3)
    ]
    return [
        r[0],
        r[1],
        p[0] - q[0] - r[0] + r[2],
        p[1] - q[1] - r[1],
        p[2] - q[2] - r[2] + q[0],
        q[1],
        q[2],
    ]


def tree_sum(terms):
    while len(terms) > 1:
        terms = [
            terms[k] + terms[k + 1] if k + 1 < len(terms) else terms[k]
            for k in range(0, len(terms), 2)
        ]
    return terms[0]


def stage_source(wanted, height, spread):
    row = height * SUB
    for at, (block, x) in enumerate(wanted):
        plane = block[x * row : (x + 1) * row, :].astype(F32)
        lines = [plane[y * SUB : (y + 1) * SUB, :] for y in range(height)]
        for j, term in enumerate(split_source(lines)):
            spread[j, at, SUB : 2 * SUB, :] = term


def rim_planes(left, right, planes):
    wanted = [(left, x) for x in range(planes - MARGIN, planes)]
    return wanted + [(right, x) for x in range(MARGIN)]


def all_planes(left, own, right, planes):
    rim = rim_planes(left, right, planes)
    return rim[:MARGIN] + [(own, x) for x in range(planes)] + rim[MARGIN:]


def by_core(core, inner, outer, stage):
    @pl.when(core[0] == 0)
    def _():
        stage(outer, inner)

    @pl.when(core[0] != 0)
    def _():
        stage(inner, outer)


def clear_rims(spread):
    zeros = jnp.zeros(spread.shape[:2] + (SUB, LANES), F32)
    spread[:, :, :SUB, :] = zeros
    spread[:, :, 2 * SUB :, :] = zeros


def stage_taps(taps, split):
    for dx in range(KS):
        rows = []
        for dy in range(KS):
            first = dx * KS * KS + dy * KS
            if first + SUB <= TAP_ROWS:
                rows.append(taps[first : first + SUB, :])
            else:
                rows.append(pltpu.roll(taps[TAP_ROWS - SUB : TAP_ROWS, :], SUB - 1, 0))
        for j, term in enumerate(split_taps(rows)):
            split[j, dx] = term


REVERSED = (0, 2, 1, 6, 8, 7, 3, 5, 4)


def convolve(spread, split, planes, held, flipped):
    terms = []
    for j in range(9):
        sums = [None] * planes
        for dz in range(KS):
            first = SUB - MARGIN + dz
            source = {x: spread[j, at, first : first + SUB, :] for at, x in enumerate(held)}
            weights = []
            for dx in range(KS):
                if flipped:
                    tap = split[REVERSED[j], KS - 1 - dx, KS - 1 - dz : KS - dz, :]
                else:
                    tap = split[j, dx, dz : dz + 1, :]
                weights.append(jnp.broadcast_to(tap, (SUB, LANES)))
            for x in range(planes):
                part = tree_sum(
                    [source[x + dx] * weights[dx] for dx in range(KS) if x + dx in source]
                )
                sums[x] = part if sums[x] is None else sums[x] + part
        terms.append(sums)
    return [join_outputs([terms[j][x] for j in range(9)]) for x in range(planes)]


def own_conv_kernel(planes, height, own, taps, out, split, spread):
    @pl.when(pl.program_id(0) == 0)
    def _():
        clear_rims(spread)

    stage_source([(own, x) for x in range(planes)], height, spread)
    stage_taps(taps, split)
    rows = convolve(spread, split, planes, range(MARGIN, MARGIN + planes), False)
    for x in range(planes):
        for y in range(height):
            at = (x * height + y) * SUB
            out[at : at + SUB, :] = rows[x][y]


def rim_conv_kernel(
    planes, height, core, inner, outer, split, partial, gain, bias, normed, centered, spread, conv
):
    step = pl.program_id(0)

    @pl.when(step == 0)
    def _():
        clear_rims(spread)

    def stage(left, right):
        stage_source(rim_planes(left, right, planes), height, spread)

    by_core(core, inner, outer, stage)
    held = list(range(MARGIN)) + list(range(MARGIN + planes, 2 * MARGIN + planes))
    rows = convolve(spread, split, planes, held, False)
    for x in range(planes):
        for y in range(height):
            at = (x * height + y) * SUB
            conv[step, at : at + SUB, :] = rows[x][y] + partial[at : at + SUB, :]

    @pl.when(step == pl.num_programs(0) - 1)
    def _():
        tiles = conv.shape[0]
        channels = tiles * LANES
        parts = [conv[k] for k in range(tiles)]
        gains = gain[...].reshape(1, channels)
        biases = bias[...].reshape(1, channels)
        average = jnp.sum(tree_sum(parts), axis=1, keepdims=True) * (1.0 / channels)
        parts = [part - average for part in parts]
        variance = jnp.sum(
            tree_sum([part * part for part in parts]), axis=1, keepdims=True
        ) * (1.0 / channels)
        inverse = lax.rsqrt(variance + norm_eps)
        for k in range(tiles):
            lanes = slice(k * LANES, (k + 1) * LANES)
            centered[:, lanes] = parts[k]
            value = parts[k] * inverse
            whole = (value * gains[:, lanes] + biases[:, lanes]).astype(BF16)
            for copy in range(normed.shape[0]):
                normed[copy, :, lanes] = whole


def input_grad_kernel(
    planes, height, core, inner, own, outer, taps, cotangent, out, spread, split
):
    @pl.when(pl.program_id(0) == 0)
    def _():
        clear_rims(spread)

    def stage(left, right):
        stage_source(all_planes(left, own, right, planes), height, spread)

    by_core(core, inner, outer, stage)
    stage_taps(taps, split)
    rows = convolve(spread, split, planes, range(2 * MARGIN + planes), True)
    for x in range(planes):
        at = x * height * SUB
        whole = jnp.concatenate(rows[x], axis=0)
        upstream = cotangent[at : at + height * SUB, :].astype(F32)
        out[at : at + height * SUB, :] = (upstream + whole).astype(BF16)


def kernel_grad_kernel(
    planes, height, which, inner, own, outer, grads, small, sent, kept, spread, products, joined, flat
):
    @pl.when(pl.program_id(0) == 0)
    def _():
        clear_rims(spread)
        products[...] = jnp.zeros(products.shape, F32)
        flat[...] = jnp.zeros(flat.shape, F32)

    def stage(left, right):
        stage_source(all_planes(left, own, right, planes), height, spread)

    by_core(which, inner, outer, stage)
    upstream = []
    for x in range(planes):
        plane = grads[x * height * SUB : (x + 1) * height * SUB, :].astype(F32)
        upstream.append(
            split_grads([plane[y * SUB : (y + 1) * SUB, :] for y in range(height)])
        )
    for j in range(9):
        for dz in range(KS):
            first = SUB - MARGIN + dz
            source = [
                spread[j, x, first : first + SUB, :] for x in range(planes + KS - 1)
            ]
            for dx in range(KS):
                products[j % 2, dx, dz * SUB : (dz + 1) * SUB, :] = tree_sum(
                    [source[x + dx] * upstream[x][j] for x in range(planes)]
                )
        for dx in range(KS):
            joined[j, dx] = tree_sum(
                [products[j % 2, dx, pl.ds(s, SUB, stride=SUB), :] for s in range(SUB)]
            )
    for dx in range(KS):
        for dy, tile in enumerate(join_taps([joined[j, dx] for j in range(9)])):
            row = dx * KS * KS + dy * KS
            flat[row : row + SUB, :] = tile
    flat[TAP_ROWS : TAP_ROWS + SUB, :] = small[...]
    step = pl.program_id(0)
    half = pl.num_programs(0) // 2

    @pl.when(step < half)
    def _():
        sent[...] = flat[...].astype(BF16)

    @pl.when(step >= half)
    def _():
        kept[...] = flat[...].astype(BF16)


def mlp_kernel(
    normed,
    weight_in,
    weight_out,
    centered,
    norm_gain,
    layer_scale,
    voxels,
    cotangent,
    block_out,
    conv_grad,
    small,
    mixed,
    back,
    mixed_grad,
):
    step = pl.program_id(0)
    gain = norm_gain[...].reshape(1, -1)
    scale = layer_scale[...].reshape(1, -1)

    @pl.when(step == 0)
    def _():
        mixed_grad[...] = (scale * cotangent[...].astype(F32)).astype(BF16)

    across = (((1,), (1,)), ((), ()))
    hidden = lax.dot_general(weight_in[...], normed[...], across, preferred_element_type=F32)
    act_grad = lax.dot_general(
        weight_out[...], mixed_grad[...], across, preferred_element_type=F32
    )
    activated, hidden_grad = [part.T for part in slopes(hidden, act_grad)]
    forward = jnp.dot(activated, weight_out[...], preferred_element_type=F32)
    backward = jnp.dot(hidden_grad, weight_in[...], preferred_element_type=F32)

    @pl.when(step == 0)
    def _():
        mixed[...] = forward
        back[...] = backward

    @pl.when(step > 0)
    def _():
        mixed[...] += forward
        back[...] += backward

    @pl.when(step == pl.num_programs(0) - 1)
    def _():
        channels = gain.shape[1]
        whole = mixed[...]
        block_out[...] = (voxels[...].astype(F32) + scale * whole).astype(BF16)
        scale_local = jnp.sum(cotangent[...].astype(F32) * whole, axis=0, keepdims=True)
        grad = back[...]
        deviation = centered[...]
        variance = jnp.sum(deviation * deviation, axis=1, keepdims=True) * (1.0 / channels)
        inverse = lax.rsqrt(variance + norm_eps)
        one = deviation * inverse
        bias_local = jnp.sum(grad, axis=0, keepdims=True)
        gain_local = jnp.sum(grad * one, axis=0, keepdims=True)
        small[...] = jnp.concatenate(
            [gain_local, bias_local, scale_local, jnp.zeros((SUB - 3, channels), F32)], axis=0
        )
        scaled = grad * gain
        average = jnp.sum(scaled, axis=1, keepdims=True) * (1.0 / channels)
        slant = jnp.sum(scaled * one, axis=1, keepdims=True) * (1.0 / channels)
        conv_grad[...] = (inverse * (scaled - average - one * slant)).astype(BF16)


def slopes(hidden, act_grad):
    bell = jnp.exp(-0.5 * hidden * hidden)
    below = 1.0 + (erf_step * root_half) * jnp.abs(hidden)
    t = pl.reciprocal(below, approx=True)
    t = t * (2.0 - below * t)
    poly = erf_terms[-1]
    for term in erf_terms[-2::-1]:
        poly = poly * t + term
    tail = poly * t * bell
    cover = jnp.where(hidden < 0.0, tail, 1.0 - tail)
    activated = (hidden * cover).astype(BF16)
    slope = cover + hidden * bell * inv_root_tau
    return activated, (act_grad * slope).astype(BF16)


def weight_grad_terms(which, weight_in, weight_out, scale, normed, cotangents, aligned):
    rows = normed.shape[1]
    line = len(cotangents)
    scales = scale[...].reshape(1, -1)
    mixed_grad = jnp.concatenate(
        [(scales * part[...].astype(F32)).astype(BF16) for part in cotangents], axis=0
    )
    for k in range(line):
        aligned[k * rows : (k + 1) * rows, :] = normed[which[4 + k]]
    across = (((1,), (1,)), ((), ()))
    hidden = lax.dot_general(weight_in[...], aligned[...], across, preferred_element_type=F32)
    act_grad = lax.dot_general(weight_out[...], mixed_grad, across, preferred_element_type=F32)
    activated, hidden_grad = slopes(hidden, act_grad)
    return (
        jnp.dot(hidden_grad, aligned[...], preferred_element_type=F32),
        jnp.dot(activated, mixed_grad, preferred_element_type=F32),
    )


def side_terms_kernel(which, weight_in, weight_out, scale, normed, *rest):
    *cotangents, sent, kept, aligned = rest
    terms = weight_grad_terms(which, weight_in, weight_out, scale, normed, cotangents, aligned)
    step = pl.program_id(0)

    @pl.when(step == 0)
    def _():
        for k in range(2):
            sent[k] = terms[k].astype(BF16)

    @pl.when(step == 1)
    def _():
        for k in range(2):
            kept[k] = terms[k].astype(kept.dtype)


def far_sum_kernel(kept, got, in_grad, out_grad):
    for k, out in enumerate((in_grad, out_grad)):
        out[...] = (kept[k].astype(F32) + got[k].astype(F32)).astype(BF16)


def last_sum_kernel(kept, got, in_far, out_far, in_grad, out_grad):
    for k, (far, out) in enumerate(((in_far, in_grad), (out_far, out_grad))):
        out[...] = (kept[k] + got[k].astype(F32)) + far[...].astype(F32)


def chip_sum_kernel(kept, got, out):
    out[...] = (kept[...].astype(F32) + got[...].astype(F32)).astype(BF16)


def spread_sum_kernel(parts, out):
    total = tree_sum([parts[k].astype(F32) for k in range(parts.shape[0])]).astype(BF16)
    for copy in range(out.shape[0]):
        out[copy] = total


def unpack_kernel(core, own, other, out, *small):
    piece, wide = own.shape[1:]

    def unpack(*halves):
        last = []
        for side, parts in enumerate(halves):
            lanes = slice(side * wide, (side + 1) * wide)
            for k in range(-(-TAP_ROWS // piece)):
                first = k * piece
                length = min(piece, TAP_ROWS - first)
                out[first : first + length, lanes] = parts[k].astype(F32)[:length, :]
            k = TAP_ROWS // piece
            last.append(parts[k].astype(F32))
        rows = jnp.concatenate(last, axis=1)
        first = TAP_ROWS % piece
        for k, line in enumerate(small):
            line[...] = rows[first + k : first + k + 1, :].reshape(line.shape)

    by_core(core, own, other, lambda outer, inner: unpack(inner, outer))


def params(limit=48):
    return pltpu.CompilerParams(vmem_limit_bytes=limit * 1024 * 1024)


def lane_block(rows):
    return pl.BlockSpec((rows, LANES), lambda c, *_: (0, c))


def whole_block(*shape):
    return pl.BlockSpec(shape, lambda *_: (0,) * len(shape))


def rims(cells):
    count = lax.axis_size("row")
    between = [(i, i + 1) for i in range(1, count - 1, 2)]
    return (
        lax.ppermute(cells, "row", [(i, i ^ 1) for i in range(count)]),
        lax.ppermute(cells, "row", between + [(j, i) for i, j in between]),
    )


def on_device(
    voxels, dw_kernel, norm_gain, norm_bias, weight_in, weight_out, layer_scale, cotangent
):
    planes, height, breadth, channels = voxels.shape
    rows = planes * height * breadth
    units = weight_in.shape[0]
    count = lax.axis_size("row")
    me = lax.axis_index("row")
    quad = 4
    line = count // quad
    lines = [[quad * k + p for k in range(line)] for p in range(quad)]
    other_core = [(i, i ^ 1) for i in range(count)]
    other_side = [(i, i ^ 2) for i in range(count)]
    tiles = channels // LANES

    own = voxels.reshape(rows, channels)
    upstream = cotangent.reshape(rows, channels)
    core = lax.rem(me, 2).astype(jnp.int32)
    parity = core.reshape(1)

    inner, outer = rims(own)

    def along_line(cells, steps):
        return lax.ppermute(cells, "row", [(i, (i + quad * steps) % count) for i in range(count)])

    upstream_line = [upstream] + [None] * (line - 1)
    upstream_line[1] = along_line(upstream, 1)
    upstream_line[-1] = along_line(upstream, -1)

    def spread_of(held):
        return pltpu.VMEM((9, held, PAD, LANES), F32)

    split_block = pl.BlockSpec((None, 9, KS, SUB, LANES), lambda c, *_: (c, 0, 0, 0, 0))
    partial, split = pl.pallas_call(
        functools.partial(own_conv_kernel, planes, height),
        grid=(tiles,),
        in_specs=[lane_block(rows), lane_block(TAP_ROWS)],
        out_specs=[lane_block(rows), split_block],
        out_shape=[
            jax.ShapeDtypeStruct((rows, channels), F32),
            jax.ShapeDtypeStruct((tiles, 9, KS, SUB, LANES), F32),
        ],
        scratch_shapes=[spread_of(planes)],
        compiler_params=params(),
        cost_estimate=NO_COST,
        name="own_conv",
    )(own, dw_kernel)

    partial, upstream_line[1], upstream_line[-1] = lax.optimization_barrier(
        (partial, upstream_line[1], upstream_line[-1])
    )
    for k in range(2, line - 1):
        upstream_line[k] = along_line(upstream_line[k - 1], 1)
    normed, centered = pl.pallas_call(
        functools.partial(rim_conv_kernel, planes, height),
        grid_spec=pltpu.PrefetchScalarGridSpec(
            num_scalar_prefetch=1,
            grid=(tiles,),
            in_specs=[
                lane_block(rows),
                lane_block(rows),
                split_block,
                lane_block(rows),
                whole_block(channels),
                whole_block(channels),
            ],
            out_specs=[
                whole_block(line, rows, channels),
                whole_block(rows, channels),
            ],
            scratch_shapes=[spread_of(2 * MARGIN), pltpu.VMEM((tiles, rows, LANES), F32)],
        ),
        out_shape=[
            jax.ShapeDtypeStruct((line, rows, channels), BF16),
            jax.ShapeDtypeStruct((rows, channels), F32),
        ],
        compiler_params=params(),
        cost_estimate=NO_COST,
        name="rim_conv",
    )(parity, inner, outer, split, partial, norm_gain, norm_bias)

    normed, centered, upstream_line[2] = lax.optimization_barrier(
        (normed, centered, upstream_line[2])
    )
    gathered = lax.all_to_all(
        normed, "row", split_axis=0, concat_axis=0, tiled=True, axis_index_groups=lines
    )

    block = 512
    whole = whole_block(rows, channels)
    block_out, conv_grad, small = pl.pallas_call(
        mlp_kernel,
        grid=(units // block,),
        in_specs=[
            pl.BlockSpec((None, rows, channels), lambda f: (0, 0, 0)),
            pl.BlockSpec((block, channels), lambda f: (f, 0)),
            pl.BlockSpec((block, channels), lambda f: (f, 0)),
            whole,
            whole_block(channels),
            whole_block(channels),
            whole,
            whole,
        ],
        out_specs=[
            whole,
            whole,
            whole_block(SUB, channels),
        ],
        out_shape=[
            jax.ShapeDtypeStruct((rows, channels), BF16),
            jax.ShapeDtypeStruct((rows, channels), BF16),
            jax.ShapeDtypeStruct((SUB, channels), F32),
        ],
        scratch_shapes=[
            pltpu.VMEM((rows, channels), F32),
            pltpu.VMEM((rows, channels), F32),
            pltpu.VMEM((rows, channels), BF16),
        ],
        compiler_params=params(),
        cost_estimate=NO_COST,
        name="mlp_both_ways",
    )(normed, weight_in, weight_out, centered, norm_gain, layer_scale, own, upstream)

    half = count // 2
    alike = [[2 * k + p for k in range(half)] for p in range(2)]
    half_tiles = tiles // 2
    wide = half_tiles * LANES
    piece = -(-(TAP_ROWS + SUB) // half)
    piece += -piece % (2 * SUB)
    padded = piece * half

    def tile_of(block_rows):
        def at(c, w):
            return 0, (c + w[1] * half_tiles) % tiles

        return pl.BlockSpec((block_rows, LANES), at)

    half_sent, half_kept = pl.pallas_call(
        functools.partial(kernel_grad_kernel, planes, height),
        grid_spec=pltpu.PrefetchScalarGridSpec(
            num_scalar_prefetch=1,
            grid=(tiles,),
            in_specs=[tile_of(rows), tile_of(rows), tile_of(rows), tile_of(rows), tile_of(SUB)],
            out_specs=[
                pl.BlockSpec((padded, LANES), lambda c, w: (0, jnp.minimum(c, half_tiles - 1))),
                pl.BlockSpec((padded, LANES), lambda c, w: (0, jnp.maximum(c - half_tiles, 0))),
            ],
            scratch_shapes=[
                spread_of(2 * MARGIN + planes),
                pltpu.VMEM((2, KS, SUB * SUB, LANES), F32),
                pltpu.VMEM((9, KS, SUB, LANES), F32),
                pltpu.VMEM((padded, LANES), F32),
            ],
        ),
        out_shape=[jax.ShapeDtypeStruct((padded, wide), BF16)] * 2,
        compiler_params=params(),
        cost_estimate=NO_COST,
        name="kernel_grad_terms",
    )(jnp.stack([core, 1 - core]), inner, own, outer, conv_grad, small)

    half_sent, conv_grad = lax.optimization_barrier((half_sent, conv_grad))
    half_got = lax.ppermute(half_sent, "row", other_core)
    grad_inner, grad_outer = rims(conv_grad)
    sums = pl.pallas_call(
        chip_sum_kernel,
        in_specs=[whole_block(padded, wide)] * 2,
        out_specs=whole_block(padded, wide),
        out_shape=jax.ShapeDtypeStruct((padded, wide), BF16),
        grid=(1,),
        compiler_params=params(),
        cost_estimate=NO_COST,
        name="kernel_grad_chip_sum",
    )(half_kept, half_got)

    share = units // count
    tokens = line * rows
    base = me // quad * quad
    side = lax.rem(me, quad) // 2
    place = lax.rem(me // quad + line - jnp.arange(line, dtype=jnp.int32), line)
    far = base + 2 * (1 - side)
    near = base + 2 * side
    which = jnp.concatenate(
        [
            jnp.stack([far + 1 - core, far + core, near + 1 - core, near + core]).astype(jnp.int32),
            place.astype(jnp.int32),
        ]
    )
    pair = (2, share, channels)

    def side_terms(first, kept_as, name):
        chunk = pl.BlockSpec((share, channels), lambda s, w: (w[s + first], 0))
        return pl.pallas_call(
            side_terms_kernel,
            grid_spec=pltpu.PrefetchScalarGridSpec(
                num_scalar_prefetch=1,
                grid=(2,),
                in_specs=[
                    chunk,
                    chunk,
                    whole_block(channels),
                    whole_block(line, rows, channels),
                ]
                + [whole_block(rows, channels)] * line,
                out_specs=[whole_block(*pair)] * 2,
                scratch_shapes=[pltpu.VMEM((tokens, channels), BF16)],
            ),
            out_shape=[jax.ShapeDtypeStruct(pair, BF16), jax.ShapeDtypeStruct(pair, kept_as)],
            compiler_params=params(),
            cost_estimate=NO_COST,
            name=name,
        )(which, weight_in, weight_out, layer_scale, gathered, *upstream_line)

    which, sums = lax.optimization_barrier((which, sums))
    far_sent, far_kept = side_terms(0, BF16, "weight_grads_far_side")
    far_sent, conv_own, grad_inner, grad_outer = lax.optimization_barrier(
        (far_sent, conv_grad, grad_inner, grad_outer)
    )
    far_got = lax.ppermute(far_sent, "row", other_core)
    scattered = lax.all_to_all(
        sums.reshape(half, piece, wide),
        "row",
        split_axis=0,
        concat_axis=0,
        tiled=True,
        axis_index_groups=alike,
    )
    voxel_grad = pl.pallas_call(
        functools.partial(input_grad_kernel, planes, height),
        grid_spec=pltpu.PrefetchScalarGridSpec(
            num_scalar_prefetch=1,
            grid=(tiles,),
            in_specs=[
                lane_block(rows),
                lane_block(rows),
                lane_block(rows),
                lane_block(TAP_ROWS),
                lane_block(rows),
            ],
            out_specs=lane_block(rows),
            scratch_shapes=[
                spread_of(2 * MARGIN + planes),
                pltpu.VMEM((9, KS, SUB, LANES), F32),
            ],
        ),
        out_shape=jax.ShapeDtypeStruct((rows, channels), BF16),
        compiler_params=params(),
        cost_estimate=NO_COST,
        name="input_grad_conv",
    )(parity, grad_inner, conv_own, grad_outer, dw_kernel, upstream)

    far_kept, voxel_grad = lax.optimization_barrier((far_kept, voxel_grad))
    in_sent, out_sent = pl.pallas_call(
        far_sum_kernel,
        grid=(1,),
        in_specs=[whole_block(*pair)] * 2,
        out_specs=[whole_block(*pair[1:])] * 2,
        out_shape=[jax.ShapeDtypeStruct(pair[1:], BF16)] * 2,
        compiler_params=params(),
        cost_estimate=NO_COST,
        name="weight_grads_far_sum",
    )(far_kept, far_got)
    in_far = lax.ppermute(in_sent, "row", other_side)

    scattered, voxel_grad = lax.optimization_barrier((scattered, voxel_grad))
    copies = pl.pallas_call(
        spread_sum_kernel,
        in_specs=[whole_block(half, piece, wide)],
        out_specs=whole_block(half, piece, wide),
        out_shape=jax.ShapeDtypeStruct((half, piece, wide), BF16),
        grid=(1,),
        compiler_params=params(),
        cost_estimate=NO_COST,
        name="kernel_grad_sum",
    )(scattered)
    which, copies = lax.optimization_barrier((which, copies))
    totals = lax.all_to_all(
        copies, "row", split_axis=0, concat_axis=0, tiled=True, axis_index_groups=alike
    )
    which, out_sent = lax.optimization_barrier((which, out_sent))
    sent, kept = side_terms(2, F32, "weight_grads_near_side")
    sent, in_far = lax.optimization_barrier((sent, in_far))
    got = lax.ppermute(sent, "row", other_core)
    out_far = lax.ppermute(out_sent, "row", other_side)

    totals, out_far = lax.optimization_barrier((totals, out_far))
    other_totals = lax.ppermute(totals, "row", other_core)
    kernel_grad, *vector_grads = pl.pallas_call(
        unpack_kernel,
        grid_spec=pltpu.PrefetchScalarGridSpec(
            num_scalar_prefetch=1,
            grid=(1,),
            in_specs=[whole_block(half, piece, wide)] * 2,
            out_specs=[whole_block(TAP_ROWS, channels)] + [whole_block(channels)] * 3,
        ),
        out_shape=[jax.ShapeDtypeStruct((TAP_ROWS, channels), F32)]
        + [jax.ShapeDtypeStruct((channels,), F32)] * 3,
        compiler_params=params(),
        cost_estimate=NO_COST,
        name="kernel_grad_unpack",
    )(parity, totals, other_totals)

    weight_in_grad, weight_out_grad = pl.pallas_call(
        last_sum_kernel,
        grid=(1,),
        in_specs=[whole_block(*pair)] * 2 + [whole_block(*pair[1:])] * 2,
        out_specs=[whole_block(*pair[1:])] * 2,
        out_shape=[jax.ShapeDtypeStruct(pair[1:], F32)] * 2,
        compiler_params=params(),
        cost_estimate=NO_COST,
        name="weight_grads_sum",
    )(kept, got, in_far, out_far)

    return (
        block_out.reshape(voxels.shape),
        voxel_grad.reshape(voxels.shape),
        kernel_grad,
        *vector_grads,
        weight_in_grad,
        weight_out_grad,
    )


def solution(mesh):
    in_specs = (
        P(("group", "row"), None, None, None),
        P(),
        P(),
        P(),
        P(),
        P(),
        P(),
        P(("group", "row"), None, None, None),
    )
    out_specs = (
        P(("group", "row"), None, None, None),
        P(("group", "row"), None, None, None),
        P("group", None),
        P("group"),
        P("group"),
        P("group"),
        P(("group", "row"), None),
        P(("group", "row"), None),
    )
    return jax.shard_map(
        on_device, mesh=mesh, in_specs=in_specs, out_specs=out_specs, check_vma=False
    )
```

```python
import functools

import jax
import jax.numpy as jnp
from jax import lax
from jax.experimental import pallas as pl
from jax.experimental.pallas import tpu as pltpu
from jax.sharding import PartitionSpec as P

KS = 7
MARGIN = KS // 2
LANES = 128
SUB = 8
PAD = 3 * SUB
TAP_ROWS = KS * KS * KS

root_half = 0.7071067811865476
inv_root_tau = 0.3989422804014327
norm_eps = 1e-06
erf_step = 0.3275911
erf_terms = tuple(
    0.5 * a for a in (0.254829592, -0.284496736, 1.421413741, -1.453152027, 1.061405429)
)

NO_COST = pl.CostEstimate(flops=0, bytes_accessed=0, transcendentals=0)

F32 = jnp.float32
BF16 = jnp.bfloat16


def split_source(v):
    terms = []
    for a, b in ((v[0] + v[2], v[1] + v[3]), (v[2], v[3]), (v[0], v[1])):
        terms += [a + b, b, a]
    return terms


def split_taps(t):
    terms = []
    for s in (
        (t[2], t[3], t[4]),
        (t[4] - t[2], t[5] - t[3], t[6] - t[4]),
        (t[0] - t[2], t[1] - t[3], t[2] - t[4]),
    ):
        terms += [s[1], s[2] - s[1], s[0] - s[1]]
    return terms


def split_grads(g):
    terms = []
    for a, b in ((g[0] + g[2], g[1] + g[3]), (g[0], g[1]), (g[2], g[3])):
        terms += [a + b, a, b]
    return terms


def join_outputs(m):
    pair = [(m[3 * k] + m[3 * k + 1], m[3 * k] + m[3 * k + 2]) for k in range(3)]
    return [
        pair[0][0] + pair[1][0],
        pair[0][1] + pair[1][1],
        pair[0][0] + pair[2][0],
        pair[0][1] + pair[2][1],
    ]


def join_taps(m):
    p, q, r = [
        (m[3 * k + 2], m[3 * k] - m[3 * k + 1] - m[3 * k + 2], m[3 * k + 1]) for k in range(3)
    ]
    return [
        r[0],
        r[1],
        p[0] - q[0] - r[0] + r[2],
        p[1] - q[1] - r[1],
        p[2] - q[2] - r[2] + q[0],
        q[1],
        q[2],
    ]


def tree_sum(terms):
    while len(terms) > 1:
        terms = [
            terms[k] + terms[k + 1] if k + 1 < len(terms) else terms[k]
            for k in range(0, len(terms), 2)
        ]
    return terms[0]


def stage_source(wanted, height, spread):
    row = height * SUB
    for at, (block, x) in enumerate(wanted):
        plane = block[x * row : (x + 1) * row, :].astype(F32)
        lines = [plane[y * SUB : (y + 1) * SUB, :] for y in range(height)]
        for j, term in enumerate(split_source(lines)):
            spread[j, at, SUB : 2 * SUB, :] = term


def rim_planes(left, right, planes):
    wanted = [(left, x) for x in range(planes - MARGIN, planes)]
    return wanted + [(right, x) for x in range(MARGIN)]


def all_planes(left, own, right, planes):
    rim = rim_planes(left, right, planes)
    return rim[:MARGIN] + [(own, x) for x in range(planes)] + rim[MARGIN:]


def by_core(core, inner, outer, stage):
    @pl.when(core[0] == 0)
    def _():
        stage(outer, inner)

    @pl.when(core[0] != 0)
    def _():
        stage(inner, outer)


def clear_rims(spread):
    zeros = jnp.zeros(spread.shape[:2] + (SUB, LANES), F32)
    spread[:, :, :SUB, :] = zeros
    spread[:, :, 2 * SUB :, :] = zeros


def stage_taps(taps, split):
    for dx in range(KS):
        rows = []
        for dy in range(KS):
            first = dx * KS * KS + dy * KS
            if first + SUB <= TAP_ROWS:
                rows.append(taps[first : first + SUB, :])
            else:
                rows.append(pltpu.roll(taps[TAP_ROWS - SUB : TAP_ROWS, :], SUB - 1, 0))
        for j, term in enumerate(split_taps(rows)):
            split[j, dx] = term


REVERSED = (0, 2, 1, 6, 8, 7, 3, 5, 4)


def convolve(spread, split, planes, held, flipped):
    terms = []
    for j in range(9):
        sums = [None] * planes
        for dz in range(KS):
            first = SUB - MARGIN + dz
            source = {x: spread[j, at, first : first + SUB, :] for at, x in enumerate(held)}
            weights = []
            for dx in range(KS):
                if flipped:
                    tap = split[REVERSED[j], KS - 1 - dx, KS - 1 - dz : KS - dz, :]
                else:
                    tap = split[j, dx, dz : dz + 1, :]
                weights.append(jnp.broadcast_to(tap, (SUB, LANES)))
            for x in range(planes):
                part = tree_sum(
                    [source[x + dx] * weights[dx] for dx in range(KS) if x + dx in source]
                )
                sums[x] = part if sums[x] is None else sums[x] + part
        terms.append(sums)
    return [join_outputs([terms[j][x] for j in range(9)]) for x in range(planes)]


def own_conv_kernel(planes, height, own, taps, out, split, spread):
    @pl.when(pl.program_id(0) == 0)
    def _():
        clear_rims(spread)

    stage_source([(own, x) for x in range(planes)], height, spread)
    stage_taps(taps, split)
    rows = convolve(spread, split, planes, range(MARGIN, MARGIN + planes), False)
    for x in range(planes):
        for y in range(height):
            at = (x * height + y) * SUB
            out[at : at + SUB, :] = rows[x][y]


def rim_conv_kernel(
    planes, height, core, inner, outer, split, partial, gain, bias, normed, centered, spread, conv
):
    step = pl.program_id(0)

    @pl.when(step == 0)
    def _():
        clear_rims(spread)

    def stage(left, right):
        stage_source(rim_planes(left, right, planes), height, spread)

    by_core(core, inner, outer, stage)
    held = list(range(MARGIN)) + list(range(MARGIN + planes, 2 * MARGIN + planes))
    rows = convolve(spread, split, planes, held, False)
    for x in range(planes):
        for y in range(height):
            at = (x * height + y) * SUB
            conv[step, at : at + SUB, :] = rows[x][y] + partial[at : at + SUB, :]

    @pl.when(step == pl.num_programs(0) - 1)
    def _():
        tiles = conv.shape[0]
        channels = tiles * LANES
        parts = [conv[k] for k in range(tiles)]
        gains = gain[...].reshape(1, channels)
        biases = bias[...].reshape(1, channels)
        average = jnp.sum(tree_sum(parts), axis=1, keepdims=True) * (1.0 / channels)
        parts = [part - average for part in parts]
        variance = jnp.sum(
            tree_sum([part * part for part in parts]), axis=1, keepdims=True
        ) * (1.0 / channels)
        inverse = lax.rsqrt(variance + norm_eps)
        for k in range(tiles):
            lanes = slice(k * LANES, (k + 1) * LANES)
            centered[:, lanes] = parts[k]
            value = parts[k] * inverse
            whole = (value * gains[:, lanes] + biases[:, lanes]).astype(BF16)
            for copy in range(normed.shape[0]):
                normed[copy, :, lanes] = whole


def input_grad_kernel(
    planes, height, core, inner, own, outer, taps, cotangent, out, spread, split
):
    @pl.when(pl.program_id(0) == 0)
    def _():
        clear_rims(spread)

    def stage(left, right):
        stage_source(all_planes(left, own, right, planes), height, spread)

    by_core(core, inner, outer, stage)
    stage_taps(taps, split)
    rows = convolve(spread, split, planes, range(2 * MARGIN + planes), True)
    for x in range(planes):
        at = x * height * SUB
        whole = jnp.concatenate(rows[x], axis=0)
        upstream = cotangent[at : at + height * SUB, :].astype(F32)
        out[at : at + height * SUB, :] = (upstream + whole).astype(BF16)


def kernel_grad_kernel(
    planes, height, which, inner, own, outer, grads, small, sent, kept, spread, products, joined, flat
):
    @pl.when(pl.program_id(0) == 0)
    def _():
        clear_rims(spread)
        products[...] = jnp.zeros(products.shape, F32)
        flat[...] = jnp.zeros(flat.shape, F32)

    def stage(left, right):
        stage_source(all_planes(left, own, right, planes), height, spread)

    by_core(which, inner, outer, stage)
    upstream = []
    for x in range(planes):
        plane = grads[x * height * SUB : (x + 1) * height * SUB, :].astype(F32)
        upstream.append(
            split_grads([plane[y * SUB : (y + 1) * SUB, :] for y in range(height)])
        )
    for j in range(9):
        for dz in range(KS):
            first = SUB - MARGIN + dz
            source = [
                spread[j, x, first : first + SUB, :] for x in range(planes + KS - 1)
            ]
            for dx in range(KS):
                products[j % 2, dx, dz * SUB : (dz + 1) * SUB, :] = tree_sum(
                    [source[x + dx] * upstream[x][j] for x in range(planes)]
                )
        for dx in range(KS):
            joined[j, dx] = tree_sum(
                [products[j % 2, dx, pl.ds(s, SUB, stride=SUB), :] for s in range(SUB)]
            )
    for dx in range(KS):
        for dy, tile in enumerate(join_taps([joined[j, dx] for j in range(9)])):
            row = dx * KS * KS + dy * KS
            flat[row : row + SUB, :] = tile
    flat[TAP_ROWS : TAP_ROWS + SUB, :] = small[...]
    step = pl.program_id(0)
    half = pl.num_programs(0) // 2

    @pl.when(step < half)
    def _():
        sent[...] = flat[...].astype(BF16)

    @pl.when(step >= half)
    def _():
        kept[...] = flat[...].astype(BF16)


def mlp_kernel(
    normed, weight_in, weight_out, centered, norm_gain, layer_scale, voxels, *rest
):
    *cotangents, block_out, conv_grad, small, together, mixed, back, mixed_grad = rest
    cotangent = cotangents[0]
    step = pl.program_id(0)
    gain = norm_gain[...].reshape(1, -1)
    scale = layer_scale[...].reshape(1, -1)

    @pl.when(step == 0)
    def _():
        mixed_grad[...] = (scale * cotangent[...].astype(F32)).astype(BF16)
        for k, part in enumerate(cotangents):
            together[k] = part[...]

    across = (((1,), (1,)), ((), ()))
    hidden = lax.dot_general(normed[...], weight_in[...], across, preferred_element_type=F32)
    act_grad = lax.dot_general(
        mixed_grad[...], weight_out[...], across, preferred_element_type=F32
    )
    activated, hidden_grad = slopes(hidden, act_grad)
    forward = jnp.dot(activated, weight_out[...], preferred_element_type=F32)
    backward = jnp.dot(hidden_grad, weight_in[...], preferred_element_type=F32)

    @pl.when(step == 0)
    def _():
        mixed[...] = forward
        back[...] = backward

    @pl.when(step > 0)
    def _():
        mixed[...] += forward
        back[...] += backward

    @pl.when(step == pl.num_programs(0) - 1)
    def _():
        channels = gain.shape[1]
        whole = mixed[...]
        block_out[...] = (voxels[...].astype(F32) + scale * whole).astype(BF16)
        scale_local = jnp.sum(cotangent[...].astype(F32) * whole, axis=0, keepdims=True)
        grad = back[...]
        deviation = centered[...]
        variance = jnp.sum(deviation * deviation, axis=1, keepdims=True) * (1.0 / channels)
        inverse = lax.rsqrt(variance + norm_eps)
        one = deviation * inverse
        bias_local = jnp.sum(grad, axis=0, keepdims=True)
        gain_local = jnp.sum(grad * one, axis=0, keepdims=True)
        small[...] = jnp.concatenate(
            [gain_local, bias_local, scale_local, jnp.zeros((SUB - 3, channels), F32)], axis=0
        )
        scaled = grad * gain
        average = jnp.sum(scaled, axis=1, keepdims=True) * (1.0 / channels)
        slant = jnp.sum(scaled * one, axis=1, keepdims=True) * (1.0 / channels)
        conv_grad[...] = (inverse * (scaled - average - one * slant)).astype(BF16)


def slopes(hidden, act_grad):
    bell = jnp.exp(-0.5 * hidden * hidden)
    below = 1.0 + (erf_step * root_half) * jnp.abs(hidden)
    t = pl.reciprocal(below, approx=True)
    t = t * (2.0 - below * t)
    poly = erf_terms[-1]
    for term in erf_terms[-2::-1]:
        poly = poly * t + term
    tail = poly * t * bell
    cover = jnp.where(hidden < 0.0, tail, 1.0 - tail)
    activated = (hidden * cover).astype(BF16)
    slope = cover + hidden * bell * inv_root_tau
    return activated, (act_grad * slope).astype(BF16)


def weight_grad_terms(which, weight_in, weight_out, scale, sets, aligned, mixed_grad):
    scales = scale[...].reshape(1, -1)
    at = 0
    for normed, cotangents in sets:
        line, rows = normed.shape[:2]
        for k in range(line):
            aligned[at : at + rows, :] = normed[which[2 + k]]
            upstream = cotangents[k].astype(F32)
            mixed_grad[at : at + rows, :] = (scales * upstream).astype(BF16)
            at += rows
    across = (((1,), (1,)), ((), ()))
    hidden = lax.dot_general(weight_in[...], aligned[...], across, preferred_element_type=F32)
    act_grad = lax.dot_general(weight_out[...], mixed_grad[...], across, preferred_element_type=F32)
    activated, hidden_grad = slopes(hidden, act_grad)
    return (
        jnp.dot(hidden_grad, aligned[...], preferred_element_type=F32),
        jnp.dot(activated, mixed_grad[...], preferred_element_type=F32),
    )


def far_side_kernel(
    which, weight_in, weight_out, scale, norm, cot, other_norm, other_cot, sent, aligned, mixed_grad
):
    sets = ((norm, cot), (other_norm, other_cot))
    terms = weight_grad_terms(which, weight_in, weight_out, scale, sets, aligned, mixed_grad)
    for k in range(2):
        sent[k] = terms[k].astype(BF16)


def near_side_kernel(
    which,
    weight_in,
    weight_out,
    scale,
    norm,
    cot,
    other_norm,
    other_cot,
    got,
    in_grad,
    out_grad,
    aligned,
    mixed_grad,
):
    sets = ((norm, cot), (other_norm, other_cot))
    terms = weight_grad_terms(which, weight_in, weight_out, scale, sets, aligned, mixed_grad)
    for k, out in enumerate((in_grad, out_grad)):
        out[...] = terms[k] + got[k].astype(F32)


def chip_sum_kernel(kept, got, out):
    out[...] = (kept[...].astype(F32) + got[...].astype(F32)).astype(BF16)


def spread_sum_kernel(parts, out):
    total = tree_sum([parts[k].astype(F32) for k in range(parts.shape[0])]).astype(BF16)
    for copy in range(out.shape[0]):
        out[copy] = total


def unpack_kernel(core, own, other, out, *small):
    piece, wide = own.shape[1:]

    def unpack(*halves):
        last = []
        for side, parts in enumerate(halves):
            lanes = slice(side * wide, (side + 1) * wide)
            for k in range(-(-TAP_ROWS // piece)):
                first = k * piece
                length = min(piece, TAP_ROWS - first)
                out[first : first + length, lanes] = parts[k].astype(F32)[:length, :]
            k = TAP_ROWS // piece
            last.append(parts[k].astype(F32))
        rows = jnp.concatenate(last, axis=1)
        first = TAP_ROWS % piece
        for k, line in enumerate(small):
            line[...] = rows[first + k : first + k + 1, :].reshape(line.shape)

    by_core(core, own, other, lambda outer, inner: unpack(inner, outer))


def params(limit=16):
    return pltpu.CompilerParams(vmem_limit_bytes=limit * 1024 * 1024)


def lane_block(rows):
    return pl.BlockSpec((rows, LANES), lambda c, *_: (0, c))


def whole_block(*shape):
    return pl.BlockSpec(shape, lambda *_: (0,) * len(shape))


def rims(cells):
    count = lax.axis_size("row")
    between = [(i, i + 1) for i in range(1, count - 1, 2)]
    return (
        lax.ppermute(cells, "row", [(i, i ^ 1) for i in range(count)]),
        lax.ppermute(cells, "row", between + [(j, i) for i, j in between]),
    )


def on_device(
    voxels, dw_kernel, norm_gain, norm_bias, weight_in, weight_out, layer_scale, cotangent
):
    planes, height, breadth, channels = voxels.shape
    rows = planes * height * breadth
    units = weight_in.shape[0]
    count = lax.axis_size("row")
    me = lax.axis_index("row")
    quad = 4
    line = count // quad
    lines = [[quad * k + p for k in range(line)] for p in range(quad)]
    other_core = [(i, i ^ 1) for i in range(count)]
    other_side = [(i, i ^ 2) for i in range(count)]
    tiles = channels // LANES

    own = voxels.reshape(rows, channels)
    upstream = cotangent.reshape(rows, channels)
    core = lax.rem(me, 2).astype(jnp.int32)
    parity = core.reshape(1)

    inner, outer = rims(own)

    def along_line(cells, steps):
        return lax.ppermute(cells, "row", [(i, (i + quad * steps) % count) for i in range(count)])

    upstream_line = [upstream] + [None] * (line - 1)
    upstream_line[1] = along_line(upstream, 1)
    upstream_line[-1] = along_line(upstream, -1)

    def spread_of(held):
        return pltpu.VMEM((9, held, PAD, LANES), F32)

    split_block = pl.BlockSpec((None, 9, KS, SUB, LANES), lambda c, *_: (c, 0, 0, 0, 0))
    partial, split = pl.pallas_call(
        functools.partial(own_conv_kernel, planes, height),
        grid=(tiles,),
        in_specs=[lane_block(rows), lane_block(TAP_ROWS)],
        out_specs=[lane_block(rows), split_block],
        out_shape=[
            jax.ShapeDtypeStruct((rows, channels), F32),
            jax.ShapeDtypeStruct((tiles, 9, KS, SUB, LANES), F32),
        ],
        scratch_shapes=[spread_of(planes)],
        compiler_params=params(),
        cost_estimate=NO_COST,
        name="own_conv",
    )(own, dw_kernel)

    partial, upstream_line[1], upstream_line[-1] = lax.optimization_barrier(
        (partial, upstream_line[1], upstream_line[-1])
    )
    for k in range(2, line - 1):
        upstream_line[k] = along_line(upstream_line[k - 1], 1)
    normed, centered = pl.pallas_call(
        functools.partial(rim_conv_kernel, planes, height),
        grid_spec=pltpu.PrefetchScalarGridSpec(
            num_scalar_prefetch=1,
            grid=(tiles,),
            in_specs=[
                lane_block(rows),
                lane_block(rows),
                split_block,
                lane_block(rows),
                whole_block(channels),
                whole_block(channels),
            ],
            out_specs=[
                whole_block(line, rows, channels),
                whole_block(rows, channels),
            ],
            scratch_shapes=[spread_of(2 * MARGIN), pltpu.VMEM((tiles, rows, LANES), F32)],
        ),
        out_shape=[
            jax.ShapeDtypeStruct((line, rows, channels), BF16),
            jax.ShapeDtypeStruct((rows, channels), F32),
        ],
        compiler_params=params(),
        cost_estimate=NO_COST,
        name="rim_conv",
    )(parity, inner, outer, split, partial, norm_gain, norm_bias)

    normed, upstream_line[2] = lax.optimization_barrier((normed, upstream_line[2]))
    gathered = lax.all_to_all(
        normed, "row", split_axis=0, concat_axis=0, tiled=True, axis_index_groups=lines
    )

    block = 384
    whole = whole_block(rows, channels)
    block_out, conv_grad, small, cotangents = pl.pallas_call(
        mlp_kernel,
        grid=(units // block,),
        in_specs=[
            pl.BlockSpec((None, rows, channels), lambda f: (0, 0, 0)),
            pl.BlockSpec((block, channels), lambda f: (f, 0)),
            pl.BlockSpec((block, channels), lambda f: (f, 0)),
            whole,
            whole_block(channels),
            whole_block(channels),
        ]
        + [whole] * (1 + line),
        out_specs=[
            whole,
            whole,
            whole_block(SUB, channels),
            whole_block(line, rows, channels),
        ],
        out_shape=[
            jax.ShapeDtypeStruct((rows, channels), BF16),
            jax.ShapeDtypeStruct((rows, channels), BF16),
            jax.ShapeDtypeStruct((SUB, channels), F32),
            jax.ShapeDtypeStruct((line, rows, channels), BF16),
        ],
        scratch_shapes=[
            pltpu.VMEM((rows, channels), F32),
            pltpu.VMEM((rows, channels), F32),
            pltpu.VMEM((rows, channels), BF16),
        ],
        compiler_params=params(48),
        cost_estimate=NO_COST,
        name="mlp_both_ways",
    )(normed, weight_in, weight_out, centered, norm_gain, layer_scale, own, *upstream_line)

    half = count // 2
    alike = [[2 * k + p for k in range(half)] for p in range(2)]
    half_tiles = tiles // 2
    wide = half_tiles * LANES
    piece = -(-(TAP_ROWS + SUB) // half)
    piece += -piece % (2 * SUB)
    padded = piece * half

    def tile_of(block_rows):
        def at(c, w):
            return 0, (c + w[1] * half_tiles) % tiles

        return pl.BlockSpec((block_rows, LANES), at)

    half_sent, half_kept = pl.pallas_call(
        functools.partial(kernel_grad_kernel, planes, height),
        grid_spec=pltpu.PrefetchScalarGridSpec(
            num_scalar_prefetch=1,
            grid=(tiles,),
            in_specs=[tile_of(rows), tile_of(rows), tile_of(rows), tile_of(rows), tile_of(SUB)],
            out_specs=[
                pl.BlockSpec((padded, LANES), lambda c, w: (0, jnp.minimum(c, half_tiles - 1))),
                pl.BlockSpec((padded, LANES), lambda c, w: (0, jnp.maximum(c - half_tiles, 0))),
            ],
            scratch_shapes=[
                spread_of(2 * MARGIN + planes),
                pltpu.VMEM((2, KS, SUB * SUB, LANES), F32),
                pltpu.VMEM((9, KS, SUB, LANES), F32),
                pltpu.VMEM((padded, LANES), F32),
            ],
        ),
        out_shape=[jax.ShapeDtypeStruct((padded, wide), BF16)] * 2,
        compiler_params=params(),
        cost_estimate=NO_COST,
        name="kernel_grad_terms",
    )(jnp.stack([core, 1 - core]), inner, own, outer, conv_grad, small)

    half_sent, conv_grad = lax.optimization_barrier((half_sent, conv_grad))
    half_got = lax.ppermute(half_sent, "row", other_core)
    grad_inner, grad_outer = rims(conv_grad)
    sums = pl.pallas_call(
        chip_sum_kernel,
        in_specs=[whole_block(padded, wide)] * 2,
        out_specs=whole_block(padded, wide),
        out_shape=jax.ShapeDtypeStruct((padded, wide), BF16),
        grid=(1,),
        compiler_params=params(),
        cost_estimate=NO_COST,
        name="kernel_grad_chip_sum",
    )(half_kept, half_got)

    share = units // count
    tokens = line * rows
    base = me // quad * quad
    side = lax.rem(me, quad) // 2
    place = lax.rem(me // quad + line - jnp.arange(line, dtype=jnp.int32), line)
    far = base + 2 * (1 - side)
    near = base + 2 * side
    which = jnp.concatenate(
        [jnp.stack([far + core, near + core]).astype(jnp.int32), place.astype(jnp.int32)]
    )
    other_gathered = lax.ppermute(gathered, "row", other_core)
    other_cotangents = lax.ppermute(cotangents, "row", other_core)
    pair = (2, share, channels)

    def side_terms(kernel, number, more, outs, name):
        chunk = pl.BlockSpec((share, channels), lambda _, w: (w[number], 0))
        return pl.pallas_call(
            kernel,
            grid_spec=pltpu.PrefetchScalarGridSpec(
                num_scalar_prefetch=1,
                grid=(1,),
                in_specs=[chunk, chunk, whole_block(channels)]
                + [whole_block(line, rows, channels)] * 4
                + [whole_block(*part.shape) for part in more],
                out_specs=[whole_block(*out.shape) for out in outs],
                scratch_shapes=[pltpu.VMEM((2 * tokens, channels), BF16)] * 2,
            ),
            out_shape=outs,
            compiler_params=params(48),
            cost_estimate=NO_COST,
            name=name,
        )(
            which,
            weight_in,
            weight_out,
            layer_scale,
            gathered,
            cotangents,
            other_gathered,
            other_cotangents,
            *more,
        )

    which, sums = lax.optimization_barrier((which, sums))
    (sent,) = side_terms(
        far_side_kernel, 0, [], [jax.ShapeDtypeStruct(pair, BF16)], "weight_grads_far_side"
    )
    sent, conv_own, grad_inner, grad_outer = lax.optimization_barrier(
        (sent, conv_grad, grad_inner, grad_outer)
    )
    got = lax.ppermute(sent, "row", other_side)
    scattered = lax.all_to_all(
        sums.reshape(half, piece, wide),
        "row",
        split_axis=0,
        concat_axis=0,
        tiled=True,
        axis_index_groups=alike,
    )
    voxel_grad = pl.pallas_call(
        functools.partial(input_grad_kernel, planes, height),
        grid_spec=pltpu.PrefetchScalarGridSpec(
            num_scalar_prefetch=1,
            grid=(tiles,),
            in_specs=[
                lane_block(rows),
                lane_block(rows),
                lane_block(rows),
                lane_block(TAP_ROWS),
                lane_block(rows),
            ],
            out_specs=lane_block(rows),
            scratch_shapes=[
                spread_of(2 * MARGIN + planes),
                pltpu.VMEM((9, KS, SUB, LANES), F32),
            ],
        ),
        out_shape=jax.ShapeDtypeStruct((rows, channels), BF16),
        compiler_params=params(),
        cost_estimate=NO_COST,
        name="input_grad_conv",
    )(parity, grad_inner, conv_own, grad_outer, dw_kernel, upstream)

    scattered, voxel_grad = lax.optimization_barrier((scattered, voxel_grad))
    copies = pl.pallas_call(
        spread_sum_kernel,
        in_specs=[whole_block(half, piece, wide)],
        out_specs=whole_block(half, piece, wide),
        out_shape=jax.ShapeDtypeStruct((half, piece, wide), BF16),
        grid=(1,),
        compiler_params=params(),
        cost_estimate=NO_COST,
        name="kernel_grad_sum",
    )(scattered)
    which, copies = lax.optimization_barrier((which, copies))
    totals = lax.all_to_all(
        copies, "row", split_axis=0, concat_axis=0, tiled=True, axis_index_groups=alike
    )
    weight_in_grad, weight_out_grad = side_terms(
        near_side_kernel,
        1,
        [got],
        [jax.ShapeDtypeStruct(pair[1:], F32)] * 2,
        "weight_grads_near_side",
    )
    totals, weight_in_grad = lax.optimization_barrier((totals, weight_in_grad))
    other_totals = lax.ppermute(totals, "row", other_core)
    kernel_grad, *vector_grads = pl.pallas_call(
        unpack_kernel,
        grid_spec=pltpu.PrefetchScalarGridSpec(
            num_scalar_prefetch=1,
            grid=(1,),
            in_specs=[whole_block(half, piece, wide)] * 2,
            out_specs=[whole_block(TAP_ROWS, channels)] + [whole_block(channels)] * 3,
        ),
        out_shape=[jax.ShapeDtypeStruct((TAP_ROWS, channels), F32)]
        + [jax.ShapeDtypeStruct((channels,), F32)] * 3,
        compiler_params=params(),
        cost_estimate=NO_COST,
        name="kernel_grad_unpack",
    )(parity, totals, other_totals)

    return (
        block_out.reshape(voxels.shape),
        voxel_grad.reshape(voxels.shape),
        kernel_grad,
        *vector_grads,
        weight_in_grad,
        weight_out_grad,
    )


def solution(mesh):
    in_specs = (
        P(("group", "row"), None, None, None),
        P(),
        P(),
        P(),
        P(),
        P(),
        P(),
        P(("group", "row"), None, None, None),
    )
    out_specs = (
        P(("group", "row"), None, None, None),
        P(("group", "row"), None, None, None),
        P("group", None),
        P("group"),
        P("group"),
        P("group"),
        P(("group", "row"), None),
        P(("group", "row"), None),
    )
    return jax.shard_map(
        on_device, mesh=mesh, in_specs=in_specs, out_specs=out_specs, check_vma=False
    )
```

```python
import functools

import jax
import jax.numpy as jnp
from jax import lax
from jax.experimental import pallas as pl
from jax.experimental.pallas import tpu as pltpu
from jax.sharding import PartitionSpec as P

KS = 7
MARGIN = KS // 2
LANES = 128
SUB = 8
PAD = 3 * SUB
TAP_ROWS = KS * KS * KS

root_half = 0.7071067811865476
inv_root_tau = 0.3989422804014327
norm_eps = 1e-06
erf_step = 0.3275911
erf_terms = tuple(
    0.5 * a for a in (0.254829592, -0.284496736, 1.421413741, -1.453152027, 1.061405429)
)

NO_COST = pl.CostEstimate(flops=0, bytes_accessed=0, transcendentals=0)

F32 = jnp.float32
BF16 = jnp.bfloat16


def split_source(v):
    terms = []
    for a, b in ((v[0] + v[2], v[1] + v[3]), (v[2], v[3]), (v[0], v[1])):
        terms += [a + b, b, a]
    return terms


def split_taps(t):
    terms = []
    for s in (
        (t[2], t[3], t[4]),
        (t[4] - t[2], t[5] - t[3], t[6] - t[4]),
        (t[0] - t[2], t[1] - t[3], t[2] - t[4]),
    ):
        terms += [s[1], s[2] - s[1], s[0] - s[1]]
    return terms


def split_grads(g):
    terms = []
    for a, b in ((g[0] + g[2], g[1] + g[3]), (g[0], g[1]), (g[2], g[3])):
        terms += [a + b, a, b]
    return terms


def join_outputs(m):
    pair = [(m[3 * k] + m[3 * k + 1], m[3 * k] + m[3 * k + 2]) for k in range(3)]
    return [
        pair[0][0] + pair[1][0],
        pair[0][1] + pair[1][1],
        pair[0][0] + pair[2][0],
        pair[0][1] + pair[2][1],
    ]


def join_taps(m):
    p, q, r = [
        (m[3 * k + 2], m[3 * k] - m[3 * k + 1] - m[3 * k + 2], m[3 * k + 1]) for k in range(3)
    ]
    return [
        r[0],
        r[1],
        p[0] - q[0] - r[0] + r[2],
        p[1] - q[1] - r[1],
        p[2] - q[2] - r[2] + q[0],
        q[1],
        q[2],
    ]


def tree_sum(terms):
    while len(terms) > 1:
        terms = [
            terms[k] + terms[k + 1] if k + 1 < len(terms) else terms[k]
            for k in range(0, len(terms), 2)
        ]
    return terms[0]


def stage_source(wanted, height, spread):
    row = height * SUB
    for at, (block, x) in enumerate(wanted):
        plane = block[x * row : (x + 1) * row, :].astype(F32)
        lines = [plane[y * SUB : (y + 1) * SUB, :] for y in range(height)]
        for j, term in enumerate(split_source(lines)):
            spread[j, at, SUB : 2 * SUB, :] = term


def rim_planes(left, right, planes):
    wanted = [(left, x) for x in range(planes - MARGIN, planes)]
    return wanted + [(right, x) for x in range(MARGIN)]


def all_planes(left, own, right, planes):
    rim = rim_planes(left, right, planes)
    return rim[:MARGIN] + [(own, x) for x in range(planes)] + rim[MARGIN:]


def by_core(core, inner, outer, stage):
    @pl.when(core[0] == 0)
    def _():
        stage(outer, inner)

    @pl.when(core[0] != 0)
    def _():
        stage(inner, outer)


def clear_rims(spread):
    zeros = jnp.zeros(spread.shape[:2] + (SUB, LANES), F32)
    spread[:, :, :SUB, :] = zeros
    spread[:, :, 2 * SUB :, :] = zeros


def stage_taps(taps, split):
    for dx in range(KS):
        rows = []
        for dy in range(KS):
            first = dx * KS * KS + dy * KS
            if first + SUB <= TAP_ROWS:
                rows.append(taps[first : first + SUB, :])
            else:
                rows.append(pltpu.roll(taps[TAP_ROWS - SUB : TAP_ROWS, :], SUB - 1, 0))
        for j, term in enumerate(split_taps(rows)):
            split[j, dx] = term


REVERSED = (0, 2, 1, 6, 8, 7, 3, 5, 4)


def convolve(spread, split, planes, held, flipped):
    terms = []
    for j in range(9):
        sums = [None] * planes
        for dz in range(KS):
            first = SUB - MARGIN + dz
            source = {x: spread[j, at, first : first + SUB, :] for at, x in enumerate(held)}
            weights = []
            for dx in range(KS):
                if flipped:
                    tap = split[REVERSED[j], KS - 1 - dx, KS - 1 - dz : KS - dz, :]
                else:
                    tap = split[j, dx, dz : dz + 1, :]
                weights.append(jnp.broadcast_to(tap, (SUB, LANES)))
            for x in range(planes):
                part = tree_sum(
                    [source[x + dx] * weights[dx] for dx in range(KS) if x + dx in source]
                )
                sums[x] = part if sums[x] is None else sums[x] + part
        terms.append(sums)
    return [join_outputs([terms[j][x] for j in range(9)]) for x in range(planes)]


def own_conv_kernel(planes, height, own, taps, out, split, spread):
    @pl.when(pl.program_id(0) == 0)
    def _():
        clear_rims(spread)

    stage_source([(own, x) for x in range(planes)], height, spread)
    stage_taps(taps, split)
    rows = convolve(spread, split, planes, range(MARGIN, MARGIN + planes), False)
    for x in range(planes):
        for y in range(height):
            at = (x * height + y) * SUB
            out[at : at + SUB, :] = rows[x][y]


def rim_conv_kernel(
    planes, height, core, inner, outer, split, partial, gain, bias, normed, centered, spread, conv
):
    step = pl.program_id(0)

    @pl.when(step == 0)
    def _():
        clear_rims(spread)

    def stage(left, right):
        stage_source(rim_planes(left, right, planes), height, spread)

    by_core(core, inner, outer, stage)
    held = list(range(MARGIN)) + list(range(MARGIN + planes, 2 * MARGIN + planes))
    rows = convolve(spread, split, planes, held, False)
    for x in range(planes):
        for y in range(height):
            at = (x * height + y) * SUB
            conv[step, at : at + SUB, :] = rows[x][y] + partial[at : at + SUB, :]

    @pl.when(step == pl.num_programs(0) - 1)
    def _():
        tiles = conv.shape[0]
        channels = tiles * LANES
        parts = [conv[k] for k in range(tiles)]
        gains = gain[...].reshape(1, channels)
        biases = bias[...].reshape(1, channels)
        average = jnp.sum(tree_sum(parts), axis=1, keepdims=True) * (1.0 / channels)
        parts = [part - average for part in parts]
        variance = jnp.sum(
            tree_sum([part * part for part in parts]), axis=1, keepdims=True
        ) * (1.0 / channels)
        inverse = lax.rsqrt(variance + norm_eps)
        for k in range(tiles):
            lanes = slice(k * LANES, (k + 1) * LANES)
            centered[:, lanes] = parts[k]
            value = parts[k] * inverse
            whole = (value * gains[:, lanes] + biases[:, lanes]).astype(BF16)
            for copy in range(normed.shape[0]):
                normed[copy, :, lanes] = whole


def input_grad_kernel(
    planes, height, core, inner, own, outer, taps, cotangent, out, spread, split
):
    @pl.when(pl.program_id(0) == 0)
    def _():
        clear_rims(spread)

    def stage(left, right):
        stage_source(all_planes(left, own, right, planes), height, spread)

    by_core(core, inner, outer, stage)
    stage_taps(taps, split)
    rows = convolve(spread, split, planes, range(2 * MARGIN + planes), True)
    for x in range(planes):
        at = x * height * SUB
        whole = jnp.concatenate(rows[x], axis=0)
        upstream = cotangent[at : at + height * SUB, :].astype(F32)
        out[at : at + height * SUB, :] = (upstream + whole).astype(BF16)


def kernel_grad_kernel(
    planes, height, which, inner, own, outer, grads, small, sent, kept, spread, products, joined, flat
):
    @pl.when(pl.program_id(0) == 0)
    def _():
        clear_rims(spread)
        products[...] = jnp.zeros(products.shape, F32)
        flat[...] = jnp.zeros(flat.shape, F32)

    def stage(left, right):
        stage_source(all_planes(left, own, right, planes), height, spread)

    by_core(which, inner, outer, stage)
    upstream = []
    for x in range(planes):
        plane = grads[x * height * SUB : (x + 1) * height * SUB, :].astype(F32)
        upstream.append(
            split_grads([plane[y * SUB : (y + 1) * SUB, :] for y in range(height)])
        )
    for j in range(9):
        for dz in range(KS):
            first = SUB - MARGIN + dz
            source = [
                spread[j, x, first : first + SUB, :] for x in range(planes + KS - 1)
            ]
            for dx in range(KS):
                products[j % 2, dx, dz * SUB : (dz + 1) * SUB, :] = tree_sum(
                    [source[x + dx] * upstream[x][j] for x in range(planes)]
                )
        for dx in range(KS):
            joined[j, dx] = tree_sum(
                [products[j % 2, dx, pl.ds(s, SUB, stride=SUB), :] for s in range(SUB)]
            )
    for dx in range(KS):
        for dy, tile in enumerate(join_taps([joined[j, dx] for j in range(9)])):
            row = dx * KS * KS + dy * KS
            flat[row : row + SUB, :] = tile
    flat[TAP_ROWS : TAP_ROWS + SUB, :] = small[...]
    step = pl.program_id(0)
    half = pl.num_programs(0) // 2

    @pl.when(step < half)
    def _():
        sent[...] = flat[...].astype(BF16)

    @pl.when(step >= half)
    def _():
        kept[...] = flat[...].astype(BF16)


def mlp_kernel(
    normed, weight_in, weight_out, centered, norm_gain, layer_scale, voxels, *rest
):
    *cotangents, block_out, conv_grad, small, together, mixed, back, mixed_grad = rest
    cotangent = cotangents[0]
    step = pl.program_id(0)
    gain = norm_gain[...].reshape(1, -1)
    scale = layer_scale[...].reshape(1, -1)

    @pl.when(step == 0)
    def _():
        mixed_grad[...] = (scale * cotangent[...].astype(F32)).astype(BF16)
        for k, part in enumerate(cotangents):
            together[k] = part[...]

    across = (((1,), (1,)), ((), ()))
    hidden = lax.dot_general(normed[...], weight_in[...], across, preferred_element_type=F32)
    act_grad = lax.dot_general(
        mixed_grad[...], weight_out[...], across, preferred_element_type=F32
    )
    activated, hidden_grad = slopes(hidden, act_grad)
    forward = jnp.dot(activated, weight_out[...], preferred_element_type=F32)
    backward = jnp.dot(hidden_grad, weight_in[...], preferred_element_type=F32)

    @pl.when(step == 0)
    def _():
        mixed[...] = forward
        back[...] = backward

    @pl.when(step > 0)
    def _():
        mixed[...] += forward
        back[...] += backward

    @pl.when(step == pl.num_programs(0) - 1)
    def _():
        channels = gain.shape[1]
        whole = mixed[...]
        block_out[...] = (voxels[...].astype(F32) + scale * whole).astype(BF16)
        scale_local = jnp.sum(cotangent[...].astype(F32) * whole, axis=0, keepdims=True)
        grad = back[...]
        deviation = centered[...]
        variance = jnp.sum(deviation * deviation, axis=1, keepdims=True) * (1.0 / channels)
        inverse = lax.rsqrt(variance + norm_eps)
        one = deviation * inverse
        bias_local = jnp.sum(grad, axis=0, keepdims=True)
        gain_local = jnp.sum(grad * one, axis=0, keepdims=True)
        small[...] = jnp.concatenate(
            [gain_local, bias_local, scale_local, jnp.zeros((SUB - 3, channels), F32)], axis=0
        )
        scaled = grad * gain
        average = jnp.sum(scaled, axis=1, keepdims=True) * (1.0 / channels)
        slant = jnp.sum(scaled * one, axis=1, keepdims=True) * (1.0 / channels)
        conv_grad[...] = (inverse * (scaled - average - one * slant)).astype(BF16)


def slopes(hidden, act_grad):
    bell = jnp.exp(-0.5 * hidden * hidden)
    below = 1.0 + (erf_step * root_half) * jnp.abs(hidden)
    t = pl.reciprocal(below, approx=True)
    t = t * (2.0 - below * t)
    poly = erf_terms[-1]
    for term in erf_terms[-2::-1]:
        poly = poly * t + term
    tail = poly * t * bell
    cover = jnp.where(hidden < 0.0, tail, 1.0 - tail)
    activated = (hidden * cover).astype(BF16)
    slope = cover + hidden * bell * inv_root_tau
    return activated, (act_grad * slope).astype(BF16)


def weight_grad_terms(which, weight_in, weight_out, scale, sets, aligned, mixed_grad):
    scales = scale[...].reshape(1, -1)
    at = 0
    for normed, cotangents in sets:
        line, rows = normed.shape[:2]
        for k in range(line):
            aligned[at : at + rows, :] = normed[which[2 + k]]
            upstream = cotangents[k].astype(F32)
            mixed_grad[at : at + rows, :] = (scales * upstream).astype(BF16)
            at += rows
    across = (((1,), (1,)), ((), ()))
    hidden = lax.dot_general(weight_in[...], aligned[...], across, preferred_element_type=F32)
    act_grad = lax.dot_general(weight_out[...], mixed_grad[...], across, preferred_element_type=F32)
    activated, hidden_grad = slopes(hidden, act_grad)
    return (
        jnp.dot(hidden_grad, aligned[...], preferred_element_type=F32),
        jnp.dot(activated, mixed_grad[...], preferred_element_type=F32),
    )


def one_side_kernel(
    which, weight_in, weight_out, scale, norm, cot, other_norm, other_cot, *rest
):
    *outs, aligned, mixed_grad = rest
    sets = ((norm, cot), (other_norm, other_cot))
    terms = weight_grad_terms(which, weight_in, weight_out, scale, sets, aligned, mixed_grad)
    for k, out in enumerate(outs):
        out[...] = terms[k].astype(out.dtype)


def last_sum_kernel(in_kept, out_kept, in_got, out_got, in_grad, out_grad):
    in_grad[...] = in_kept[...] + in_got[...].astype(F32)
    out_grad[...] = out_kept[...] + out_got[...].astype(F32)


def chip_sum_kernel(kept, got, out):
    out[...] = (kept[...].astype(F32) + got[...].astype(F32)).astype(BF16)


def spread_sum_kernel(parts, out):
    total = tree_sum([parts[k].astype(F32) for k in range(parts.shape[0])]).astype(BF16)
    for copy in range(out.shape[0]):
        out[copy] = total


def unpack_kernel(core, own, other, out, *small):
    piece, wide = own.shape[1:]

    def unpack(*halves):
        last = []
        for side, parts in enumerate(halves):
            lanes = slice(side * wide, (side + 1) * wide)
            for k in range(-(-TAP_ROWS // piece)):
                first = k * piece
                length = min(piece, TAP_ROWS - first)
                out[first : first + length, lanes] = parts[k].astype(F32)[:length, :]
            k = TAP_ROWS // piece
            last.append(parts[k].astype(F32))
        rows = jnp.concatenate(last, axis=1)
        first = TAP_ROWS % piece
        for k, line in enumerate(small):
            line[...] = rows[first + k : first + k + 1, :].reshape(line.shape)

    by_core(core, own, other, lambda outer, inner: unpack(inner, outer))


def params(limit=44):
    return pltpu.CompilerParams(vmem_limit_bytes=limit * 1024 * 1024)


def lane_block(rows):
    return pl.BlockSpec((rows, LANES), lambda c, *_: (0, c))


def whole_block(*shape):
    return pl.BlockSpec(shape, lambda *_: (0,) * len(shape))


def rims(cells):
    count = lax.axis_size("row")
    between = [(i, i + 1) for i in range(1, count - 1, 2)]
    return (
        lax.ppermute(cells, "row", [(i, i ^ 1) for i in range(count)]),
        lax.ppermute(cells, "row", between + [(j, i) for i, j in between]),
    )


def on_device(
    voxels, dw_kernel, norm_gain, norm_bias, weight_in, weight_out, layer_scale, cotangent
):
    planes, height, breadth, channels = voxels.shape
    rows = planes * height * breadth
    units = weight_in.shape[0]
    count = lax.axis_size("row")
    me = lax.axis_index("row")
    quad = 4
    line = count // quad
    lines = [[quad * k + p for k in range(line)] for p in range(quad)]
    other_core = [(i, i ^ 1) for i in range(count)]
    other_side = [(i, i ^ 2) for i in range(count)]
    tiles = channels // LANES

    own = voxels.reshape(rows, channels)
    upstream = cotangent.reshape(rows, channels)
    core = lax.rem(me, 2).astype(jnp.int32)
    parity = core.reshape(1)

    inner, outer = rims(own)

    def along_line(cells, steps):
        return lax.ppermute(cells, "row", [(i, (i + quad * steps) % count) for i in range(count)])

    upstream_line = [upstream] + [None] * (line - 1)
    upstream_line[1] = along_line(upstream, 1)
    upstream_line[-1] = along_line(upstream, -1)

    def spread_of(held):
        return pltpu.VMEM((9, held, PAD, LANES), F32)

    split_block = pl.BlockSpec((None, 9, KS, SUB, LANES), lambda c, *_: (c, 0, 0, 0, 0))
    partial, split = pl.pallas_call(
        functools.partial(own_conv_kernel, planes, height),
        grid=(tiles,),
        in_specs=[lane_block(rows), lane_block(TAP_ROWS)],
        out_specs=[lane_block(rows), split_block],
        out_shape=[
            jax.ShapeDtypeStruct((rows, channels), F32),
            jax.ShapeDtypeStruct((tiles, 9, KS, SUB, LANES), F32),
        ],
        scratch_shapes=[spread_of(planes)],
        compiler_params=params(),
        cost_estimate=NO_COST,
        name="own_conv",
    )(own, dw_kernel)

    partial, upstream_line[1], upstream_line[-1] = lax.optimization_barrier(
        (partial, upstream_line[1], upstream_line[-1])
    )
    for k in range(2, line - 1):
        upstream_line[k] = along_line(upstream_line[k - 1], 1)
    normed, centered = pl.pallas_call(
        functools.partial(rim_conv_kernel, planes, height),
        grid_spec=pltpu.PrefetchScalarGridSpec(
            num_scalar_prefetch=1,
            grid=(tiles,),
            in_specs=[
                lane_block(rows),
                lane_block(rows),
                split_block,
                lane_block(rows),
                whole_block(channels),
                whole_block(channels),
            ],
            out_specs=[
                whole_block(line, rows, channels),
                whole_block(rows, channels),
            ],
            scratch_shapes=[spread_of(2 * MARGIN), pltpu.VMEM((tiles, rows, LANES), F32)],
        ),
        out_shape=[
            jax.ShapeDtypeStruct((line, rows, channels), BF16),
            jax.ShapeDtypeStruct((rows, channels), F32),
        ],
        compiler_params=params(),
        cost_estimate=NO_COST,
        name="rim_conv",
    )(parity, inner, outer, split, partial, norm_gain, norm_bias)

    normed, upstream_line[2] = lax.optimization_barrier((normed, upstream_line[2]))
    gathered = lax.all_to_all(
        normed, "row", split_axis=0, concat_axis=0, tiled=True, axis_index_groups=lines
    )

    block = 512
    whole = whole_block(rows, channels)
    block_out, conv_grad, small, cotangents = pl.pallas_call(
        mlp_kernel,
        grid=(units // block,),
        in_specs=[
            pl.BlockSpec((None, rows, channels), lambda f: (0, 0, 0)),
            pl.BlockSpec((block, channels), lambda f: (f, 0)),
            pl.BlockSpec((block, channels), lambda f: (f, 0)),
            whole,
            whole_block(channels),
            whole_block(channels),
        ]
        + [whole] * (1 + line),
        out_specs=[
            whole,
            whole,
            whole_block(SUB, channels),
            whole_block(line, rows, channels),
        ],
        out_shape=[
            jax.ShapeDtypeStruct((rows, channels), BF16),
            jax.ShapeDtypeStruct((rows, channels), BF16),
            jax.ShapeDtypeStruct((SUB, channels), F32),
            jax.ShapeDtypeStruct((line, rows, channels), BF16),
        ],
        scratch_shapes=[
            pltpu.VMEM((rows, channels), F32),
            pltpu.VMEM((rows, channels), F32),
            pltpu.VMEM((rows, channels), BF16),
        ],
        compiler_params=params(),
        cost_estimate=NO_COST,
        name="mlp_both_ways",
    )(normed, weight_in, weight_out, centered, norm_gain, layer_scale, own, *upstream_line)

    half = count // 2
    alike = [[2 * k + p for k in range(half)] for p in range(2)]
    half_tiles = tiles // 2
    wide = half_tiles * LANES
    piece = -(-(TAP_ROWS + SUB) // half)
    piece += -piece % (2 * SUB)
    padded = piece * half

    def tile_of(block_rows):
        def at(c, w):
            return 0, (c + w[1] * half_tiles) % tiles

        return pl.BlockSpec((block_rows, LANES), at)

    half_sent, half_kept = pl.pallas_call(
        functools.partial(kernel_grad_kernel, planes, height),
        grid_spec=pltpu.PrefetchScalarGridSpec(
            num_scalar_prefetch=1,
            grid=(tiles,),
            in_specs=[tile_of(rows), tile_of(rows), tile_of(rows), tile_of(rows), tile_of(SUB)],
            out_specs=[
                pl.BlockSpec((padded, LANES), lambda c, w: (0, jnp.minimum(c, half_tiles - 1))),
                pl.BlockSpec((padded, LANES), lambda c, w: (0, jnp.maximum(c - half_tiles, 0))),
            ],
            scratch_shapes=[
                spread_of(2 * MARGIN + planes),
                pltpu.VMEM((2, KS, SUB * SUB, LANES), F32),
                pltpu.VMEM((9, KS, SUB, LANES), F32),
                pltpu.VMEM((padded, LANES), F32),
            ],
        ),
        out_shape=[jax.ShapeDtypeStruct((padded, wide), BF16)] * 2,
        compiler_params=params(),
        cost_estimate=NO_COST,
        name="kernel_grad_terms",
    )(jnp.stack([core, 1 - core]), inner, own, outer, conv_grad, small)

    half_sent, conv_grad, gathered = lax.optimization_barrier((half_sent, conv_grad, gathered))
    half_got = lax.ppermute(half_sent, "row", other_core)
    grad_inner, grad_outer = rims(conv_grad)
    sums = pl.pallas_call(
        chip_sum_kernel,
        in_specs=[whole_block(padded, wide)] * 2,
        out_specs=whole_block(padded, wide),
        out_shape=jax.ShapeDtypeStruct((padded, wide), BF16),
        grid=(1,),
        compiler_params=params(),
        cost_estimate=NO_COST,
        name="kernel_grad_chip_sum",
    )(half_kept, half_got)

    share = units // count
    tokens = line * rows
    base = me // quad * quad
    side = lax.rem(me, quad) // 2
    place = lax.rem(me // quad + line - jnp.arange(line, dtype=jnp.int32), line)
    far = base + 2 * (1 - side)
    near = base + 2 * side
    which = jnp.concatenate(
        [jnp.stack([far + core, near + core]).astype(jnp.int32), place.astype(jnp.int32)]
    )
    other_gathered = lax.ppermute(gathered, "row", other_core)
    other_cotangents = lax.ppermute(cotangents, "row", other_core)
    single = (share, channels)

    def side_terms(number, dtype, name):
        chunk = pl.BlockSpec((share, channels), lambda _, w: (w[number], 0))
        return pl.pallas_call(
            one_side_kernel,
            grid_spec=pltpu.PrefetchScalarGridSpec(
                num_scalar_prefetch=1,
                grid=(1,),
                in_specs=[chunk, chunk, whole_block(channels)]
                + [whole_block(line, rows, channels)] * 4,
                out_specs=[whole_block(*single)] * 2,
                scratch_shapes=[pltpu.VMEM((2 * tokens, channels), BF16)] * 2,
            ),
            out_shape=[jax.ShapeDtypeStruct(single, dtype)] * 2,
            compiler_params=params(),
            cost_estimate=NO_COST,
            name=name,
        )(
            which,
            weight_in,
            weight_out,
            layer_scale,
            gathered,
            cotangents,
            other_gathered,
            other_cotangents,
        )

    which, sums = lax.optimization_barrier((which, sums))
    in_sent, out_sent = side_terms(0, BF16, "weight_grads_far_side")
    in_sent, conv_own, grad_inner, grad_outer = lax.optimization_barrier(
        (in_sent, conv_grad, grad_inner, grad_outer)
    )
    in_got = lax.ppermute(in_sent, "row", other_side)
    out_got = lax.ppermute(out_sent, "row", other_side)
    scattered = lax.all_to_all(
        sums.reshape(half, piece, wide),
        "row",
        split_axis=0,
        concat_axis=0,
        tiled=True,
        axis_index_groups=alike,
    )
    voxel_grad = pl.pallas_call(
        functools.partial(input_grad_kernel, planes, height),
        grid_spec=pltpu.PrefetchScalarGridSpec(
            num_scalar_prefetch=1,
            grid=(tiles,),
            in_specs=[
                lane_block(rows),
                lane_block(rows),
                lane_block(rows),
                lane_block(TAP_ROWS),
                lane_block(rows),
            ],
            out_specs=lane_block(rows),
            scratch_shapes=[
                spread_of(2 * MARGIN + planes),
                pltpu.VMEM((9, KS, SUB, LANES), F32),
            ],
        ),
        out_shape=jax.ShapeDtypeStruct((rows, channels), BF16),
        compiler_params=params(),
        cost_estimate=NO_COST,
        name="input_grad_conv",
    )(parity, grad_inner, conv_own, grad_outer, dw_kernel, upstream)

    scattered, voxel_grad = lax.optimization_barrier((scattered, voxel_grad))
    copies = pl.pallas_call(
        spread_sum_kernel,
        in_specs=[whole_block(half, piece, wide)],
        out_specs=whole_block(half, piece, wide),
        out_shape=jax.ShapeDtypeStruct((half, piece, wide), BF16),
        grid=(1,),
        compiler_params=params(),
        cost_estimate=NO_COST,
        name="kernel_grad_sum",
    )(scattered)
    which, copies = lax.optimization_barrier((which, copies))
    totals = lax.all_to_all(
        copies, "row", split_axis=0, concat_axis=0, tiled=True, axis_index_groups=alike
    )
    which, in_got = lax.optimization_barrier((which, in_got))
    in_kept, out_kept = side_terms(1, F32, "weight_grads_near_side")
    totals, in_kept = lax.optimization_barrier((totals, in_kept))
    other_totals = lax.ppermute(totals, "row", other_core)
    kernel_grad, *vector_grads = pl.pallas_call(
        unpack_kernel,
        grid_spec=pltpu.PrefetchScalarGridSpec(
            num_scalar_prefetch=1,
            grid=(1,),
            in_specs=[whole_block(half, piece, wide)] * 2,
            out_specs=[whole_block(TAP_ROWS, channels)] + [whole_block(channels)] * 3,
        ),
        out_shape=[jax.ShapeDtypeStruct((TAP_ROWS, channels), F32)]
        + [jax.ShapeDtypeStruct((channels,), F32)] * 3,
        compiler_params=params(),
        cost_estimate=NO_COST,
        name="kernel_grad_unpack",
    )(parity, totals, other_totals)

    weight_in_grad, weight_out_grad = pl.pallas_call(
        last_sum_kernel,
        grid=(1,),
        in_specs=[whole_block(*single)] * 4,
        out_specs=[whole_block(*single)] * 2,
        out_shape=[jax.ShapeDtypeStruct(single, F32)] * 2,
        compiler_params=params(),
        cost_estimate=NO_COST,
        name="weight_grads_sum",
    )(in_kept, out_kept, in_got, out_got)

    return (
        block_out.reshape(voxels.shape),
        voxel_grad.reshape(voxels.shape),
        kernel_grad,
        *vector_grads,
        weight_in_grad,
        weight_out_grad,
    )


def solution(mesh):
    in_specs = (
        P(("group", "row"), None, None, None),
        P(),
        P(),
        P(),
        P(),
        P(),
        P(),
        P(("group", "row"), None, None, None),
    )
    out_specs = (
        P(("group", "row"), None, None, None),
        P(("group", "row"), None, None, None),
        P("group", None),
        P("group"),
        P("group"),
        P("group"),
        P(("group", "row"), None),
        P(("group", "row"), None),
    )
    return jax.shard_map(
        on_device, mesh=mesh, in_specs=in_specs, out_specs=out_specs, check_vma=False
    )
```

```python
import functools

import jax
import jax.numpy as jnp
from jax import lax
from jax.experimental import pallas as pl
from jax.experimental.pallas import tpu as pltpu
from jax.sharding import PartitionSpec as P

KS = 7
MARGIN = KS // 2
LANES = 128
SUB = 8
PAD = 3 * SUB
TAP_ROWS = KS * KS * KS

root_half = 0.7071067811865476
inv_root_tau = 0.3989422804014327
norm_eps = 1e-06
erf_step = 0.3275911
erf_terms = tuple(
    0.5 * a for a in (0.254829592, -0.284496736, 1.421413741, -1.453152027, 1.061405429)
)

NO_COST = pl.CostEstimate(flops=0, bytes_accessed=0, transcendentals=0)

F32 = jnp.float32
BF16 = jnp.bfloat16


def split_source(v):
    terms = []
    for a, b in ((v[0] + v[2], v[1] + v[3]), (v[2], v[3]), (v[0], v[1])):
        terms += [a + b, b, a]
    return terms


def split_taps(t):
    terms = []
    for s in (
        (t[2], t[3], t[4]),
        (t[4] - t[2], t[5] - t[3], t[6] - t[4]),
        (t[0] - t[2], t[1] - t[3], t[2] - t[4]),
    ):
        terms += [s[1], s[2] - s[1], s[0] - s[1]]
    return terms


def split_grads(g):
    terms = []
    for a, b in ((g[0] + g[2], g[1] + g[3]), (g[0], g[1]), (g[2], g[3])):
        terms += [a + b, a, b]
    return terms


def join_outputs(m):
    pair = [(m[3 * k] + m[3 * k + 1], m[3 * k] + m[3 * k + 2]) for k in range(3)]
    return [
        pair[0][0] + pair[1][0],
        pair[0][1] + pair[1][1],
        pair[0][0] + pair[2][0],
        pair[0][1] + pair[2][1],
    ]


def join_taps(m):
    p, q, r = [
        (m[3 * k + 2], m[3 * k] - m[3 * k + 1] - m[3 * k + 2], m[3 * k + 1]) for k in range(3)
    ]
    return [
        r[0],
        r[1],
        p[0] - q[0] - r[0] + r[2],
        p[1] - q[1] - r[1],
        p[2] - q[2] - r[2] + q[0],
        q[1],
        q[2],
    ]


def tree_sum(terms):
    while len(terms) > 1:
        terms = [
            terms[k] + terms[k + 1] if k + 1 < len(terms) else terms[k]
            for k in range(0, len(terms), 2)
        ]
    return terms[0]


def stage_source(wanted, height, spread):
    row = height * SUB
    for at, (block, x) in enumerate(wanted):
        plane = block[x * row : (x + 1) * row, :].astype(F32)
        lines = [plane[y * SUB : (y + 1) * SUB, :] for y in range(height)]
        for j, term in enumerate(split_source(lines)):
            spread[j, at, SUB : 2 * SUB, :] = term


def rim_planes(left, right, planes):
    wanted = [(left, x) for x in range(planes - MARGIN, planes)]
    return wanted + [(right, x) for x in range(MARGIN)]


def all_planes(left, own, right, planes):
    rim = rim_planes(left, right, planes)
    return rim[:MARGIN] + [(own, x) for x in range(planes)] + rim[MARGIN:]


def by_core(core, inner, outer, stage):
    @pl.when(core[0] == 0)
    def _():
        stage(outer, inner)

    @pl.when(core[0] != 0)
    def _():
        stage(inner, outer)


def clear_rims(spread):
    zeros = jnp.zeros(spread.shape[:2] + (SUB, LANES), F32)
    spread[:, :, :SUB, :] = zeros
    spread[:, :, 2 * SUB :, :] = zeros


def stage_taps(taps, split):
    for dx in range(KS):
        rows = []
        for dy in range(KS):
            first = dx * KS * KS + dy * KS
            if first + SUB <= TAP_ROWS:
                rows.append(taps[first : first + SUB, :])
            else:
                rows.append(pltpu.roll(taps[TAP_ROWS - SUB : TAP_ROWS, :], SUB - 1, 0))
        for j, term in enumerate(split_taps(rows)):
            split[j, dx] = term


REVERSED = (0, 2, 1, 6, 8, 7, 3, 5, 4)


def convolve(spread, split, planes, held, flipped):
    terms = []
    for j in range(9):
        sums = [None] * planes
        for dz in range(KS):
            first = SUB - MARGIN + dz
            source = {x: spread[j, at, first : first + SUB, :] for at, x in enumerate(held)}
            weights = []
            for dx in range(KS):
                if flipped:
                    tap = split[REVERSED[j], KS - 1 - dx, KS - 1 - dz : KS - dz, :]
                else:
                    tap = split[j, dx, dz : dz + 1, :]
                weights.append(jnp.broadcast_to(tap, (SUB, LANES)))
            for x in range(planes):
                part = tree_sum(
                    [source[x + dx] * weights[dx] for dx in range(KS) if x + dx in source]
                )
                sums[x] = part if sums[x] is None else sums[x] + part
        terms.append(sums)
    return [join_outputs([terms[j][x] for j in range(9)]) for x in range(planes)]


def own_conv_kernel(planes, height, own, taps, out, split, spread):
    @pl.when(pl.program_id(0) == 0)
    def _():
        clear_rims(spread)

    stage_source([(own, x) for x in range(planes)], height, spread)
    stage_taps(taps, split)
    rows = convolve(spread, split, planes, range(MARGIN, MARGIN + planes), False)
    for x in range(planes):
        for y in range(height):
            at = (x * height + y) * SUB
            out[at : at + SUB, :] = rows[x][y]


def rim_conv_kernel(
    planes, height, core, inner, outer, split, partial, gain, bias, normed, centered, spread, conv
):
    step = pl.program_id(0)

    @pl.when(step == 0)
    def _():
        clear_rims(spread)

    def stage(left, right):
        stage_source(rim_planes(left, right, planes), height, spread)

    by_core(core, inner, outer, stage)
    held = list(range(MARGIN)) + list(range(MARGIN + planes, 2 * MARGIN + planes))
    rows = convolve(spread, split, planes, held, False)
    for x in range(planes):
        for y in range(height):
            at = (x * height + y) * SUB
            conv[step, at : at + SUB, :] = rows[x][y] + partial[at : at + SUB, :]

    @pl.when(step == pl.num_programs(0) - 1)
    def _():
        tiles = conv.shape[0]
        channels = tiles * LANES
        parts = [conv[k] for k in range(tiles)]
        gains = gain[...].reshape(1, channels)
        biases = bias[...].reshape(1, channels)
        average = jnp.sum(tree_sum(parts), axis=1, keepdims=True) * (1.0 / channels)
        parts = [part - average for part in parts]
        variance = jnp.sum(
            tree_sum([part * part for part in parts]), axis=1, keepdims=True
        ) * (1.0 / channels)
        inverse = lax.rsqrt(variance + norm_eps)
        for k in range(tiles):
            lanes = slice(k * LANES, (k + 1) * LANES)
            centered[:, lanes] = parts[k]
            value = parts[k] * inverse
            whole = (value * gains[:, lanes] + biases[:, lanes]).astype(BF16)
            for copy in range(normed.shape[0]):
                normed[copy, :, lanes] = whole


def input_grad_kernel(
    planes, height, core, inner, own, outer, taps, cotangent, out, token, spread, split
):
    @pl.when(pl.program_id(0) == 0)
    def _():
        clear_rims(spread)

    def stage(left, right):
        stage_source(all_planes(left, own, right, planes), height, spread)

    by_core(core, inner, outer, stage)
    stage_taps(taps, split)
    token[...] = jnp.zeros(token.shape, F32)
    rows = convolve(spread, split, planes, range(2 * MARGIN + planes), True)
    for x in range(planes):
        at = x * height * SUB
        whole = jnp.concatenate(rows[x], axis=0)
        upstream = cotangent[at : at + height * SUB, :].astype(F32)
        out[at : at + height * SUB, :] = (upstream + whole).astype(BF16)


def kernel_grad_kernel(
    planes,
    height,
    which,
    inner,
    own,
    outer,
    grads,
    small,
    sent,
    kept,
    passed,
    token,
    spread,
    products,
    joined,
    flat,
):
    passed[...] = grads[...]
    token[...] = jnp.zeros(token.shape, F32)

    @pl.when(pl.program_id(0) == 0)
    def _():
        clear_rims(spread)
        products[...] = jnp.zeros(products.shape, F32)
        flat[...] = jnp.zeros(flat.shape, F32)

    def stage(left, right):
        stage_source(all_planes(left, own, right, planes), height, spread)

    by_core(which, inner, outer, stage)
    upstream = []
    for x in range(planes):
        plane = grads[x * height * SUB : (x + 1) * height * SUB, :].astype(F32)
        upstream.append(
            split_grads([plane[y * SUB : (y + 1) * SUB, :] for y in range(height)])
        )
    for j in range(9):
        for dz in range(KS):
            first = SUB - MARGIN + dz
            source = [
                spread[j, x, first : first + SUB, :] for x in range(planes + KS - 1)
            ]
            for dx in range(KS):
                products[j % 2, dx, dz * SUB : (dz + 1) * SUB, :] = tree_sum(
                    [source[x + dx] * upstream[x][j] for x in range(planes)]
                )
        for dx in range(KS):
            joined[j, dx] = tree_sum(
                [products[j % 2, dx, pl.ds(s, SUB, stride=SUB), :] for s in range(SUB)]
            )
    for dx in range(KS):
        for dy, tile in enumerate(join_taps([joined[j, dx] for j in range(9)])):
            row = dx * KS * KS + dy * KS
            flat[row : row + SUB, :] = tile
    flat[TAP_ROWS : TAP_ROWS + SUB, :] = small[...]
    step = pl.program_id(0)
    half = pl.num_programs(0) // 2

    @pl.when(step < half)
    def _():
        sent[...] = flat[...].astype(BF16)

    @pl.when(step >= half)
    def _():
        kept[...] = flat[...].astype(BF16)


def mlp_kernel(
    normed, weight_in, weight_out, centered, norm_gain, layer_scale, voxels, *rest
):
    *cotangents, block_out, conv_grad, small, together, mixed, back, mixed_grad = rest
    cotangent = cotangents[0]
    step = pl.program_id(0)
    gain = norm_gain[...].reshape(1, -1)
    scale = layer_scale[...].reshape(1, -1)

    @pl.when(step == 0)
    def _():
        mixed_grad[...] = (scale * cotangent[...].astype(F32)).astype(BF16)
        for k, part in enumerate(cotangents):
            together[k] = part[...]

    across = (((1,), (1,)), ((), ()))
    hidden = lax.dot_general(normed[...], weight_in[...], across, preferred_element_type=F32)
    act_grad = lax.dot_general(
        mixed_grad[...], weight_out[...], across, preferred_element_type=F32
    )
    activated, hidden_grad = slopes(hidden, act_grad)
    forward = jnp.dot(activated, weight_out[...], preferred_element_type=F32)
    backward = jnp.dot(hidden_grad, weight_in[...], preferred_element_type=F32)

    @pl.when(step == 0)
    def _():
        mixed[...] = forward
        back[...] = backward

    @pl.when(step > 0)
    def _():
        mixed[...] += forward
        back[...] += backward

    @pl.when(step == pl.num_programs(0) - 1)
    def _():
        channels = gain.shape[1]
        whole = mixed[...]
        block_out[...] = (voxels[...].astype(F32) + scale * whole).astype(BF16)
        scale_local = jnp.sum(cotangent[...].astype(F32) * whole, axis=0, keepdims=True)
        grad = back[...]
        deviation = centered[...]
        variance = jnp.sum(deviation * deviation, axis=1, keepdims=True) * (1.0 / channels)
        inverse = lax.rsqrt(variance + norm_eps)
        one = deviation * inverse
        bias_local = jnp.sum(grad, axis=0, keepdims=True)
        gain_local = jnp.sum(grad * one, axis=0, keepdims=True)
        small[...] = jnp.concatenate(
            [gain_local, bias_local, scale_local, jnp.zeros((SUB - 3, channels), F32)], axis=0
        )
        scaled = grad * gain
        average = jnp.sum(scaled, axis=1, keepdims=True) * (1.0 / channels)
        slant = jnp.sum(scaled * one, axis=1, keepdims=True) * (1.0 / channels)
        conv_grad[...] = (inverse * (scaled - average - one * slant)).astype(BF16)


def slopes(hidden, act_grad):
    bell = jnp.exp(-0.5 * hidden * hidden)
    below = 1.0 + (erf_step * root_half) * jnp.abs(hidden)
    t = pl.reciprocal(below, approx=True)
    t = t * (2.0 - below * t)
    poly = erf_terms[-1]
    for term in erf_terms[-2::-1]:
        poly = poly * t + term
    tail = poly * t * bell
    cover = jnp.where(hidden < 0.0, tail, 1.0 - tail)
    activated = (hidden * cover).astype(BF16)
    slope = cover + hidden * bell * inv_root_tau
    return activated, (act_grad * slope).astype(BF16)


def weight_grad_terms(which, weight_in, weight_out, scale, sets, aligned, mixed_grad):
    scales = scale[...].reshape(1, -1)
    at = 0
    for normed, cotangents in sets:
        line, rows = normed.shape[:2]
        for k in range(line):
            aligned[at : at + rows, :] = normed[which[2 + k]]
            upstream = cotangents[k].astype(F32)
            mixed_grad[at : at + rows, :] = (scales * upstream).astype(BF16)
            at += rows
    across = (((1,), (1,)), ((), ()))
    hidden = lax.dot_general(weight_in[...], aligned[...], across, preferred_element_type=F32)
    act_grad = lax.dot_general(weight_out[...], mixed_grad[...], across, preferred_element_type=F32)
    activated, hidden_grad = slopes(hidden, act_grad)
    return (
        jnp.dot(hidden_grad, aligned[...], preferred_element_type=F32),
        jnp.dot(activated, mixed_grad[...], preferred_element_type=F32),
    )


def one_side_kernel(
    which, weight_in, weight_out, scale, norm, cot, other_norm, other_cot, *rest
):
    in_out, out_out, *token, aligned, mixed_grad = rest
    sets = ((norm, cot), (other_norm, other_cot))
    terms = weight_grad_terms(which, weight_in, weight_out, scale, sets, aligned, mixed_grad)
    in_out[...] = terms[0].astype(in_out.dtype)
    out_out[...] = terms[1].astype(out_out.dtype)
    for line in token:
        line[...] = jnp.zeros(line.shape, F32)


def last_sum_kernel(in_kept, out_kept, in_got, out_got, in_grad, out_grad):
    in_grad[...] = in_kept[...] + in_got[...].astype(F32)
    out_grad[...] = out_kept[...] + out_got[...].astype(F32)


def chip_sum_kernel(kept, got, out):
    out[...] = (kept[...].astype(F32) + got[...].astype(F32)).astype(BF16)


def spread_sum_kernel(parts, out):
    total = tree_sum([parts[k].astype(F32) for k in range(parts.shape[0])]).astype(BF16)
    for copy in range(out.shape[0]):
        out[copy] = total


def unpack_kernel(core, own, other, out, *small):
    piece, wide = own.shape[1:]

    def unpack(*halves):
        last = []
        for side, parts in enumerate(halves):
            lanes = slice(side * wide, (side + 1) * wide)
            for k in range(-(-TAP_ROWS // piece)):
                first = k * piece
                length = min(piece, TAP_ROWS - first)
                out[first : first + length, lanes] = parts[k].astype(F32)[:length, :]
            k = TAP_ROWS // piece
            last.append(parts[k].astype(F32))
        rows = jnp.concatenate(last, axis=1)
        first = TAP_ROWS % piece
        for k, line in enumerate(small):
            line[...] = rows[first + k : first + k + 1, :].reshape(line.shape)

    by_core(core, own, other, lambda outer, inner: unpack(inner, outer))


def params(limit=48):
    return pltpu.CompilerParams(vmem_limit_bytes=limit * 1024 * 1024)


def follow(kernel, scalars, inputs, count):
    def body(*refs):
        head = refs[: scalars + inputs]
        return kernel(*head, *refs[scalars + inputs + count :])

    return body


IN_PLACE = pl.BlockSpec(memory_space=pl.ANY)


def lane_block(rows):
    return pl.BlockSpec((rows, LANES), lambda c, *_: (0, c))


def whole_block(*shape):
    return pl.BlockSpec(shape, lambda *_: (0,) * len(shape))


def rims(cells):
    count = lax.axis_size("row")
    between = [(i, i + 1) for i in range(1, count - 1, 2)]
    return (
        lax.ppermute(cells, "row", [(i, i ^ 1) for i in range(count)]),
        lax.ppermute(cells, "row", between + [(j, i) for i, j in between]),
    )


def on_device(
    voxels, dw_kernel, norm_gain, norm_bias, weight_in, weight_out, layer_scale, cotangent
):
    planes, height, breadth, channels = voxels.shape
    rows = planes * height * breadth
    units = weight_in.shape[0]
    count = lax.axis_size("row")
    me = lax.axis_index("row")
    quad = 4
    line = count // quad
    lines = [[quad * k + p for k in range(line)] for p in range(quad)]
    other_core = [(i, i ^ 1) for i in range(count)]
    other_side = [(i, i ^ 2) for i in range(count)]
    tiles = channels // LANES

    own = voxels.reshape(rows, channels)
    upstream = cotangent.reshape(rows, channels)
    core = lax.rem(me, 2).astype(jnp.int32)
    parity = core.reshape(1)

    inner, outer = rims(own)

    def along_line(cells, steps):
        return lax.ppermute(cells, "row", [(i, (i + quad * steps) % count) for i in range(count)])

    upstream_line = [upstream] + [None] * (line - 1)
    upstream_line[1] = along_line(upstream, 1)
    upstream_line[-1] = along_line(upstream, -1)

    def spread_of(held):
        return pltpu.VMEM((9, held, PAD, LANES), F32)

    split_block = pl.BlockSpec((None, 9, KS, SUB, LANES), lambda c, *_: (c, 0, 0, 0, 0))
    partial, split = pl.pallas_call(
        functools.partial(own_conv_kernel, planes, height),
        grid=(tiles,),
        in_specs=[lane_block(rows), lane_block(TAP_ROWS)],
        out_specs=[lane_block(rows), split_block],
        out_shape=[
            jax.ShapeDtypeStruct((rows, channels), F32),
            jax.ShapeDtypeStruct((tiles, 9, KS, SUB, LANES), F32),
        ],
        scratch_shapes=[spread_of(planes)],
        compiler_params=params(),
        cost_estimate=NO_COST,
        name="own_conv",
    )(own, dw_kernel)

    for k in range(2, line - 1):
        upstream_line[k] = along_line(upstream_line[k - 1], 1)
    normed, centered = pl.pallas_call(
        follow(functools.partial(rim_conv_kernel, planes, height), 1, 6, 2),
        grid_spec=pltpu.PrefetchScalarGridSpec(
            num_scalar_prefetch=1,
            grid=(tiles,),
            in_specs=[
                lane_block(rows),
                lane_block(rows),
                split_block,
                lane_block(rows),
                whole_block(channels),
                whole_block(channels),
                IN_PLACE,
                IN_PLACE,
            ],
            out_specs=[
                whole_block(line, rows, channels),
                whole_block(rows, channels),
            ],
            scratch_shapes=[spread_of(2 * MARGIN), pltpu.VMEM((tiles, rows, LANES), F32)],
        ),
        out_shape=[
            jax.ShapeDtypeStruct((line, rows, channels), BF16),
            jax.ShapeDtypeStruct((rows, channels), F32),
        ],
        compiler_params=params(),
        cost_estimate=NO_COST,
        name="rim_conv",
    )(
        parity,
        inner,
        outer,
        split,
        partial,
        norm_gain,
        norm_bias,
        upstream_line[1],
        upstream_line[-1],
    )

    normed, upstream_line[2] = lax.optimization_barrier((normed, upstream_line[2]))
    gathered = lax.all_to_all(
        normed, "row", split_axis=0, concat_axis=0, tiled=True, axis_index_groups=lines
    )

    block = 512
    whole = whole_block(rows, channels)
    block_out, conv_grad, small, cotangents = pl.pallas_call(
        mlp_kernel,
        grid=(units // block,),
        in_specs=[
            pl.BlockSpec((None, rows, channels), lambda f: (0, 0, 0)),
            pl.BlockSpec((block, channels), lambda f: (f, 0)),
            pl.BlockSpec((block, channels), lambda f: (f, 0)),
            whole,
            whole_block(channels),
            whole_block(channels),
        ]
        + [whole] * (1 + line),
        out_specs=[
            whole,
            whole,
            whole_block(SUB, channels),
            whole_block(line, rows, channels),
        ],
        out_shape=[
            jax.ShapeDtypeStruct((rows, channels), BF16),
            jax.ShapeDtypeStruct((rows, channels), BF16),
            jax.ShapeDtypeStruct((SUB, channels), F32),
            jax.ShapeDtypeStruct((line, rows, channels), BF16),
        ],
        scratch_shapes=[
            pltpu.VMEM((rows, channels), F32),
            pltpu.VMEM((rows, channels), F32),
            pltpu.VMEM((rows, channels), BF16),
        ],
        compiler_params=params(),
        cost_estimate=NO_COST,
        name="mlp_both_ways",
    )(normed, weight_in, weight_out, centered, norm_gain, layer_scale, own, *upstream_line)

    half = count // 2
    alike = [[2 * k + p for k in range(half)] for p in range(2)]
    half_tiles = tiles // 2
    wide = half_tiles * LANES
    piece = -(-(TAP_ROWS + SUB) // half)
    piece += -piece % (2 * SUB)
    padded = piece * half

    def tile_of(block_rows):
        def at(c, w):
            return 0, (c + w[1] * half_tiles) % tiles

        return pl.BlockSpec((block_rows, LANES), at)

    half_sent, half_kept, conv_grad, token = pl.pallas_call(
        functools.partial(kernel_grad_kernel, planes, height),
        grid_spec=pltpu.PrefetchScalarGridSpec(
            num_scalar_prefetch=1,
            grid=(tiles,),
            in_specs=[tile_of(rows), tile_of(rows), tile_of(rows), tile_of(rows), tile_of(SUB)],
            out_specs=[
                pl.BlockSpec((padded, LANES), lambda c, w: (0, jnp.minimum(c, half_tiles - 1))),
                pl.BlockSpec((padded, LANES), lambda c, w: (0, jnp.maximum(c - half_tiles, 0))),
                tile_of(rows),
                whole_block(SUB, LANES),
            ],
            scratch_shapes=[
                spread_of(2 * MARGIN + planes),
                pltpu.VMEM((2, KS, SUB * SUB, LANES), F32),
                pltpu.VMEM((9, KS, SUB, LANES), F32),
                pltpu.VMEM((padded, LANES), F32),
            ],
        ),
        out_shape=[jax.ShapeDtypeStruct((padded, wide), BF16)] * 2
        + [
            jax.ShapeDtypeStruct((rows, channels), BF16),
            jax.ShapeDtypeStruct((SUB, LANES), F32),
        ],
        compiler_params=params(),
        cost_estimate=NO_COST,
        name="kernel_grad_terms",
    )(jnp.stack([core, 1 - core]), inner, own, outer, conv_grad, small)

    half_got = lax.ppermute(half_sent, "row", other_core)
    gathered, token = lax.optimization_barrier((gathered, token))
    grad_inner, grad_outer = rims(conv_grad)
    sums = pl.pallas_call(
        follow(chip_sum_kernel, 0, 2, 1),
        in_specs=[whole_block(padded, wide)] * 2 + [IN_PLACE],
        out_specs=whole_block(padded, wide),
        out_shape=jax.ShapeDtypeStruct((padded, wide), BF16),
        grid=(1,),
        compiler_params=params(),
        cost_estimate=NO_COST,
        name="kernel_grad_chip_sum",
    )(half_kept, half_got, token)

    share = units // count
    tokens = line * rows
    base = me // quad * quad
    side = lax.rem(me, quad) // 2
    place = lax.rem(me // quad + line - jnp.arange(line, dtype=jnp.int32), line)
    far = base + 2 * (1 - side)
    near = base + 2 * side
    which = jnp.concatenate(
        [jnp.stack([far + core, near + core]).astype(jnp.int32), place.astype(jnp.int32)]
    )
    other_gathered = lax.ppermute(gathered, "row", other_core)
    other_cotangents = lax.ppermute(cotangents, "row", other_core)
    single = (share, channels)

    def side_terms(number, dtype, after, token, name):
        chunk = pl.BlockSpec((share, channels), lambda _, w: (w[number], 0))
        return pl.pallas_call(
            follow(one_side_kernel, 1, 7, 1),
            grid_spec=pltpu.PrefetchScalarGridSpec(
                num_scalar_prefetch=1,
                grid=(1,),
                in_specs=[chunk, chunk, whole_block(channels)]
                + [whole_block(line, rows, channels)] * 4
                + [IN_PLACE],
                out_specs=[whole_block(*single)] * 2 + [whole_block(SUB, LANES)] * token,
                scratch_shapes=[pltpu.VMEM((2 * tokens, channels), BF16)] * 2,
            ),
            out_shape=[jax.ShapeDtypeStruct(single, dtype)] * 2
            + [jax.ShapeDtypeStruct((SUB, LANES), F32)] * token,
            compiler_params=params(),
            cost_estimate=NO_COST,
            name=name,
        )(
            which,
            weight_in,
            weight_out,
            layer_scale,
            gathered,
            cotangents,
            other_gathered,
            other_cotangents,
            after,
        )

    in_sent, out_sent = side_terms(0, BF16, sums, 0, "weight_grads_far_side")
    in_got = lax.ppermute(in_sent, "row", other_side)
    out_got = lax.ppermute(out_sent, "row", other_side)
    scattered = lax.all_to_all(
        sums.reshape(half, piece, wide),
        "row",
        split_axis=0,
        concat_axis=0,
        tiled=True,
        axis_index_groups=alike,
    )
    voxel_grad, token = pl.pallas_call(
        follow(functools.partial(input_grad_kernel, planes, height), 1, 5, 1),
        grid_spec=pltpu.PrefetchScalarGridSpec(
            num_scalar_prefetch=1,
            grid=(tiles,),
            in_specs=[
                lane_block(rows),
                lane_block(rows),
                lane_block(rows),
                lane_block(TAP_ROWS),
                lane_block(rows),
                IN_PLACE,
            ],
            out_specs=[lane_block(rows), whole_block(SUB, LANES)],
            scratch_shapes=[
                spread_of(2 * MARGIN + planes),
                pltpu.VMEM((9, KS, SUB, LANES), F32),
            ],
        ),
        out_shape=[
            jax.ShapeDtypeStruct((rows, channels), BF16),
            jax.ShapeDtypeStruct((SUB, LANES), F32),
        ],
        compiler_params=params(),
        cost_estimate=NO_COST,
        name="input_grad_conv",
    )(parity, grad_inner, conv_grad, grad_outer, dw_kernel, upstream, in_sent)

    copies = pl.pallas_call(
        follow(spread_sum_kernel, 0, 1, 2),
        in_specs=[whole_block(half, piece, wide), IN_PLACE, IN_PLACE],
        out_specs=whole_block(half, piece, wide),
        out_shape=jax.ShapeDtypeStruct((half, piece, wide), BF16),
        grid=(1,),
        compiler_params=params(),
        cost_estimate=NO_COST,
        name="kernel_grad_sum",
    )(scattered, token, in_got)
    totals = lax.all_to_all(
        copies, "row", split_axis=0, concat_axis=0, tiled=True, axis_index_groups=alike
    )
    in_kept, out_kept, token = side_terms(1, F32, copies, 1, "weight_grads_near_side")
    totals, token = lax.optimization_barrier((totals, token))
    other_totals = lax.ppermute(totals, "row", other_core)
    kernel_grad, *vector_grads = pl.pallas_call(
        follow(unpack_kernel, 1, 2, 1),
        grid_spec=pltpu.PrefetchScalarGridSpec(
            num_scalar_prefetch=1,
            grid=(1,),
            in_specs=[whole_block(half, piece, wide)] * 2 + [IN_PLACE],
            out_specs=[whole_block(TAP_ROWS, channels)] + [whole_block(channels)] * 3,
        ),
        out_shape=[jax.ShapeDtypeStruct((TAP_ROWS, channels), F32)]
        + [jax.ShapeDtypeStruct((channels,), F32)] * 3,
        compiler_params=params(),
        cost_estimate=NO_COST,
        name="kernel_grad_unpack",
    )(parity, totals, other_totals, token)

    weight_in_grad, weight_out_grad = pl.pallas_call(
        last_sum_kernel,
        grid=(1,),
        in_specs=[whole_block(*single)] * 4,
        out_specs=[whole_block(*single)] * 2,
        out_shape=[jax.ShapeDtypeStruct(single, F32)] * 2,
        compiler_params=params(),
        cost_estimate=NO_COST,
        name="weight_grads_sum",
    )(in_kept, out_kept, in_got, out_got)

    return (
        block_out.reshape(voxels.shape),
        voxel_grad.reshape(voxels.shape),
        kernel_grad,
        *vector_grads,
        weight_in_grad,
        weight_out_grad,
    )


def solution(mesh):
    in_specs = (
        P(("group", "row"), None, None, None),
        P(),
        P(),
        P(),
        P(),
        P(),
        P(),
        P(("group", "row"), None, None, None),
    )
    out_specs = (
        P(("group", "row"), None, None, None),
        P(("group", "row"), None, None, None),
        P("group", None),
        P("group"),
        P("group"),
        P("group"),
        P(("group", "row"), None),
        P(("group", "row"), None),
    )
    return jax.shard_map(
        on_device, mesh=mesh, in_specs=in_specs, out_specs=out_specs, check_vma=False
    )
```

```python
import functools

import jax
import jax.numpy as jnp
from jax import lax
from jax.experimental import pallas as pl
from jax.experimental.pallas import tpu as pltpu
from jax.sharding import PartitionSpec as P

KS = 7
MARGIN = KS // 2
LANES = 128
SUB = 8
PAD = 3 * SUB
TAP_ROWS = KS * KS * KS

root_half = 0.7071067811865476
inv_root_tau = 0.3989422804014327
norm_eps = 1e-06
erf_step = 0.3275911
erf_terms = tuple(
    0.5 * a for a in (0.254829592, -0.284496736, 1.421413741, -1.453152027, 1.061405429)
)

NO_COST = pl.CostEstimate(flops=0, bytes_accessed=0, transcendentals=0)

F32 = jnp.float32
BF16 = jnp.bfloat16


def split_source(v):
    terms = []
    for a, b in ((v[0] + v[2], v[1] + v[3]), (v[2], v[3]), (v[0], v[1])):
        terms += [a + b, b, a]
    return terms


def split_taps(t):
    terms = []
    for s in (
        (t[2], t[3], t[4]),
        (t[4] - t[2], t[5] - t[3], t[6] - t[4]),
        (t[0] - t[2], t[1] - t[3], t[2] - t[4]),
    ):
        terms += [s[1], s[2] - s[1], s[0] - s[1]]
    return terms


def split_grads(g):
    terms = []
    for a, b in ((g[0] + g[2], g[1] + g[3]), (g[0], g[1]), (g[2], g[3])):
        terms += [a + b, a, b]
    return terms


def join_outputs(m):
    pair = [(m[3 * k] + m[3 * k + 1], m[3 * k] + m[3 * k + 2]) for k in range(3)]
    return [
        pair[0][0] + pair[1][0],
        pair[0][1] + pair[1][1],
        pair[0][0] + pair[2][0],
        pair[0][1] + pair[2][1],
    ]


def join_taps(m):
    p, q, r = [
        (m[3 * k + 2], m[3 * k] - m[3 * k + 1] - m[3 * k + 2], m[3 * k + 1]) for k in range(3)
    ]
    return [
        r[0],
        r[1],
        p[0] - q[0] - r[0] + r[2],
        p[1] - q[1] - r[1],
        p[2] - q[2] - r[2] + q[0],
        q[1],
        q[2],
    ]


def tree_sum(terms):
    while len(terms) > 1:
        terms = [
            terms[k] + terms[k + 1] if k + 1 < len(terms) else terms[k]
            for k in range(0, len(terms), 2)
        ]
    return terms[0]


def stage_source(wanted, height, spread):
    row = height * SUB
    for at, (block, x) in enumerate(wanted):
        plane = block[x * row : (x + 1) * row, :].astype(F32)
        lines = [plane[y * SUB : (y + 1) * SUB, :] for y in range(height)]
        for j, term in enumerate(split_source(lines)):
            spread[j, at, SUB : 2 * SUB, :] = term


def rim_planes(left, right, planes):
    wanted = [(left, x) for x in range(planes - MARGIN, planes)]
    return wanted + [(right, x) for x in range(MARGIN)]


def all_planes(left, own, right, planes):
    rim = rim_planes(left, right, planes)
    return rim[:MARGIN] + [(own, x) for x in range(planes)] + rim[MARGIN:]


def by_core(core, inner, outer, stage):
    @pl.when(core[0] == 0)
    def _():
        stage(outer, inner)

    @pl.when(core[0] != 0)
    def _():
        stage(inner, outer)


def clear_rims(spread):
    zeros = jnp.zeros(spread.shape[:2] + (SUB, LANES), F32)
    spread[:, :, :SUB, :] = zeros
    spread[:, :, 2 * SUB :, :] = zeros


def stage_taps(taps, split):
    for dx in range(KS):
        rows = []
        for dy in range(KS):
            first = dx * KS * KS + dy * KS
            if first + SUB <= TAP_ROWS:
                rows.append(taps[first : first + SUB, :])
            else:
                rows.append(pltpu.roll(taps[TAP_ROWS - SUB : TAP_ROWS, :], SUB - 1, 0))
        for j, term in enumerate(split_taps(rows)):
            split[j, dx] = term


REVERSED = (0, 2, 1, 6, 8, 7, 3, 5, 4)


def convolve(spread, split, planes, held, flipped):
    terms = []
    for j in range(9):
        sums = [None] * planes
        for dz in range(KS):
            first = SUB - MARGIN + dz
            source = {x: spread[j, at, first : first + SUB, :] for at, x in enumerate(held)}
            weights = []
            for dx in range(KS):
                if flipped:
                    tap = split[REVERSED[j], KS - 1 - dx, KS - 1 - dz : KS - dz, :]
                else:
                    tap = split[j, dx, dz : dz + 1, :]
                weights.append(jnp.broadcast_to(tap, (SUB, LANES)))
            for x in range(planes):
                part = tree_sum(
                    [source[x + dx] * weights[dx] for dx in range(KS) if x + dx in source]
                )
                sums[x] = part if sums[x] is None else sums[x] + part
        terms.append(sums)
    return [join_outputs([terms[j][x] for j in range(9)]) for x in range(planes)]


def own_conv_kernel(planes, height, own, taps, out, split, spread):
    @pl.when(pl.program_id(0) == 0)
    def _():
        clear_rims(spread)

    stage_source([(own, x) for x in range(planes)], height, spread)
    stage_taps(taps, split)
    rows = convolve(spread, split, planes, range(MARGIN, MARGIN + planes), False)
    for x in range(planes):
        for y in range(height):
            at = (x * height + y) * SUB
            out[at : at + SUB, :] = rows[x][y]


def rim_conv_kernel(
    planes, height, core, inner, outer, split, partial, gain, bias, normed, centered, spread, conv
):
    step = pl.program_id(0)

    @pl.when(step == 0)
    def _():
        clear_rims(spread)

    def stage(left, right):
        stage_source(rim_planes(left, right, planes), height, spread)

    by_core(core, inner, outer, stage)
    held = list(range(MARGIN)) + list(range(MARGIN + planes, 2 * MARGIN + planes))
    rows = convolve(spread, split, planes, held, False)
    for x in range(planes):
        for y in range(height):
            at = (x * height + y) * SUB
            conv[step, at : at + SUB, :] = rows[x][y] + partial[at : at + SUB, :]

    @pl.when(step == pl.num_programs(0) - 1)
    def _():
        tiles = conv.shape[0]
        channels = tiles * LANES
        parts = [conv[k] for k in range(tiles)]
        gains = gain[...].reshape(1, channels)
        biases = bias[...].reshape(1, channels)
        average = jnp.sum(tree_sum(parts), axis=1, keepdims=True) * (1.0 / channels)
        parts = [part - average for part in parts]
        variance = jnp.sum(
            tree_sum([part * part for part in parts]), axis=1, keepdims=True
        ) * (1.0 / channels)
        inverse = lax.rsqrt(variance + norm_eps)
        for k in range(tiles):
            lanes = slice(k * LANES, (k + 1) * LANES)
            centered[:, lanes] = parts[k]
            value = parts[k] * inverse
            whole = (value * gains[:, lanes] + biases[:, lanes]).astype(BF16)
            for copy in range(normed.shape[0]):
                normed[copy, :, lanes] = whole


def input_grad_kernel(
    planes, height, core, inner, own, outer, taps, cotangent, out, token, spread, split
):
    @pl.when(pl.program_id(0) == 0)
    def _():
        clear_rims(spread)

    def stage(left, right):
        stage_source(all_planes(left, own, right, planes), height, spread)

    by_core(core, inner, outer, stage)
    stage_taps(taps, split)
    token[...] = jnp.zeros(token.shape, F32)
    rows = convolve(spread, split, planes, range(2 * MARGIN + planes), True)
    for x in range(planes):
        at = x * height * SUB
        whole = jnp.concatenate(rows[x], axis=0)
        upstream = cotangent[at : at + height * SUB, :].astype(F32)
        out[at : at + height * SUB, :] = (upstream + whole).astype(BF16)


def kernel_grad_kernel(
    planes,
    height,
    which,
    inner,
    own,
    outer,
    grads,
    small,
    sent,
    kept,
    passed,
    token,
    spread,
    products,
    joined,
    flat,
):
    passed[...] = grads[...]
    token[...] = jnp.zeros(token.shape, F32)

    @pl.when(pl.program_id(0) == 0)
    def _():
        clear_rims(spread)
        products[...] = jnp.zeros(products.shape, F32)
        flat[...] = jnp.zeros(flat.shape, F32)

    def stage(left, right):
        stage_source(all_planes(left, own, right, planes), height, spread)

    by_core(which, inner, outer, stage)
    upstream = []
    for x in range(planes):
        plane = grads[x * height * SUB : (x + 1) * height * SUB, :].astype(F32)
        upstream.append(
            split_grads([plane[y * SUB : (y + 1) * SUB, :] for y in range(height)])
        )
    for j in range(9):
        for dz in range(KS):
            first = SUB - MARGIN + dz
            source = [
                spread[j, x, first : first + SUB, :] for x in range(planes + KS - 1)
            ]
            for dx in range(KS):
                products[j % 2, dx, dz * SUB : (dz + 1) * SUB, :] = tree_sum(
                    [source[x + dx] * upstream[x][j] for x in range(planes)]
                )
        for dx in range(KS):
            joined[j, dx] = tree_sum(
                [products[j % 2, dx, pl.ds(s, SUB, stride=SUB), :] for s in range(SUB)]
            )
    for dx in range(KS):
        for dy, tile in enumerate(join_taps([joined[j, dx] for j in range(9)])):
            row = dx * KS * KS + dy * KS
            flat[row : row + SUB, :] = tile
    flat[TAP_ROWS : TAP_ROWS + SUB, :] = small[...]
    step = pl.program_id(0)
    half = pl.num_programs(0) // 2

    @pl.when(step < half)
    def _():
        sent[...] = flat[...].astype(BF16)

    @pl.when(step >= half)
    def _():
        kept[...] = flat[...].astype(BF16)


def mlp_kernel(
    normed, weight_in, weight_out, centered, norm_gain, layer_scale, voxels, *rest
):
    *cotangents, block_out, conv_grad, small, together, mixed, back, mixed_grad = rest
    cotangent = cotangents[0]
    step = pl.program_id(0)
    gain = norm_gain[...].reshape(1, -1)
    scale = layer_scale[...].reshape(1, -1)

    @pl.when(step == 0)
    def _():
        mixed_grad[...] = (scale * cotangent[...].astype(F32)).astype(BF16)
        for k, part in enumerate(cotangents):
            together[k] = part[...]

    across = (((1,), (1,)), ((), ()))
    hidden = lax.dot_general(normed[...], weight_in[...], across, preferred_element_type=F32)
    act_grad = lax.dot_general(
        mixed_grad[...], weight_out[...], across, preferred_element_type=F32
    )
    activated, hidden_grad = slopes(hidden, act_grad)
    forward = jnp.dot(activated, weight_out[...], preferred_element_type=F32)
    backward = jnp.dot(hidden_grad, weight_in[...], preferred_element_type=F32)

    @pl.when(step == 0)
    def _():
        mixed[...] = forward
        back[...] = backward

    @pl.when(step > 0)
    def _():
        mixed[...] += forward
        back[...] += backward

    @pl.when(step == pl.num_programs(0) - 1)
    def _():
        channels = gain.shape[1]
        whole = mixed[...]
        block_out[...] = (voxels[...].astype(F32) + scale * whole).astype(BF16)
        scale_local = jnp.sum(cotangent[...].astype(F32) * whole, axis=0, keepdims=True)
        grad = back[...]
        deviation = centered[...]
        variance = jnp.sum(deviation * deviation, axis=1, keepdims=True) * (1.0 / channels)
        inverse = lax.rsqrt(variance + norm_eps)
        one = deviation * inverse
        bias_local = jnp.sum(grad, axis=0, keepdims=True)
        gain_local = jnp.sum(grad * one, axis=0, keepdims=True)
        small[...] = jnp.concatenate(
            [gain_local, bias_local, scale_local, jnp.zeros((SUB - 3, channels), F32)], axis=0
        )
        scaled = grad * gain
        average = jnp.sum(scaled, axis=1, keepdims=True) * (1.0 / channels)
        slant = jnp.sum(scaled * one, axis=1, keepdims=True) * (1.0 / channels)
        conv_grad[...] = (inverse * (scaled - average - one * slant)).astype(BF16)


def slopes(hidden, act_grad):
    bell = jnp.exp(-0.5 * hidden * hidden)
    below = 1.0 + (erf_step * root_half) * jnp.abs(hidden)
    t = pl.reciprocal(below, approx=True)
    t = t * (2.0 - below * t)
    poly = erf_terms[-1]
    for term in erf_terms[-2::-1]:
        poly = poly * t + term
    tail = poly * t * bell
    cover = jnp.where(hidden < 0.0, tail, 1.0 - tail)
    activated = (hidden * cover).astype(BF16)
    slope = cover + hidden * bell * inv_root_tau
    return activated, (act_grad * slope).astype(BF16)


def weight_grad_terms(which, weight_in, weight_out, scale, sets, aligned, mixed_grad):
    scales = scale[...].reshape(1, -1)
    at = 0
    for normed, cotangents in sets:
        line, rows = normed.shape[:2]
        for k in range(line):
            aligned[at : at + rows, :] = normed[which[2 + k]]
            upstream = cotangents[k].astype(F32)
            mixed_grad[at : at + rows, :] = (scales * upstream).astype(BF16)
            at += rows
    across = (((1,), (1,)), ((), ()))
    hidden = lax.dot_general(weight_in[...], aligned[...], across, preferred_element_type=F32)
    act_grad = lax.dot_general(weight_out[...], mixed_grad[...], across, preferred_element_type=F32)
    activated, hidden_grad = slopes(hidden, act_grad)
    return (
        jnp.dot(hidden_grad, aligned[...], preferred_element_type=F32),
        jnp.dot(activated, mixed_grad[...], preferred_element_type=F32),
    )


def far_side_kernel(
    which, weight_in, weight_out, scale, norm, cot, other_norm, other_cot, sent, aligned, mixed_grad
):
    sets = ((norm, cot), (other_norm, other_cot))
    terms = weight_grad_terms(which, weight_in, weight_out, scale, sets, aligned, mixed_grad)
    for k in range(2):
        sent[k] = terms[k].astype(BF16)


def near_side_kernel(
    which,
    weight_in,
    weight_out,
    scale,
    norm,
    cot,
    other_norm,
    other_cot,
    got,
    in_grad,
    out_grad,
    aligned,
    mixed_grad,
):
    sets = ((norm, cot), (other_norm, other_cot))
    terms = weight_grad_terms(which, weight_in, weight_out, scale, sets, aligned, mixed_grad)
    for k, out in enumerate((in_grad, out_grad)):
        out[...] = terms[k] + got[k].astype(F32)


def chip_sum_kernel(kept, got, out):
    out[...] = (kept[...].astype(F32) + got[...].astype(F32)).astype(BF16)


def spread_sum_kernel(parts, out):
    total = tree_sum([parts[k].astype(F32) for k in range(parts.shape[0])]).astype(BF16)
    for copy in range(out.shape[0]):
        out[copy] = total


def unpack_kernel(core, own, other, out, *small):
    piece, wide = own.shape[1:]

    def unpack(*halves):
        last = []
        for side, parts in enumerate(halves):
            lanes = slice(side * wide, (side + 1) * wide)
            for k in range(-(-TAP_ROWS // piece)):
                first = k * piece
                length = min(piece, TAP_ROWS - first)
                out[first : first + length, lanes] = parts[k].astype(F32)[:length, :]
            k = TAP_ROWS // piece
            last.append(parts[k].astype(F32))
        rows = jnp.concatenate(last, axis=1)
        first = TAP_ROWS % piece
        for k, line in enumerate(small):
            line[...] = rows[first + k : first + k + 1, :].reshape(line.shape)

    by_core(core, own, other, lambda outer, inner: unpack(inner, outer))


def params(limit=48):
    return pltpu.CompilerParams(vmem_limit_bytes=limit * 1024 * 1024)


def follow(kernel, scalars, inputs, count):
    def body(*refs):
        head = refs[: scalars + inputs]
        return kernel(*head, *refs[scalars + inputs + count :])

    return body


IN_PLACE = pl.BlockSpec(memory_space=pl.ANY)


def lane_block(rows):
    return pl.BlockSpec((rows, LANES), lambda c, *_: (0, c))


def whole_block(*shape):
    return pl.BlockSpec(shape, lambda *_: (0,) * len(shape))


def rims(cells):
    count = lax.axis_size("row")
    between = [(i, i + 1) for i in range(1, count - 1, 2)]
    return (
        lax.ppermute(cells, "row", [(i, i ^ 1) for i in range(count)]),
        lax.ppermute(cells, "row", between + [(j, i) for i, j in between]),
    )


def on_device(
    voxels, dw_kernel, norm_gain, norm_bias, weight_in, weight_out, layer_scale, cotangent
):
    planes, height, breadth, channels = voxels.shape
    rows = planes * height * breadth
    units = weight_in.shape[0]
    count = lax.axis_size("row")
    me = lax.axis_index("row")
    quad = 4
    line = count // quad
    lines = [[quad * k + p for k in range(line)] for p in range(quad)]
    other_core = [(i, i ^ 1) for i in range(count)]
    other_side = [(i, i ^ 2) for i in range(count)]
    tiles = channels // LANES

    own = voxels.reshape(rows, channels)
    upstream = cotangent.reshape(rows, channels)
    core = lax.rem(me, 2).astype(jnp.int32)
    parity = core.reshape(1)

    inner, outer = rims(own)

    def along_line(cells, steps):
        return lax.ppermute(cells, "row", [(i, (i + quad * steps) % count) for i in range(count)])

    upstream_line = [upstream] + [None] * (line - 1)
    upstream_line[1] = along_line(upstream, 1)
    upstream_line[-1] = along_line(upstream, -1)

    def spread_of(held):
        return pltpu.VMEM((9, held, PAD, LANES), F32)

    split_block = pl.BlockSpec((None, 9, KS, SUB, LANES), lambda c, *_: (c, 0, 0, 0, 0))
    partial, split = pl.pallas_call(
        functools.partial(own_conv_kernel, planes, height),
        grid=(tiles,),
        in_specs=[lane_block(rows), lane_block(TAP_ROWS)],
        out_specs=[lane_block(rows), split_block],
        out_shape=[
            jax.ShapeDtypeStruct((rows, channels), F32),
            jax.ShapeDtypeStruct((tiles, 9, KS, SUB, LANES), F32),
        ],
        scratch_shapes=[spread_of(planes)],
        compiler_params=params(),
        cost_estimate=NO_COST,
        name="own_conv",
    )(own, dw_kernel)

    for k in range(2, line - 1):
        upstream_line[k] = along_line(upstream_line[k - 1], 1)
    normed, centered = pl.pallas_call(
        follow(functools.partial(rim_conv_kernel, planes, height), 1, 6, 2),
        grid_spec=pltpu.PrefetchScalarGridSpec(
            num_scalar_prefetch=1,
            grid=(tiles,),
            in_specs=[
                lane_block(rows),
                lane_block(rows),
                split_block,
                lane_block(rows),
                whole_block(channels),
                whole_block(channels),
                IN_PLACE,
                IN_PLACE,
            ],
            out_specs=[
                whole_block(line, rows, channels),
                whole_block(rows, channels),
            ],
            scratch_shapes=[spread_of(2 * MARGIN), pltpu.VMEM((tiles, rows, LANES), F32)],
        ),
        out_shape=[
            jax.ShapeDtypeStruct((line, rows, channels), BF16),
            jax.ShapeDtypeStruct((rows, channels), F32),
        ],
        compiler_params=params(),
        cost_estimate=NO_COST,
        name="rim_conv",
    )(
        parity,
        inner,
        outer,
        split,
        partial,
        norm_gain,
        norm_bias,
        upstream_line[1],
        upstream_line[-1],
    )

    normed, upstream_line[2] = lax.optimization_barrier((normed, upstream_line[2]))
    gathered = lax.all_to_all(
        normed, "row", split_axis=0, concat_axis=0, tiled=True, axis_index_groups=lines
    )

    block = 512
    whole = whole_block(rows, channels)
    block_out, conv_grad, small, cotangents = pl.pallas_call(
        mlp_kernel,
        grid=(units // block,),
        in_specs=[
            pl.BlockSpec((None, rows, channels), lambda f: (0, 0, 0)),
            pl.BlockSpec((block, channels), lambda f: (f, 0)),
            pl.BlockSpec((block, channels), lambda f: (f, 0)),
            whole,
            whole_block(channels),
            whole_block(channels),
        ]
        + [whole] * (1 + line),
        out_specs=[
            whole,
            whole,
            whole_block(SUB, channels),
            whole_block(line, rows, channels),
        ],
        out_shape=[
            jax.ShapeDtypeStruct((rows, channels), BF16),
            jax.ShapeDtypeStruct((rows, channels), BF16),
            jax.ShapeDtypeStruct((SUB, channels), F32),
            jax.ShapeDtypeStruct((line, rows, channels), BF16),
        ],
        scratch_shapes=[
            pltpu.VMEM((rows, channels), F32),
            pltpu.VMEM((rows, channels), F32),
            pltpu.VMEM((rows, channels), BF16),
        ],
        compiler_params=params(),
        cost_estimate=NO_COST,
        name="mlp_both_ways",
    )(normed, weight_in, weight_out, centered, norm_gain, layer_scale, own, *upstream_line)

    half = count // 2
    alike = [[2 * k + p for k in range(half)] for p in range(2)]
    half_tiles = tiles // 2
    wide = half_tiles * LANES
    piece = -(-(TAP_ROWS + SUB) // half)
    piece += -piece % (2 * SUB)
    padded = piece * half

    def tile_of(block_rows):
        def at(c, w):
            return 0, (c + w[1] * half_tiles) % tiles

        return pl.BlockSpec((block_rows, LANES), at)

    half_sent, half_kept, conv_grad, token = pl.pallas_call(
        functools.partial(kernel_grad_kernel, planes, height),
        grid_spec=pltpu.PrefetchScalarGridSpec(
            num_scalar_prefetch=1,
            grid=(tiles,),
            in_specs=[tile_of(rows), tile_of(rows), tile_of(rows), tile_of(rows), tile_of(SUB)],
            out_specs=[
                pl.BlockSpec((padded, LANES), lambda c, w: (0, jnp.minimum(c, half_tiles - 1))),
                pl.BlockSpec((padded, LANES), lambda c, w: (0, jnp.maximum(c - half_tiles, 0))),
                tile_of(rows),
                whole_block(SUB, LANES),
            ],
            scratch_shapes=[
                spread_of(2 * MARGIN + planes),
                pltpu.VMEM((2, KS, SUB * SUB, LANES), F32),
                pltpu.VMEM((9, KS, SUB, LANES), F32),
                pltpu.VMEM((padded, LANES), F32),
            ],
        ),
        out_shape=[jax.ShapeDtypeStruct((padded, wide), BF16)] * 2
        + [
            jax.ShapeDtypeStruct((rows, channels), BF16),
            jax.ShapeDtypeStruct((SUB, LANES), F32),
        ],
        compiler_params=params(),
        cost_estimate=NO_COST,
        name="kernel_grad_terms",
    )(jnp.stack([core, 1 - core]), inner, own, outer, conv_grad, small)

    half_got = lax.ppermute(half_sent, "row", other_core)
    gathered, token = lax.optimization_barrier((gathered, token))
    grad_inner, grad_outer = rims(conv_grad)
    sums = pl.pallas_call(
        follow(chip_sum_kernel, 0, 2, 1),
        in_specs=[whole_block(padded, wide)] * 2 + [IN_PLACE],
        out_specs=whole_block(padded, wide),
        out_shape=jax.ShapeDtypeStruct((padded, wide), BF16),
        grid=(1,),
        compiler_params=params(),
        cost_estimate=NO_COST,
        name="kernel_grad_chip_sum",
    )(half_kept, half_got, token)

    share = units // count
    tokens = line * rows
    base = me // quad * quad
    side = lax.rem(me, quad) // 2
    place = lax.rem(me // quad + line - jnp.arange(line, dtype=jnp.int32), line)
    far = base + 2 * (1 - side)
    near = base + 2 * side
    which = jnp.concatenate(
        [jnp.stack([far + core, near + core]).astype(jnp.int32), place.astype(jnp.int32)]
    )
    other_gathered = lax.ppermute(gathered, "row", other_core)
    other_cotangents = lax.ppermute(cotangents, "row", other_core)

    def side_terms(kernel, number, more, after, outs, name):
        chunk = pl.BlockSpec((share, channels), lambda _, w: (w[number], 0))
        return pl.pallas_call(
            follow(kernel, 1, 7 + len(more), len(after)),
            grid_spec=pltpu.PrefetchScalarGridSpec(
                num_scalar_prefetch=1,
                grid=(1,),
                in_specs=[chunk, chunk, whole_block(channels)]
                + [whole_block(line, rows, channels)] * 4
                + [whole_block(*part.shape) for part in more]
                + [IN_PLACE] * len(after),
                out_specs=[whole_block(*out.shape) for out in outs],
                scratch_shapes=[pltpu.VMEM((2 * tokens, channels), BF16)] * 2,
            ),
            out_shape=outs,
            compiler_params=params(),
            cost_estimate=NO_COST,
            name=name,
        )(
            which,
            weight_in,
            weight_out,
            layer_scale,
            gathered,
            cotangents,
            other_gathered,
            other_cotangents,
            *more,
            *after,
        )

    pair = jax.ShapeDtypeStruct((2, share, channels), BF16)
    single = jax.ShapeDtypeStruct((share, channels), F32)
    (sent,) = side_terms(
        far_side_kernel, 0, [], [sums, grad_inner, grad_outer], [pair], "weight_grads_far_side"
    )
    got = lax.ppermute(sent, "row", other_side)
    scattered = lax.all_to_all(
        sums.reshape(half, piece, wide),
        "row",
        split_axis=0,
        concat_axis=0,
        tiled=True,
        axis_index_groups=alike,
    )
    voxel_grad, token = pl.pallas_call(
        follow(functools.partial(input_grad_kernel, planes, height), 1, 5, 1),
        grid_spec=pltpu.PrefetchScalarGridSpec(
            num_scalar_prefetch=1,
            grid=(tiles,),
            in_specs=[
                lane_block(rows),
                lane_block(rows),
                lane_block(rows),
                lane_block(TAP_ROWS),
                lane_block(rows),
                IN_PLACE,
            ],
            out_specs=[lane_block(rows), whole_block(SUB, LANES)],
            scratch_shapes=[
                spread_of(2 * MARGIN + planes),
                pltpu.VMEM((9, KS, SUB, LANES), F32),
            ],
        ),
        out_shape=[
            jax.ShapeDtypeStruct((rows, channels), BF16),
            jax.ShapeDtypeStruct((SUB, LANES), F32),
        ],
        compiler_params=params(),
        cost_estimate=NO_COST,
        name="input_grad_conv",
    )(parity, grad_inner, conv_grad, grad_outer, dw_kernel, upstream, sent)

    copies = pl.pallas_call(
        follow(spread_sum_kernel, 0, 1, 1),
        in_specs=[whole_block(half, piece, wide), IN_PLACE],
        out_specs=whole_block(half, piece, wide),
        out_shape=jax.ShapeDtypeStruct((half, piece, wide), BF16),
        grid=(1,),
        compiler_params=params(),
        cost_estimate=NO_COST,
        name="kernel_grad_sum",
    )(scattered, token)
    totals = lax.all_to_all(
        copies, "row", split_axis=0, concat_axis=0, tiled=True, axis_index_groups=alike
    )
    weight_in_grad, weight_out_grad = side_terms(
        near_side_kernel, 1, [got], [copies], [single, single], "weight_grads_near_side"
    )
    totals, weight_in_grad = lax.optimization_barrier((totals, weight_in_grad))
    other_totals = lax.ppermute(totals, "row", other_core)
    kernel_grad, *vector_grads = pl.pallas_call(
        unpack_kernel,
        grid_spec=pltpu.PrefetchScalarGridSpec(
            num_scalar_prefetch=1,
            grid=(1,),
            in_specs=[whole_block(half, piece, wide)] * 2,
            out_specs=[whole_block(TAP_ROWS, channels)] + [whole_block(channels)] * 3,
        ),
        out_shape=[jax.ShapeDtypeStruct((TAP_ROWS, channels), F32)]
        + [jax.ShapeDtypeStruct((channels,), F32)] * 3,
        compiler_params=params(),
        cost_estimate=NO_COST,
        name="kernel_grad_unpack",
    )(parity, totals, other_totals)

    return (
        block_out.reshape(voxels.shape),
        voxel_grad.reshape(voxels.shape),
        kernel_grad,
        *vector_grads,
        weight_in_grad,
        weight_out_grad,
    )


def solution(mesh):
    in_specs = (
        P(("group", "row"), None, None, None),
        P(),
        P(),
        P(),
        P(),
        P(),
        P(),
        P(("group", "row"), None, None, None),
    )
    out_specs = (
        P(("group", "row"), None, None, None),
        P(("group", "row"), None, None, None),
        P("group", None),
        P("group"),
        P("group"),
        P("group"),
        P(("group", "row"), None),
        P(("group", "row"), None),
    )
    return jax.shard_map(
        on_device, mesh=mesh, in_specs=in_specs, out_specs=out_specs, check_vma=False
    )
```

```python
import functools

import jax
import jax.numpy as jnp
from jax import lax
from jax.experimental import pallas as pl
from jax.experimental.pallas import tpu as pltpu
from jax.sharding import PartitionSpec as P

KS = 7
MARGIN = KS // 2
LANES = 128
SUB = 8
PAD = 3 * SUB
TAP_ROWS = KS * KS * KS

root_half = 0.7071067811865476
inv_root_tau = 0.3989422804014327
norm_eps = 1e-06
erf_step = 0.3275911
erf_terms = tuple(
    0.5 * a for a in (0.254829592, -0.284496736, 1.421413741, -1.453152027, 1.061405429)
)

NO_COST = pl.CostEstimate(flops=0, bytes_accessed=0, transcendentals=0)

F32 = jnp.float32
BF16 = jnp.bfloat16


def split_source(v):
    terms = []
    for a, b in ((v[0] + v[2], v[1] + v[3]), (v[2], v[3]), (v[0], v[1])):
        terms += [a + b, b, a]
    return terms


def split_taps(t):
    terms = []
    for s in (
        (t[2], t[3], t[4]),
        (t[4] - t[2], t[5] - t[3], t[6] - t[4]),
        (t[0] - t[2], t[1] - t[3], t[2] - t[4]),
    ):
        terms += [s[1], s[2] - s[1], s[0] - s[1]]
    return terms


def split_grads(g):
    terms = []
    for a, b in ((g[0] + g[2], g[1] + g[3]), (g[0], g[1]), (g[2], g[3])):
        terms += [a + b, a, b]
    return terms


def join_outputs(m):
    pair = [(m[3 * k] + m[3 * k + 1], m[3 * k] + m[3 * k + 2]) for k in range(3)]
    return [
        pair[0][0] + pair[1][0],
        pair[0][1] + pair[1][1],
        pair[0][0] + pair[2][0],
        pair[0][1] + pair[2][1],
    ]


def join_taps(m):
    p, q, r = [
        (m[3 * k + 2], m[3 * k] - m[3 * k + 1] - m[3 * k + 2], m[3 * k + 1]) for k in range(3)
    ]
    return [
        r[0],
        r[1],
        p[0] - q[0] - r[0] + r[2],
        p[1] - q[1] - r[1],
        p[2] - q[2] - r[2] + q[0],
        q[1],
        q[2],
    ]


def tree_sum(terms):
    while len(terms) > 1:
        terms = [
            terms[k] + terms[k + 1] if k + 1 < len(terms) else terms[k]
            for k in range(0, len(terms), 2)
        ]
    return terms[0]


def stage_source(wanted, height, spread):
    row = height * SUB
    for at, (block, x) in enumerate(wanted):
        plane = block[x * row : (x + 1) * row, :].astype(F32)
        lines = [plane[y * SUB : (y + 1) * SUB, :] for y in range(height)]
        for j, term in enumerate(split_source(lines)):
            spread[j, at, SUB : 2 * SUB, :] = term


def rim_planes(left, right, planes):
    wanted = [(left, x) for x in range(planes - MARGIN, planes)]
    return wanted + [(right, x) for x in range(MARGIN)]


def all_planes(left, own, right, planes):
    rim = rim_planes(left, right, planes)
    return rim[:MARGIN] + [(own, x) for x in range(planes)] + rim[MARGIN:]


def by_core(core, inner, outer, stage):
    @pl.when(core[0] == 0)
    def _():
        stage(outer, inner)

    @pl.when(core[0] != 0)
    def _():
        stage(inner, outer)


def clear_rims(spread):
    zeros = jnp.zeros(spread.shape[:2] + (SUB, LANES), F32)
    spread[:, :, :SUB, :] = zeros
    spread[:, :, 2 * SUB :, :] = zeros


def stage_taps(taps, split):
    for dx in range(KS):
        rows = []
        for dy in range(KS):
            first = dx * KS * KS + dy * KS
            if first + SUB <= TAP_ROWS:
                rows.append(taps[first : first + SUB, :])
            else:
                rows.append(pltpu.roll(taps[TAP_ROWS - SUB : TAP_ROWS, :], SUB - 1, 0))
        for j, term in enumerate(split_taps(rows)):
            split[j, dx] = term


REVERSED = (0, 2, 1, 6, 8, 7, 3, 5, 4)


def convolve(spread, split, planes, held, flipped):
    terms = []
    for j in range(9):
        sums = [None] * planes
        for dz in range(KS):
            first = SUB - MARGIN + dz
            source = {x: spread[j, at, first : first + SUB, :] for at, x in enumerate(held)}
            weights = []
            for dx in range(KS):
                if flipped:
                    tap = split[REVERSED[j], KS - 1 - dx, KS - 1 - dz : KS - dz, :]
                else:
                    tap = split[j, dx, dz : dz + 1, :]
                weights.append(jnp.broadcast_to(tap, (SUB, LANES)))
            for x in range(planes):
                part = tree_sum(
                    [source[x + dx] * weights[dx] for dx in range(KS) if x + dx in source]
                )
                sums[x] = part if sums[x] is None else sums[x] + part
        terms.append(sums)
    return [join_outputs([terms[j][x] for j in range(9)]) for x in range(planes)]


def own_conv_kernel(planes, height, own, taps, out, split, spread):
    @pl.when(pl.program_id(0) == 0)
    def _():
        clear_rims(spread)

    stage_source([(own, x) for x in range(planes)], height, spread)
    stage_taps(taps, split)
    rows = convolve(spread, split, planes, range(MARGIN, MARGIN + planes), False)
    for x in range(planes):
        for y in range(height):
            at = (x * height + y) * SUB
            out[at : at + SUB, :] = rows[x][y]


def rim_conv_kernel(
    planes, height, core, inner, outer, split, partial, gain, bias, normed, centered, spread, conv
):
    step = pl.program_id(0)

    @pl.when(step == 0)
    def _():
        clear_rims(spread)

    def stage(left, right):
        stage_source(rim_planes(left, right, planes), height, spread)

    by_core(core, inner, outer, stage)
    held = list(range(MARGIN)) + list(range(MARGIN + planes, 2 * MARGIN + planes))
    rows = convolve(spread, split, planes, held, False)
    for x in range(planes):
        for y in range(height):
            at = (x * height + y) * SUB
            conv[step, at : at + SUB, :] = rows[x][y] + partial[at : at + SUB, :]

    @pl.when(step == pl.num_programs(0) - 1)
    def _():
        tiles = conv.shape[0]
        channels = tiles * LANES
        parts = [conv[k] for k in range(tiles)]
        gains = gain[...].reshape(1, channels)
        biases = bias[...].reshape(1, channels)
        average = jnp.sum(tree_sum(parts), axis=1, keepdims=True) * (1.0 / channels)
        parts = [part - average for part in parts]
        variance = jnp.sum(
            tree_sum([part * part for part in parts]), axis=1, keepdims=True
        ) * (1.0 / channels)
        inverse = lax.rsqrt(variance + norm_eps)
        for k in range(tiles):
            lanes = slice(k * LANES, (k + 1) * LANES)
            centered[:, lanes] = parts[k]
            value = parts[k] * inverse
            whole = (value * gains[:, lanes] + biases[:, lanes]).astype(BF16)
            for copy in range(normed.shape[0]):
                normed[copy, :, lanes] = whole


def input_grad_kernel(
    planes, height, core, inner, own, outer, taps, cotangent, out, token, spread, split
):
    @pl.when(pl.program_id(0) == 0)
    def _():
        clear_rims(spread)

    def stage(left, right):
        stage_source(all_planes(left, own, right, planes), height, spread)

    by_core(core, inner, outer, stage)
    stage_taps(taps, split)
    token[...] = jnp.zeros(token.shape, F32)
    rows = convolve(spread, split, planes, range(2 * MARGIN + planes), True)
    for x in range(planes):
        at = x * height * SUB
        whole = jnp.concatenate(rows[x], axis=0)
        upstream = cotangent[at : at + height * SUB, :].astype(F32)
        out[at : at + height * SUB, :] = (upstream + whole).astype(BF16)


def kernel_grad_kernel(
    planes,
    height,
    which,
    inner,
    own,
    outer,
    grads,
    small,
    sent,
    kept,
    passed,
    spread,
    products,
    joined,
    flat,
):
    passed[...] = grads[...]

    @pl.when(pl.program_id(0) == 0)
    def _():
        clear_rims(spread)
        products[...] = jnp.zeros(products.shape, F32)
        flat[...] = jnp.zeros(flat.shape, F32)

    def stage(left, right):
        stage_source(all_planes(left, own, right, planes), height, spread)

    by_core(which, inner, outer, stage)
    upstream = []
    for x in range(planes):
        plane = grads[x * height * SUB : (x + 1) * height * SUB, :].astype(F32)
        upstream.append(
            split_grads([plane[y * SUB : (y + 1) * SUB, :] for y in range(height)])
        )
    for j in range(9):
        for dz in range(KS):
            first = SUB - MARGIN + dz
            source = [
                spread[j, x, first : first + SUB, :] for x in range(planes + KS - 1)
            ]
            for dx in range(KS):
                products[j % 2, dx, dz * SUB : (dz + 1) * SUB, :] = tree_sum(
                    [source[x + dx] * upstream[x][j] for x in range(planes)]
                )
        for dx in range(KS):
            joined[j, dx] = tree_sum(
                [products[j % 2, dx, pl.ds(s, SUB, stride=SUB), :] for s in range(SUB)]
            )
    for dx in range(KS):
        for dy, tile in enumerate(join_taps([joined[j, dx] for j in range(9)])):
            row = dx * KS * KS + dy * KS
            flat[row : row + SUB, :] = tile
    flat[TAP_ROWS : TAP_ROWS + SUB, :] = small[...]
    step = pl.program_id(0)
    half = pl.num_programs(0) // 2

    @pl.when(step < half)
    def _():
        sent[...] = flat[...].astype(BF16)

    @pl.when(step >= half)
    def _():
        kept[...] = flat[...].astype(BF16)


def mlp_kernel(
    normed, weight_in, weight_out, centered, norm_gain, layer_scale, voxels, *rest
):
    *cotangents, block_out, conv_grad, small, together, mixed, back, mixed_grad = rest
    cotangent = cotangents[0]
    step = pl.program_id(0)
    gain = norm_gain[...].reshape(1, -1)
    scale = layer_scale[...].reshape(1, -1)

    @pl.when(step == 0)
    def _():
        mixed_grad[...] = (scale * cotangent[...].astype(F32)).astype(BF16)
        for k, part in enumerate(cotangents):
            together[k] = part[...]

    across = (((1,), (1,)), ((), ()))
    hidden = lax.dot_general(normed[...], weight_in[...], across, preferred_element_type=F32)
    act_grad = lax.dot_general(
        mixed_grad[...], weight_out[...], across, preferred_element_type=F32
    )
    activated, hidden_grad = slopes(hidden, act_grad)
    forward = jnp.dot(activated, weight_out[...], preferred_element_type=F32)
    backward = jnp.dot(hidden_grad, weight_in[...], preferred_element_type=F32)

    @pl.when(step == 0)
    def _():
        mixed[...] = forward
        back[...] = backward

    @pl.when(step > 0)
    def _():
        mixed[...] += forward
        back[...] += backward

    @pl.when(step == pl.num_programs(0) - 1)
    def _():
        channels = gain.shape[1]
        whole = mixed[...]
        block_out[...] = (voxels[...].astype(F32) + scale * whole).astype(BF16)
        scale_local = jnp.sum(cotangent[...].astype(F32) * whole, axis=0, keepdims=True)
        grad = back[...]
        deviation = centered[...]
        variance = jnp.sum(deviation * deviation, axis=1, keepdims=True) * (1.0 / channels)
        inverse = lax.rsqrt(variance + norm_eps)
        one = deviation * inverse
        bias_local = jnp.sum(grad, axis=0, keepdims=True)
        gain_local = jnp.sum(grad * one, axis=0, keepdims=True)
        small[...] = jnp.concatenate(
            [gain_local, bias_local, scale_local, jnp.zeros((SUB - 3, channels), F32)], axis=0
        )
        scaled = grad * gain
        average = jnp.sum(scaled, axis=1, keepdims=True) * (1.0 / channels)
        slant = jnp.sum(scaled * one, axis=1, keepdims=True) * (1.0 / channels)
        conv_grad[...] = (inverse * (scaled - average - one * slant)).astype(BF16)


def slopes(hidden, act_grad):
    bell = jnp.exp(-0.5 * hidden * hidden)
    below = 1.0 + (erf_step * root_half) * jnp.abs(hidden)
    t = pl.reciprocal(below, approx=True)
    t = t * (2.0 - below * t)
    poly = erf_terms[-1]
    for term in erf_terms[-2::-1]:
        poly = poly * t + term
    tail = poly * t * bell
    cover = jnp.where(hidden < 0.0, tail, 1.0 - tail)
    activated = (hidden * cover).astype(BF16)
    slope = cover + hidden * bell * inv_root_tau
    return activated, (act_grad * slope).astype(BF16)


def weight_grad_terms(which, weight_in, weight_out, scale, sets, aligned, mixed_grad):
    scales = scale[...].reshape(1, -1)
    at = 0
    for normed, cotangents in sets:
        line, rows = normed.shape[:2]
        for k in range(line):
            aligned[at : at + rows, :] = normed[which[2 + k]]
            upstream = cotangents[k].astype(F32)
            mixed_grad[at : at + rows, :] = (scales * upstream).astype(BF16)
            at += rows
    across = (((1,), (1,)), ((), ()))
    hidden = lax.dot_general(weight_in[...], aligned[...], across, preferred_element_type=F32)
    act_grad = lax.dot_general(weight_out[...], mixed_grad[...], across, preferred_element_type=F32)
    activated, hidden_grad = slopes(hidden, act_grad)
    return (
        jnp.dot(hidden_grad, aligned[...], preferred_element_type=F32),
        jnp.dot(activated, mixed_grad[...], preferred_element_type=F32),
    )


def far_side_kernel(
    which, weight_in, weight_out, scale, norm, cot, other_norm, other_cot, sent, aligned, mixed_grad
):
    sets = ((norm, cot), (other_norm, other_cot))
    terms = weight_grad_terms(which, weight_in, weight_out, scale, sets, aligned, mixed_grad)
    for k in range(2):
        sent[k] = terms[k].astype(BF16)


def near_side_kernel(
    which,
    weight_in,
    weight_out,
    scale,
    norm,
    cot,
    other_norm,
    other_cot,
    got,
    in_grad,
    out_grad,
    aligned,
    mixed_grad,
):
    sets = ((norm, cot), (other_norm, other_cot))
    terms = weight_grad_terms(which, weight_in, weight_out, scale, sets, aligned, mixed_grad)
    for k, out in enumerate((in_grad, out_grad)):
        out[...] = terms[k] + got[k].astype(F32)


def chip_sum_kernel(kept, got, out, token):
    token[...] = jnp.zeros(token.shape, F32)
    out[...] = (kept[...].astype(F32) + got[...].astype(F32)).astype(BF16)


def spread_sum_kernel(parts, out):
    total = tree_sum([parts[k].astype(F32) for k in range(parts.shape[0])]).astype(BF16)
    for copy in range(out.shape[0]):
        out[copy] = total


def unpack_kernel(core, own, other, out, *small):
    piece, wide = own.shape[1:]

    def unpack(*halves):
        last = []
        for side, parts in enumerate(halves):
            lanes = slice(side * wide, (side + 1) * wide)
            for k in range(-(-TAP_ROWS // piece)):
                first = k * piece
                length = min(piece, TAP_ROWS - first)
                out[first : first + length, lanes] = parts[k].astype(F32)[:length, :]
            k = TAP_ROWS // piece
            last.append(parts[k].astype(F32))
        rows = jnp.concatenate(last, axis=1)
        first = TAP_ROWS % piece
        for k, line in enumerate(small):
            line[...] = rows[first + k : first + k + 1, :].reshape(line.shape)

    by_core(core, own, other, lambda outer, inner: unpack(inner, outer))


def params(limit=48):
    return pltpu.CompilerParams(vmem_limit_bytes=limit * 1024 * 1024)


def follow(kernel, scalars, inputs, count):
    def body(*refs):
        head = refs[: scalars + inputs]
        return kernel(*head, *refs[scalars + inputs + count :])

    return body


IN_PLACE = pl.BlockSpec(memory_space=pl.ANY)


def lane_block(rows):
    return pl.BlockSpec((rows, LANES), lambda c, *_: (0, c))


def whole_block(*shape):
    return pl.BlockSpec(shape, lambda *_: (0,) * len(shape))


def rims(cells):
    count = lax.axis_size("row")
    between = [(i, i + 1) for i in range(1, count - 1, 2)]
    return (
        lax.ppermute(cells, "row", [(i, i ^ 1) for i in range(count)]),
        lax.ppermute(cells, "row", between + [(j, i) for i, j in between]),
    )


def on_device(
    voxels, dw_kernel, norm_gain, norm_bias, weight_in, weight_out, layer_scale, cotangent
):
    planes, height, breadth, channels = voxels.shape
    rows = planes * height * breadth
    units = weight_in.shape[0]
    count = lax.axis_size("row")
    me = lax.axis_index("row")
    quad = 4
    line = count // quad
    lines = [[quad * k + p for k in range(line)] for p in range(quad)]
    other_core = [(i, i ^ 1) for i in range(count)]
    other_side = [(i, i ^ 2) for i in range(count)]
    tiles = channels // LANES

    own = voxels.reshape(rows, channels)
    upstream = cotangent.reshape(rows, channels)
    core = lax.rem(me, 2).astype(jnp.int32)
    parity = core.reshape(1)

    inner, outer = rims(own)

    def along_line(cells, steps):
        return lax.ppermute(cells, "row", [(i, (i + quad * steps) % count) for i in range(count)])

    upstream_line = [upstream] + [None] * (line - 1)
    upstream_line[1] = along_line(upstream, 1)
    upstream_line[-1] = along_line(upstream, -1)

    def spread_of(held):
        return pltpu.VMEM((9, held, PAD, LANES), F32)

    split_block = pl.BlockSpec((None, 9, KS, SUB, LANES), lambda c, *_: (c, 0, 0, 0, 0))
    partial, split = pl.pallas_call(
        functools.partial(own_conv_kernel, planes, height),
        grid=(tiles,),
        in_specs=[lane_block(rows), lane_block(TAP_ROWS)],
        out_specs=[lane_block(rows), split_block],
        out_shape=[
            jax.ShapeDtypeStruct((rows, channels), F32),
            jax.ShapeDtypeStruct((tiles, 9, KS, SUB, LANES), F32),
        ],
        scratch_shapes=[spread_of(planes)],
        compiler_params=params(),
        cost_estimate=NO_COST,
        name="own_conv",
    )(own, dw_kernel)

    for k in range(2, line - 1):
        upstream_line[k] = along_line(upstream_line[k - 1], 1)
    normed, centered = pl.pallas_call(
        follow(functools.partial(rim_conv_kernel, planes, height), 1, 6, 2),
        grid_spec=pltpu.PrefetchScalarGridSpec(
            num_scalar_prefetch=1,
            grid=(tiles,),
            in_specs=[
                lane_block(rows),
                lane_block(rows),
                split_block,
                lane_block(rows),
                whole_block(channels),
                whole_block(channels),
                IN_PLACE,
                IN_PLACE,
            ],
            out_specs=[
                whole_block(line, rows, channels),
                whole_block(rows, channels),
            ],
            scratch_shapes=[spread_of(2 * MARGIN), pltpu.VMEM((tiles, rows, LANES), F32)],
        ),
        out_shape=[
            jax.ShapeDtypeStruct((line, rows, channels), BF16),
            jax.ShapeDtypeStruct((rows, channels), F32),
        ],
        compiler_params=params(),
        cost_estimate=NO_COST,
        name="rim_conv",
    )(
        parity,
        inner,
        outer,
        split,
        partial,
        norm_gain,
        norm_bias,
        upstream_line[1],
        upstream_line[-1],
    )

    normed, upstream_line[2] = lax.optimization_barrier((normed, upstream_line[2]))
    gathered = lax.all_to_all(
        normed, "row", split_axis=0, concat_axis=0, tiled=True, axis_index_groups=lines
    )

    block = 512
    whole = whole_block(rows, channels)
    block_out, conv_grad, small, cotangents = pl.pallas_call(
        mlp_kernel,
        grid=(units // block,),
        in_specs=[
            pl.BlockSpec((None, rows, channels), lambda f: (0, 0, 0)),
            pl.BlockSpec((block, channels), lambda f: (f, 0)),
            pl.BlockSpec((block, channels), lambda f: (f, 0)),
            whole,
            whole_block(channels),
            whole_block(channels),
        ]
        + [whole] * (1 + line),
        out_specs=[
            whole,
            whole,
            whole_block(SUB, channels),
            whole_block(line, rows, channels),
        ],
        out_shape=[
            jax.ShapeDtypeStruct((rows, channels), BF16),
            jax.ShapeDtypeStruct((rows, channels), BF16),
            jax.ShapeDtypeStruct((SUB, channels), F32),
            jax.ShapeDtypeStruct((line, rows, channels), BF16),
        ],
        scratch_shapes=[
            pltpu.VMEM((rows, channels), F32),
            pltpu.VMEM((rows, channels), F32),
            pltpu.VMEM((rows, channels), BF16),
        ],
        compiler_params=params(),
        cost_estimate=NO_COST,
        name="mlp_both_ways",
    )(normed, weight_in, weight_out, centered, norm_gain, layer_scale, own, *upstream_line)

    half = count // 2
    alike = [[2 * k + p for k in range(half)] for p in range(2)]
    half_tiles = tiles // 2
    wide = half_tiles * LANES
    piece = -(-(TAP_ROWS + SUB) // half)
    piece += -piece % (2 * SUB)
    padded = piece * half

    def tile_of(block_rows):
        def at(c, w):
            return 0, (c + w[1] * half_tiles) % tiles

        return pl.BlockSpec((block_rows, LANES), at)

    half_sent, half_kept, conv_grad = pl.pallas_call(
        functools.partial(kernel_grad_kernel, planes, height),
        grid_spec=pltpu.PrefetchScalarGridSpec(
            num_scalar_prefetch=1,
            grid=(tiles,),
            in_specs=[tile_of(rows), tile_of(rows), tile_of(rows), tile_of(rows), tile_of(SUB)],
            out_specs=[
                pl.BlockSpec((padded, LANES), lambda c, w: (0, jnp.minimum(c, half_tiles - 1))),
                pl.BlockSpec((padded, LANES), lambda c, w: (0, jnp.maximum(c - half_tiles, 0))),
                tile_of(rows),
            ],
            scratch_shapes=[
                spread_of(2 * MARGIN + planes),
                pltpu.VMEM((2, KS, SUB * SUB, LANES), F32),
                pltpu.VMEM((9, KS, SUB, LANES), F32),
                pltpu.VMEM((padded, LANES), F32),
            ],
        ),
        out_shape=[jax.ShapeDtypeStruct((padded, wide), BF16)] * 2
        + [
            jax.ShapeDtypeStruct((rows, channels), BF16),
        ],
        compiler_params=params(),
        cost_estimate=NO_COST,
        name="kernel_grad_terms",
    )(jnp.stack([core, 1 - core]), inner, own, outer, conv_grad, small)

    half_got = lax.ppermute(half_sent, "row", other_core)
    grad_inner, grad_outer = rims(conv_grad)
    sums, token = pl.pallas_call(
        follow(chip_sum_kernel, 0, 2, 2),
        in_specs=[whole_block(padded, wide)] * 2 + [IN_PLACE] * 2,
        out_specs=[whole_block(padded, wide), whole_block(SUB, LANES)],
        out_shape=[
            jax.ShapeDtypeStruct((padded, wide), BF16),
            jax.ShapeDtypeStruct((SUB, LANES), F32),
        ],
        grid=(1,),
        compiler_params=params(),
        cost_estimate=NO_COST,
        name="kernel_grad_chip_sum",
    )(half_kept, half_got, grad_inner, grad_outer)
    gathered, token = lax.optimization_barrier((gathered, token))

    share = units // count
    tokens = line * rows
    base = me // quad * quad
    side = lax.rem(me, quad) // 2
    place = lax.rem(me // quad + line - jnp.arange(line, dtype=jnp.int32), line)
    far = base + 2 * (1 - side)
    near = base + 2 * side
    which = jnp.concatenate(
        [jnp.stack([far + core, near + core]).astype(jnp.int32), place.astype(jnp.int32)]
    )
    other_gathered = lax.ppermute(gathered, "row", other_core)
    other_cotangents = lax.ppermute(cotangents, "row", other_core)

    def side_terms(kernel, number, more, after, outs, name):
        chunk = pl.BlockSpec((share, channels), lambda _, w: (w[number], 0))
        return pl.pallas_call(
            follow(kernel, 1, 7 + len(more), len(after)),
            grid_spec=pltpu.PrefetchScalarGridSpec(
                num_scalar_prefetch=1,
                grid=(1,),
                in_specs=[chunk, chunk, whole_block(channels)]
                + [whole_block(line, rows, channels)] * 4
                + [whole_block(*part.shape) for part in more]
                + [IN_PLACE] * len(after),
                out_specs=[whole_block(*out.shape) for out in outs],
                scratch_shapes=[pltpu.VMEM((2 * tokens, channels), BF16)] * 2,
            ),
            out_shape=outs,
            compiler_params=params(),
            cost_estimate=NO_COST,
            name=name,
        )(
            which,
            weight_in,
            weight_out,
            layer_scale,
            gathered,
            cotangents,
            other_gathered,
            other_cotangents,
            *more,
            *after,
        )

    pair = jax.ShapeDtypeStruct((2, share, channels), BF16)
    single = jax.ShapeDtypeStruct((share, channels), F32)
    (sent,) = side_terms(
        far_side_kernel, 0, [], [sums, token], [pair], "weight_grads_far_side"
    )
    got = lax.ppermute(sent, "row", other_side)
    scattered = lax.all_to_all(
        sums.reshape(half, piece, wide),
        "row",
        split_axis=0,
        concat_axis=0,
        tiled=True,
        axis_index_groups=alike,
    )
    voxel_grad, token = pl.pallas_call(
        follow(functools.partial(input_grad_kernel, planes, height), 1, 5, 1),
        grid_spec=pltpu.PrefetchScalarGridSpec(
            num_scalar_prefetch=1,
            grid=(tiles,),
            in_specs=[
                lane_block(rows),
                lane_block(rows),
                lane_block(rows),
                lane_block(TAP_ROWS),
                lane_block(rows),
                IN_PLACE,
            ],
            out_specs=[lane_block(rows), whole_block(SUB, LANES)],
            scratch_shapes=[
                spread_of(2 * MARGIN + planes),
                pltpu.VMEM((9, KS, SUB, LANES), F32),
            ],
        ),
        out_shape=[
            jax.ShapeDtypeStruct((rows, channels), BF16),
            jax.ShapeDtypeStruct((SUB, LANES), F32),
        ],
        compiler_params=params(),
        cost_estimate=NO_COST,
        name="input_grad_conv",
    )(parity, grad_inner, conv_grad, grad_outer, dw_kernel, upstream, sent)

    copies = pl.pallas_call(
        follow(spread_sum_kernel, 0, 1, 1),
        in_specs=[whole_block(half, piece, wide), IN_PLACE],
        out_specs=whole_block(half, piece, wide),
        out_shape=jax.ShapeDtypeStruct((half, piece, wide), BF16),
        grid=(1,),
        compiler_params=params(),
        cost_estimate=NO_COST,
        name="kernel_grad_sum",
    )(scattered, token)
    totals = lax.all_to_all(
        copies, "row", split_axis=0, concat_axis=0, tiled=True, axis_index_groups=alike
    )
    weight_in_grad, weight_out_grad = side_terms(
        near_side_kernel, 1, [got], [copies], [single, single], "weight_grads_near_side"
    )
    totals, weight_in_grad = lax.optimization_barrier((totals, weight_in_grad))
    other_totals = lax.ppermute(totals, "row", other_core)
    kernel_grad, *vector_grads = pl.pallas_call(
        unpack_kernel,
        grid_spec=pltpu.PrefetchScalarGridSpec(
            num_scalar_prefetch=1,
            grid=(1,),
            in_specs=[whole_block(half, piece, wide)] * 2,
            out_specs=[whole_block(TAP_ROWS, channels)] + [whole_block(channels)] * 3,
        ),
        out_shape=[jax.ShapeDtypeStruct((TAP_ROWS, channels), F32)]
        + [jax.ShapeDtypeStruct((channels,), F32)] * 3,
        compiler_params=params(),
        cost_estimate=NO_COST,
        name="kernel_grad_unpack",
    )(parity, totals, other_totals)

    return (
        block_out.reshape(voxels.shape),
        voxel_grad.reshape(voxels.shape),
        kernel_grad,
        *vector_grads,
        weight_in_grad,
        weight_out_grad,
    )


def solution(mesh):
    in_specs = (
        P(("group", "row"), None, None, None),
        P(),
        P(),
        P(),
        P(),
        P(),
        P(),
        P(("group", "row"), None, None, None),
    )
    out_specs = (
        P(("group", "row"), None, None, None),
        P(("group", "row"), None, None, None),
        P("group", None),
        P("group"),
        P("group"),
        P("group"),
        P(("group", "row"), None),
        P(("group", "row"), None),
    )
    return jax.shard_map(
        on_device, mesh=mesh, in_specs=in_specs, out_specs=out_specs, check_vma=False
    )
```

```python
import functools

import jax
import jax.numpy as jnp
from jax import lax
from jax.experimental import pallas as pl
from jax.experimental.pallas import tpu as pltpu
from jax.sharding import PartitionSpec as P

KS = 7
MARGIN = KS // 2
LANES = 128
SUB = 8
PAD = 3 * SUB
TAP_ROWS = KS * KS * KS

root_half = 0.7071067811865476
inv_root_tau = 0.3989422804014327
norm_eps = 1e-06
erf_step = 0.3275911
erf_terms = tuple(
    0.5 * a for a in (0.254829592, -0.284496736, 1.421413741, -1.453152027, 1.061405429)
)

NO_COST = pl.CostEstimate(flops=0, bytes_accessed=0, transcendentals=0)

F32 = jnp.float32
BF16 = jnp.bfloat16


def split_source(v):
    terms = []
    for a, b in ((v[0] + v[2], v[1] + v[3]), (v[2], v[3]), (v[0], v[1])):
        terms += [a + b, b, a]
    return terms


def split_taps(t):
    terms = []
    for s in (
        (t[2], t[3], t[4]),
        (t[4] - t[2], t[5] - t[3], t[6] - t[4]),
        (t[0] - t[2], t[1] - t[3], t[2] - t[4]),
    ):
        terms += [s[1], s[2] - s[1], s[0] - s[1]]
    return terms


def split_grads(g):
    terms = []
    for a, b in ((g[0] + g[2], g[1] + g[3]), (g[0], g[1]), (g[2], g[3])):
        terms += [a + b, a, b]
    return terms


def join_outputs(m):
    pair = [(m[3 * k] + m[3 * k + 1], m[3 * k] + m[3 * k + 2]) for k in range(3)]
    return [
        pair[0][0] + pair[1][0],
        pair[0][1] + pair[1][1],
        pair[0][0] + pair[2][0],
        pair[0][1] + pair[2][1],
    ]


def join_taps(m):
    p, q, r = [
        (m[3 * k + 2], m[3 * k] - m[3 * k + 1] - m[3 * k + 2], m[3 * k + 1]) for k in range(3)
    ]
    return [
        r[0],
        r[1],
        p[0] - q[0] - r[0] + r[2],
        p[1] - q[1] - r[1],
        p[2] - q[2] - r[2] + q[0],
        q[1],
        q[2],
    ]


def tree_sum(terms):
    while len(terms) > 1:
        terms = [
            terms[k] + terms[k + 1] if k + 1 < len(terms) else terms[k]
            for k in range(0, len(terms), 2)
        ]
    return terms[0]


def stage_source(wanted, height, spread):
    row = height * SUB
    for at, (block, x) in enumerate(wanted):
        plane = block[x * row : (x + 1) * row, :].astype(F32)
        lines = [plane[y * SUB : (y + 1) * SUB, :] for y in range(height)]
        for j, term in enumerate(split_source(lines)):
            spread[j, at, SUB : 2 * SUB, :] = term


def rim_planes(left, right, planes):
    wanted = [(left, x) for x in range(planes - MARGIN, planes)]
    return wanted + [(right, x) for x in range(MARGIN)]


def all_planes(left, own, right, planes):
    rim = rim_planes(left, right, planes)
    return rim[:MARGIN] + [(own, x) for x in range(planes)] + rim[MARGIN:]


def by_core(core, inner, outer, stage):
    @pl.when(core[0] == 0)
    def _():
        stage(outer, inner)

    @pl.when(core[0] != 0)
    def _():
        stage(inner, outer)


def clear_rims(spread):
    zeros = jnp.zeros(spread.shape[:2] + (SUB, LANES), F32)
    spread[:, :, :SUB, :] = zeros
    spread[:, :, 2 * SUB :, :] = zeros


def stage_taps(taps, split):
    for dx in range(KS):
        rows = []
        for dy in range(KS):
            first = dx * KS * KS + dy * KS
            if first + SUB <= TAP_ROWS:
                rows.append(taps[first : first + SUB, :])
            else:
                rows.append(pltpu.roll(taps[TAP_ROWS - SUB : TAP_ROWS, :], SUB - 1, 0))
        for j, term in enumerate(split_taps(rows)):
            split[j, dx] = term


REVERSED = (0, 2, 1, 6, 8, 7, 3, 5, 4)


def convolve(spread, split, planes, held, flipped):
    terms = []
    for j in range(9):
        sums = [None] * planes
        for dz in range(KS):
            first = SUB - MARGIN + dz
            source = {x: spread[j, at, first : first + SUB, :] for at, x in enumerate(held)}
            weights = []
            for dx in range(KS):
                if flipped:
                    tap = split[REVERSED[j], KS - 1 - dx, KS - 1 - dz : KS - dz, :]
                else:
                    tap = split[j, dx, dz : dz + 1, :]
                weights.append(jnp.broadcast_to(tap, (SUB, LANES)))
            for x in range(planes):
                part = tree_sum(
                    [source[x + dx] * weights[dx] for dx in range(KS) if x + dx in source]
                )
                sums[x] = part if sums[x] is None else sums[x] + part
        terms.append(sums)
    return [join_outputs([terms[j][x] for j in range(9)]) for x in range(planes)]


def own_conv_kernel(planes, height, own, taps, gain, bias, out, split, vectors, spread):
    @pl.when(pl.program_id(0) == 0)
    def _():
        for k, line in enumerate((gain, bias)):
            vectors[k : k + 1, :] = line[...].reshape(1, -1)
        clear_rims(spread)

    stage_source([(own, x) for x in range(planes)], height, spread)
    stage_taps(taps, split)
    rows = convolve(spread, split, planes, range(MARGIN, MARGIN + planes), False)
    for x in range(planes):
        for y in range(height):
            at = (x * height + y) * SUB
            out[at : at + SUB, :] = rows[x][y]


def rim_conv_kernel(
    planes, height, core, inner, outer, split, partial, vectors, normed, centered, spread, conv
):
    step = pl.program_id(0)

    @pl.when(step == 0)
    def _():
        clear_rims(spread)

    def stage(left, right):
        stage_source(rim_planes(left, right, planes), height, spread)

    by_core(core, inner, outer, stage)
    held = list(range(MARGIN)) + list(range(MARGIN + planes, 2 * MARGIN + planes))
    rows = convolve(spread, split, planes, held, False)
    for x in range(planes):
        for y in range(height):
            at = (x * height + y) * SUB
            conv[step, at : at + SUB, :] = rows[x][y] + partial[at : at + SUB, :]

    @pl.when(step == pl.num_programs(0) - 1)
    def _():
        tiles = conv.shape[0]
        channels = tiles * LANES
        parts = [conv[k] for k in range(tiles)]
        gains = vectors[0:1, :]
        biases = vectors[1:2, :]
        average = jnp.sum(tree_sum(parts), axis=1, keepdims=True) * (1.0 / channels)
        parts = [part - average for part in parts]
        variance = jnp.sum(
            tree_sum([part * part for part in parts]), axis=1, keepdims=True
        ) * (1.0 / channels)
        inverse = lax.rsqrt(variance + norm_eps)
        for k in range(tiles):
            lanes = slice(k * LANES, (k + 1) * LANES)
            centered[:, lanes] = parts[k]
            value = parts[k] * inverse
            whole = (value * gains[:, lanes] + biases[:, lanes]).astype(BF16)
            normed[:, lanes] = whole


def input_grad_kernel(
    planes, height, core, inner, own, outer, taps, cotangent, out, token, spread, split
):
    @pl.when(pl.program_id(0) == 0)
    def _():
        clear_rims(spread)

    def stage(left, right):
        stage_source(all_planes(left, own, right, planes), height, spread)

    by_core(core, inner, outer, stage)
    stage_taps(taps, split)
    token[...] = jnp.zeros(token.shape, F32)
    rows = convolve(spread, split, planes, range(2 * MARGIN + planes), True)
    for x in range(planes):
        at = x * height * SUB
        whole = jnp.concatenate(rows[x], axis=0)
        upstream = cotangent[at : at + height * SUB, :].astype(F32)
        out[at : at + height * SUB, :] = (upstream + whole).astype(BF16)


def kernel_grad_kernel(
    planes,
    height,
    which,
    inner,
    own,
    outer,
    grads,
    small,
    sent,
    kept,
    passed,
    spread,
    products,
    joined,
    flat,
):
    passed[...] = grads[...]

    @pl.when(pl.program_id(0) == 0)
    def _():
        clear_rims(spread)
        products[...] = jnp.zeros(products.shape, F32)
        flat[...] = jnp.zeros(flat.shape, F32)

    def stage(left, right):
        stage_source(all_planes(left, own, right, planes), height, spread)

    by_core(which, inner, outer, stage)
    upstream = []
    for x in range(planes):
        plane = grads[x * height * SUB : (x + 1) * height * SUB, :].astype(F32)
        upstream.append(
            split_grads([plane[y * SUB : (y + 1) * SUB, :] for y in range(height)])
        )
    for j in range(9):
        for dz in range(KS):
            first = SUB - MARGIN + dz
            source = [
                spread[j, x, first : first + SUB, :] for x in range(planes + KS - 1)
            ]
            for dx in range(KS):
                products[j % 2, dx, dz * SUB : (dz + 1) * SUB, :] = tree_sum(
                    [source[x + dx] * upstream[x][j] for x in range(planes)]
                )
        for dx in range(KS):
            joined[j, dx] = tree_sum(
                [products[j % 2, dx, pl.ds(s, SUB, stride=SUB), :] for s in range(SUB)]
            )
    for dx in range(KS):
        for dy, tile in enumerate(join_taps([joined[j, dx] for j in range(9)])):
            row = dx * KS * KS + dy * KS
            flat[row : row + SUB, :] = tile
    flat[TAP_ROWS : TAP_ROWS + SUB, :] = small[...]
    step = pl.program_id(0)
    half = pl.num_programs(0) // 2

    @pl.when(step < half)
    def _():
        sent[...] = flat[...].astype(BF16)

    @pl.when(step >= half)
    def _():
        kept[...] = flat[...].astype(BF16)


def mlp_kernel(
    normed, weight_in, weight_out, centered, norm_gain, layer_scale, voxels, *rest
):
    *cotangents, block_out, conv_grad, small, together, mixed, back, mixed_grad = rest
    cotangent = cotangents[0]
    step = pl.program_id(0)
    gain = norm_gain[...].reshape(1, -1)
    scale = layer_scale[...].reshape(1, -1)

    @pl.when(step == 0)
    def _():
        mixed_grad[...] = (scale * cotangent[...].astype(F32)).astype(BF16)
        for k, part in enumerate(cotangents):
            together[k] = part[...]

    across = (((1,), (1,)), ((), ()))
    hidden = lax.dot_general(normed[...], weight_in[...], across, preferred_element_type=F32)
    act_grad = lax.dot_general(
        mixed_grad[...], weight_out[...], across, preferred_element_type=F32
    )
    activated, hidden_grad = slopes(hidden, act_grad)
    forward = jnp.dot(activated, weight_out[...], preferred_element_type=F32)
    backward = jnp.dot(hidden_grad, weight_in[...], preferred_element_type=F32)

    @pl.when(step == 0)
    def _():
        mixed[...] = forward
        back[...] = backward

    @pl.when(step > 0)
    def _():
        mixed[...] += forward
        back[...] += backward

    @pl.when(step == pl.num_programs(0) - 1)
    def _():
        channels = gain.shape[1]
        whole = mixed[...]
        block_out[...] = (voxels[...].astype(F32) + scale * whole).astype(BF16)
        scale_local = jnp.sum(cotangent[...].astype(F32) * whole, axis=0, keepdims=True)
        grad = back[...]
        deviation = centered[...]
        variance = jnp.sum(deviation * deviation, axis=1, keepdims=True) * (1.0 / channels)
        inverse = lax.rsqrt(variance + norm_eps)
        one = deviation * inverse
        bias_local = jnp.sum(grad, axis=0, keepdims=True)
        gain_local = jnp.sum(grad * one, axis=0, keepdims=True)
        small[...] = jnp.concatenate(
            [gain_local, bias_local, scale_local, jnp.zeros((SUB - 3, channels), F32)], axis=0
        )
        scaled = grad * gain
        average = jnp.sum(scaled, axis=1, keepdims=True) * (1.0 / channels)
        slant = jnp.sum(scaled * one, axis=1, keepdims=True) * (1.0 / channels)
        conv_grad[...] = (inverse * (scaled - average - one * slant)).astype(BF16)


def slopes(hidden, act_grad):
    bell = jnp.exp(-0.5 * hidden * hidden)
    below = 1.0 + (erf_step * root_half) * jnp.abs(hidden)
    t = pl.reciprocal(below, approx=True)
    t = t * (2.0 - below * t)
    poly = erf_terms[-1]
    for term in erf_terms[-2::-1]:
        poly = poly * t + term
    tail = poly * t * bell
    cover = jnp.where(hidden < 0.0, tail, 1.0 - tail)
    activated = (hidden * cover).astype(BF16)
    slope = cover + hidden * bell * inv_root_tau
    return activated, (act_grad * slope).astype(BF16)


def weight_grad_terms(weight_in, weight_out, scale, sets, aligned, mixed_grad):
    scales = scale[...].reshape(1, -1)
    at = 0
    for normed, cotangents in sets:
        line, rows = normed.shape[:2]
        for k in range(line):
            aligned[at : at + rows, :] = normed[k]
            upstream = cotangents[k].astype(F32)
            mixed_grad[at : at + rows, :] = (scales * upstream).astype(BF16)
            at += rows
    across = (((1,), (1,)), ((), ()))
    hidden = lax.dot_general(weight_in[...], aligned[...], across, preferred_element_type=F32)
    act_grad = lax.dot_general(weight_out[...], mixed_grad[...], across, preferred_element_type=F32)
    activated, hidden_grad = slopes(hidden, act_grad)
    return (
        jnp.dot(hidden_grad, aligned[...], preferred_element_type=F32),
        jnp.dot(activated, mixed_grad[...], preferred_element_type=F32),
    )


def far_side_kernel(
    which, weight_in, weight_out, scale, norm, cot, other_norm, other_cot, sent, aligned, mixed_grad
):
    sets = ((norm, cot), (other_norm, other_cot))
    terms = weight_grad_terms(weight_in, weight_out, scale, sets, aligned, mixed_grad)
    for k in range(2):
        sent[k] = terms[k].astype(BF16)


def near_side_kernel(
    which,
    weight_in,
    weight_out,
    scale,
    norm,
    cot,
    other_norm,
    other_cot,
    got,
    in_grad,
    out_grad,
    aligned,
    mixed_grad,
):
    sets = ((norm, cot), (other_norm, other_cot))
    terms = weight_grad_terms(weight_in, weight_out, scale, sets, aligned, mixed_grad)
    for k, out in enumerate((in_grad, out_grad)):
        out[...] = terms[k] + got[k].astype(F32)


def chip_sum_kernel(kept, got, *rest):
    *blocks, out, together = rest
    for k, block in enumerate(blocks):
        together[k] = block[...]
    out[...] = (kept[...].astype(F32) + got[...].astype(F32)).astype(BF16)


def spread_sum_kernel(parts, out):
    total = tree_sum([parts[k].astype(F32) for k in range(parts.shape[0])]).astype(BF16)
    for copy in range(out.shape[0]):
        out[copy] = total


def unpack_kernel(core, own, other, out, *small):
    piece, wide = own.shape[1:]

    def unpack(*halves):
        last = []
        for side, parts in enumerate(halves):
            lanes = slice(side * wide, (side + 1) * wide)
            for k in range(-(-TAP_ROWS // piece)):
                first = k * piece
                length = min(piece, TAP_ROWS - first)
                out[first : first + length, lanes] = parts[k].astype(F32)[:length, :]
            k = TAP_ROWS // piece
            last.append(parts[k].astype(F32))
        rows = jnp.concatenate(last, axis=1)
        first = TAP_ROWS % piece
        for k, line in enumerate(small):
            line[...] = rows[first + k : first + k + 1, :].reshape(line.shape)

    by_core(core, own, other, lambda outer, inner: unpack(inner, outer))


def params(limit=48):
    return pltpu.CompilerParams(vmem_limit_bytes=limit * 1024 * 1024)


def follow(kernel, scalars, inputs, count):
    def body(*refs):
        head = refs[: scalars + inputs]
        return kernel(*head, *refs[scalars + inputs + count :])

    return body


IN_PLACE = pl.BlockSpec(memory_space=pl.ANY)


def lane_block(rows):
    return pl.BlockSpec((rows, LANES), lambda c, *_: (0, c))


def whole_block(*shape):
    return pl.BlockSpec(shape, lambda *_: (0,) * len(shape))


def rims(cells):
    count = lax.axis_size("row")
    between = [(i, i + 1) for i in range(1, count - 1, 2)]
    return (
        lax.ppermute(cells, "row", [(i, i ^ 1) for i in range(count)]),
        lax.ppermute(cells, "row", between + [(j, i) for i, j in between]),
    )


def on_device(
    voxels, dw_kernel, norm_gain, norm_bias, weight_in, weight_out, layer_scale, cotangent
):
    planes, height, breadth, channels = voxels.shape
    rows = planes * height * breadth
    units = weight_in.shape[0]
    count = lax.axis_size("row")
    me = lax.axis_index("row")
    quad = 4
    line = count // quad
    other_core = [(i, i ^ 1) for i in range(count)]
    other_side = [(i, i ^ 2) for i in range(count)]
    tiles = channels // LANES

    own = voxels.reshape(rows, channels)
    upstream = cotangent.reshape(rows, channels)
    core = lax.rem(me, 2).astype(jnp.int32)
    parity = core.reshape(1)

    inner, outer = rims(own)

    def along_line(cells, steps):
        return lax.ppermute(cells, "row", [(i, (i + quad * steps) % count) for i in range(count)])

    upstream_line = [upstream] + [None] * (line - 1)
    upstream_line[1] = along_line(upstream, 1)
    upstream_line[-1] = along_line(upstream, -1)

    def spread_of(held):
        return pltpu.VMEM((9, held, PAD, LANES), F32)

    split_block = pl.BlockSpec((None, 9, KS, SUB, LANES), lambda c, *_: (c, 0, 0, 0, 0))
    partial, split, vectors = pl.pallas_call(
        functools.partial(own_conv_kernel, planes, height),
        grid=(tiles,),
        in_specs=[lane_block(rows), lane_block(TAP_ROWS)] + [whole_block(channels)] * 2,
        out_specs=[lane_block(rows), split_block, whole_block(SUB, channels)],
        out_shape=[
            jax.ShapeDtypeStruct((rows, channels), F32),
            jax.ShapeDtypeStruct((tiles, 9, KS, SUB, LANES), F32),
            jax.ShapeDtypeStruct((SUB, channels), F32),
        ],
        scratch_shapes=[spread_of(planes)],
        compiler_params=params(),
        cost_estimate=NO_COST,
        name="own_conv",
    )(own, dw_kernel, norm_gain, norm_bias)

    for k in range(2, line - 1):
        upstream_line[k] = along_line(upstream_line[k - 1], 1)
    normed, centered = pl.pallas_call(
        follow(functools.partial(rim_conv_kernel, planes, height), 1, 5, 2),
        grid_spec=pltpu.PrefetchScalarGridSpec(
            num_scalar_prefetch=1,
            grid=(tiles,),
            in_specs=[
                lane_block(rows),
                lane_block(rows),
                split_block,
                lane_block(rows),
                whole_block(SUB, channels),
                IN_PLACE,
                IN_PLACE,
            ],
            out_specs=[
                whole_block(rows, channels),
                whole_block(rows, channels),
            ],
            scratch_shapes=[spread_of(2 * MARGIN), pltpu.VMEM((tiles, rows, LANES), F32)],
        ),
        out_shape=[
            jax.ShapeDtypeStruct((rows, channels), BF16),
            jax.ShapeDtypeStruct((rows, channels), F32),
        ],
        compiler_params=params(),
        cost_estimate=NO_COST,
        name="rim_conv",
    )(
        parity,
        inner,
        outer,
        split,
        partial,
        vectors,
        upstream_line[1],
        upstream_line[-1],
    )

    normed, upstream_line[2] = lax.optimization_barrier((normed, upstream_line[2]))
    norm_line = [normed] + [None] * (line - 1)
    norm_line[1] = along_line(normed, 1)
    norm_line[-1] = along_line(normed, -1)

    block = 512
    whole = whole_block(rows, channels)
    block_out, conv_grad, small, cotangents = pl.pallas_call(
        mlp_kernel,
        grid=(units // block,),
        in_specs=[
            whole,
            pl.BlockSpec((block, channels), lambda f: (f, 0)),
            pl.BlockSpec((block, channels), lambda f: (f, 0)),
            whole,
            whole_block(channels),
            whole_block(channels),
        ]
        + [whole] * (1 + line),
        out_specs=[
            whole,
            whole,
            whole_block(SUB, channels),
            whole_block(line, rows, channels),
        ],
        out_shape=[
            jax.ShapeDtypeStruct((rows, channels), BF16),
            jax.ShapeDtypeStruct((rows, channels), BF16),
            jax.ShapeDtypeStruct((SUB, channels), F32),
            jax.ShapeDtypeStruct((line, rows, channels), BF16),
        ],
        scratch_shapes=[
            pltpu.VMEM((rows, channels), F32),
            pltpu.VMEM((rows, channels), F32),
            pltpu.VMEM((rows, channels), BF16),
        ],
        compiler_params=params(),
        cost_estimate=NO_COST,
        name="mlp_both_ways",
    )(normed, weight_in, weight_out, centered, norm_gain, layer_scale, own, *upstream_line)

    small, norm_line[1], norm_line[-1] = lax.optimization_barrier(
        (small, norm_line[1], norm_line[-1])
    )
    for k in range(2, line - 1):
        norm_line[k] = along_line(norm_line[k - 1], 1)

    half = count // 2
    alike = [[2 * k + p for k in range(half)] for p in range(2)]
    half_tiles = tiles // 2
    wide = half_tiles * LANES
    piece = -(-(TAP_ROWS + SUB) // half)
    piece += -piece % (2 * SUB)
    padded = piece * half

    def tile_of(block_rows):
        def at(c, w):
            return 0, (c + w[1] * half_tiles) % tiles

        return pl.BlockSpec((block_rows, LANES), at)

    half_sent, half_kept, conv_grad = pl.pallas_call(
        functools.partial(kernel_grad_kernel, planes, height),
        grid_spec=pltpu.PrefetchScalarGridSpec(
            num_scalar_prefetch=1,
            grid=(tiles,),
            in_specs=[tile_of(rows), tile_of(rows), tile_of(rows), tile_of(rows), tile_of(SUB)],
            out_specs=[
                pl.BlockSpec((padded, LANES), lambda c, w: (0, jnp.minimum(c, half_tiles - 1))),
                pl.BlockSpec((padded, LANES), lambda c, w: (0, jnp.maximum(c - half_tiles, 0))),
                tile_of(rows),
            ],
            scratch_shapes=[
                spread_of(2 * MARGIN + planes),
                pltpu.VMEM((2, KS, SUB * SUB, LANES), F32),
                pltpu.VMEM((9, KS, SUB, LANES), F32),
                pltpu.VMEM((padded, LANES), F32),
            ],
        ),
        out_shape=[jax.ShapeDtypeStruct((padded, wide), BF16)] * 2
        + [
            jax.ShapeDtypeStruct((rows, channels), BF16),
        ],
        compiler_params=params(),
        cost_estimate=NO_COST,
        name="kernel_grad_terms",
    )(jnp.stack([core, 1 - core]), inner, own, outer, conv_grad, small)

    half_got = lax.ppermute(half_sent, "row", other_core)
    conv_grad, norm_line[2] = lax.optimization_barrier((conv_grad, norm_line[2]))
    grad_inner, grad_outer = rims(conv_grad)
    sums, gathered = pl.pallas_call(
        follow(chip_sum_kernel, 0, 2 + line, 2),
        in_specs=[whole_block(padded, wide)] * 2 + [whole] * line + [IN_PLACE] * 2,
        out_specs=[whole_block(padded, wide), whole_block(line, rows, channels)],
        out_shape=[
            jax.ShapeDtypeStruct((padded, wide), BF16),
            jax.ShapeDtypeStruct((line, rows, channels), BF16),
        ],
        grid=(1,),
        compiler_params=params(),
        cost_estimate=NO_COST,
        name="kernel_grad_chip_sum",
    )(half_kept, half_got, *norm_line, grad_inner, grad_outer)

    share = units // count
    tokens = line * rows
    base = me // quad * quad
    side = lax.rem(me, quad) // 2
    far = base + 2 * (1 - side)
    near = base + 2 * side
    which = jnp.stack([far + core, near + core]).astype(jnp.int32)
    other_gathered = lax.ppermute(gathered, "row", other_core)
    other_cotangents = lax.ppermute(cotangents, "row", other_core)

    def side_terms(kernel, number, more, after, outs, name):
        chunk = pl.BlockSpec((share, channels), lambda _, w: (w[number], 0))
        return pl.pallas_call(
            follow(kernel, 1, 7 + len(more), len(after)),
            grid_spec=pltpu.PrefetchScalarGridSpec(
                num_scalar_prefetch=1,
                grid=(1,),
                in_specs=[chunk, chunk, whole_block(channels)]
                + [whole_block(line, rows, channels)] * 4
                + [whole_block(*part.shape) for part in more]
                + [IN_PLACE] * len(after),
                out_specs=[whole_block(*out.shape) for out in outs],
                scratch_shapes=[pltpu.VMEM((2 * tokens, channels), BF16)] * 2,
            ),
            out_shape=outs,
            compiler_params=params(),
            cost_estimate=NO_COST,
            name=name,
        )(
            which,
            weight_in,
            weight_out,
            layer_scale,
            gathered,
            cotangents,
            other_gathered,
            other_cotangents,
            *more,
            *after,
        )

    pair = jax.ShapeDtypeStruct((2, share, channels), BF16)
    single = jax.ShapeDtypeStruct((share, channels), F32)
    (sent,) = side_terms(
        far_side_kernel, 0, [], [sums], [pair], "weight_grads_far_side"
    )
    got = lax.ppermute(sent, "row", other_side)
    scattered = lax.all_to_all(
        sums.reshape(half, piece, wide),
        "row",
        split_axis=0,
        concat_axis=0,
        tiled=True,
        axis_index_groups=alike,
    )
    voxel_grad, token = pl.pallas_call(
        follow(functools.partial(input_grad_kernel, planes, height), 1, 5, 1),
        grid_spec=pltpu.PrefetchScalarGridSpec(
            num_scalar_prefetch=1,
            grid=(tiles,),
            in_specs=[
                lane_block(rows),
                lane_block(rows),
                lane_block(rows),
                lane_block(TAP_ROWS),
                lane_block(rows),
                IN_PLACE,
            ],
            out_specs=[lane_block(rows), whole_block(SUB, LANES)],
            scratch_shapes=[
                spread_of(2 * MARGIN + planes),
                pltpu.VMEM((9, KS, SUB, LANES), F32),
            ],
        ),
        out_shape=[
            jax.ShapeDtypeStruct((rows, channels), BF16),
            jax.ShapeDtypeStruct((SUB, LANES), F32),
        ],
        compiler_params=params(),
        cost_estimate=NO_COST,
        name="input_grad_conv",
    )(parity, grad_inner, conv_grad, grad_outer, dw_kernel, upstream, sent)

    copies = pl.pallas_call(
        follow(spread_sum_kernel, 0, 1, 1),
        in_specs=[whole_block(half, piece, wide), IN_PLACE],
        out_specs=whole_block(half, piece, wide),
        out_shape=jax.ShapeDtypeStruct((half, piece, wide), BF16),
        grid=(1,),
        compiler_params=params(),
        cost_estimate=NO_COST,
        name="kernel_grad_sum",
    )(scattered, token)
    totals = lax.all_to_all(
        copies, "row", split_axis=0, concat_axis=0, tiled=True, axis_index_groups=alike
    )
    weight_in_grad, weight_out_grad = side_terms(
        near_side_kernel, 1, [got], [copies], [single, single], "weight_grads_near_side"
    )
    totals, weight_in_grad = lax.optimization_barrier((totals, weight_in_grad))
    other_totals = lax.ppermute(totals, "row", other_core)
    kernel_grad, *vector_grads = pl.pallas_call(
        unpack_kernel,
        grid_spec=pltpu.PrefetchScalarGridSpec(
            num_scalar_prefetch=1,
            grid=(1,),
            in_specs=[whole_block(half, piece, wide)] * 2,
            out_specs=[whole_block(TAP_ROWS, channels)] + [whole_block(channels)] * 3,
        ),
        out_shape=[jax.ShapeDtypeStruct((TAP_ROWS, channels), F32)]
        + [jax.ShapeDtypeStruct((channels,), F32)] * 3,
        compiler_params=params(),
        cost_estimate=NO_COST,
        name="kernel_grad_unpack",
    )(parity, totals, other_totals)

    return (
        block_out.reshape(voxels.shape),
        voxel_grad.reshape(voxels.shape),
        kernel_grad,
        *vector_grads,
        weight_in_grad,
        weight_out_grad,
    )


def solution(mesh):
    in_specs = (
        P(("group", "row"), None, None, None),
        P(),
        P(),
        P(),
        P(),
        P(),
        P(),
        P(("group", "row"), None, None, None),
    )
    out_specs = (
        P(("group", "row"), None, None, None),
        P(("group", "row"), None, None, None),
        P("group", None),
        P("group"),
        P("group"),
        P("group"),
        P(("group", "row"), None),
        P(("group", "row"), None),
    )
    return jax.shard_map(
        on_device, mesh=mesh, in_specs=in_specs, out_specs=out_specs, check_vma=False
    )
```

```python
import functools

import jax
import jax.numpy as jnp
from jax import lax
from jax.experimental import pallas as pl
from jax.experimental.pallas import tpu as pltpu
from jax.sharding import PartitionSpec as P

KS = 7
MARGIN = KS // 2
LANES = 128
SUB = 8
PAD = 3 * SUB
TAP_ROWS = KS * KS * KS

root_half = 0.7071067811865476
inv_root_tau = 0.3989422804014327
norm_eps = 1e-06
erf_step = 0.3275911
erf_terms = tuple(
    0.5 * a for a in (0.254829592, -0.284496736, 1.421413741, -1.453152027, 1.061405429)
)

NO_COST = pl.CostEstimate(flops=0, bytes_accessed=0, transcendentals=0)

F32 = jnp.float32
BF16 = jnp.bfloat16


def split_source(v):
    terms = []
    for a, b in ((v[0] + v[2], v[1] + v[3]), (v[2], v[3]), (v[0], v[1])):
        terms += [a + b, b, a]
    return terms


def split_taps(t):
    terms = []
    for s in (
        (t[2], t[3], t[4]),
        (t[4] - t[2], t[5] - t[3], t[6] - t[4]),
        (t[0] - t[2], t[1] - t[3], t[2] - t[4]),
    ):
        terms += [s[1], s[2] - s[1], s[0] - s[1]]
    return terms


def split_grads(g):
    terms = []
    for a, b in ((g[0] + g[2], g[1] + g[3]), (g[0], g[1]), (g[2], g[3])):
        terms += [a + b, a, b]
    return terms


def join_outputs(m):
    pair = [(m[3 * k] + m[3 * k + 1], m[3 * k] + m[3 * k + 2]) for k in range(3)]
    return [
        pair[0][0] + pair[1][0],
        pair[0][1] + pair[1][1],
        pair[0][0] + pair[2][0],
        pair[0][1] + pair[2][1],
    ]


def join_taps(m):
    p, q, r = [
        (m[3 * k + 2], m[3 * k] - m[3 * k + 1] - m[3 * k + 2], m[3 * k + 1]) for k in range(3)
    ]
    return [
        r[0],
        r[1],
        p[0] - q[0] - r[0] + r[2],
        p[1] - q[1] - r[1],
        p[2] - q[2] - r[2] + q[0],
        q[1],
        q[2],
    ]


def tree_sum(terms):
    while len(terms) > 1:
        terms = [
            terms[k] + terms[k + 1] if k + 1 < len(terms) else terms[k]
            for k in range(0, len(terms), 2)
        ]
    return terms[0]


def stage_source(wanted, height, spread):
    row = height * SUB
    for at, (block, x) in enumerate(wanted):
        plane = block[x * row : (x + 1) * row, :].astype(F32)
        lines = [plane[y * SUB : (y + 1) * SUB, :] for y in range(height)]
        for j, term in enumerate(split_source(lines)):
            spread[j, at, SUB : 2 * SUB, :] = term


def rim_planes(left, right, planes):
    wanted = [(left, x) for x in range(planes - MARGIN, planes)]
    return wanted + [(right, x) for x in range(MARGIN)]


def all_planes(left, own, right, planes):
    rim = rim_planes(left, right, planes)
    return rim[:MARGIN] + [(own, x) for x in range(planes)] + rim[MARGIN:]


def by_core(core, inner, outer, stage):
    @pl.when(core[0] == 0)
    def _():
        stage(outer, inner)

    @pl.when(core[0] != 0)
    def _():
        stage(inner, outer)


def clear_rims(spread):
    zeros = jnp.zeros(spread.shape[:2] + (SUB, LANES), F32)
    spread[:, :, :SUB, :] = zeros
    spread[:, :, 2 * SUB :, :] = zeros


def stage_taps(taps, split):
    for dx in range(KS):
        rows = []
        for dy in range(KS):
            first = dx * KS * KS + dy * KS
            if first + SUB <= TAP_ROWS:
                rows.append(taps[first : first + SUB, :])
            else:
                rows.append(pltpu.roll(taps[TAP_ROWS - SUB : TAP_ROWS, :], SUB - 1, 0))
        for j, term in enumerate(split_taps(rows)):
            split[j, dx] = term


REVERSED = (0, 2, 1, 6, 8, 7, 3, 5, 4)


def convolve(spread, split, planes, held, flipped):
    terms = []
    for j in range(9):
        sums = [None] * planes
        for dz in range(KS):
            first = SUB - MARGIN + dz
            source = {x: spread[j, at, first : first + SUB, :] for at, x in enumerate(held)}
            weights = []
            for dx in range(KS):
                if flipped:
                    tap = split[REVERSED[j], KS - 1 - dx, KS - 1 - dz : KS - dz, :]
                else:
                    tap = split[j, dx, dz : dz + 1, :]
                weights.append(jnp.broadcast_to(tap, (SUB, LANES)))
            for x in range(planes):
                part = tree_sum(
                    [source[x + dx] * weights[dx] for dx in range(KS) if x + dx in source]
                )
                sums[x] = part if sums[x] is None else sums[x] + part
        terms.append(sums)
    return [join_outputs([terms[j][x] for j in range(9)]) for x in range(planes)]


def own_conv_kernel(planes, height, own, taps, gain, bias, out, split, vectors, spread):
    @pl.when(pl.program_id(0) == 0)
    def _():
        for k, line in enumerate((gain, bias)):
            vectors[k : k + 1, :] = line[...].reshape(1, -1)
        clear_rims(spread)

    stage_source([(own, x) for x in range(planes)], height, spread)
    stage_taps(taps, split)
    rows = convolve(spread, split, planes, range(MARGIN, MARGIN + planes), False)
    for x in range(planes):
        for y in range(height):
            at = (x * height + y) * SUB
            out[at : at + SUB, :] = rows[x][y]


def rim_conv_kernel(
    planes, height, core, inner, outer, split, partial, vectors, normed, centered, spread, conv
):
    step = pl.program_id(0)

    @pl.when(step == 0)
    def _():
        clear_rims(spread)

    def stage(left, right):
        stage_source(rim_planes(left, right, planes), height, spread)

    by_core(core, inner, outer, stage)
    held = list(range(MARGIN)) + list(range(MARGIN + planes, 2 * MARGIN + planes))
    rows = convolve(spread, split, planes, held, False)
    for x in range(planes):
        for y in range(height):
            at = (x * height + y) * SUB
            conv[step, at : at + SUB, :] = rows[x][y] + partial[at : at + SUB, :]

    @pl.when(step == pl.num_programs(0) - 1)
    def _():
        tiles = conv.shape[0]
        channels = tiles * LANES
        parts = [conv[k] for k in range(tiles)]
        gains = vectors[0:1, :]
        biases = vectors[1:2, :]
        average = jnp.sum(tree_sum(parts), axis=1, keepdims=True) * (1.0 / channels)
        parts = [part - average for part in parts]
        variance = jnp.sum(
            tree_sum([part * part for part in parts]), axis=1, keepdims=True
        ) * (1.0 / channels)
        inverse = lax.rsqrt(variance + norm_eps)
        for k in range(tiles):
            lanes = slice(k * LANES, (k + 1) * LANES)
            centered[:, lanes] = parts[k]
            value = parts[k] * inverse
            whole = (value * gains[:, lanes] + biases[:, lanes]).astype(BF16)
            normed[:, lanes] = whole


def input_grad_kernel(
    planes, height, core, inner, own, outer, taps, cotangent, out, token, spread, split
):
    @pl.when(pl.program_id(0) == 0)
    def _():
        clear_rims(spread)

    def stage(left, right):
        stage_source(all_planes(left, own, right, planes), height, spread)

    by_core(core, inner, outer, stage)
    stage_taps(taps, split)
    token[...] = jnp.zeros(token.shape, F32)
    rows = convolve(spread, split, planes, range(2 * MARGIN + planes), True)
    for x in range(planes):
        at = x * height * SUB
        whole = jnp.concatenate(rows[x], axis=0)
        upstream = cotangent[at : at + height * SUB, :].astype(F32)
        out[at : at + height * SUB, :] = (upstream + whole).astype(BF16)


def kernel_grad_kernel(
    planes,
    height,
    which,
    inner,
    own,
    outer,
    grads,
    small,
    sent,
    kept,
    spread,
    products,
    joined,
    flat,
):
    @pl.when(pl.program_id(0) == 0)
    def _():
        clear_rims(spread)
        products[...] = jnp.zeros(products.shape, F32)
        flat[...] = jnp.zeros(flat.shape, F32)

    def stage(left, right):
        stage_source(all_planes(left, own, right, planes), height, spread)

    by_core(which, inner, outer, stage)
    upstream = []
    for x in range(planes):
        plane = grads[x * height * SUB : (x + 1) * height * SUB, :].astype(F32)
        upstream.append(
            split_grads([plane[y * SUB : (y + 1) * SUB, :] for y in range(height)])
        )
    for j in range(9):
        for dz in range(KS):
            first = SUB - MARGIN + dz
            source = [
                spread[j, x, first : first + SUB, :] for x in range(planes + KS - 1)
            ]
            for dx in range(KS):
                products[j % 2, dx, dz * SUB : (dz + 1) * SUB, :] = tree_sum(
                    [source[x + dx] * upstream[x][j] for x in range(planes)]
                )
        for dx in range(KS):
            joined[j, dx] = tree_sum(
                [products[j % 2, dx, pl.ds(s, SUB, stride=SUB), :] for s in range(SUB)]
            )
    for dx in range(KS):
        for dy, tile in enumerate(join_taps([joined[j, dx] for j in range(9)])):
            row = dx * KS * KS + dy * KS
            flat[row : row + SUB, :] = tile
    flat[TAP_ROWS : TAP_ROWS + SUB, :] = small[...]
    step = pl.program_id(0)
    half = pl.num_programs(0) // 2

    @pl.when(step < half)
    def _():
        sent[...] = flat[...].astype(BF16)

    @pl.when(step >= half)
    def _():
        kept[...] = flat[...].astype(BF16)


def mlp_kernel(
    normed, weight_in, weight_out, centered, norm_gain, layer_scale, voxels, *rest
):
    *cotangents, block_out, conv_grad, small, together, mixed, back, mixed_grad = rest
    cotangent = cotangents[0]
    step = pl.program_id(0)
    gain = norm_gain[...].reshape(1, -1)
    scale = layer_scale[...].reshape(1, -1)

    @pl.when(step == 0)
    def _():
        mixed_grad[...] = (scale * cotangent[...].astype(F32)).astype(BF16)
        for k, part in enumerate(cotangents):
            together[k] = part[...]

    across = (((1,), (1,)), ((), ()))
    hidden = lax.dot_general(normed[...], weight_in[...], across, preferred_element_type=F32)
    act_grad = lax.dot_general(
        mixed_grad[...], weight_out[...], across, preferred_element_type=F32
    )
    activated, hidden_grad = slopes(hidden, act_grad)
    forward = jnp.dot(activated, weight_out[...], preferred_element_type=F32)
    backward = jnp.dot(hidden_grad, weight_in[...], preferred_element_type=F32)

    @pl.when(step == 0)
    def _():
        mixed[...] = forward
        back[...] = backward

    @pl.when(step > 0)
    def _():
        mixed[...] += forward
        back[...] += backward

    @pl.when(step == pl.num_programs(0) - 1)
    def _():
        channels = gain.shape[1]
        whole = mixed[...]
        block_out[...] = (voxels[...].astype(F32) + scale * whole).astype(BF16)
        scale_local = jnp.sum(cotangent[...].astype(F32) * whole, axis=0, keepdims=True)
        grad = back[...]
        deviation = centered[...]
        variance = jnp.sum(deviation * deviation, axis=1, keepdims=True) * (1.0 / channels)
        inverse = lax.rsqrt(variance + norm_eps)
        one = deviation * inverse
        bias_local = jnp.sum(grad, axis=0, keepdims=True)
        gain_local = jnp.sum(grad * one, axis=0, keepdims=True)
        small[...] = jnp.concatenate(
            [gain_local, bias_local, scale_local, jnp.zeros((SUB - 3, channels), F32)], axis=0
        )
        scaled = grad * gain
        average = jnp.sum(scaled, axis=1, keepdims=True) * (1.0 / channels)
        slant = jnp.sum(scaled * one, axis=1, keepdims=True) * (1.0 / channels)
        conv_grad[...] = (inverse * (scaled - average - one * slant)).astype(BF16)


def slopes(hidden, act_grad):
    bell = jnp.exp(-0.5 * hidden * hidden)
    below = 1.0 + (erf_step * root_half) * jnp.abs(hidden)
    t = pl.reciprocal(below, approx=True)
    t = t * (2.0 - below * t)
    poly = erf_terms[-1]
    for term in erf_terms[-2::-1]:
        poly = poly * t + term
    tail = poly * t * bell
    cover = jnp.where(hidden < 0.0, tail, 1.0 - tail)
    activated = (hidden * cover).astype(BF16)
    slope = cover + hidden * bell * inv_root_tau
    return activated, (act_grad * slope).astype(BF16)


def weight_grad_terms(weight_in, weight_out, scale, sets, aligned, mixed_grad):
    scales = scale[...].reshape(1, -1)
    at = 0
    for normed, cotangents in sets:
        line, rows = normed.shape[:2]
        for k in range(line):
            aligned[at : at + rows, :] = normed[k]
            upstream = cotangents[k].astype(F32)
            mixed_grad[at : at + rows, :] = (scales * upstream).astype(BF16)
            at += rows
    across = (((1,), (1,)), ((), ()))
    hidden = lax.dot_general(weight_in[...], aligned[...], across, preferred_element_type=F32)
    act_grad = lax.dot_general(weight_out[...], mixed_grad[...], across, preferred_element_type=F32)
    activated, hidden_grad = slopes(hidden, act_grad)
    return (
        jnp.dot(hidden_grad, aligned[...], preferred_element_type=F32),
        jnp.dot(activated, mixed_grad[...], preferred_element_type=F32),
    )


def far_side_kernel(
    which, weight_in, weight_out, scale, norm, cot, other_norm, other_cot, sent, aligned, mixed_grad
):
    sets = ((norm, cot), (other_norm, other_cot))
    terms = weight_grad_terms(weight_in, weight_out, scale, sets, aligned, mixed_grad)
    for k in range(2):
        sent[k] = terms[k].astype(BF16)


def near_side_kernel(
    which,
    weight_in,
    weight_out,
    scale,
    norm,
    cot,
    other_norm,
    other_cot,
    got,
    in_grad,
    out_grad,
    aligned,
    mixed_grad,
):
    sets = ((norm, cot), (other_norm, other_cot))
    terms = weight_grad_terms(weight_in, weight_out, scale, sets, aligned, mixed_grad)
    for k, out in enumerate((in_grad, out_grad)):
        out[...] = terms[k] + got[k].astype(F32)


def chip_sum_kernel(kept, got, *rest):
    *blocks, out, together = rest
    for k, block in enumerate(blocks):
        together[k] = block[...]
    out[...] = (kept[...].astype(F32) + got[...].astype(F32)).astype(BF16)


def spread_sum_kernel(parts, out):
    total = tree_sum([parts[k].astype(F32) for k in range(parts.shape[0])]).astype(BF16)
    for copy in range(out.shape[0]):
        out[copy] = total


def unpack_kernel(core, own, other, out, *small):
    piece, wide = own.shape[1:]

    def unpack(*halves):
        last = []
        for side, parts in enumerate(halves):
            lanes = slice(side * wide, (side + 1) * wide)
            for k in range(-(-TAP_ROWS // piece)):
                first = k * piece
                length = min(piece, TAP_ROWS - first)
                out[first : first + length, lanes] = parts[k].astype(F32)[:length, :]
            k = TAP_ROWS // piece
            last.append(parts[k].astype(F32))
        rows = jnp.concatenate(last, axis=1)
        first = TAP_ROWS % piece
        for k, line in enumerate(small):
            line[...] = rows[first + k : first + k + 1, :].reshape(line.shape)

    by_core(core, own, other, lambda outer, inner: unpack(inner, outer))


def params(limit=48):
    return pltpu.CompilerParams(vmem_limit_bytes=limit * 1024 * 1024)


def follow(kernel, scalars, inputs, count):
    def body(*refs):
        head = refs[: scalars + inputs]
        return kernel(*head, *refs[scalars + inputs + count :])

    return body


IN_PLACE = pl.BlockSpec(memory_space=pl.ANY)


def lane_block(rows):
    return pl.BlockSpec((rows, LANES), lambda c, *_: (0, c))


def whole_block(*shape):
    return pl.BlockSpec(shape, lambda *_: (0,) * len(shape))


def rims(cells):
    count = lax.axis_size("row")
    between = [(i, i + 1) for i in range(1, count - 1, 2)]
    return (
        lax.ppermute(cells, "row", [(i, i ^ 1) for i in range(count)]),
        lax.ppermute(cells, "row", between + [(j, i) for i, j in between]),
    )


def on_device(
    voxels, dw_kernel, norm_gain, norm_bias, weight_in, weight_out, layer_scale, cotangent
):
    planes, height, breadth, channels = voxels.shape
    rows = planes * height * breadth
    units = weight_in.shape[0]
    count = lax.axis_size("row")
    me = lax.axis_index("row")
    quad = 4
    line = count // quad
    other_core = [(i, i ^ 1) for i in range(count)]
    other_side = [(i, i ^ 2) for i in range(count)]
    tiles = channels // LANES

    own = voxels.reshape(rows, channels)
    upstream = cotangent.reshape(rows, channels)
    core = lax.rem(me, 2).astype(jnp.int32)
    parity = core.reshape(1)

    inner, outer = rims(own)

    def along_line(cells, steps):
        return lax.ppermute(cells, "row", [(i, (i + quad * steps) % count) for i in range(count)])

    upstream_line = [upstream] + [None] * (line - 1)
    upstream_line[1] = along_line(upstream, 1)
    upstream_line[-1] = along_line(upstream, -1)

    def spread_of(held):
        return pltpu.VMEM((9, held, PAD, LANES), F32)

    split_block = pl.BlockSpec((None, 9, KS, SUB, LANES), lambda c, *_: (c, 0, 0, 0, 0))
    partial, split, vectors = pl.pallas_call(
        functools.partial(own_conv_kernel, planes, height),
        grid=(tiles,),
        in_specs=[lane_block(rows), lane_block(TAP_ROWS)] + [whole_block(channels)] * 2,
        out_specs=[lane_block(rows), split_block, whole_block(SUB, channels)],
        out_shape=[
            jax.ShapeDtypeStruct((rows, channels), F32),
            jax.ShapeDtypeStruct((tiles, 9, KS, SUB, LANES), F32),
            jax.ShapeDtypeStruct((SUB, channels), F32),
        ],
        scratch_shapes=[spread_of(planes)],
        compiler_params=params(),
        cost_estimate=NO_COST,
        name="own_conv",
    )(own, dw_kernel, norm_gain, norm_bias)

    for k in range(2, line - 1):
        upstream_line[k] = along_line(upstream_line[k - 1], 1)
    normed, centered = pl.pallas_call(
        follow(functools.partial(rim_conv_kernel, planes, height), 1, 5, 2),
        grid_spec=pltpu.PrefetchScalarGridSpec(
            num_scalar_prefetch=1,
            grid=(tiles,),
            in_specs=[
                lane_block(rows),
                lane_block(rows),
                split_block,
                lane_block(rows),
                whole_block(SUB, channels),
                IN_PLACE,
                IN_PLACE,
            ],
            out_specs=[
                whole_block(rows, channels),
                whole_block(rows, channels),
            ],
            scratch_shapes=[spread_of(2 * MARGIN), pltpu.VMEM((tiles, rows, LANES), F32)],
        ),
        out_shape=[
            jax.ShapeDtypeStruct((rows, channels), BF16),
            jax.ShapeDtypeStruct((rows, channels), F32),
        ],
        compiler_params=params(),
        cost_estimate=NO_COST,
        name="rim_conv",
    )(
        parity,
        inner,
        outer,
        split,
        partial,
        vectors,
        upstream_line[1],
        upstream_line[-1],
    )

    normed, upstream_line[2] = lax.optimization_barrier((normed, upstream_line[2]))
    norm_line = [normed] + [None] * (line - 1)
    norm_line[1] = along_line(normed, 1)
    norm_line[-1] = along_line(normed, -1)

    block = 512
    whole = whole_block(rows, channels)
    block_out, conv_grad, small, cotangents = pl.pallas_call(
        mlp_kernel,
        grid=(units // block,),
        in_specs=[
            whole,
            pl.BlockSpec((block, channels), lambda f: (f, 0)),
            pl.BlockSpec((block, channels), lambda f: (f, 0)),
            whole,
            whole_block(channels),
            whole_block(channels),
        ]
        + [whole] * (1 + line),
        out_specs=[
            whole,
            whole,
            whole_block(SUB, channels),
            whole_block(line, rows, channels),
        ],
        out_shape=[
            jax.ShapeDtypeStruct((rows, channels), BF16),
            jax.ShapeDtypeStruct((rows, channels), BF16),
            jax.ShapeDtypeStruct((SUB, channels), F32),
            jax.ShapeDtypeStruct((line, rows, channels), BF16),
        ],
        scratch_shapes=[
            pltpu.VMEM((rows, channels), F32),
            pltpu.VMEM((rows, channels), F32),
            pltpu.VMEM((rows, channels), BF16),
        ],
        compiler_params=params(),
        cost_estimate=NO_COST,
        name="mlp_both_ways",
    )(normed, weight_in, weight_out, centered, norm_gain, layer_scale, own, *upstream_line)

    small, norm_line[1], norm_line[-1] = lax.optimization_barrier(
        (small, norm_line[1], norm_line[-1])
    )
    for k in range(2, line - 1):
        norm_line[k] = along_line(norm_line[k - 1], 1)

    grad_inner, grad_outer = rims(conv_grad)

    half = count // 2
    alike = [[2 * k + p for k in range(half)] for p in range(2)]
    half_tiles = tiles // 2
    wide = half_tiles * LANES
    piece = -(-(TAP_ROWS + SUB) // half)
    piece += -piece % (2 * SUB)
    padded = piece * half

    def tile_of(block_rows):
        def at(c, w):
            return 0, (c + w[1] * half_tiles) % tiles

        return pl.BlockSpec((block_rows, LANES), at)

    half_sent, half_kept = pl.pallas_call(
        functools.partial(kernel_grad_kernel, planes, height),
        grid_spec=pltpu.PrefetchScalarGridSpec(
            num_scalar_prefetch=1,
            grid=(tiles,),
            in_specs=[tile_of(rows), tile_of(rows), tile_of(rows), tile_of(rows), tile_of(SUB)],
            out_specs=[
                pl.BlockSpec((padded, LANES), lambda c, w: (0, jnp.minimum(c, half_tiles - 1))),
                pl.BlockSpec((padded, LANES), lambda c, w: (0, jnp.maximum(c - half_tiles, 0))),
            ],
            scratch_shapes=[
                spread_of(2 * MARGIN + planes),
                pltpu.VMEM((2, KS, SUB * SUB, LANES), F32),
                pltpu.VMEM((9, KS, SUB, LANES), F32),
                pltpu.VMEM((padded, LANES), F32),
            ],
        ),
        out_shape=[jax.ShapeDtypeStruct((padded, wide), BF16)] * 2,
        compiler_params=params(),
        cost_estimate=NO_COST,
        name="kernel_grad_terms",
    )(jnp.stack([core, 1 - core]), inner, own, outer, conv_grad, small)

    half_sent, norm_line[2], grad_inner, grad_outer = lax.optimization_barrier(
        (half_sent, norm_line[2], grad_inner, grad_outer)
    )
    half_got = lax.ppermute(half_sent, "row", other_core)
    sums, gathered = pl.pallas_call(
        chip_sum_kernel,
        in_specs=[whole_block(padded, wide)] * 2 + [whole] * line,
        out_specs=[whole_block(padded, wide), whole_block(line, rows, channels)],
        out_shape=[
            jax.ShapeDtypeStruct((padded, wide), BF16),
            jax.ShapeDtypeStruct((line, rows, channels), BF16),
        ],
        grid=(1,),
        compiler_params=params(),
        cost_estimate=NO_COST,
        name="kernel_grad_chip_sum",
    )(half_kept, half_got, *norm_line)

    share = units // count
    tokens = line * rows
    base = me // quad * quad
    side = lax.rem(me, quad) // 2
    far = base + 2 * (1 - side)
    near = base + 2 * side
    which = jnp.stack([far + core, near + core]).astype(jnp.int32)
    other_gathered = lax.ppermute(gathered, "row", other_core)
    other_cotangents = lax.ppermute(cotangents, "row", other_core)

    def side_terms(kernel, number, more, after, outs, name):
        chunk = pl.BlockSpec((share, channels), lambda _, w: (w[number], 0))
        return pl.pallas_call(
            follow(kernel, 1, 7 + len(more), len(after)),
            grid_spec=pltpu.PrefetchScalarGridSpec(
                num_scalar_prefetch=1,
                grid=(1,),
                in_specs=[chunk, chunk, whole_block(channels)]
                + [whole_block(line, rows, channels)] * 4
                + [whole_block(*part.shape) for part in more]
                + [IN_PLACE] * len(after),
                out_specs=[whole_block(*out.shape) for out in outs],
                scratch_shapes=[pltpu.VMEM((2 * tokens, channels), BF16)] * 2,
            ),
            out_shape=outs,
            compiler_params=params(),
            cost_estimate=NO_COST,
            name=name,
        )(
            which,
            weight_in,
            weight_out,
            layer_scale,
            gathered,
            cotangents,
            other_gathered,
            other_cotangents,
            *more,
            *after,
        )

    pair = jax.ShapeDtypeStruct((2, share, channels), BF16)
    single = jax.ShapeDtypeStruct((share, channels), F32)
    (sent,) = side_terms(
        far_side_kernel, 0, [], [sums], [pair], "weight_grads_far_side"
    )
    got = lax.ppermute(sent, "row", other_side)
    scattered = lax.all_to_all(
        sums.reshape(half, piece, wide),
        "row",
        split_axis=0,
        concat_axis=0,
        tiled=True,
        axis_index_groups=alike,
    )
    voxel_grad, token = pl.pallas_call(
        follow(functools.partial(input_grad_kernel, planes, height), 1, 5, 1),
        grid_spec=pltpu.PrefetchScalarGridSpec(
            num_scalar_prefetch=1,
            grid=(tiles,),
            in_specs=[
                lane_block(rows),
                lane_block(rows),
                lane_block(rows),
                lane_block(TAP_ROWS),
                lane_block(rows),
                IN_PLACE,
            ],
            out_specs=[lane_block(rows), whole_block(SUB, LANES)],
            scratch_shapes=[
                spread_of(2 * MARGIN + planes),
                pltpu.VMEM((9, KS, SUB, LANES), F32),
            ],
        ),
        out_shape=[
            jax.ShapeDtypeStruct((rows, channels), BF16),
            jax.ShapeDtypeStruct((SUB, LANES), F32),
        ],
        compiler_params=params(),
        cost_estimate=NO_COST,
        name="input_grad_conv",
    )(parity, grad_inner, conv_grad, grad_outer, dw_kernel, upstream, sent)

    copies = pl.pallas_call(
        follow(spread_sum_kernel, 0, 1, 1),
        in_specs=[whole_block(half, piece, wide), IN_PLACE],
        out_specs=whole_block(half, piece, wide),
        out_shape=jax.ShapeDtypeStruct((half, piece, wide), BF16),
        grid=(1,),
        compiler_params=params(),
        cost_estimate=NO_COST,
        name="kernel_grad_sum",
    )(scattered, token)
    totals = lax.all_to_all(
        copies, "row", split_axis=0, concat_axis=0, tiled=True, axis_index_groups=alike
    )
    weight_in_grad, weight_out_grad = side_terms(
        near_side_kernel, 1, [got], [copies], [single, single], "weight_grads_near_side"
    )
    totals, weight_in_grad = lax.optimization_barrier((totals, weight_in_grad))
    other_totals = lax.ppermute(totals, "row", other_core)
    kernel_grad, *vector_grads = pl.pallas_call(
        unpack_kernel,
        grid_spec=pltpu.PrefetchScalarGridSpec(
            num_scalar_prefetch=1,
            grid=(1,),
            in_specs=[whole_block(half, piece, wide)] * 2,
            out_specs=[whole_block(TAP_ROWS, channels)] + [whole_block(channels)] * 3,
        ),
        out_shape=[jax.ShapeDtypeStruct((TAP_ROWS, channels), F32)]
        + [jax.ShapeDtypeStruct((channels,), F32)] * 3,
        compiler_params=params(),
        cost_estimate=NO_COST,
        name="kernel_grad_unpack",
    )(parity, totals, other_totals)

    return (
        block_out.reshape(voxels.shape),
        voxel_grad.reshape(voxels.shape),
        kernel_grad,
        *vector_grads,
        weight_in_grad,
        weight_out_grad,
    )


def solution(mesh):
    in_specs = (
        P(("group", "row"), None, None, None),
        P(),
        P(),
        P(),
        P(),
        P(),
        P(),
        P(("group", "row"), None, None, None),
    )
    out_specs = (
        P(("group", "row"), None, None, None),
        P(("group", "row"), None, None, None),
        P("group", None),
        P("group"),
        P("group"),
        P("group"),
        P(("group", "row"), None),
        P(("group", "row"), None),
    )
    return jax.shard_map(
        on_device, mesh=mesh, in_specs=in_specs, out_specs=out_specs, check_vma=False
    )
```

```python
import functools

import jax
import jax.numpy as jnp
from jax import lax
from jax.experimental import pallas as pl
from jax.experimental.pallas import tpu as pltpu
from jax.sharding import PartitionSpec as P

KS = 7
MARGIN = KS // 2
LANES = 128
SUB = 8
PAD = 3 * SUB
TAP_ROWS = KS * KS * KS

root_half = 0.7071067811865476
inv_root_tau = 0.3989422804014327
norm_eps = 1e-06
erf_step = 0.3275911
erf_terms = tuple(
    0.5 * a for a in (0.254829592, -0.284496736, 1.421413741, -1.453152027, 1.061405429)
)

NO_COST = pl.CostEstimate(flops=0, bytes_accessed=0, transcendentals=0)

F32 = jnp.float32
BF16 = jnp.bfloat16


def split_source(v):
    terms = []
    for a, b in ((v[0] + v[2], v[1] + v[3]), (v[2], v[3]), (v[0], v[1])):
        terms += [a + b, b, a]
    return terms


def split_taps(t):
    terms = []
    for s in (
        (t[2], t[3], t[4]),
        (t[4] - t[2], t[5] - t[3], t[6] - t[4]),
        (t[0] - t[2], t[1] - t[3], t[2] - t[4]),
    ):
        terms += [s[1], s[2] - s[1], s[0] - s[1]]
    return terms


def split_grads(g):
    terms = []
    for a, b in ((g[0] + g[2], g[1] + g[3]), (g[0], g[1]), (g[2], g[3])):
        terms += [a + b, a, b]
    return terms


def join_outputs(m):
    pair = [(m[3 * k] + m[3 * k + 1], m[3 * k] + m[3 * k + 2]) for k in range(3)]
    return [
        pair[0][0] + pair[1][0],
        pair[0][1] + pair[1][1],
        pair[0][0] + pair[2][0],
        pair[0][1] + pair[2][1],
    ]


def join_taps(m):
    p, q, r = [
        (m[3 * k + 2], m[3 * k] - m[3 * k + 1] - m[3 * k + 2], m[3 * k + 1]) for k in range(3)
    ]
    return [
        r[0],
        r[1],
        p[0] - q[0] - r[0] + r[2],
        p[1] - q[1] - r[1],
        p[2] - q[2] - r[2] + q[0],
        q[1],
        q[2],
    ]


def tree_sum(terms):
    while len(terms) > 1:
        terms = [
            terms[k] + terms[k + 1] if k + 1 < len(terms) else terms[k]
            for k in range(0, len(terms), 2)
        ]
    return terms[0]


def stage_source(wanted, height, spread):
    row = height * SUB
    for at, (block, x) in enumerate(wanted):
        plane = block[x * row : (x + 1) * row, :].astype(F32)
        lines = [plane[y * SUB : (y + 1) * SUB, :] for y in range(height)]
        for j, term in enumerate(split_source(lines)):
            spread[j, at, SUB : 2 * SUB, :] = term


def rim_planes(left, right, planes):
    wanted = [(left, x) for x in range(planes - MARGIN, planes)]
    return wanted + [(right, x) for x in range(MARGIN)]


def all_planes(left, own, right, planes):
    rim = rim_planes(left, right, planes)
    return rim[:MARGIN] + [(own, x) for x in range(planes)] + rim[MARGIN:]


def by_core(core, inner, outer, stage):
    @pl.when(core[0] == 0)
    def _():
        stage(outer, inner)

    @pl.when(core[0] != 0)
    def _():
        stage(inner, outer)


def clear_rims(spread):
    zeros = jnp.zeros(spread.shape[:2] + (SUB, LANES), F32)
    spread[:, :, :SUB, :] = zeros
    spread[:, :, 2 * SUB :, :] = zeros


def stage_taps(taps, split):
    for dx in range(KS):
        rows = []
        for dy in range(KS):
            first = dx * KS * KS + dy * KS
            if first + SUB <= TAP_ROWS:
                rows.append(taps[first : first + SUB, :])
            else:
                rows.append(pltpu.roll(taps[TAP_ROWS - SUB : TAP_ROWS, :], SUB - 1, 0))
        for j, term in enumerate(split_taps(rows)):
            split[j, dx] = term


REVERSED = (0, 2, 1, 6, 8, 7, 3, 5, 4)


def convolve(spread, split, planes, held, flipped):
    terms = []
    for j in range(9):
        sums = [None] * planes
        for dz in range(KS):
            first = SUB - MARGIN + dz
            source = {x: spread[j, at, first : first + SUB, :] for at, x in enumerate(held)}
            weights = []
            for dx in range(KS):
                if flipped:
                    tap = split[REVERSED[j], KS - 1 - dx, KS - 1 - dz : KS - dz, :]
                else:
                    tap = split[j, dx, dz : dz + 1, :]
                weights.append(jnp.broadcast_to(tap, (SUB, LANES)))
            for x in range(planes):
                part = tree_sum(
                    [source[x + dx] * weights[dx] for dx in range(KS) if x + dx in source]
                )
                sums[x] = part if sums[x] is None else sums[x] + part
        terms.append(sums)
    return [join_outputs([terms[j][x] for j in range(9)]) for x in range(planes)]


def own_conv_kernel(planes, height, own, taps, gain, bias, out, split, vectors, spread):
    @pl.when(pl.program_id(0) == 0)
    def _():
        for k, line in enumerate((gain, bias)):
            vectors[k : k + 1, :] = line[...].reshape(1, -1)
        clear_rims(spread)

    stage_source([(own, x) for x in range(planes)], height, spread)
    stage_taps(taps, split)
    rows = convolve(spread, split, planes, range(MARGIN, MARGIN + planes), False)
    for x in range(planes):
        for y in range(height):
            at = (x * height + y) * SUB
            out[at : at + SUB, :] = rows[x][y]


def rim_conv_kernel(
    planes, height, core, inner, outer, split, partial, vectors, normed, centered, spread, conv
):
    step = pl.program_id(0)

    @pl.when(step == 0)
    def _():
        clear_rims(spread)

    def stage(left, right):
        stage_source(rim_planes(left, right, planes), height, spread)

    by_core(core, inner, outer, stage)
    held = list(range(MARGIN)) + list(range(MARGIN + planes, 2 * MARGIN + planes))
    rows = convolve(spread, split, planes, held, False)
    for x in range(planes):
        for y in range(height):
            at = (x * height + y) * SUB
            conv[step, at : at + SUB, :] = rows[x][y] + partial[at : at + SUB, :]

    @pl.when(step == pl.num_programs(0) - 1)
    def _():
        tiles = conv.shape[0]
        channels = tiles * LANES
        parts = [conv[k] for k in range(tiles)]
        gains = vectors[0:1, :]
        biases = vectors[1:2, :]
        average = jnp.sum(tree_sum(parts), axis=1, keepdims=True) * (1.0 / channels)
        parts = [part - average for part in parts]
        variance = jnp.sum(
            tree_sum([part * part for part in parts]), axis=1, keepdims=True
        ) * (1.0 / channels)
        inverse = lax.rsqrt(variance + norm_eps)
        for k in range(tiles):
            lanes = slice(k * LANES, (k + 1) * LANES)
            centered[:, lanes] = parts[k]
            value = parts[k] * inverse
            whole = (value * gains[:, lanes] + biases[:, lanes]).astype(BF16)
            normed[:, lanes] = whole


def input_grad_kernel(
    planes, height, core, inner, own, outer, taps, cotangent, out, token, spread, split
):
    @pl.when(pl.program_id(0) == 0)
    def _():
        clear_rims(spread)

    def stage(left, right):
        stage_source(all_planes(left, own, right, planes), height, spread)

    by_core(core, inner, outer, stage)
    stage_taps(taps, split)
    token[...] = jnp.zeros(token.shape, F32)
    rows = convolve(spread, split, planes, range(2 * MARGIN + planes), True)
    for x in range(planes):
        at = x * height * SUB
        whole = jnp.concatenate(rows[x], axis=0)
        upstream = cotangent[at : at + height * SUB, :].astype(F32)
        out[at : at + height * SUB, :] = (upstream + whole).astype(BF16)


def kernel_grad_kernel(
    planes,
    height,
    which,
    inner,
    own,
    outer,
    grads,
    small,
    sent,
    kept,
    spread,
    products,
    joined,
    flat,
):
    @pl.when(pl.program_id(0) == 0)
    def _():
        clear_rims(spread)
        products[...] = jnp.zeros(products.shape, F32)
        flat[...] = jnp.zeros(flat.shape, F32)

    def stage(left, right):
        stage_source(all_planes(left, own, right, planes), height, spread)

    by_core(which, inner, outer, stage)
    upstream = []
    for x in range(planes):
        plane = grads[x * height * SUB : (x + 1) * height * SUB, :].astype(F32)
        upstream.append(
            split_grads([plane[y * SUB : (y + 1) * SUB, :] for y in range(height)])
        )
    for j in range(9):
        for dz in range(KS):
            first = SUB - MARGIN + dz
            source = [
                spread[j, x, first : first + SUB, :] for x in range(planes + KS - 1)
            ]
            for dx in range(KS):
                products[j % 2, dx, dz * SUB : (dz + 1) * SUB, :] = tree_sum(
                    [source[x + dx] * upstream[x][j] for x in range(planes)]
                )
        for dx in range(KS):
            joined[j, dx] = tree_sum(
                [products[j % 2, dx, pl.ds(s, SUB, stride=SUB), :] for s in range(SUB)]
            )
    for dx in range(KS):
        for dy, tile in enumerate(join_taps([joined[j, dx] for j in range(9)])):
            row = dx * KS * KS + dy * KS
            flat[row : row + SUB, :] = tile
    flat[TAP_ROWS : TAP_ROWS + SUB, :] = small[...]
    step = pl.program_id(0)
    half = pl.num_programs(0) // 2

    @pl.when(step < half)
    def _():
        sent[...] = flat[...].astype(BF16)

    @pl.when(step >= half)
    def _():
        kept[...] = flat[...].astype(BF16)


def mlp_kernel(
    normed, weight_in, weight_out, centered, norm_gain, layer_scale, voxels, *rest
):
    *cotangents, block_out, conv_grad, small, together, mixed, back, mixed_grad = rest
    cotangent = cotangents[0]
    step = pl.program_id(0)
    gain = norm_gain[...].reshape(1, -1)
    scale = layer_scale[...].reshape(1, -1)

    @pl.when(step == 0)
    def _():
        mixed_grad[...] = (scale * cotangent[...].astype(F32)).astype(BF16)
        for k, part in enumerate(cotangents):
            together[k] = part[...]

    across = (((1,), (1,)), ((), ()))
    hidden = lax.dot_general(normed[...], weight_in[...], across, preferred_element_type=F32)
    act_grad = lax.dot_general(
        mixed_grad[...], weight_out[...], across, preferred_element_type=F32
    )
    activated, hidden_grad = slopes(hidden, act_grad)
    forward = jnp.dot(activated, weight_out[...], preferred_element_type=F32)
    backward = jnp.dot(hidden_grad, weight_in[...], preferred_element_type=F32)

    @pl.when(step == 0)
    def _():
        mixed[...] = forward
        back[...] = backward

    @pl.when(step > 0)
    def _():
        mixed[...] += forward
        back[...] += backward

    @pl.when(step == pl.num_programs(0) - 1)
    def _():
        channels = gain.shape[1]
        whole = mixed[...]
        block_out[...] = (voxels[...].astype(F32) + scale * whole).astype(BF16)
        scale_local = jnp.sum(cotangent[...].astype(F32) * whole, axis=0, keepdims=True)
        grad = back[...]
        deviation = centered[...]
        variance = jnp.sum(deviation * deviation, axis=1, keepdims=True) * (1.0 / channels)
        inverse = lax.rsqrt(variance + norm_eps)
        one = deviation * inverse
        bias_local = jnp.sum(grad, axis=0, keepdims=True)
        gain_local = jnp.sum(grad * one, axis=0, keepdims=True)
        small[...] = jnp.concatenate(
            [gain_local, bias_local, scale_local, jnp.zeros((SUB - 3, channels), F32)], axis=0
        )
        scaled = grad * gain
        average = jnp.sum(scaled, axis=1, keepdims=True) * (1.0 / channels)
        slant = jnp.sum(scaled * one, axis=1, keepdims=True) * (1.0 / channels)
        conv_grad[...] = (inverse * (scaled - average - one * slant)).astype(BF16)


def slopes(hidden, act_grad):
    bell = jnp.exp(-0.5 * hidden * hidden)
    below = 1.0 + (erf_step * root_half) * jnp.abs(hidden)
    t = pl.reciprocal(below, approx=True)
    t = t * (2.0 - below * t)
    poly = erf_terms[-1]
    for term in erf_terms[-2::-1]:
        poly = poly * t + term
    tail = poly * t * bell
    cover = jnp.where(hidden < 0.0, tail, 1.0 - tail)
    activated = (hidden * cover).astype(BF16)
    slope = cover + hidden * bell * inv_root_tau
    return activated, (act_grad * slope).astype(BF16)


def weight_grad_terms(weight_in, weight_out, scale, sets, aligned, mixed_grad):
    scales = scale[...].reshape(1, -1)
    at = 0
    for normed, cotangents in sets:
        line, rows = normed.shape[:2]
        for k in range(line):
            aligned[at : at + rows, :] = normed[k]
            upstream = cotangents[k].astype(F32)
            mixed_grad[at : at + rows, :] = (scales * upstream).astype(BF16)
            at += rows
    across = (((1,), (1,)), ((), ()))
    hidden = lax.dot_general(weight_in[...], aligned[...], across, preferred_element_type=F32)
    act_grad = lax.dot_general(weight_out[...], mixed_grad[...], across, preferred_element_type=F32)
    activated, hidden_grad = slopes(hidden, act_grad)
    return (
        jnp.dot(hidden_grad, aligned[...], preferred_element_type=F32),
        jnp.dot(activated, mixed_grad[...], preferred_element_type=F32),
    )


def far_side_kernel(
    which, weight_in, weight_out, scale, norm, cot, other_norm, other_cot, sent, aligned, mixed_grad
):
    sets = ((norm, cot), (other_norm, other_cot))
    terms = weight_grad_terms(weight_in, weight_out, scale, sets, aligned, mixed_grad)
    for k in range(2):
        sent[k] = terms[k].astype(BF16)


def near_side_kernel(
    which,
    weight_in,
    weight_out,
    scale,
    norm,
    cot,
    other_norm,
    other_cot,
    got,
    in_grad,
    out_grad,
    aligned,
    mixed_grad,
):
    sets = ((norm, cot), (other_norm, other_cot))
    terms = weight_grad_terms(weight_in, weight_out, scale, sets, aligned, mixed_grad)
    for k, out in enumerate((in_grad, out_grad)):
        out[...] = terms[k] + got[k].astype(F32)


def chip_sum_kernel(kept, got, *rest):
    *blocks, out, together = rest
    for k, block in enumerate(blocks):
        together[k] = block[...]
    out[...] = (kept[...].astype(F32) + got[...].astype(F32)).astype(BF16)


def spread_sum_kernel(parts, out):
    total = tree_sum([parts[k].astype(F32) for k in range(parts.shape[0])]).astype(BF16)
    for copy in range(out.shape[0]):
        out[copy] = total


def unpack_kernel(core, own, other, out, *small):
    piece, wide = own.shape[1:]

    def unpack(*halves):
        last = []
        for side, parts in enumerate(halves):
            lanes = slice(side * wide, (side + 1) * wide)
            for k in range(-(-TAP_ROWS // piece)):
                first = k * piece
                length = min(piece, TAP_ROWS - first)
                out[first : first + length, lanes] = parts[k].astype(F32)[:length, :]
            k = TAP_ROWS // piece
            last.append(parts[k].astype(F32))
        rows = jnp.concatenate(last, axis=1)
        first = TAP_ROWS % piece
        for k, line in enumerate(small):
            line[...] = rows[first + k : first + k + 1, :].reshape(line.shape)

    by_core(core, own, other, lambda outer, inner: unpack(inner, outer))


def params(limit=48):
    return pltpu.CompilerParams(vmem_limit_bytes=limit * 1024 * 1024)


def follow(kernel, scalars, inputs, count):
    def body(*refs):
        head = refs[: scalars + inputs]
        return kernel(*head, *refs[scalars + inputs + count :])

    return body


IN_PLACE = pl.BlockSpec(memory_space=pl.ANY)


def lane_block(rows):
    return pl.BlockSpec((rows, LANES), lambda c, *_: (0, c))


def whole_block(*shape):
    return pl.BlockSpec(shape, lambda *_: (0,) * len(shape))


def rims(cells):
    count = lax.axis_size("row")
    between = [(i, i + 1) for i in range(1, count - 1, 2)]
    return (
        lax.ppermute(cells, "row", [(i, i ^ 1) for i in range(count)]),
        lax.ppermute(cells, "row", between + [(j, i) for i, j in between]),
    )


def on_device(
    voxels, dw_kernel, norm_gain, norm_bias, weight_in, weight_out, layer_scale, cotangent
):
    planes, height, breadth, channels = voxels.shape
    rows = planes * height * breadth
    units = weight_in.shape[0]
    count = lax.axis_size("row")
    me = lax.axis_index("row")
    quad = 4
    line = count // quad
    other_core = [(i, i ^ 1) for i in range(count)]
    other_side = [(i, i ^ 2) for i in range(count)]
    tiles = channels // LANES

    own = voxels.reshape(rows, channels)
    upstream = cotangent.reshape(rows, channels)
    core = lax.rem(me, 2).astype(jnp.int32)
    parity = core.reshape(1)

    inner, outer = rims(own)

    def along_line(cells, steps):
        return lax.ppermute(cells, "row", [(i, (i + quad * steps) % count) for i in range(count)])

    upstream_line = [upstream] + [None] * (line - 1)
    upstream_line[1] = along_line(upstream, 1)
    upstream_line[-1] = along_line(upstream, -1)

    def spread_of(held):
        return pltpu.VMEM((9, held, PAD, LANES), F32)

    split_block = pl.BlockSpec((None, 9, KS, SUB, LANES), lambda c, *_: (c, 0, 0, 0, 0))
    partial, split, vectors = pl.pallas_call(
        functools.partial(own_conv_kernel, planes, height),
        grid=(tiles,),
        in_specs=[lane_block(rows), lane_block(TAP_ROWS)] + [whole_block(channels)] * 2,
        out_specs=[lane_block(rows), split_block, whole_block(SUB, channels)],
        out_shape=[
            jax.ShapeDtypeStruct((rows, channels), F32),
            jax.ShapeDtypeStruct((tiles, 9, KS, SUB, LANES), F32),
            jax.ShapeDtypeStruct((SUB, channels), F32),
        ],
        scratch_shapes=[spread_of(planes)],
        compiler_params=params(),
        cost_estimate=NO_COST,
        name="own_conv",
    )(own, dw_kernel, norm_gain, norm_bias)

    for k in range(2, line - 1):
        upstream_line[k] = along_line(upstream_line[k - 1], 1)
    normed, centered = pl.pallas_call(
        follow(functools.partial(rim_conv_kernel, planes, height), 1, 5, 2),
        grid_spec=pltpu.PrefetchScalarGridSpec(
            num_scalar_prefetch=1,
            grid=(tiles,),
            in_specs=[
                lane_block(rows),
                lane_block(rows),
                split_block,
                lane_block(rows),
                whole_block(SUB, channels),
                IN_PLACE,
                IN_PLACE,
            ],
            out_specs=[
                whole_block(rows, channels),
                whole_block(rows, channels),
            ],
            scratch_shapes=[spread_of(2 * MARGIN), pltpu.VMEM((tiles, rows, LANES), F32)],
        ),
        out_shape=[
            jax.ShapeDtypeStruct((rows, channels), BF16),
            jax.ShapeDtypeStruct((rows, channels), F32),
        ],
        compiler_params=params(),
        cost_estimate=NO_COST,
        name="rim_conv",
    )(
        parity,
        inner,
        outer,
        split,
        partial,
        vectors,
        upstream_line[1],
        upstream_line[-1],
    )

    normed, upstream_line[2] = lax.optimization_barrier((normed, upstream_line[2]))
    norm_line = [normed] + [None] * (line - 1)
    norm_line[1] = along_line(normed, 1)
    norm_line[-1] = along_line(normed, -1)

    block = 1024
    whole = whole_block(rows, channels)
    block_out, conv_grad, small, cotangents = pl.pallas_call(
        mlp_kernel,
        grid=(units // block,),
        in_specs=[
            whole,
            pl.BlockSpec((block, channels), lambda f: (f, 0)),
            pl.BlockSpec((block, channels), lambda f: (f, 0)),
            whole,
            whole_block(channels),
            whole_block(channels),
        ]
        + [whole] * (1 + line),
        out_specs=[
            whole,
            whole,
            whole_block(SUB, channels),
            whole_block(line, rows, channels),
        ],
        out_shape=[
            jax.ShapeDtypeStruct((rows, channels), BF16),
            jax.ShapeDtypeStruct((rows, channels), BF16),
            jax.ShapeDtypeStruct((SUB, channels), F32),
            jax.ShapeDtypeStruct((line, rows, channels), BF16),
        ],
        scratch_shapes=[
            pltpu.VMEM((rows, channels), F32),
            pltpu.VMEM((rows, channels), F32),
            pltpu.VMEM((rows, channels), BF16),
        ],
        compiler_params=params(),
        cost_estimate=NO_COST,
        name="mlp_both_ways",
    )(normed, weight_in, weight_out, centered, norm_gain, layer_scale, own, *upstream_line)

    small, norm_line[1], norm_line[-1] = lax.optimization_barrier(
        (small, norm_line[1], norm_line[-1])
    )
    for k in range(2, line - 1):
        norm_line[k] = along_line(norm_line[k - 1], 1)

    grad_inner, grad_outer = rims(conv_grad)

    half = count // 2
    alike = [[2 * k + p for k in range(half)] for p in range(2)]
    half_tiles = tiles // 2
    wide = half_tiles * LANES
    piece = -(-(TAP_ROWS + SUB) // half)
    piece += -piece % (2 * SUB)
    padded = piece * half

    def tile_of(block_rows):
        def at(c, w):
            return 0, (c + w[1] * half_tiles) % tiles

        return pl.BlockSpec((block_rows, LANES), at)

    half_sent, half_kept = pl.pallas_call(
        functools.partial(kernel_grad_kernel, planes, height),
        grid_spec=pltpu.PrefetchScalarGridSpec(
            num_scalar_prefetch=1,
            grid=(tiles,),
            in_specs=[tile_of(rows), tile_of(rows), tile_of(rows), tile_of(rows), tile_of(SUB)],
            out_specs=[
                pl.BlockSpec((padded, LANES), lambda c, w: (0, jnp.minimum(c, half_tiles - 1))),
                pl.BlockSpec((padded, LANES), lambda c, w: (0, jnp.maximum(c - half_tiles, 0))),
            ],
            scratch_shapes=[
                spread_of(2 * MARGIN + planes),
                pltpu.VMEM((2, KS, SUB * SUB, LANES), F32),
                pltpu.VMEM((9, KS, SUB, LANES), F32),
                pltpu.VMEM((padded, LANES), F32),
            ],
        ),
        out_shape=[jax.ShapeDtypeStruct((padded, wide), BF16)] * 2,
        compiler_params=params(),
        cost_estimate=NO_COST,
        name="kernel_grad_terms",
    )(jnp.stack([core, 1 - core]), inner, own, outer, conv_grad, small)

    half_sent, norm_line[2], grad_inner, grad_outer = lax.optimization_barrier(
        (half_sent, norm_line[2], grad_inner, grad_outer)
    )
    half_got = lax.ppermute(half_sent, "row", other_core)
    sums, gathered = pl.pallas_call(
        chip_sum_kernel,
        in_specs=[whole_block(padded, wide)] * 2 + [whole] * line,
        out_specs=[whole_block(padded, wide), whole_block(line, rows, channels)],
        out_shape=[
            jax.ShapeDtypeStruct((padded, wide), BF16),
            jax.ShapeDtypeStruct((line, rows, channels), BF16),
        ],
        grid=(1,),
        compiler_params=params(),
        cost_estimate=NO_COST,
        name="kernel_grad_chip_sum",
    )(half_kept, half_got, *norm_line)

    share = units // count
    tokens = line * rows
    base = me // quad * quad
    side = lax.rem(me, quad) // 2
    far = base + 2 * (1 - side)
    near = base + 2 * side
    which = jnp.stack([far + core, near + core]).astype(jnp.int32)
    other_gathered = lax.ppermute(gathered, "row", other_core)
    other_cotangents = lax.ppermute(cotangents, "row", other_core)

    def side_terms(kernel, number, more, after, outs, name):
        chunk = pl.BlockSpec((share, channels), lambda _, w: (w[number], 0))
        return pl.pallas_call(
            follow(kernel, 1, 7 + len(more), len(after)),
            grid_spec=pltpu.PrefetchScalarGridSpec(
                num_scalar_prefetch=1,
                grid=(1,),
                in_specs=[chunk, chunk, whole_block(channels)]
                + [pl.BlockSpec(memory_space=pltpu.VMEM)] * 4
                + [whole_block(*part.shape) for part in more]
                + [IN_PLACE] * len(after),
                out_specs=[whole_block(*out.shape) for out in outs],
                scratch_shapes=[pltpu.VMEM((2 * tokens, channels), BF16)] * 2,
            ),
            out_shape=outs,
            compiler_params=params(),
            cost_estimate=NO_COST,
            name=name,
        )(
            which,
            weight_in,
            weight_out,
            layer_scale,
            gathered,
            cotangents,
            other_gathered,
            other_cotangents,
            *more,
            *after,
        )

    pair = jax.ShapeDtypeStruct((2, share, channels), BF16)
    single = jax.ShapeDtypeStruct((share, channels), F32)
    (sent,) = side_terms(
        far_side_kernel, 0, [], [sums], [pair], "weight_grads_far_side"
    )
    got = lax.ppermute(sent, "row", other_side)
    scattered = lax.all_to_all(
        sums.reshape(half, piece, wide),
        "row",
        split_axis=0,
        concat_axis=0,
        tiled=True,
        axis_index_groups=alike,
    )
    voxel_grad, token = pl.pallas_call(
        follow(functools.partial(input_grad_kernel, planes, height), 1, 5, 1),
        grid_spec=pltpu.PrefetchScalarGridSpec(
            num_scalar_prefetch=1,
            grid=(tiles,),
            in_specs=[
                lane_block(rows),
                lane_block(rows),
                lane_block(rows),
                lane_block(TAP_ROWS),
                lane_block(rows),
                IN_PLACE,
            ],
            out_specs=[lane_block(rows), whole_block(SUB, LANES)],
            scratch_shapes=[
                spread_of(2 * MARGIN + planes),
                pltpu.VMEM((9, KS, SUB, LANES), F32),
            ],
        ),
        out_shape=[
            jax.ShapeDtypeStruct((rows, channels), BF16),
            jax.ShapeDtypeStruct((SUB, LANES), F32),
        ],
        compiler_params=params(),
        cost_estimate=NO_COST,
        name="input_grad_conv",
    )(parity, grad_inner, conv_grad, grad_outer, dw_kernel, upstream, sent)

    copies = pl.pallas_call(
        follow(spread_sum_kernel, 0, 1, 1),
        in_specs=[whole_block(half, piece, wide), IN_PLACE],
        out_specs=whole_block(half, piece, wide),
        out_shape=jax.ShapeDtypeStruct((half, piece, wide), BF16),
        grid=(1,),
        compiler_params=params(),
        cost_estimate=NO_COST,
        name="kernel_grad_sum",
    )(scattered, token)
    totals = lax.all_to_all(
        copies, "row", split_axis=0, concat_axis=0, tiled=True, axis_index_groups=alike
    )
    weight_in_grad, weight_out_grad = side_terms(
        near_side_kernel, 1, [got], [copies], [single, single], "weight_grads_near_side"
    )
    totals, weight_in_grad = lax.optimization_barrier((totals, weight_in_grad))
    other_totals = lax.ppermute(totals, "row", other_core)
    kernel_grad, *vector_grads = pl.pallas_call(
        unpack_kernel,
        grid_spec=pltpu.PrefetchScalarGridSpec(
            num_scalar_prefetch=1,
            grid=(1,),
            in_specs=[whole_block(half, piece, wide)] * 2,
            out_specs=[whole_block(TAP_ROWS, channels)] + [whole_block(channels)] * 3,
        ),
        out_shape=[jax.ShapeDtypeStruct((TAP_ROWS, channels), F32)]
        + [jax.ShapeDtypeStruct((channels,), F32)] * 3,
        compiler_params=params(),
        cost_estimate=NO_COST,
        name="kernel_grad_unpack",
    )(parity, totals, other_totals)

    return (
        block_out.reshape(voxels.shape),
        voxel_grad.reshape(voxels.shape),
        kernel_grad,
        *vector_grads,
        weight_in_grad,
        weight_out_grad,
    )


def solution(mesh):
    in_specs = (
        P(("group", "row"), None, None, None),
        P(),
        P(),
        P(),
        P(),
        P(),
        P(),
        P(("group", "row"), None, None, None),
    )
    out_specs = (
        P(("group", "row"), None, None, None),
        P(("group", "row"), None, None, None),
        P("group", None),
        P("group"),
        P("group"),
        P("group"),
        P(("group", "row"), None),
        P(("group", "row"), None),
    )
    return jax.shard_map(
        on_device, mesh=mesh, in_specs=in_specs, out_specs=out_specs, check_vma=False
    )
```

```python
import functools

import jax
import jax.numpy as jnp
from jax import lax
from jax.experimental import pallas as pl
from jax.experimental.pallas import tpu as pltpu
from jax.sharding import PartitionSpec as P

KS = 7
MARGIN = KS // 2
LANES = 128
SUB = 8
PAD = 3 * SUB
TAP_ROWS = KS * KS * KS

root_half = 0.7071067811865476
inv_root_tau = 0.3989422804014327
norm_eps = 1e-06
erf_step = 0.3275911
erf_terms = tuple(
    0.5 * a for a in (0.254829592, -0.284496736, 1.421413741, -1.453152027, 1.061405429)
)

NO_COST = pl.CostEstimate(flops=0, bytes_accessed=0, transcendentals=0)

F32 = jnp.float32
BF16 = jnp.bfloat16


def split_source(v):
    terms = []
    for a, b in ((v[0] + v[2], v[1] + v[3]), (v[2], v[3]), (v[0], v[1])):
        terms += [a + b, b, a]
    return terms


def split_taps(t):
    terms = []
    for s in (
        (t[2], t[3], t[4]),
        (t[4] - t[2], t[5] - t[3], t[6] - t[4]),
        (t[0] - t[2], t[1] - t[3], t[2] - t[4]),
    ):
        terms += [s[1], s[2] - s[1], s[0] - s[1]]
    return terms


def split_grads(g):
    terms = []
    for a, b in ((g[0] + g[2], g[1] + g[3]), (g[0], g[1]), (g[2], g[3])):
        terms += [a + b, a, b]
    return terms


def join_outputs(m):
    pair = [(m[3 * k] + m[3 * k + 1], m[3 * k] + m[3 * k + 2]) for k in range(3)]
    return [
        pair[0][0] + pair[1][0],
        pair[0][1] + pair[1][1],
        pair[0][0] + pair[2][0],
        pair[0][1] + pair[2][1],
    ]


def join_taps(m):
    p, q, r = [
        (m[3 * k + 2], m[3 * k] - m[3 * k + 1] - m[3 * k + 2], m[3 * k + 1]) for k in range(3)
    ]
    return [
        r[0],
        r[1],
        p[0] - q[0] - r[0] + r[2],
        p[1] - q[1] - r[1],
        p[2] - q[2] - r[2] + q[0],
        q[1],
        q[2],
    ]


def tree_sum(terms):
    while len(terms) > 1:
        terms = [
            terms[k] + terms[k + 1] if k + 1 < len(terms) else terms[k]
            for k in range(0, len(terms), 2)
        ]
    return terms[0]


def stage_source(wanted, height, spread):
    row = height * SUB
    for at, (block, x) in enumerate(wanted):
        plane = block[x * row : (x + 1) * row, :].astype(F32)
        lines = [plane[y * SUB : (y + 1) * SUB, :] for y in range(height)]
        for j, term in enumerate(split_source(lines)):
            spread[j, at, SUB : 2 * SUB, :] = term


def rim_planes(left, right, planes):
    wanted = [(left, x) for x in range(planes - MARGIN, planes)]
    return wanted + [(right, x) for x in range(MARGIN)]


def all_planes(left, own, right, planes):
    rim = rim_planes(left, right, planes)
    return rim[:MARGIN] + [(own, x) for x in range(planes)] + rim[MARGIN:]


def by_core(core, inner, outer, stage):
    @pl.when(core[0] == 0)
    def _():
        stage(outer, inner)

    @pl.when(core[0] != 0)
    def _():
        stage(inner, outer)


def clear_rims(spread):
    zeros = jnp.zeros(spread.shape[:2] + (SUB, LANES), F32)
    spread[:, :, :SUB, :] = zeros
    spread[:, :, 2 * SUB :, :] = zeros


def stage_taps(taps, split):
    for dx in range(KS):
        rows = []
        for dy in range(KS):
            first = dx * KS * KS + dy * KS
            if first + SUB <= TAP_ROWS:
                rows.append(taps[first : first + SUB, :])
            else:
                rows.append(pltpu.roll(taps[TAP_ROWS - SUB : TAP_ROWS, :], SUB - 1, 0))
        for j, term in enumerate(split_taps(rows)):
            split[j, dx] = term


REVERSED = (0, 2, 1, 6, 8, 7, 3, 5, 4)


def convolve(spread, split, planes, held, flipped):
    terms = []
    for j in range(9):
        sums = [None] * planes
        for dz in range(KS):
            first = SUB - MARGIN + dz
            source = {x: spread[j, at, first : first + SUB, :] for at, x in enumerate(held)}
            weights = []
            for dx in range(KS):
                if flipped:
                    tap = split[REVERSED[j], KS - 1 - dx, KS - 1 - dz : KS - dz, :]
                else:
                    tap = split[j, dx, dz : dz + 1, :]
                weights.append(jnp.broadcast_to(tap, (SUB, LANES)))
            for x in range(planes):
                part = tree_sum(
                    [source[x + dx] * weights[dx] for dx in range(KS) if x + dx in source]
                )
                sums[x] = part if sums[x] is None else sums[x] + part
        terms.append(sums)
    return [join_outputs([terms[j][x] for j in range(9)]) for x in range(planes)]


def own_conv_kernel(planes, height, own, taps, gain, bias, out, split, vectors, spread):
    @pl.when(pl.program_id(0) == 0)
    def _():
        for k, line in enumerate((gain, bias)):
            vectors[k : k + 1, :] = line[...].reshape(1, -1)
        clear_rims(spread)

    stage_source([(own, x) for x in range(planes)], height, spread)
    stage_taps(taps, split)
    rows = convolve(spread, split, planes, range(MARGIN, MARGIN + planes), False)
    for x in range(planes):
        for y in range(height):
            at = (x * height + y) * SUB
            out[at : at + SUB, :] = rows[x][y]


def rim_conv_kernel(
    planes, height, core, inner, outer, split, partial, vectors, normed, centered, spread, conv
):
    step = pl.program_id(0)

    @pl.when(step == 0)
    def _():
        clear_rims(spread)

    def stage(left, right):
        stage_source(rim_planes(left, right, planes), height, spread)

    by_core(core, inner, outer, stage)
    held = list(range(MARGIN)) + list(range(MARGIN + planes, 2 * MARGIN + planes))
    rows = convolve(spread, split, planes, held, False)
    for x in range(planes):
        for y in range(height):
            at = (x * height + y) * SUB
            conv[step, at : at + SUB, :] = rows[x][y] + partial[at : at + SUB, :]

    @pl.when(step == pl.num_programs(0) - 1)
    def _():
        tiles = conv.shape[0]
        channels = tiles * LANES
        parts = [conv[k] for k in range(tiles)]
        gains = vectors[0:1, :]
        biases = vectors[1:2, :]
        average = jnp.sum(tree_sum(parts), axis=1, keepdims=True) * (1.0 / channels)
        parts = [part - average for part in parts]
        variance = jnp.sum(
            tree_sum([part * part for part in parts]), axis=1, keepdims=True
        ) * (1.0 / channels)
        inverse = lax.rsqrt(variance + norm_eps)
        for k in range(tiles):
            lanes = slice(k * LANES, (k + 1) * LANES)
            centered[:, lanes] = parts[k]
            value = parts[k] * inverse
            whole = (value * gains[:, lanes] + biases[:, lanes]).astype(BF16)
            normed[:, lanes] = whole


def input_grad_kernel(
    planes, height, core, inner, own, outer, taps, cotangent, out, token, spread, split
):
    @pl.when(pl.program_id(0) == 0)
    def _():
        clear_rims(spread)

    def stage(left, right):
        stage_source(all_planes(left, own, right, planes), height, spread)

    by_core(core, inner, outer, stage)
    stage_taps(taps, split)
    token[...] = jnp.zeros(token.shape, F32)
    rows = convolve(spread, split, planes, range(2 * MARGIN + planes), True)
    for x in range(planes):
        at = x * height * SUB
        whole = jnp.concatenate(rows[x], axis=0)
        upstream = cotangent[at : at + height * SUB, :].astype(F32)
        out[at : at + height * SUB, :] = (upstream + whole).astype(BF16)


def kernel_grad_kernel(
    planes,
    height,
    which,
    inner,
    own,
    outer,
    grads,
    small,
    sent,
    kept,
    spread,
    products,
    joined,
    flat,
):
    @pl.when(pl.program_id(0) == 0)
    def _():
        clear_rims(spread)
        products[...] = jnp.zeros(products.shape, F32)
        flat[...] = jnp.zeros(flat.shape, F32)

    def stage(left, right):
        stage_source(all_planes(left, own, right, planes), height, spread)

    by_core(which, inner, outer, stage)
    upstream = []
    for x in range(planes):
        plane = grads[x * height * SUB : (x + 1) * height * SUB, :].astype(F32)
        upstream.append(
            split_grads([plane[y * SUB : (y + 1) * SUB, :] for y in range(height)])
        )
    for j in range(9):
        for dz in range(KS):
            first = SUB - MARGIN + dz
            source = [
                spread[j, x, first : first + SUB, :] for x in range(planes + KS - 1)
            ]
            for dx in range(KS):
                products[j % 2, dx, dz * SUB : (dz + 1) * SUB, :] = tree_sum(
                    [source[x + dx] * upstream[x][j] for x in range(planes)]
                )
        for dx in range(KS):
            joined[j, dx] = tree_sum(
                [products[j % 2, dx, pl.ds(s, SUB, stride=SUB), :] for s in range(SUB)]
            )
    for dx in range(KS):
        for dy, tile in enumerate(join_taps([joined[j, dx] for j in range(9)])):
            row = dx * KS * KS + dy * KS
            flat[row : row + SUB, :] = tile
    flat[TAP_ROWS : TAP_ROWS + SUB, :] = small[...]
    step = pl.program_id(0)
    half = pl.num_programs(0) // 2

    @pl.when(step < half)
    def _():
        sent[...] = flat[...].astype(BF16)

    @pl.when(step >= half)
    def _():
        kept[...] = flat[...].astype(BF16)


def mlp_kernel(
    normed, weight_in, weight_out, centered, norm_gain, layer_scale, voxels, *rest
):
    *cotangents, block_out, conv_grad, small, together, mixed, back, mixed_grad = rest
    cotangent = cotangents[0]
    step = pl.program_id(0)
    gain = norm_gain[...].reshape(1, -1)
    scale = layer_scale[...].reshape(1, -1)

    @pl.when(step == 0)
    def _():
        mixed_grad[...] = (scale * cotangent[...].astype(F32)).astype(BF16)
        for k, part in enumerate(cotangents):
            together[k] = part[...]

    across = (((1,), (1,)), ((), ()))
    hidden = lax.dot_general(normed[...], weight_in[...], across, preferred_element_type=F32)
    act_grad = lax.dot_general(
        mixed_grad[...], weight_out[...], across, preferred_element_type=F32
    )
    activated, hidden_grad = slopes(hidden, act_grad)
    forward = jnp.dot(activated, weight_out[...], preferred_element_type=F32)
    backward = jnp.dot(hidden_grad, weight_in[...], preferred_element_type=F32)

    @pl.when(step == 0)
    def _():
        mixed[...] = forward
        back[...] = backward

    @pl.when(step > 0)
    def _():
        mixed[...] += forward
        back[...] += backward

    @pl.when(step == pl.num_programs(0) - 1)
    def _():
        channels = gain.shape[1]
        whole = mixed[...]
        block_out[...] = (voxels[...].astype(F32) + scale * whole).astype(BF16)
        scale_local = jnp.sum(cotangent[...].astype(F32) * whole, axis=0, keepdims=True)
        grad = back[...]
        deviation = centered[...]
        variance = jnp.sum(deviation * deviation, axis=1, keepdims=True) * (1.0 / channels)
        inverse = lax.rsqrt(variance + norm_eps)
        one = deviation * inverse
        bias_local = jnp.sum(grad, axis=0, keepdims=True)
        gain_local = jnp.sum(grad * one, axis=0, keepdims=True)
        small[...] = jnp.concatenate(
            [gain_local, bias_local, scale_local, jnp.zeros((SUB - 3, channels), F32)], axis=0
        )
        scaled = grad * gain
        average = jnp.sum(scaled, axis=1, keepdims=True) * (1.0 / channels)
        slant = jnp.sum(scaled * one, axis=1, keepdims=True) * (1.0 / channels)
        conv_grad[...] = (inverse * (scaled - average - one * slant)).astype(BF16)


def slopes(hidden, act_grad):
    bell = jnp.exp(-0.5 * hidden * hidden)
    below = 1.0 + (erf_step * root_half) * jnp.abs(hidden)
    t = pl.reciprocal(below, approx=True)
    t = t * (2.0 - below * t)
    poly = erf_terms[-1]
    for term in erf_terms[-2::-1]:
        poly = poly * t + term
    tail = poly * t * bell
    cover = jnp.where(hidden < 0.0, tail, 1.0 - tail)
    activated = (hidden * cover).astype(BF16)
    slope = cover + hidden * bell * inv_root_tau
    return activated, (act_grad * slope).astype(BF16)


def weight_grad_terms(weight_in, weight_out, scale, sets):
    scales = scale[...].reshape(1, -1)
    across = (((1,), (1,)), ((), ()))
    in_terms, out_terms = [], []
    for norm, cot in sets:
        channels = norm.shape[2]
        normed = norm[...].reshape(-1, channels)
        upstream = cot[...].reshape(-1, channels).astype(F32)
        mixed_grad = (scales * upstream).astype(BF16)
        hidden = lax.dot_general(weight_in[...], normed, across, preferred_element_type=F32)
        act_grad = lax.dot_general(weight_out[...], mixed_grad, across, preferred_element_type=F32)
        activated, hidden_grad = slopes(hidden, act_grad)
        in_terms.append(jnp.dot(hidden_grad, normed, preferred_element_type=F32))
        out_terms.append(jnp.dot(activated, mixed_grad, preferred_element_type=F32))
    return tree_sum(in_terms), tree_sum(out_terms)


def one_side_kernel(
    which, weight_in, weight_out, scale, norm, cot, other_norm, other_cot, out
):
    del which
    sets = ((norm, cot), (other_norm, other_cot))
    terms = weight_grad_terms(weight_in, weight_out, scale, sets)
    for k in range(2):
        out[k] = terms[k].astype(out.dtype)


def last_sum_kernel(kept, got, in_grad, out_grad):
    for k, out in enumerate((in_grad, out_grad)):
        out[...] = kept[k] + got[k].astype(F32)


def chip_sum_kernel(kept, got, *rest):
    *blocks, out, together = rest
    for k, block in enumerate(blocks):
        together[k] = block[...]
    out[...] = (kept[...].astype(F32) + got[...].astype(F32)).astype(BF16)


def spread_sum_kernel(parts, out):
    total = tree_sum([parts[k].astype(F32) for k in range(parts.shape[0])]).astype(BF16)
    for copy in range(out.shape[0]):
        out[copy] = total


def unpack_kernel(core, own, other, out, *small):
    piece, wide = own.shape[1:]

    def unpack(*halves):
        last = []
        for side, parts in enumerate(halves):
            lanes = slice(side * wide, (side + 1) * wide)
            for k in range(-(-TAP_ROWS // piece)):
                first = k * piece
                length = min(piece, TAP_ROWS - first)
                out[first : first + length, lanes] = parts[k].astype(F32)[:length, :]
            k = TAP_ROWS // piece
            last.append(parts[k].astype(F32))
        rows = jnp.concatenate(last, axis=1)
        first = TAP_ROWS % piece
        for k, line in enumerate(small):
            line[...] = rows[first + k : first + k + 1, :].reshape(line.shape)

    by_core(core, own, other, lambda outer, inner: unpack(inner, outer))


def params(limit=48):
    return pltpu.CompilerParams(vmem_limit_bytes=limit * 1024 * 1024)


def follow(kernel, scalars, inputs, count):
    def body(*refs):
        head = refs[: scalars + inputs]
        return kernel(*head, *refs[scalars + inputs + count :])

    return body


IN_PLACE = pl.BlockSpec(memory_space=pl.ANY)


def lane_block(rows):
    return pl.BlockSpec((rows, LANES), lambda c, *_: (0, c))


def whole_block(*shape):
    return pl.BlockSpec(shape, lambda *_: (0,) * len(shape))


def rims(cells):
    count = lax.axis_size("row")
    between = [(i, i + 1) for i in range(1, count - 1, 2)]
    return (
        lax.ppermute(cells, "row", [(i, i ^ 1) for i in range(count)]),
        lax.ppermute(cells, "row", between + [(j, i) for i, j in between]),
    )


def on_device(
    voxels, dw_kernel, norm_gain, norm_bias, weight_in, weight_out, layer_scale, cotangent
):
    planes, height, breadth, channels = voxels.shape
    rows = planes * height * breadth
    units = weight_in.shape[0]
    count = lax.axis_size("row")
    me = lax.axis_index("row")
    quad = 4
    line = count // quad
    other_core = [(i, i ^ 1) for i in range(count)]
    other_side = [(i, i ^ 2) for i in range(count)]
    tiles = channels // LANES

    own = voxels.reshape(rows, channels)
    upstream = cotangent.reshape(rows, channels)
    core = lax.rem(me, 2).astype(jnp.int32)
    parity = core.reshape(1)

    inner, outer = rims(own)

    def along_line(cells, steps):
        return lax.ppermute(cells, "row", [(i, (i + quad * steps) % count) for i in range(count)])

    upstream_line = [upstream] + [None] * (line - 1)
    upstream_line[1] = along_line(upstream, 1)
    upstream_line[-1] = along_line(upstream, -1)

    def spread_of(held):
        return pltpu.VMEM((9, held, PAD, LANES), F32)

    split_block = pl.BlockSpec((None, 9, KS, SUB, LANES), lambda c, *_: (c, 0, 0, 0, 0))
    partial, split, vectors = pl.pallas_call(
        functools.partial(own_conv_kernel, planes, height),
        grid=(tiles,),
        in_specs=[lane_block(rows), lane_block(TAP_ROWS)] + [whole_block(channels)] * 2,
        out_specs=[lane_block(rows), split_block, whole_block(SUB, channels)],
        out_shape=[
            jax.ShapeDtypeStruct((rows, channels), F32),
            jax.ShapeDtypeStruct((tiles, 9, KS, SUB, LANES), F32),
            jax.ShapeDtypeStruct((SUB, channels), F32),
        ],
        scratch_shapes=[spread_of(planes)],
        compiler_params=params(),
        cost_estimate=NO_COST,
        name="own_conv",
    )(own, dw_kernel, norm_gain, norm_bias)

    for k in range(2, line - 1):
        upstream_line[k] = along_line(upstream_line[k - 1], 1)
    normed, centered = pl.pallas_call(
        follow(functools.partial(rim_conv_kernel, planes, height), 1, 5, 2),
        grid_spec=pltpu.PrefetchScalarGridSpec(
            num_scalar_prefetch=1,
            grid=(tiles,),
            in_specs=[
                lane_block(rows),
                lane_block(rows),
                split_block,
                lane_block(rows),
                whole_block(SUB, channels),
                IN_PLACE,
                IN_PLACE,
            ],
            out_specs=[
                whole_block(rows, channels),
                whole_block(rows, channels),
            ],
            scratch_shapes=[spread_of(2 * MARGIN), pltpu.VMEM((tiles, rows, LANES), F32)],
        ),
        out_shape=[
            jax.ShapeDtypeStruct((rows, channels), BF16),
            jax.ShapeDtypeStruct((rows, channels), F32),
        ],
        compiler_params=params(),
        cost_estimate=NO_COST,
        name="rim_conv",
    )(
        parity,
        inner,
        outer,
        split,
        partial,
        vectors,
        upstream_line[1],
        upstream_line[-1],
    )

    normed, upstream_line[2] = lax.optimization_barrier((normed, upstream_line[2]))
    norm_line = [normed] + [None] * (line - 1)
    norm_line[1] = along_line(normed, 1)
    norm_line[-1] = along_line(normed, -1)

    block = 1024
    whole = whole_block(rows, channels)
    block_out, conv_grad, small, cotangents = pl.pallas_call(
        mlp_kernel,
        grid=(units // block,),
        in_specs=[
            whole,
            pl.BlockSpec((block, channels), lambda f: (f, 0)),
            pl.BlockSpec((block, channels), lambda f: (f, 0)),
            whole,
            whole_block(channels),
            whole_block(channels),
        ]
        + [whole] * (1 + line),
        out_specs=[
            whole,
            whole,
            whole_block(SUB, channels),
            whole_block(line, rows, channels),
        ],
        out_shape=[
            jax.ShapeDtypeStruct((rows, channels), BF16),
            jax.ShapeDtypeStruct((rows, channels), BF16),
            jax.ShapeDtypeStruct((SUB, channels), F32),
            jax.ShapeDtypeStruct((line, rows, channels), BF16),
        ],
        scratch_shapes=[
            pltpu.VMEM((rows, channels), F32),
            pltpu.VMEM((rows, channels), F32),
            pltpu.VMEM((rows, channels), BF16),
        ],
        compiler_params=params(),
        cost_estimate=NO_COST,
        name="mlp_both_ways",
    )(normed, weight_in, weight_out, centered, norm_gain, layer_scale, own, *upstream_line)

    small, norm_line[1], norm_line[-1] = lax.optimization_barrier(
        (small, norm_line[1], norm_line[-1])
    )
    for k in range(2, line - 1):
        norm_line[k] = along_line(norm_line[k - 1], 1)

    grad_inner, grad_outer = rims(conv_grad)

    half = count // 2
    alike = [[2 * k + p for k in range(half)] for p in range(2)]
    half_tiles = tiles // 2
    wide = half_tiles * LANES
    piece = -(-(TAP_ROWS + SUB) // half)
    piece += -piece % (2 * SUB)
    padded = piece * half

    def tile_of(block_rows):
        def at(c, w):
            return 0, (c + w[1] * half_tiles) % tiles

        return pl.BlockSpec((block_rows, LANES), at)

    half_sent, half_kept = pl.pallas_call(
        functools.partial(kernel_grad_kernel, planes, height),
        grid_spec=pltpu.PrefetchScalarGridSpec(
            num_scalar_prefetch=1,
            grid=(tiles,),
            in_specs=[tile_of(rows), tile_of(rows), tile_of(rows), tile_of(rows), tile_of(SUB)],
            out_specs=[
                pl.BlockSpec((padded, LANES), lambda c, w: (0, jnp.minimum(c, half_tiles - 1))),
                pl.BlockSpec((padded, LANES), lambda c, w: (0, jnp.maximum(c - half_tiles, 0))),
            ],
            scratch_shapes=[
                spread_of(2 * MARGIN + planes),
                pltpu.VMEM((2, KS, SUB * SUB, LANES), F32),
                pltpu.VMEM((9, KS, SUB, LANES), F32),
                pltpu.VMEM((padded, LANES), F32),
            ],
        ),
        out_shape=[jax.ShapeDtypeStruct((padded, wide), BF16)] * 2,
        compiler_params=params(),
        cost_estimate=NO_COST,
        name="kernel_grad_terms",
    )(jnp.stack([core, 1 - core]), inner, own, outer, conv_grad, small)

    half_sent, norm_line[2], grad_inner, grad_outer = lax.optimization_barrier(
        (half_sent, norm_line[2], grad_inner, grad_outer)
    )
    half_got = lax.ppermute(half_sent, "row", other_core)
    sums, gathered = pl.pallas_call(
        chip_sum_kernel,
        in_specs=[whole_block(padded, wide)] * 2 + [whole] * line,
        out_specs=[whole_block(padded, wide), whole_block(line, rows, channels)],
        out_shape=[
            jax.ShapeDtypeStruct((padded, wide), BF16),
            jax.ShapeDtypeStruct((line, rows, channels), BF16),
        ],
        grid=(1,),
        compiler_params=params(),
        cost_estimate=NO_COST,
        name="kernel_grad_chip_sum",
    )(half_kept, half_got, *norm_line)

    share = units // count
    tokens = line * rows
    base = me // quad * quad
    side = lax.rem(me, quad) // 2
    far = base + 2 * (1 - side)
    near = base + 2 * side
    which = jnp.stack([far + core, near + core]).astype(jnp.int32)
    other_gathered = lax.ppermute(gathered, "row", other_core)
    other_cotangents = lax.ppermute(cotangents, "row", other_core)

    def side_terms(number, dtype, after, name):
        chunk = pl.BlockSpec((share, channels), lambda _, w: (w[number], 0))
        return pl.pallas_call(
            follow(one_side_kernel, 1, 7, 1),
            grid_spec=pltpu.PrefetchScalarGridSpec(
                num_scalar_prefetch=1,
                grid=(1,),
                in_specs=[chunk, chunk, whole_block(channels)]
                + [pl.BlockSpec(memory_space=pltpu.VMEM)] * 4
                + [IN_PLACE],
                out_specs=whole_block(2, share, channels),
            ),
            out_shape=jax.ShapeDtypeStruct((2, share, channels), dtype),
            compiler_params=params(),
            cost_estimate=NO_COST,
            name=name,
        )(
            which,
            weight_in,
            weight_out,
            layer_scale,
            gathered,
            cotangents,
            other_gathered,
            other_cotangents,
            after,
        )

    sent = side_terms(0, BF16, sums, "weight_grads_far_side")
    got = lax.ppermute(sent, "row", other_side)
    scattered = lax.all_to_all(
        sums.reshape(half, piece, wide),
        "row",
        split_axis=0,
        concat_axis=0,
        tiled=True,
        axis_index_groups=alike,
    )
    voxel_grad, token = pl.pallas_call(
        follow(functools.partial(input_grad_kernel, planes, height), 1, 5, 1),
        grid_spec=pltpu.PrefetchScalarGridSpec(
            num_scalar_prefetch=1,
            grid=(tiles,),
            in_specs=[
                lane_block(rows),
                lane_block(rows),
                lane_block(rows),
                lane_block(TAP_ROWS),
                lane_block(rows),
                IN_PLACE,
            ],
            out_specs=[lane_block(rows), whole_block(SUB, LANES)],
            scratch_shapes=[
                spread_of(2 * MARGIN + planes),
                pltpu.VMEM((9, KS, SUB, LANES), F32),
            ],
        ),
        out_shape=[
            jax.ShapeDtypeStruct((rows, channels), BF16),
            jax.ShapeDtypeStruct((SUB, LANES), F32),
        ],
        compiler_params=params(),
        cost_estimate=NO_COST,
        name="input_grad_conv",
    )(parity, grad_inner, conv_grad, grad_outer, dw_kernel, upstream, sent)

    copies = pl.pallas_call(
        follow(spread_sum_kernel, 0, 1, 1),
        in_specs=[whole_block(half, piece, wide), IN_PLACE],
        out_specs=whole_block(half, piece, wide),
        out_shape=jax.ShapeDtypeStruct((half, piece, wide), BF16),
        grid=(1,),
        compiler_params=params(),
        cost_estimate=NO_COST,
        name="kernel_grad_sum",
    )(scattered, token)
    totals = lax.all_to_all(
        copies, "row", split_axis=0, concat_axis=0, tiled=True, axis_index_groups=alike
    )
    kept = side_terms(1, F32, copies, "weight_grads_near_side")
    totals, kept = lax.optimization_barrier((totals, kept))
    other_totals = lax.ppermute(totals, "row", other_core)
    kernel_grad, *vector_grads = pl.pallas_call(
        unpack_kernel,
        grid_spec=pltpu.PrefetchScalarGridSpec(
            num_scalar_prefetch=1,
            grid=(1,),
            in_specs=[whole_block(half, piece, wide)] * 2,
            out_specs=[whole_block(TAP_ROWS, channels)] + [whole_block(channels)] * 3,
        ),
        out_shape=[jax.ShapeDtypeStruct((TAP_ROWS, channels), F32)]
        + [jax.ShapeDtypeStruct((channels,), F32)] * 3,
        compiler_params=params(),
        cost_estimate=NO_COST,
        name="kernel_grad_unpack",
    )(parity, totals, other_totals)

    weight_in_grad, weight_out_grad = pl.pallas_call(
        last_sum_kernel,
        grid=(1,),
        in_specs=[whole_block(2, share, channels)] * 2,
        out_specs=[whole_block(share, channels)] * 2,
        out_shape=[jax.ShapeDtypeStruct((share, channels), F32)] * 2,
        compiler_params=params(),
        cost_estimate=NO_COST,
        name="weight_grads_sum",
    )(kept, got)

    return (
        block_out.reshape(voxels.shape),
        voxel_grad.reshape(voxels.shape),
        kernel_grad,
        *vector_grads,
        weight_in_grad,
        weight_out_grad,
    )


def solution(mesh):
    in_specs = (
        P(("group", "row"), None, None, None),
        P(),
        P(),
        P(),
        P(),
        P(),
        P(),
        P(("group", "row"), None, None, None),
    )
    out_specs = (
        P(("group", "row"), None, None, None),
        P(("group", "row"), None, None, None),
        P("group", None),
        P("group"),
        P("group"),
        P("group"),
        P(("group", "row"), None),
        P(("group", "row"), None),
    )
    return jax.shard_map(
        on_device, mesh=mesh, in_specs=in_specs, out_specs=out_specs, check_vma=False
    )
```

```python
import functools

import jax
import jax.numpy as jnp
from jax import lax
from jax.experimental import pallas as pl
from jax.experimental.pallas import tpu as pltpu
from jax.sharding import PartitionSpec as P

KS = 7
MARGIN = KS // 2
LANES = 128
SUB = 8
PAD = 3 * SUB
TAP_ROWS = KS * KS * KS

root_half = 0.7071067811865476
inv_root_tau = 0.3989422804014327
norm_eps = 1e-06
erf_step = 0.3275911
erf_terms = tuple(
    0.5 * a for a in (0.254829592, -0.284496736, 1.421413741, -1.453152027, 1.061405429)
)

NO_COST = pl.CostEstimate(flops=0, bytes_accessed=0, transcendentals=0)

F32 = jnp.float32
BF16 = jnp.bfloat16


def split_source(v):
    terms = []
    for a, b in ((v[0] + v[2], v[1] + v[3]), (v[2], v[3]), (v[0], v[1])):
        terms += [a + b, b, a]
    return terms


def split_taps(t):
    terms = []
    for s in (
        (t[2], t[3], t[4]),
        (t[4] - t[2], t[5] - t[3], t[6] - t[4]),
        (t[0] - t[2], t[1] - t[3], t[2] - t[4]),
    ):
        terms += [s[1], s[2] - s[1], s[0] - s[1]]
    return terms


def split_grads(g):
    terms = []
    for a, b in ((g[0] + g[2], g[1] + g[3]), (g[0], g[1]), (g[2], g[3])):
        terms += [a + b, a, b]
    return terms


def join_outputs(m):
    pair = [(m[3 * k] + m[3 * k + 1], m[3 * k] + m[3 * k + 2]) for k in range(3)]
    return [
        pair[0][0] + pair[1][0],
        pair[0][1] + pair[1][1],
        pair[0][0] + pair[2][0],
        pair[0][1] + pair[2][1],
    ]


def join_taps(m):
    p, q, r = [
        (m[3 * k + 2], m[3 * k] - m[3 * k + 1] - m[3 * k + 2], m[3 * k + 1]) for k in range(3)
    ]
    return [
        r[0],
        r[1],
        p[0] - q[0] - r[0] + r[2],
        p[1] - q[1] - r[1],
        p[2] - q[2] - r[2] + q[0],
        q[1],
        q[2],
    ]


def tree_sum(terms):
    while len(terms) > 1:
        terms = [
            terms[k] + terms[k + 1] if k + 1 < len(terms) else terms[k]
            for k in range(0, len(terms), 2)
        ]
    return terms[0]


def stage_source(wanted, height, spread):
    row = height * SUB
    for at, (block, x) in enumerate(wanted):
        plane = block[x * row : (x + 1) * row, :].astype(F32)
        lines = [plane[y * SUB : (y + 1) * SUB, :] for y in range(height)]
        for j, term in enumerate(split_source(lines)):
            spread[j, at, SUB : 2 * SUB, :] = term


def rim_planes(left, right, planes):
    wanted = [(left, x) for x in range(planes - MARGIN, planes)]
    return wanted + [(right, x) for x in range(MARGIN)]


def all_planes(left, own, right, planes):
    rim = rim_planes(left, right, planes)
    return rim[:MARGIN] + [(own, x) for x in range(planes)] + rim[MARGIN:]


def by_core(core, inner, outer, stage):
    @pl.when(core[0] == 0)
    def _():
        stage(outer, inner)

    @pl.when(core[0] != 0)
    def _():
        stage(inner, outer)


def clear_rims(spread):
    zeros = jnp.zeros(spread.shape[:2] + (SUB, LANES), F32)
    spread[:, :, :SUB, :] = zeros
    spread[:, :, 2 * SUB :, :] = zeros


def stage_taps(taps, split):
    for dx in range(KS):
        rows = []
        for dy in range(KS):
            first = dx * KS * KS + dy * KS
            if first + SUB <= TAP_ROWS:
                rows.append(taps[first : first + SUB, :])
            else:
                rows.append(pltpu.roll(taps[TAP_ROWS - SUB : TAP_ROWS, :], SUB - 1, 0))
        for j, term in enumerate(split_taps(rows)):
            split[j, dx] = term


REVERSED = (0, 2, 1, 6, 8, 7, 3, 5, 4)


def convolve(spread, split, planes, held, flipped):
    terms = []
    for j in range(9):
        sums = [None] * planes
        for dz in range(KS):
            first = SUB - MARGIN + dz
            source = {x: spread[j, at, first : first + SUB, :] for at, x in enumerate(held)}
            weights = []
            for dx in range(KS):
                if flipped:
                    tap = split[REVERSED[j], KS - 1 - dx, KS - 1 - dz : KS - dz, :]
                else:
                    tap = split[j, dx, dz : dz + 1, :]
                weights.append(jnp.broadcast_to(tap, (SUB, LANES)))
            for x in range(planes):
                part = tree_sum(
                    [source[x + dx] * weights[dx] for dx in range(KS) if x + dx in source]
                )
                sums[x] = part if sums[x] is None else sums[x] + part
        terms.append(sums)
    return [join_outputs([terms[j][x] for j in range(9)]) for x in range(planes)]


def own_conv_kernel(planes, height, own, taps, gain, bias, out, split, vectors, spread):
    @pl.when(pl.program_id(0) == 0)
    def _():
        for k, line in enumerate((gain, bias)):
            vectors[k : k + 1, :] = line[...].reshape(1, -1)
        clear_rims(spread)

    stage_source([(own, x) for x in range(planes)], height, spread)
    stage_taps(taps, split)
    rows = convolve(spread, split, planes, range(MARGIN, MARGIN + planes), False)
    for x in range(planes):
        for y in range(height):
            at = (x * height + y) * SUB
            out[at : at + SUB, :] = rows[x][y]


def rim_conv_kernel(
    planes, height, core, inner, outer, split, partial, vectors, normed, centered, spread, conv
):
    step = pl.program_id(0)

    @pl.when(step == 0)
    def _():
        clear_rims(spread)

    def stage(left, right):
        stage_source(rim_planes(left, right, planes), height, spread)

    by_core(core, inner, outer, stage)
    held = list(range(MARGIN)) + list(range(MARGIN + planes, 2 * MARGIN + planes))
    rows = convolve(spread, split, planes, held, False)
    for x in range(planes):
        for y in range(height):
            at = (x * height + y) * SUB
            conv[step, at : at + SUB, :] = rows[x][y] + partial[at : at + SUB, :]

    @pl.when(step == pl.num_programs(0) - 1)
    def _():
        tiles = conv.shape[0]
        channels = tiles * LANES
        parts = [conv[k] for k in range(tiles)]
        gains = vectors[0:1, :]
        biases = vectors[1:2, :]
        average = jnp.sum(tree_sum(parts), axis=1, keepdims=True) * (1.0 / channels)
        parts = [part - average for part in parts]
        variance = jnp.sum(
            tree_sum([part * part for part in parts]), axis=1, keepdims=True
        ) * (1.0 / channels)
        inverse = lax.rsqrt(variance + norm_eps)
        for k in range(tiles):
            lanes = slice(k * LANES, (k + 1) * LANES)
            centered[:, lanes] = parts[k]
            value = parts[k] * inverse
            whole = (value * gains[:, lanes] + biases[:, lanes]).astype(BF16)
            normed[:, lanes] = whole


def input_grad_kernel(
    planes, height, core, inner, own, outer, taps, cotangent, out, token, spread, split
):
    @pl.when(pl.program_id(0) == 0)
    def _():
        clear_rims(spread)

    def stage(left, right):
        stage_source(all_planes(left, own, right, planes), height, spread)

    by_core(core, inner, outer, stage)
    stage_taps(taps, split)
    token[...] = jnp.zeros(token.shape, F32)
    rows = convolve(spread, split, planes, range(2 * MARGIN + planes), True)
    for x in range(planes):
        at = x * height * SUB
        whole = jnp.concatenate(rows[x], axis=0)
        upstream = cotangent[at : at + height * SUB, :].astype(F32)
        out[at : at + height * SUB, :] = (upstream + whole).astype(BF16)


def kernel_grad_kernel(
    planes,
    height,
    which,
    inner,
    own,
    outer,
    grads,
    small,
    sent,
    kept,
    spread,
    products,
    joined,
    flat,
):
    @pl.when(pl.program_id(0) == 0)
    def _():
        clear_rims(spread)
        products[...] = jnp.zeros(products.shape, F32)
        flat[...] = jnp.zeros(flat.shape, F32)

    def stage(left, right):
        stage_source(all_planes(left, own, right, planes), height, spread)

    by_core(which, inner, outer, stage)
    upstream = []
    for x in range(planes):
        plane = grads[x * height * SUB : (x + 1) * height * SUB, :].astype(F32)
        upstream.append(
            split_grads([plane[y * SUB : (y + 1) * SUB, :] for y in range(height)])
        )
    for j in range(9):
        for dz in range(KS):
            first = SUB - MARGIN + dz
            source = [
                spread[j, x, first : first + SUB, :] for x in range(planes + KS - 1)
            ]
            for dx in range(KS):
                products[j % 2, dx, dz * SUB : (dz + 1) * SUB, :] = tree_sum(
                    [source[x + dx] * upstream[x][j] for x in range(planes)]
                )
        for dx in range(KS):
            joined[j, dx] = tree_sum(
                [products[j % 2, dx, pl.ds(s, SUB, stride=SUB), :] for s in range(SUB)]
            )
    for dx in range(KS):
        for dy, tile in enumerate(join_taps([joined[j, dx] for j in range(9)])):
            row = dx * KS * KS + dy * KS
            flat[row : row + SUB, :] = tile
    flat[TAP_ROWS : TAP_ROWS + SUB, :] = small[...]
    step = pl.program_id(0)
    half = pl.num_programs(0) // 2

    @pl.when(step < half)
    def _():
        sent[...] = flat[...].astype(BF16)

    @pl.when(step >= half)
    def _():
        kept[...] = flat[...].astype(BF16)


def mlp_kernel(
    normed, weight_in, weight_out, centered, norm_gain, layer_scale, voxels, *rest
):
    *cotangents, block_out, conv_grad, small, together, mixed, back, mixed_grad = rest
    cotangent = cotangents[0]
    step = pl.program_id(0)
    gain = norm_gain[...].reshape(1, -1)
    scale = layer_scale[...].reshape(1, -1)

    @pl.when(step == 0)
    def _():
        mixed_grad[...] = (scale * cotangent[...].astype(F32)).astype(BF16)
        for k, part in enumerate(cotangents):
            together[k] = part[...]

    across = (((1,), (1,)), ((), ()))
    hidden = lax.dot_general(normed[...], weight_in[...], across, preferred_element_type=F32)
    act_grad = lax.dot_general(
        mixed_grad[...], weight_out[...], across, preferred_element_type=F32
    )
    activated, hidden_grad = slopes(hidden, act_grad)
    forward = jnp.dot(activated, weight_out[...], preferred_element_type=F32)
    backward = jnp.dot(hidden_grad, weight_in[...], preferred_element_type=F32)

    @pl.when(step == 0)
    def _():
        mixed[...] = forward
        back[...] = backward

    @pl.when(step > 0)
    def _():
        mixed[...] += forward
        back[...] += backward

    @pl.when(step == pl.num_programs(0) - 1)
    def _():
        channels = gain.shape[1]
        whole = mixed[...]
        block_out[...] = (voxels[...].astype(F32) + scale * whole).astype(BF16)
        scale_local = jnp.sum(cotangent[...].astype(F32) * whole, axis=0, keepdims=True)
        grad = back[...]
        deviation = centered[...]
        variance = jnp.sum(deviation * deviation, axis=1, keepdims=True) * (1.0 / channels)
        inverse = lax.rsqrt(variance + norm_eps)
        one = deviation * inverse
        bias_local = jnp.sum(grad, axis=0, keepdims=True)
        gain_local = jnp.sum(grad * one, axis=0, keepdims=True)
        small[...] = jnp.concatenate(
            [gain_local, bias_local, scale_local, jnp.zeros((SUB - 3, channels), F32)], axis=0
        )
        scaled = grad * gain
        average = jnp.sum(scaled, axis=1, keepdims=True) * (1.0 / channels)
        slant = jnp.sum(scaled * one, axis=1, keepdims=True) * (1.0 / channels)
        conv_grad[...] = (inverse * (scaled - average - one * slant)).astype(BF16)


def slopes(hidden, act_grad):
    bell = jnp.exp(-0.5 * hidden * hidden)
    below = 1.0 + (erf_step * root_half) * jnp.abs(hidden)
    t = pl.reciprocal(below, approx=True)
    t = t * (2.0 - below * t)
    poly = erf_terms[-1]
    for term in erf_terms[-2::-1]:
        poly = poly * t + term
    tail = poly * t * bell
    cover = jnp.where(hidden < 0.0, tail, 1.0 - tail)
    activated = (hidden * cover).astype(BF16)
    slope = cover + hidden * bell * inv_root_tau
    return activated, (act_grad * slope).astype(BF16)


def weight_grad_terms(weight_in, weight_out, scale, sets):
    scales = scale[...].reshape(1, -1)
    across = (((1,), (1,)), ((), ()))
    in_terms, out_terms = [], []
    for norm, cot in sets:
        channels = norm.shape[2]
        normed = norm[...].reshape(-1, channels)
        upstream = cot[...].reshape(-1, channels).astype(F32)
        mixed_grad = (scales * upstream).astype(BF16)
        hidden = lax.dot_general(weight_in[...], normed, across, preferred_element_type=F32)
        act_grad = lax.dot_general(weight_out[...], mixed_grad, across, preferred_element_type=F32)
        activated, hidden_grad = slopes(hidden, act_grad)
        in_terms.append(jnp.dot(hidden_grad, normed, preferred_element_type=F32))
        out_terms.append(jnp.dot(activated, mixed_grad, preferred_element_type=F32))
    return tree_sum(in_terms), tree_sum(out_terms)


def far_side_kernel(which, weight_in, weight_out, scale, norm, cot, other_norm, other_cot, sent):
    del which
    sets = ((norm, cot), (other_norm, other_cot))
    terms = weight_grad_terms(weight_in, weight_out, scale, sets)
    for k in range(2):
        sent[k] = terms[k].astype(BF16)


def near_side_kernel(
    which, weight_in, weight_out, scale, norm, cot, other_norm, other_cot, got, in_grad, out_grad
):
    del which
    sets = ((norm, cot), (other_norm, other_cot))
    terms = weight_grad_terms(weight_in, weight_out, scale, sets)
    for k, out in enumerate((in_grad, out_grad)):
        out[...] = terms[k] + got[k].astype(F32)


def chip_sum_kernel(kept, got, *rest):
    *blocks, out, together = rest
    for k, block in enumerate(blocks):
        together[k] = block[...]
    out[...] = (kept[...].astype(F32) + got[...].astype(F32)).astype(BF16)


def spread_sum_kernel(parts, out):
    total = tree_sum([parts[k].astype(F32) for k in range(parts.shape[0])]).astype(BF16)
    for copy in range(out.shape[0]):
        out[copy] = total


def unpack_kernel(core, own, other, out, *small):
    piece, wide = own.shape[1:]

    def unpack(*halves):
        last = []
        for side, parts in enumerate(halves):
            lanes = slice(side * wide, (side + 1) * wide)
            for k in range(-(-TAP_ROWS // piece)):
                first = k * piece
                length = min(piece, TAP_ROWS - first)
                out[first : first + length, lanes] = parts[k].astype(F32)[:length, :]
            k = TAP_ROWS // piece
            last.append(parts[k].astype(F32))
        rows = jnp.concatenate(last, axis=1)
        first = TAP_ROWS % piece
        for k, line in enumerate(small):
            line[...] = rows[first + k : first + k + 1, :].reshape(line.shape)

    by_core(core, own, other, lambda outer, inner: unpack(inner, outer))


def params(limit=48):
    return pltpu.CompilerParams(vmem_limit_bytes=limit * 1024 * 1024)


def follow(kernel, scalars, inputs, count):
    def body(*refs):
        head = refs[: scalars + inputs]
        return kernel(*head, *refs[scalars + inputs + count :])

    return body


IN_PLACE = pl.BlockSpec(memory_space=pl.ANY)


def lane_block(rows):
    return pl.BlockSpec((rows, LANES), lambda c, *_: (0, c))


def whole_block(*shape):
    return pl.BlockSpec(shape, lambda *_: (0,) * len(shape))


def rims(cells):
    count = lax.axis_size("row")
    between = [(i, i + 1) for i in range(1, count - 1, 2)]
    return (
        lax.ppermute(cells, "row", [(i, i ^ 1) for i in range(count)]),
        lax.ppermute(cells, "row", between + [(j, i) for i, j in between]),
    )


def on_device(
    voxels, dw_kernel, norm_gain, norm_bias, weight_in, weight_out, layer_scale, cotangent
):
    planes, height, breadth, channels = voxels.shape
    rows = planes * height * breadth
    units = weight_in.shape[0]
    count = lax.axis_size("row")
    me = lax.axis_index("row")
    quad = 4
    line = count // quad
    other_core = [(i, i ^ 1) for i in range(count)]
    other_side = [(i, i ^ 2) for i in range(count)]
    tiles = channels // LANES

    own = voxels.reshape(rows, channels)
    upstream = cotangent.reshape(rows, channels)
    core = lax.rem(me, 2).astype(jnp.int32)
    parity = core.reshape(1)

    inner, outer = rims(own)

    def along_line(cells, steps):
        return lax.ppermute(cells, "row", [(i, (i + quad * steps) % count) for i in range(count)])

    upstream_line = [upstream] + [None] * (line - 1)
    upstream_line[1] = along_line(upstream, 1)
    upstream_line[-1] = along_line(upstream, -1)

    def spread_of(held):
        return pltpu.VMEM((9, held, PAD, LANES), F32)

    split_block = pl.BlockSpec((None, 9, KS, SUB, LANES), lambda c, *_: (c, 0, 0, 0, 0))
    partial, split, vectors = pl.pallas_call(
        functools.partial(own_conv_kernel, planes, height),
        grid=(tiles,),
        in_specs=[lane_block(rows), lane_block(TAP_ROWS)] + [whole_block(channels)] * 2,
        out_specs=[lane_block(rows), split_block, whole_block(SUB, channels)],
        out_shape=[
            jax.ShapeDtypeStruct((rows, channels), F32),
            jax.ShapeDtypeStruct((tiles, 9, KS, SUB, LANES), F32),
            jax.ShapeDtypeStruct((SUB, channels), F32),
        ],
        scratch_shapes=[spread_of(planes)],
        compiler_params=params(),
        cost_estimate=NO_COST,
        name="own_conv",
    )(own, dw_kernel, norm_gain, norm_bias)

    for k in range(2, line - 1):
        upstream_line[k] = along_line(upstream_line[k - 1], 1)
    normed, centered = pl.pallas_call(
        follow(functools.partial(rim_conv_kernel, planes, height), 1, 5, 2),
        grid_spec=pltpu.PrefetchScalarGridSpec(
            num_scalar_prefetch=1,
            grid=(tiles,),
            in_specs=[
                lane_block(rows),
                lane_block(rows),
                split_block,
                lane_block(rows),
                whole_block(SUB, channels),
                IN_PLACE,
                IN_PLACE,
            ],
            out_specs=[
                whole_block(rows, channels),
                whole_block(rows, channels),
            ],
            scratch_shapes=[spread_of(2 * MARGIN), pltpu.VMEM((tiles, rows, LANES), F32)],
        ),
        out_shape=[
            jax.ShapeDtypeStruct((rows, channels), BF16),
            jax.ShapeDtypeStruct((rows, channels), F32),
        ],
        compiler_params=params(),
        cost_estimate=NO_COST,
        name="rim_conv",
    )(
        parity,
        inner,
        outer,
        split,
        partial,
        vectors,
        upstream_line[1],
        upstream_line[-1],
    )

    normed, upstream_line[2] = lax.optimization_barrier((normed, upstream_line[2]))
    norm_line = [normed] + [None] * (line - 1)
    norm_line[1] = along_line(normed, 1)
    norm_line[-1] = along_line(normed, -1)

    block = 1024
    whole = whole_block(rows, channels)
    block_out, conv_grad, small, cotangents = pl.pallas_call(
        mlp_kernel,
        grid=(units // block,),
        in_specs=[
            whole,
            pl.BlockSpec((block, channels), lambda f: (f, 0)),
            pl.BlockSpec((block, channels), lambda f: (f, 0)),
            whole,
            whole_block(channels),
            whole_block(channels),
        ]
        + [whole] * (1 + line),
        out_specs=[
            whole,
            whole,
            whole_block(SUB, channels),
            whole_block(line, rows, channels),
        ],
        out_shape=[
            jax.ShapeDtypeStruct((rows, channels), BF16),
            jax.ShapeDtypeStruct((rows, channels), BF16),
            jax.ShapeDtypeStruct((SUB, channels), F32),
            jax.ShapeDtypeStruct((line, rows, channels), BF16),
        ],
        scratch_shapes=[
            pltpu.VMEM((rows, channels), F32),
            pltpu.VMEM((rows, channels), F32),
            pltpu.VMEM((rows, channels), BF16),
        ],
        compiler_params=params(),
        cost_estimate=NO_COST,
        name="mlp_both_ways",
    )(normed, weight_in, weight_out, centered, norm_gain, layer_scale, own, *upstream_line)

    small, norm_line[1], norm_line[-1] = lax.optimization_barrier(
        (small, norm_line[1], norm_line[-1])
    )
    for k in range(2, line - 1):
        norm_line[k] = along_line(norm_line[k - 1], 1)

    grad_inner, grad_outer = rims(conv_grad)

    half = count // 2
    alike = [[2 * k + p for k in range(half)] for p in range(2)]
    half_tiles = tiles // 2
    wide = half_tiles * LANES
    piece = -(-(TAP_ROWS + SUB) // half)
    piece += -piece % (2 * SUB)
    padded = piece * half

    def tile_of(block_rows):
        def at(c, w):
            return 0, (c + w[1] * half_tiles) % tiles

        return pl.BlockSpec((block_rows, LANES), at)

    half_sent, half_kept = pl.pallas_call(
        functools.partial(kernel_grad_kernel, planes, height),
        grid_spec=pltpu.PrefetchScalarGridSpec(
            num_scalar_prefetch=1,
            grid=(tiles,),
            in_specs=[tile_of(rows), tile_of(rows), tile_of(rows), tile_of(rows), tile_of(SUB)],
            out_specs=[
                pl.BlockSpec((padded, LANES), lambda c, w: (0, jnp.minimum(c, half_tiles - 1))),
                pl.BlockSpec((padded, LANES), lambda c, w: (0, jnp.maximum(c - half_tiles, 0))),
            ],
            scratch_shapes=[
                spread_of(2 * MARGIN + planes),
                pltpu.VMEM((2, KS, SUB * SUB, LANES), F32),
                pltpu.VMEM((9, KS, SUB, LANES), F32),
                pltpu.VMEM((padded, LANES), F32),
            ],
        ),
        out_shape=[jax.ShapeDtypeStruct((padded, wide), BF16)] * 2,
        compiler_params=params(),
        cost_estimate=NO_COST,
        name="kernel_grad_terms",
    )(jnp.stack([core, 1 - core]), inner, own, outer, conv_grad, small)

    half_sent, norm_line[2], grad_inner, grad_outer = lax.optimization_barrier(
        (half_sent, norm_line[2], grad_inner, grad_outer)
    )
    half_got = lax.ppermute(half_sent, "row", other_core)
    sums, gathered = pl.pallas_call(
        chip_sum_kernel,
        in_specs=[whole_block(padded, wide)] * 2 + [whole] * line,
        out_specs=[whole_block(padded, wide), whole_block(line, rows, channels)],
        out_shape=[
            jax.ShapeDtypeStruct((padded, wide), BF16),
            jax.ShapeDtypeStruct((line, rows, channels), BF16),
        ],
        grid=(1,),
        compiler_params=params(),
        cost_estimate=NO_COST,
        name="kernel_grad_chip_sum",
    )(half_kept, half_got, *norm_line)

    share = units // count
    tokens = line * rows
    base = me // quad * quad
    side = lax.rem(me, quad) // 2
    far = base + 2 * (1 - side)
    near = base + 2 * side
    which = jnp.stack([far + core, near + core]).astype(jnp.int32)
    other_gathered = lax.ppermute(gathered, "row", other_core)
    other_cotangents = lax.ppermute(cotangents, "row", other_core)

    def side_terms(kernel, number, more, after, outs, name):
        chunk = pl.BlockSpec((share, channels), lambda _, w: (w[number], 0))
        return pl.pallas_call(
            follow(kernel, 1, 7 + len(more), 1),
            grid_spec=pltpu.PrefetchScalarGridSpec(
                num_scalar_prefetch=1,
                grid=(1,),
                in_specs=[chunk, chunk, whole_block(channels)]
                + [pl.BlockSpec(memory_space=pltpu.VMEM)] * 4
                + [whole_block(*part.shape) for part in more]
                + [IN_PLACE],
                out_specs=[whole_block(*out.shape) for out in outs],
            ),
            out_shape=outs,
            compiler_params=params(),
            cost_estimate=NO_COST,
            name=name,
        )(
            which,
            weight_in,
            weight_out,
            layer_scale,
            gathered,
            cotangents,
            other_gathered,
            other_cotangents,
            *more,
            after,
        )

    pair = jax.ShapeDtypeStruct((2, share, channels), BF16)
    single = jax.ShapeDtypeStruct((share, channels), F32)
    (sent,) = side_terms(far_side_kernel, 0, [], sums, [pair], "weight_grads_far_side")
    got = lax.ppermute(sent, "row", other_side)
    scattered = lax.all_to_all(
        sums.reshape(half, piece, wide),
        "row",
        split_axis=0,
        concat_axis=0,
        tiled=True,
        axis_index_groups=alike,
    )
    voxel_grad, token = pl.pallas_call(
        follow(functools.partial(input_grad_kernel, planes, height), 1, 5, 1),
        grid_spec=pltpu.PrefetchScalarGridSpec(
            num_scalar_prefetch=1,
            grid=(tiles,),
            in_specs=[
                lane_block(rows),
                lane_block(rows),
                lane_block(rows),
                lane_block(TAP_ROWS),
                lane_block(rows),
                IN_PLACE,
            ],
            out_specs=[lane_block(rows), whole_block(SUB, LANES)],
            scratch_shapes=[
                spread_of(2 * MARGIN + planes),
                pltpu.VMEM((9, KS, SUB, LANES), F32),
            ],
        ),
        out_shape=[
            jax.ShapeDtypeStruct((rows, channels), BF16),
            jax.ShapeDtypeStruct((SUB, LANES), F32),
        ],
        compiler_params=params(),
        cost_estimate=NO_COST,
        name="input_grad_conv",
    )(parity, grad_inner, conv_grad, grad_outer, dw_kernel, upstream, sent)

    copies = pl.pallas_call(
        follow(spread_sum_kernel, 0, 1, 1),
        in_specs=[whole_block(half, piece, wide), IN_PLACE],
        out_specs=whole_block(half, piece, wide),
        out_shape=jax.ShapeDtypeStruct((half, piece, wide), BF16),
        grid=(1,),
        compiler_params=params(),
        cost_estimate=NO_COST,
        name="kernel_grad_sum",
    )(scattered, token)
    totals = lax.all_to_all(
        copies, "row", split_axis=0, concat_axis=0, tiled=True, axis_index_groups=alike
    )
    weight_in_grad, weight_out_grad = side_terms(
        near_side_kernel, 1, [got], copies, [single, single], "weight_grads_near_side"
    )
    totals, weight_in_grad = lax.optimization_barrier((totals, weight_in_grad))
    other_totals = lax.ppermute(totals, "row", other_core)
    kernel_grad, *vector_grads = pl.pallas_call(
        unpack_kernel,
        grid_spec=pltpu.PrefetchScalarGridSpec(
            num_scalar_prefetch=1,
            grid=(1,),
            in_specs=[whole_block(half, piece, wide)] * 2,
            out_specs=[whole_block(TAP_ROWS, channels)] + [whole_block(channels)] * 3,
        ),
        out_shape=[jax.ShapeDtypeStruct((TAP_ROWS, channels), F32)]
        + [jax.ShapeDtypeStruct((channels,), F32)] * 3,
        compiler_params=params(),
        cost_estimate=NO_COST,
        name="kernel_grad_unpack",
    )(parity, totals, other_totals)

    return (
        block_out.reshape(voxels.shape),
        voxel_grad.reshape(voxels.shape),
        kernel_grad,
        *vector_grads,
        weight_in_grad,
        weight_out_grad,
    )


def solution(mesh):
    in_specs = (
        P(("group", "row"), None, None, None),
        P(),
        P(),
        P(),
        P(),
        P(),
        P(),
        P(("group", "row"), None, None, None),
    )
    out_specs = (
        P(("group", "row"), None, None, None),
        P(("group", "row"), None, None, None),
        P("group", None),
        P("group"),
        P("group"),
        P("group"),
        P(("group", "row"), None),
        P(("group", "row"), None),
    )
    return jax.shard_map(
        on_device, mesh=mesh, in_specs=in_specs, out_specs=out_specs, check_vma=False
    )
```

```python
import functools

import jax
import jax.numpy as jnp
from jax import lax
from jax.experimental import pallas as pl
from jax.experimental.pallas import tpu as pltpu
from jax.sharding import PartitionSpec as P

KS = 7
MARGIN = KS // 2
LANES = 128
SUB = 8
PAD = 3 * SUB
TAP_ROWS = KS * KS * KS

root_half = 0.7071067811865476
inv_root_tau = 0.3989422804014327
norm_eps = 1e-06

NO_COST = pl.CostEstimate(flops=0, bytes_accessed=0, transcendentals=0)

F32 = jnp.float32
BF16 = jnp.bfloat16


def split_source(v):
    terms = []
    for a, b in ((v[0] + v[2], v[1] + v[3]), (v[2], v[3]), (v[0], v[1])):
        terms += [a + b, b, a]
    return terms


def split_taps(t):
    terms = []
    for s in (
        (t[2], t[3], t[4]),
        (t[4] - t[2], t[5] - t[3], t[6] - t[4]),
        (t[0] - t[2], t[1] - t[3], t[2] - t[4]),
    ):
        terms += [s[1], s[2] - s[1], s[0] - s[1]]
    return terms


def split_grads(g):
    terms = []
    for a, b in ((g[0] + g[2], g[1] + g[3]), (g[0], g[1]), (g[2], g[3])):
        terms += [a + b, a, b]
    return terms


def join_outputs(m):
    pair = [(m[3 * k] + m[3 * k + 1], m[3 * k] + m[3 * k + 2]) for k in range(3)]
    return [
        pair[0][0] + pair[1][0],
        pair[0][1] + pair[1][1],
        pair[0][0] + pair[2][0],
        pair[0][1] + pair[2][1],
    ]


def join_taps(m):
    p, q, r = [
        (m[3 * k + 2], m[3 * k] - m[3 * k + 1] - m[3 * k + 2], m[3 * k + 1]) for k in range(3)
    ]
    return [
        r[0],
        r[1],
        p[0] - q[0] - r[0] + r[2],
        p[1] - q[1] - r[1],
        p[2] - q[2] - r[2] + q[0],
        q[1],
        q[2],
    ]


def tree_sum(terms):
    while len(terms) > 1:
        terms = [
            terms[k] + terms[k + 1] if k + 1 < len(terms) else terms[k]
            for k in range(0, len(terms), 2)
        ]
    return terms[0]


def stage_source(wanted, height, spread):
    row = height * SUB
    for at, (block, x) in enumerate(wanted):
        plane = block[x * row : (x + 1) * row, :].astype(F32)
        lines = [plane[y * SUB : (y + 1) * SUB, :] for y in range(height)]
        for j, term in enumerate(split_source(lines)):
            spread[j, at, SUB : 2 * SUB, :] = term


def rim_planes(left, right, planes):
    wanted = [(left, x) for x in range(planes - MARGIN, planes)]
    return wanted + [(right, x) for x in range(MARGIN)]


def all_planes(left, own, right, planes):
    rim = rim_planes(left, right, planes)
    return rim[:MARGIN] + [(own, x) for x in range(planes)] + rim[MARGIN:]


def by_core(core, inner, outer, stage):
    @pl.when(core[0] == 0)
    def _():
        stage(outer, inner)

    @pl.when(core[0] != 0)
    def _():
        stage(inner, outer)


def clear_rims(spread):
    zeros = jnp.zeros(spread.shape[:2] + (SUB, LANES), F32)
    spread[:, :, :SUB, :] = zeros
    spread[:, :, 2 * SUB :, :] = zeros


def stage_taps(taps, split):
    for dx in range(KS):
        rows = []
        for dy in range(KS):
            first = dx * KS * KS + dy * KS
            if first + SUB <= TAP_ROWS:
                rows.append(taps[first : first + SUB, :])
            else:
                rows.append(pltpu.roll(taps[TAP_ROWS - SUB : TAP_ROWS, :], SUB - 1, 0))
        for j, term in enumerate(split_taps(rows)):
            split[j, dx] = term


REVERSED = (0, 2, 1, 6, 8, 7, 3, 5, 4)


def convolve(spread, split, planes, held, flipped):
    terms = []
    for j in range(9):
        sums = [None] * planes
        for dz in range(KS):
            first = SUB - MARGIN + dz
            source = {x: spread[j, at, first : first + SUB, :] for at, x in enumerate(held)}
            weights = []
            for dx in range(KS):
                if flipped:
                    tap = split[REVERSED[j], KS - 1 - dx, KS - 1 - dz : KS - dz, :]
                else:
                    tap = split[j, dx, dz : dz + 1, :]
                weights.append(jnp.broadcast_to(tap, (SUB, LANES)))
            for x in range(planes):
                part = tree_sum(
                    [source[x + dx] * weights[dx] for dx in range(KS) if x + dx in source]
                )
                sums[x] = part if sums[x] is None else sums[x] + part
        terms.append(sums)
    return [join_outputs([terms[j][x] for j in range(9)]) for x in range(planes)]


def own_conv_kernel(planes, height, own, taps, gain, bias, out, split, vectors, spread):
    @pl.when(pl.program_id(0) == 0)
    def _():
        for k, line in enumerate((gain, bias)):
            vectors[k : k + 1, :] = line[...].reshape(1, -1)
        clear_rims(spread)

    stage_source([(own, x) for x in range(planes)], height, spread)
    stage_taps(taps, split)
    rows = convolve(spread, split, planes, range(MARGIN, MARGIN + planes), False)
    for x in range(planes):
        for y in range(height):
            at = (x * height + y) * SUB
            out[at : at + SUB, :] = rows[x][y]


def rim_conv_kernel(
    planes, height, core, inner, outer, split, partial, vectors, normed, centered, spread, conv
):
    step = pl.program_id(0)

    @pl.when(step == 0)
    def _():
        clear_rims(spread)

    def stage(left, right):
        stage_source(rim_planes(left, right, planes), height, spread)

    by_core(core, inner, outer, stage)
    held = list(range(MARGIN)) + list(range(MARGIN + planes, 2 * MARGIN + planes))
    rows = convolve(spread, split, planes, held, False)
    for x in range(planes):
        for y in range(height):
            at = (x * height + y) * SUB
            conv[step, at : at + SUB, :] = rows[x][y] + partial[at : at + SUB, :]

    @pl.when(step == pl.num_programs(0) - 1)
    def _():
        tiles = conv.shape[0]
        channels = tiles * LANES
        parts = [conv[k] for k in range(tiles)]
        gains = vectors[0:1, :]
        biases = vectors[1:2, :]
        average = jnp.sum(tree_sum(parts), axis=1, keepdims=True) * (1.0 / channels)
        parts = [part - average for part in parts]
        variance = jnp.sum(
            tree_sum([part * part for part in parts]), axis=1, keepdims=True
        ) * (1.0 / channels)
        inverse = lax.rsqrt(variance + norm_eps)
        for k in range(tiles):
            lanes = slice(k * LANES, (k + 1) * LANES)
            centered[:, lanes] = parts[k]
            value = parts[k] * inverse
            whole = (value * gains[:, lanes] + biases[:, lanes]).astype(BF16)
            normed[:, lanes] = whole


def input_grad_kernel(
    planes, height, core, inner, own, outer, taps, cotangent, out, token, spread, split
):
    @pl.when(pl.program_id(0) == 0)
    def _():
        clear_rims(spread)

    def stage(left, right):
        stage_source(all_planes(left, own, right, planes), height, spread)

    by_core(core, inner, outer, stage)
    stage_taps(taps, split)
    token[...] = jnp.zeros(token.shape, F32)
    rows = convolve(spread, split, planes, range(2 * MARGIN + planes), True)
    for x in range(planes):
        at = x * height * SUB
        whole = jnp.concatenate(rows[x], axis=0)
        upstream = cotangent[at : at + height * SUB, :].astype(F32)
        out[at : at + height * SUB, :] = (upstream + whole).astype(BF16)


def kernel_grad_kernel(
    planes,
    height,
    which,
    inner,
    own,
    outer,
    grads,
    small,
    sent,
    kept,
    spread,
    products,
    joined,
    flat,
):
    @pl.when(pl.program_id(0) == 0)
    def _():
        clear_rims(spread)
        products[...] = jnp.zeros(products.shape, F32)
        flat[...] = jnp.zeros(flat.shape, F32)

    def stage(left, right):
        stage_source(all_planes(left, own, right, planes), height, spread)

    by_core(which, inner, outer, stage)
    upstream = []
    for x in range(planes):
        plane = grads[x * height * SUB : (x + 1) * height * SUB, :].astype(F32)
        upstream.append(
            split_grads([plane[y * SUB : (y + 1) * SUB, :] for y in range(height)])
        )
    for j in range(9):
        for dz in range(KS):
            first = SUB - MARGIN + dz
            source = [
                spread[j, x, first : first + SUB, :] for x in range(planes + KS - 1)
            ]
            for dx in range(KS):
                products[j % 2, dx, dz * SUB : (dz + 1) * SUB, :] = tree_sum(
                    [source[x + dx] * upstream[x][j] for x in range(planes)]
                )
        for dx in range(KS):
            joined[j, dx] = tree_sum(
                [products[j % 2, dx, pl.ds(s, SUB, stride=SUB), :] for s in range(SUB)]
            )
    for dx in range(KS):
        for dy, tile in enumerate(join_taps([joined[j, dx] for j in range(9)])):
            row = dx * KS * KS + dy * KS
            flat[row : row + SUB, :] = tile
    flat[TAP_ROWS : TAP_ROWS + SUB, :] = small[...]
    step = pl.program_id(0)
    half = pl.num_programs(0) // 2

    @pl.when(step < half)
    def _():
        sent[...] = flat[...].astype(BF16)

    @pl.when(step >= half)
    def _():
        kept[...] = flat[...].astype(BF16)


def mlp_kernel(
    normed, weight_in, weight_out, centered, norm_gain, layer_scale, voxels, *rest
):
    *cotangents, block_out, conv_grad, small, together, mixed, back, mixed_grad = rest
    cotangent = cotangents[0]
    step = pl.program_id(0)
    gain = norm_gain[...].reshape(1, -1)
    scale = layer_scale[...].reshape(1, -1)

    @pl.when(step == 0)
    def _():
        mixed_grad[...] = (scale * cotangent[...].astype(F32)).astype(BF16)
        for k, part in enumerate(cotangents):
            together[k] = part[...]

    across = (((1,), (1,)), ((), ()))
    hidden = lax.dot_general(normed[...], weight_in[...], across, preferred_element_type=F32)
    act_grad = lax.dot_general(
        mixed_grad[...], weight_out[...], across, preferred_element_type=F32
    )
    activated, hidden_grad = slopes(hidden, act_grad)
    forward = jnp.dot(activated, weight_out[...], preferred_element_type=F32)
    backward = jnp.dot(hidden_grad, weight_in[...], preferred_element_type=F32)

    @pl.when(step == 0)
    def _():
        mixed[...] = forward
        back[...] = backward

    @pl.when(step > 0)
    def _():
        mixed[...] += forward
        back[...] += backward

    @pl.when(step == pl.num_programs(0) - 1)
    def _():
        channels = gain.shape[1]
        whole = mixed[...]
        block_out[...] = (voxels[...].astype(F32) + scale * whole).astype(BF16)
        scale_local = jnp.sum(cotangent[...].astype(F32) * whole, axis=0, keepdims=True)
        grad = back[...]
        deviation = centered[...]
        variance = jnp.sum(deviation * deviation, axis=1, keepdims=True) * (1.0 / channels)
        inverse = lax.rsqrt(variance + norm_eps)
        one = deviation * inverse
        bias_local = jnp.sum(grad, axis=0, keepdims=True)
        gain_local = jnp.sum(grad * one, axis=0, keepdims=True)
        small[...] = jnp.concatenate(
            [gain_local, bias_local, scale_local, jnp.zeros((SUB - 3, channels), F32)], axis=0
        )
        scaled = grad * gain
        average = jnp.sum(scaled, axis=1, keepdims=True) * (1.0 / channels)
        slant = jnp.sum(scaled * one, axis=1, keepdims=True) * (1.0 / channels)
        conv_grad[...] = (inverse * (scaled - average - one * slant)).astype(BF16)


def slopes(hidden, act_grad):
    cover = 0.5 * (1.0 + lax.erf(hidden * root_half))
    activated = (hidden * cover).astype(BF16)
    slope = cover + hidden * jnp.exp(-0.5 * hidden * hidden) * inv_root_tau
    return activated, (act_grad * slope).astype(BF16)


def weight_grad_terms(weight_in, weight_out, scale, sets):
    scales = scale[...].reshape(1, -1)
    across = (((1,), (1,)), ((), ()))
    in_terms, out_terms = [], []
    for norm, cot in sets:
        channels = norm.shape[2]
        normed = norm[...].reshape(-1, channels)
        upstream = cot[...].reshape(-1, channels).astype(F32)
        mixed_grad = (scales * upstream).astype(BF16)
        hidden = lax.dot_general(weight_in[...], normed, across, preferred_element_type=F32)
        act_grad = lax.dot_general(weight_out[...], mixed_grad, across, preferred_element_type=F32)
        activated, hidden_grad = slopes(hidden, act_grad)
        in_terms.append(jnp.dot(hidden_grad, normed, preferred_element_type=F32))
        out_terms.append(jnp.dot(activated, mixed_grad, preferred_element_type=F32))
    return tree_sum(in_terms), tree_sum(out_terms)


def far_side_kernel(which, weight_in, weight_out, scale, norm, cot, other_norm, other_cot, sent):
    del which
    sets = ((norm, cot), (other_norm, other_cot))
    terms = weight_grad_terms(weight_in, weight_out, scale, sets)
    for k in range(2):
        sent[k] = terms[k].astype(BF16)


def near_side_kernel(
    which, weight_in, weight_out, scale, norm, cot, other_norm, other_cot, got, in_grad, out_grad
):
    del which
    sets = ((norm, cot), (other_norm, other_cot))
    terms = weight_grad_terms(weight_in, weight_out, scale, sets)
    for k, out in enumerate((in_grad, out_grad)):
        out[...] = terms[k] + got[k].astype(F32)


def chip_sum_kernel(kept, got, *rest):
    *blocks, out, together = rest
    for k, block in enumerate(blocks):
        together[k] = block[...]
    out[...] = (kept[...].astype(F32) + got[...].astype(F32)).astype(BF16)


def spread_sum_kernel(parts, out):
    total = tree_sum([parts[k].astype(F32) for k in range(parts.shape[0])]).astype(BF16)
    for copy in range(out.shape[0]):
        out[copy] = total


def unpack_kernel(core, own, other, out, *small):
    piece, wide = own.shape[1:]

    def unpack(*halves):
        last = []
        for side, parts in enumerate(halves):
            lanes = slice(side * wide, (side + 1) * wide)
            for k in range(-(-TAP_ROWS // piece)):
                first = k * piece
                length = min(piece, TAP_ROWS - first)
                out[first : first + length, lanes] = parts[k].astype(F32)[:length, :]
            k = TAP_ROWS // piece
            last.append(parts[k].astype(F32))
        rows = jnp.concatenate(last, axis=1)
        first = TAP_ROWS % piece
        for k, line in enumerate(small):
            line[...] = rows[first + k : first + k + 1, :].reshape(line.shape)

    by_core(core, own, other, lambda outer, inner: unpack(inner, outer))


def params(limit=48):
    return pltpu.CompilerParams(vmem_limit_bytes=limit * 1024 * 1024)


def follow(kernel, scalars, inputs, count):
    def body(*refs):
        head = refs[: scalars + inputs]
        return kernel(*head, *refs[scalars + inputs + count :])

    return body


IN_PLACE = pl.BlockSpec(memory_space=pl.ANY)


def lane_block(rows):
    return pl.BlockSpec((rows, LANES), lambda c, *_: (0, c))


def whole_block(*shape):
    return pl.BlockSpec(shape, lambda *_: (0,) * len(shape))


def rims(cells):
    count = lax.axis_size("row")
    between = [(i, i + 1) for i in range(1, count - 1, 2)]
    return (
        lax.ppermute(cells, "row", [(i, i ^ 1) for i in range(count)]),
        lax.ppermute(cells, "row", between + [(j, i) for i, j in between]),
    )


def on_device(
    voxels, dw_kernel, norm_gain, norm_bias, weight_in, weight_out, layer_scale, cotangent
):
    planes, height, breadth, channels = voxels.shape
    rows = planes * height * breadth
    units = weight_in.shape[0]
    count = lax.axis_size("row")
    me = lax.axis_index("row")
    quad = 4
    line = count // quad
    other_core = [(i, i ^ 1) for i in range(count)]
    other_side = [(i, i ^ 2) for i in range(count)]
    tiles = channels // LANES

    own = voxels.reshape(rows, channels)
    upstream = cotangent.reshape(rows, channels)
    core = lax.rem(me, 2).astype(jnp.int32)
    parity = core.reshape(1)

    inner, outer = rims(own)

    def along_line(cells, steps):
        return lax.ppermute(cells, "row", [(i, (i + quad * steps) % count) for i in range(count)])

    upstream_line = [upstream] + [None] * (line - 1)
    upstream_line[1] = along_line(upstream, 1)
    upstream_line[-1] = along_line(upstream, -1)

    def spread_of(held):
        return pltpu.VMEM((9, held, PAD, LANES), F32)

    split_block = pl.BlockSpec((None, 9, KS, SUB, LANES), lambda c, *_: (c, 0, 0, 0, 0))
    partial, split, vectors = pl.pallas_call(
        functools.partial(own_conv_kernel, planes, height),
        grid=(tiles,),
        in_specs=[lane_block(rows), lane_block(TAP_ROWS)] + [whole_block(channels)] * 2,
        out_specs=[lane_block(rows), split_block, whole_block(SUB, channels)],
        out_shape=[
            jax.ShapeDtypeStruct((rows, channels), F32),
            jax.ShapeDtypeStruct((tiles, 9, KS, SUB, LANES), F32),
            jax.ShapeDtypeStruct((SUB, channels), F32),
        ],
        scratch_shapes=[spread_of(planes)],
        compiler_params=params(),
        cost_estimate=NO_COST,
        name="own_conv",
    )(own, dw_kernel, norm_gain, norm_bias)

    for k in range(2, line - 1):
        upstream_line[k] = along_line(upstream_line[k - 1], 1)
    normed, centered = pl.pallas_call(
        follow(functools.partial(rim_conv_kernel, planes, height), 1, 5, 2),
        grid_spec=pltpu.PrefetchScalarGridSpec(
            num_scalar_prefetch=1,
            grid=(tiles,),
            in_specs=[
                lane_block(rows),
                lane_block(rows),
                split_block,
                lane_block(rows),
                whole_block(SUB, channels),
                IN_PLACE,
                IN_PLACE,
            ],
            out_specs=[
                whole_block(rows, channels),
                whole_block(rows, channels),
            ],
            scratch_shapes=[spread_of(2 * MARGIN), pltpu.VMEM((tiles, rows, LANES), F32)],
        ),
        out_shape=[
            jax.ShapeDtypeStruct((rows, channels), BF16),
            jax.ShapeDtypeStruct((rows, channels), F32),
        ],
        compiler_params=params(),
        cost_estimate=NO_COST,
        name="rim_conv",
    )(
        parity,
        inner,
        outer,
        split,
        partial,
        vectors,
        upstream_line[1],
        upstream_line[-1],
    )

    normed, upstream_line[2] = lax.optimization_barrier((normed, upstream_line[2]))
    norm_line = [normed] + [None] * (line - 1)
    norm_line[1] = along_line(normed, 1)
    norm_line[-1] = along_line(normed, -1)

    block = 1024
    whole = whole_block(rows, channels)
    block_out, conv_grad, small, cotangents = pl.pallas_call(
        mlp_kernel,
        grid=(units // block,),
        in_specs=[
            whole,
            pl.BlockSpec((block, channels), lambda f: (f, 0)),
            pl.BlockSpec((block, channels), lambda f: (f, 0)),
            whole,
            whole_block(channels),
            whole_block(channels),
        ]
        + [whole] * (1 + line),
        out_specs=[
            whole,
            whole,
            whole_block(SUB, channels),
            whole_block(line, rows, channels),
        ],
        out_shape=[
            jax.ShapeDtypeStruct((rows, channels), BF16),
            jax.ShapeDtypeStruct((rows, channels), BF16),
            jax.ShapeDtypeStruct((SUB, channels), F32),
            jax.ShapeDtypeStruct((line, rows, channels), BF16),
        ],
        scratch_shapes=[
            pltpu.VMEM((rows, channels), F32),
            pltpu.VMEM((rows, channels), F32),
            pltpu.VMEM((rows, channels), BF16),
        ],
        compiler_params=params(),
        cost_estimate=NO_COST,
        name="mlp_both_ways",
    )(normed, weight_in, weight_out, centered, norm_gain, layer_scale, own, *upstream_line)

    small, norm_line[1], norm_line[-1] = lax.optimization_barrier(
        (small, norm_line[1], norm_line[-1])
    )
    for k in range(2, line - 1):
        norm_line[k] = along_line(norm_line[k - 1], 1)

    grad_inner, grad_outer = rims(conv_grad)

    half = count // 2
    alike = [[2 * k + p for k in range(half)] for p in range(2)]
    half_tiles = tiles // 2
    wide = half_tiles * LANES
    piece = -(-(TAP_ROWS + SUB) // half)
    piece += -piece % (2 * SUB)
    padded = piece * half

    def tile_of(block_rows):
        def at(c, w):
            return 0, (c + w[1] * half_tiles) % tiles

        return pl.BlockSpec((block_rows, LANES), at)

    half_sent, half_kept = pl.pallas_call(
        functools.partial(kernel_grad_kernel, planes, height),
        grid_spec=pltpu.PrefetchScalarGridSpec(
            num_scalar_prefetch=1,
            grid=(tiles,),
            in_specs=[tile_of(rows), tile_of(rows), tile_of(rows), tile_of(rows), tile_of(SUB)],
            out_specs=[
                pl.BlockSpec((padded, LANES), lambda c, w: (0, jnp.minimum(c, half_tiles - 1))),
                pl.BlockSpec((padded, LANES), lambda c, w: (0, jnp.maximum(c - half_tiles, 0))),
            ],
            scratch_shapes=[
                spread_of(2 * MARGIN + planes),
                pltpu.VMEM((2, KS, SUB * SUB, LANES), F32),
                pltpu.VMEM((9, KS, SUB, LANES), F32),
                pltpu.VMEM((padded, LANES), F32),
            ],
        ),
        out_shape=[jax.ShapeDtypeStruct((padded, wide), BF16)] * 2,
        compiler_params=params(),
        cost_estimate=NO_COST,
        name="kernel_grad_terms",
    )(jnp.stack([core, 1 - core]), inner, own, outer, conv_grad, small)

    half_sent, norm_line[2], grad_inner, grad_outer = lax.optimization_barrier(
        (half_sent, norm_line[2], grad_inner, grad_outer)
    )
    half_got = lax.ppermute(half_sent, "row", other_core)
    sums, gathered = pl.pallas_call(
        chip_sum_kernel,
        in_specs=[whole_block(padded, wide)] * 2 + [whole] * line,
        out_specs=[whole_block(padded, wide), whole_block(line, rows, channels)],
        out_shape=[
            jax.ShapeDtypeStruct((padded, wide), BF16),
            jax.ShapeDtypeStruct((line, rows, channels), BF16),
        ],
        grid=(1,),
        compiler_params=params(),
        cost_estimate=NO_COST,
        name="kernel_grad_chip_sum",
    )(half_kept, half_got, *norm_line)

    share = units // count
    tokens = line * rows
    base = me // quad * quad
    side = lax.rem(me, quad) // 2
    far = base + 2 * (1 - side)
    near = base + 2 * side
    which = jnp.stack([far + core, near + core]).astype(jnp.int32)
    other_gathered = lax.ppermute(gathered, "row", other_core)
    other_cotangents = lax.ppermute(cotangents, "row", other_core)

    def side_terms(kernel, number, more, after, outs, name):
        chunk = pl.BlockSpec((share, channels), lambda _, w: (w[number], 0))
        return pl.pallas_call(
            follow(kernel, 1, 7 + len(more), 1),
            grid_spec=pltpu.PrefetchScalarGridSpec(
                num_scalar_prefetch=1,
                grid=(1,),
                in_specs=[chunk, chunk, whole_block(channels)]
                + [pl.BlockSpec(memory_space=pltpu.VMEM)] * 4
                + [whole_block(*part.shape) for part in more]
                + [IN_PLACE],
                out_specs=[whole_block(*out.shape) for out in outs],
            ),
            out_shape=outs,
            compiler_params=params(),
            cost_estimate=NO_COST,
            name=name,
        )(
            which,
            weight_in,
            weight_out,
            layer_scale,
            gathered,
            cotangents,
            other_gathered,
            other_cotangents,
            *more,
            after,
        )

    pair = jax.ShapeDtypeStruct((2, share, channels), BF16)
    single = jax.ShapeDtypeStruct((share, channels), F32)
    (sent,) = side_terms(far_side_kernel, 0, [], sums, [pair], "weight_grads_far_side")
    got = lax.ppermute(sent, "row", other_side)
    scattered = lax.all_to_all(
        sums.reshape(half, piece, wide),
        "row",
        split_axis=0,
        concat_axis=0,
        tiled=True,
        axis_index_groups=alike,
    )
    voxel_grad, token = pl.pallas_call(
        follow(functools.partial(input_grad_kernel, planes, height), 1, 5, 1),
        grid_spec=pltpu.PrefetchScalarGridSpec(
            num_scalar_prefetch=1,
            grid=(tiles,),
            in_specs=[
                lane_block(rows),
                lane_block(rows),
                lane_block(rows),
                lane_block(TAP_ROWS),
                lane_block(rows),
                IN_PLACE,
            ],
            out_specs=[lane_block(rows), whole_block(SUB, LANES)],
            scratch_shapes=[
                spread_of(2 * MARGIN + planes),
                pltpu.VMEM((9, KS, SUB, LANES), F32),
            ],
        ),
        out_shape=[
            jax.ShapeDtypeStruct((rows, channels), BF16),
            jax.ShapeDtypeStruct((SUB, LANES), F32),
        ],
        compiler_params=params(),
        cost_estimate=NO_COST,
        name="input_grad_conv",
    )(parity, grad_inner, conv_grad, grad_outer, dw_kernel, upstream, sent)

    copies = pl.pallas_call(
        follow(spread_sum_kernel, 0, 1, 1),
        in_specs=[whole_block(half, piece, wide), IN_PLACE],
        out_specs=whole_block(half, piece, wide),
        out_shape=jax.ShapeDtypeStruct((half, piece, wide), BF16),
        grid=(1,),
        compiler_params=params(),
        cost_estimate=NO_COST,
        name="kernel_grad_sum",
    )(scattered, token)
    totals = lax.all_to_all(
        copies, "row", split_axis=0, concat_axis=0, tiled=True, axis_index_groups=alike
    )
    weight_in_grad, weight_out_grad = side_terms(
        near_side_kernel, 1, [got], copies, [single, single], "weight_grads_near_side"
    )
    totals, weight_in_grad = lax.optimization_barrier((totals, weight_in_grad))
    other_totals = lax.ppermute(totals, "row", other_core)
    kernel_grad, *vector_grads = pl.pallas_call(
        unpack_kernel,
        grid_spec=pltpu.PrefetchScalarGridSpec(
            num_scalar_prefetch=1,
            grid=(1,),
            in_specs=[whole_block(half, piece, wide)] * 2,
            out_specs=[whole_block(TAP_ROWS, channels)] + [whole_block(channels)] * 3,
        ),
        out_shape=[jax.ShapeDtypeStruct((TAP_ROWS, channels), F32)]
        + [jax.ShapeDtypeStruct((channels,), F32)] * 3,
        compiler_params=params(),
        cost_estimate=NO_COST,
        name="kernel_grad_unpack",
    )(parity, totals, other_totals)

    return (
        block_out.reshape(voxels.shape),
        voxel_grad.reshape(voxels.shape),
        kernel_grad,
        *vector_grads,
        weight_in_grad,
        weight_out_grad,
    )


def solution(mesh):
    in_specs = (
        P(("group", "row"), None, None, None),
        P(),
        P(),
        P(),
        P(),
        P(),
        P(),
        P(("group", "row"), None, None, None),
    )
    out_specs = (
        P(("group", "row"), None, None, None),
        P(("group", "row"), None, None, None),
        P("group", None),
        P("group"),
        P("group"),
        P("group"),
        P(("group", "row"), None),
        P(("group", "row"), None),
    )
    return jax.shard_map(
        on_device, mesh=mesh, in_specs=in_specs, out_specs=out_specs, check_vma=False
    )
```

```python
import functools

import jax
import jax.numpy as jnp
from jax import lax
from jax.experimental import pallas as pl
from jax.experimental.pallas import tpu as pltpu
from jax.sharding import PartitionSpec as P

KS = 7
MARGIN = KS // 2
LANES = 128
SUB = 8
PAD = 3 * SUB
TAP_ROWS = KS * KS * KS

root_half = 0.7071067811865476
inv_root_tau = 0.3989422804014327
norm_eps = 1e-06

NO_COST = pl.CostEstimate(flops=0, bytes_accessed=0, transcendentals=0)

F32 = jnp.float32
BF16 = jnp.bfloat16


def split_source(v):
    terms = []
    for a, b in ((v[0] + v[2], v[1] + v[3]), (v[2], v[3]), (v[0], v[1])):
        terms += [a + b, b, a]
    return terms


def split_taps(t):
    terms = []
    for s in (
        (t[2], t[3], t[4]),
        (t[4] - t[2], t[5] - t[3], t[6] - t[4]),
        (t[0] - t[2], t[1] - t[3], t[2] - t[4]),
    ):
        terms += [s[1], s[2] - s[1], s[0] - s[1]]
    return terms


def split_grads(g):
    terms = []
    for a, b in ((g[0] + g[2], g[1] + g[3]), (g[0], g[1]), (g[2], g[3])):
        terms += [a + b, a, b]
    return terms


def join_outputs(m):
    pair = [(m[3 * k] + m[3 * k + 1], m[3 * k] + m[3 * k + 2]) for k in range(3)]
    return [
        pair[0][0] + pair[1][0],
        pair[0][1] + pair[1][1],
        pair[0][0] + pair[2][0],
        pair[0][1] + pair[2][1],
    ]


def join_taps(m):
    p, q, r = [
        (m[3 * k + 2], m[3 * k] - m[3 * k + 1] - m[3 * k + 2], m[3 * k + 1]) for k in range(3)
    ]
    return [
        r[0],
        r[1],
        p[0] - q[0] - r[0] + r[2],
        p[1] - q[1] - r[1],
        p[2] - q[2] - r[2] + q[0],
        q[1],
        q[2],
    ]


def tree_sum(terms):
    while len(terms) > 1:
        terms = [
            terms[k] + terms[k + 1] if k + 1 < len(terms) else terms[k]
            for k in range(0, len(terms), 2)
        ]
    return terms[0]


def stage_source(wanted, height, spread):
    row = height * SUB
    for at, (block, x) in enumerate(wanted):
        plane = block[x * row : (x + 1) * row, :].astype(F32)
        lines = [plane[y * SUB : (y + 1) * SUB, :] for y in range(height)]
        for j, term in enumerate(split_source(lines)):
            spread[j, at, SUB : 2 * SUB, :] = term


def rim_planes(left, right, planes):
    wanted = [(left, x) for x in range(planes - MARGIN, planes)]
    return wanted + [(right, x) for x in range(MARGIN)]


def all_planes(left, own, right, planes):
    rim = rim_planes(left, right, planes)
    return rim[:MARGIN] + [(own, x) for x in range(planes)] + rim[MARGIN:]


def by_core(core, inner, outer, stage):
    @pl.when(core[0] == 0)
    def _():
        stage(outer, inner)

    @pl.when(core[0] != 0)
    def _():
        stage(inner, outer)


def clear_rims(spread):
    zeros = jnp.zeros(spread.shape[:2] + (SUB, LANES), F32)
    spread[:, :, :SUB, :] = zeros
    spread[:, :, 2 * SUB :, :] = zeros


def stage_taps(taps, split):
    for dx in range(KS):
        rows = []
        for dy in range(KS):
            first = dx * KS * KS + dy * KS
            if first + SUB <= TAP_ROWS:
                rows.append(taps[first : first + SUB, :])
            else:
                rows.append(pltpu.roll(taps[TAP_ROWS - SUB : TAP_ROWS, :], SUB - 1, 0))
        for j, term in enumerate(split_taps(rows)):
            split[j, dx] = term


REVERSED = (0, 2, 1, 6, 8, 7, 3, 5, 4)


def convolve(spread, split, planes, held, flipped):
    terms = []
    for j in range(9):
        sums = [None] * planes
        for dz in range(KS):
            first = SUB - MARGIN + dz
            source = {x: spread[j, at, first : first + SUB, :] for at, x in enumerate(held)}
            weights = []
            for dx in range(KS):
                if flipped:
                    tap = split[REVERSED[j], KS - 1 - dx, KS - 1 - dz : KS - dz, :]
                else:
                    tap = split[j, dx, dz : dz + 1, :]
                weights.append(jnp.broadcast_to(tap, (SUB, LANES)))
            for x in range(planes):
                part = tree_sum(
                    [source[x + dx] * weights[dx] for dx in range(KS) if x + dx in source]
                )
                sums[x] = part if sums[x] is None else sums[x] + part
        terms.append(sums)
    return [join_outputs([terms[j][x] for j in range(9)]) for x in range(planes)]


def own_conv_kernel(planes, height, own, taps, gain, bias, out, split, vectors, spread):
    @pl.when(pl.program_id(0) == 0)
    def _():
        for k, line in enumerate((gain, bias)):
            vectors[k : k + 1, :] = line[...].reshape(1, -1)
        clear_rims(spread)

    stage_source([(own, x) for x in range(planes)], height, spread)
    stage_taps(taps, split)
    rows = convolve(spread, split, planes, range(MARGIN, MARGIN + planes), False)
    for x in range(planes):
        for y in range(height):
            at = (x * height + y) * SUB
            out[at : at + SUB, :] = rows[x][y]


def rim_conv_kernel(
    planes, height, core, inner, outer, split, partial, vectors, normed, centered, spread, conv
):
    step = pl.program_id(0)

    @pl.when(step == 0)
    def _():
        clear_rims(spread)

    def stage(left, right):
        stage_source(rim_planes(left, right, planes), height, spread)

    by_core(core, inner, outer, stage)
    held = list(range(MARGIN)) + list(range(MARGIN + planes, 2 * MARGIN + planes))
    rows = convolve(spread, split, planes, held, False)
    for x in range(planes):
        for y in range(height):
            at = (x * height + y) * SUB
            conv[step, at : at + SUB, :] = rows[x][y] + partial[at : at + SUB, :]

    @pl.when(step == pl.num_programs(0) - 1)
    def _():
        tiles = conv.shape[0]
        channels = tiles * LANES
        parts = [conv[k] for k in range(tiles)]
        gains = vectors[0:1, :]
        biases = vectors[1:2, :]
        average = jnp.sum(tree_sum(parts), axis=1, keepdims=True) * (1.0 / channels)
        parts = [part - average for part in parts]
        variance = jnp.sum(
            tree_sum([part * part for part in parts]), axis=1, keepdims=True
        ) * (1.0 / channels)
        inverse = lax.rsqrt(variance + norm_eps)
        for k in range(tiles):
            lanes = slice(k * LANES, (k + 1) * LANES)
            centered[:, lanes] = parts[k]
            value = parts[k] * inverse
            whole = (value * gains[:, lanes] + biases[:, lanes]).astype(BF16)
            normed[:, lanes] = whole


def input_grad_kernel(
    planes, height, core, inner, own, outer, taps, cotangent, out, token, spread, split
):
    @pl.when(pl.program_id(0) == 0)
    def _():
        clear_rims(spread)

    def stage(left, right):
        stage_source(all_planes(left, own, right, planes), height, spread)

    by_core(core, inner, outer, stage)
    stage_taps(taps, split)
    token[...] = jnp.zeros(token.shape, F32)
    rows = convolve(spread, split, planes, range(2 * MARGIN + planes), True)
    for x in range(planes):
        at = x * height * SUB
        whole = jnp.concatenate(rows[x], axis=0)
        upstream = cotangent[at : at + height * SUB, :].astype(F32)
        out[at : at + height * SUB, :] = (upstream + whole).astype(BF16)


def kernel_grad_kernel(
    planes,
    height,
    which,
    inner,
    own,
    outer,
    grads,
    small,
    sent,
    kept,
    spread,
    products,
    joined,
    flat,
):
    @pl.when(pl.program_id(0) == 0)
    def _():
        clear_rims(spread)
        products[...] = jnp.zeros(products.shape, F32)
        flat[...] = jnp.zeros(flat.shape, F32)

    def stage(left, right):
        stage_source(all_planes(left, own, right, planes), height, spread)

    by_core(which, inner, outer, stage)
    upstream = []
    for x in range(planes):
        plane = grads[x * height * SUB : (x + 1) * height * SUB, :].astype(F32)
        upstream.append(
            split_grads([plane[y * SUB : (y + 1) * SUB, :] for y in range(height)])
        )
    for j in range(9):
        for dz in range(KS):
            first = SUB - MARGIN + dz
            source = [
                spread[j, x, first : first + SUB, :] for x in range(planes + KS - 1)
            ]
            for dx in range(KS):
                products[j % 2, dx, dz * SUB : (dz + 1) * SUB, :] = tree_sum(
                    [source[x + dx] * upstream[x][j] for x in range(planes)]
                )
        for dx in range(KS):
            joined[j, dx] = tree_sum(
                [products[j % 2, dx, pl.ds(s, SUB, stride=SUB), :] for s in range(SUB)]
            )
    for dx in range(KS):
        for dy, tile in enumerate(join_taps([joined[j, dx] for j in range(9)])):
            row = dx * KS * KS + dy * KS
            flat[row : row + SUB, :] = tile
    flat[TAP_ROWS : TAP_ROWS + SUB, :] = small[...]
    step = pl.program_id(0)
    half = pl.num_programs(0) // 2

    @pl.when(step < half)
    def _():
        sent[...] = flat[...].astype(BF16)

    @pl.when(step >= half)
    def _():
        kept[...] = flat[...].astype(BF16)


def mlp_kernel(
    normed, weight_in, weight_out, centered, norm_gain, layer_scale, voxels, *rest
):
    *cotangents, block_out, conv_grad, small, together, mixed, back, mixed_grad = rest
    cotangent = cotangents[0]
    step = pl.program_id(0)
    gain = norm_gain[...].reshape(1, -1)
    scale = layer_scale[...].reshape(1, -1)

    @pl.when(step == 0)
    def _():
        mixed_grad[...] = (scale * cotangent[...].astype(F32)).astype(BF16)
        for k, part in enumerate(cotangents):
            together[k] = part[...]

    across = (((1,), (1,)), ((), ()))
    hidden = lax.dot_general(normed[...], weight_in[...], across, preferred_element_type=F32)
    act_grad = lax.dot_general(
        mixed_grad[...], weight_out[...], across, preferred_element_type=F32
    )
    activated, hidden_grad = slopes(hidden, act_grad)
    forward = jnp.dot(activated, weight_out[...], preferred_element_type=F32)
    backward = jnp.dot(hidden_grad, weight_in[...], preferred_element_type=F32)

    @pl.when(step == 0)
    def _():
        mixed[...] = forward
        back[...] = backward

    @pl.when(step > 0)
    def _():
        mixed[...] += forward
        back[...] += backward

    @pl.when(step == pl.num_programs(0) - 1)
    def _():
        channels = gain.shape[1]
        whole = mixed[...]
        block_out[...] = (voxels[...].astype(F32) + scale * whole).astype(BF16)
        scale_local = jnp.sum(cotangent[...].astype(F32) * whole, axis=0, keepdims=True)
        grad = back[...]
        deviation = centered[...]
        variance = jnp.sum(deviation * deviation, axis=1, keepdims=True) * (1.0 / channels)
        inverse = lax.rsqrt(variance + norm_eps)
        one = deviation * inverse
        bias_local = jnp.sum(grad, axis=0, keepdims=True)
        gain_local = jnp.sum(grad * one, axis=0, keepdims=True)
        small[...] = jnp.concatenate(
            [gain_local, bias_local, scale_local, jnp.zeros((SUB - 3, channels), F32)], axis=0
        )
        scaled = grad * gain
        average = jnp.sum(scaled, axis=1, keepdims=True) * (1.0 / channels)
        slant = jnp.sum(scaled * one, axis=1, keepdims=True) * (1.0 / channels)
        conv_grad[...] = (inverse * (scaled - average - one * slant)).astype(BF16)


def slopes(hidden, act_grad):
    cover = 0.5 * (1.0 + lax.erf(hidden * root_half))
    activated = (hidden * cover).astype(BF16)
    slope = cover + hidden * jnp.exp(-0.5 * hidden * hidden) * inv_root_tau
    return activated, (act_grad * slope).astype(BF16)


def weight_grad_terms(weight_in, weight_out, scale, sets):
    scales = scale[...].reshape(1, -1)
    across = (((1,), (1,)), ((), ()))
    in_terms, out_terms = [], []
    for norm, cot in sets:
        channels = norm.shape[2]
        normed = norm[...].reshape(-1, channels)
        upstream = cot[...].reshape(-1, channels).astype(F32)
        mixed_grad = (scales * upstream).astype(BF16)
        hidden = lax.dot_general(weight_in[...], normed, across, preferred_element_type=F32)
        act_grad = lax.dot_general(weight_out[...], mixed_grad, across, preferred_element_type=F32)
        activated, hidden_grad = slopes(hidden, act_grad)
        in_terms.append(jnp.dot(hidden_grad, normed, preferred_element_type=F32))
        out_terms.append(jnp.dot(activated, mixed_grad, preferred_element_type=F32))
    return tree_sum(in_terms), tree_sum(out_terms)


def far_side_kernel(which, weight_in, weight_out, scale, norm, cot, other_norm, other_cot, sent):
    del which
    sets = ((norm, cot), (other_norm, other_cot))
    terms = weight_grad_terms(weight_in, weight_out, scale, sets)
    for k in range(2):
        sent[k] = terms[k].astype(BF16)


def near_side_kernel(
    which, weight_in, weight_out, scale, norm, cot, other_norm, other_cot, got, in_grad, out_grad
):
    del which
    sets = ((norm, cot), (other_norm, other_cot))
    terms = weight_grad_terms(weight_in, weight_out, scale, sets)
    for k, out in enumerate((in_grad, out_grad)):
        out[...] = terms[k] + got[k].astype(F32)


def chip_sum_kernel(kept, got, *rest):
    *blocks, out, together = rest
    for k, block in enumerate(blocks):
        together[k] = block[...]
    out[...] = (kept[...].astype(F32) + got[...].astype(F32)).astype(BF16)


def spread_sum_kernel(parts, out):
    total = tree_sum([parts[k].astype(F32) for k in range(parts.shape[0])]).astype(BF16)
    for copy in range(out.shape[0]):
        out[copy] = total


def unpack_kernel(core, own, other, out, *small):
    piece, wide = own.shape[1:]

    def unpack(*halves):
        last = []
        for side, parts in enumerate(halves):
            lanes = slice(side * wide, (side + 1) * wide)
            for k in range(-(-TAP_ROWS // piece)):
                first = k * piece
                length = min(piece, TAP_ROWS - first)
                out[first : first + length, lanes] = parts[k].astype(F32)[:length, :]
            k = TAP_ROWS // piece
            last.append(parts[k].astype(F32))
        rows = jnp.concatenate(last, axis=1)
        first = TAP_ROWS % piece
        for k, line in enumerate(small):
            line[...] = rows[first + k : first + k + 1, :].reshape(line.shape)

    by_core(core, own, other, lambda outer, inner: unpack(inner, outer))


def params(limit=48):
    return pltpu.CompilerParams(vmem_limit_bytes=limit * 1024 * 1024)


def follow(kernel, scalars, inputs, count):
    def body(*refs):
        head = refs[: scalars + inputs]
        return kernel(*head, *refs[scalars + inputs + count :])

    return body


IN_PLACE = pl.BlockSpec(memory_space=pl.ANY)


def lane_block(rows):
    return pl.BlockSpec((rows, LANES), lambda c, *_: (0, c))


def whole_block(*shape):
    return pl.BlockSpec(shape, lambda *_: (0,) * len(shape))


def rims(cells):
    count = lax.axis_size("row")
    between = [(i, i + 1) for i in range(1, count - 1, 2)]
    return (
        lax.ppermute(cells, "row", [(i, i ^ 1) for i in range(count)]),
        lax.ppermute(cells, "row", between + [(j, i) for i, j in between]),
    )


def on_device(
    voxels, dw_kernel, norm_gain, norm_bias, weight_in, weight_out, layer_scale, cotangent
):
    planes, height, breadth, channels = voxels.shape
    rows = planes * height * breadth
    units = weight_in.shape[0]
    count = lax.axis_size("row")
    me = lax.axis_index("row")
    quad = 4
    line = count // quad
    other_core = [(i, i ^ 1) for i in range(count)]
    other_side = [(i, i ^ 2) for i in range(count)]
    tiles = channels // LANES

    own = voxels.reshape(rows, channels)
    upstream = cotangent.reshape(rows, channels)
    core = lax.rem(me, 2).astype(jnp.int32)
    parity = core.reshape(1)

    inner, outer = rims(own)

    def along_line(cells, steps):
        return lax.ppermute(cells, "row", [(i, (i + quad * steps) % count) for i in range(count)])

    upstream_line = [upstream] + [None] * (line - 1)
    upstream_line[1] = along_line(upstream, 1)
    upstream_line[-1] = along_line(upstream, -1)

    def spread_of(held):
        return pltpu.VMEM((9, held, PAD, LANES), F32)

    split_block = pl.BlockSpec((None, 9, KS, SUB, LANES), lambda c, *_: (c, 0, 0, 0, 0))
    partial, split, vectors = pl.pallas_call(
        functools.partial(own_conv_kernel, planes, height),
        grid=(tiles,),
        in_specs=[lane_block(rows), lane_block(TAP_ROWS)] + [whole_block(channels)] * 2,
        out_specs=[lane_block(rows), split_block, whole_block(SUB, channels)],
        out_shape=[
            jax.ShapeDtypeStruct((rows, channels), F32),
            jax.ShapeDtypeStruct((tiles, 9, KS, SUB, LANES), F32),
            jax.ShapeDtypeStruct((SUB, channels), F32),
        ],
        scratch_shapes=[spread_of(planes)],
        compiler_params=params(),
        cost_estimate=NO_COST,
        name="own_conv",
    )(own, dw_kernel, norm_gain, norm_bias)

    for k in range(2, line - 1):
        upstream_line[k] = along_line(upstream_line[k - 1], 1)
    normed, centered = pl.pallas_call(
        follow(functools.partial(rim_conv_kernel, planes, height), 1, 5, 2),
        grid_spec=pltpu.PrefetchScalarGridSpec(
            num_scalar_prefetch=1,
            grid=(tiles,),
            in_specs=[
                lane_block(rows),
                lane_block(rows),
                split_block,
                lane_block(rows),
                whole_block(SUB, channels),
                IN_PLACE,
                IN_PLACE,
            ],
            out_specs=[
                whole_block(rows, channels),
                whole_block(rows, channels),
            ],
            scratch_shapes=[spread_of(2 * MARGIN), pltpu.VMEM((tiles, rows, LANES), F32)],
        ),
        out_shape=[
            jax.ShapeDtypeStruct((rows, channels), BF16),
            jax.ShapeDtypeStruct((rows, channels), F32),
        ],
        compiler_params=params(),
        cost_estimate=NO_COST,
        name="rim_conv",
    )(
        parity,
        inner,
        outer,
        split,
        partial,
        vectors,
        upstream_line[1],
        upstream_line[-1],
    )

    normed, upstream_line[2] = lax.optimization_barrier((normed, upstream_line[2]))
    norm_line = [normed] + [None] * (line - 1)
    norm_line[1] = along_line(normed, 1)
    norm_line[-1] = along_line(normed, -1)

    block = 1024
    whole = whole_block(rows, channels)
    block_out, conv_grad, small, cotangents = pl.pallas_call(
        mlp_kernel,
        grid=(units // block,),
        in_specs=[
            whole,
            pl.BlockSpec((block, channels), lambda f: (f, 0)),
            pl.BlockSpec((block, channels), lambda f: (f, 0)),
            whole,
            whole_block(channels),
            whole_block(channels),
        ]
        + [whole] * (1 + line),
        out_specs=[
            whole,
            whole,
            whole_block(SUB, channels),
            whole_block(line, rows, channels),
        ],
        out_shape=[
            jax.ShapeDtypeStruct((rows, channels), BF16),
            jax.ShapeDtypeStruct((rows, channels), BF16),
            jax.ShapeDtypeStruct((SUB, channels), F32),
            jax.ShapeDtypeStruct((line, rows, channels), BF16),
        ],
        scratch_shapes=[
            pltpu.VMEM((rows, channels), F32),
            pltpu.VMEM((rows, channels), F32),
            pltpu.VMEM((rows, channels), BF16),
        ],
        compiler_params=params(),
        cost_estimate=NO_COST,
        name="mlp_both_ways",
    )(normed, weight_in, weight_out, centered, norm_gain, layer_scale, own, *upstream_line)

    small, norm_line[1], norm_line[-1] = lax.optimization_barrier(
        (small, norm_line[1], norm_line[-1])
    )
    for k in range(2, line - 1):
        norm_line[k] = along_line(norm_line[k - 1], 1)

    grad_inner, grad_outer = rims(conv_grad)

    half = count // 2
    alike = [[2 * k + p for k in range(half)] for p in range(2)]
    half_tiles = tiles // 2
    wide = half_tiles * LANES
    piece = -(-(TAP_ROWS + SUB) // half)
    piece += -piece % (2 * SUB)
    padded = piece * half

    def tile_of(block_rows):
        def at(c, w):
            return 0, (c + w[1] * half_tiles) % tiles

        return pl.BlockSpec((block_rows, LANES), at)

    half_sent, half_kept = pl.pallas_call(
        functools.partial(kernel_grad_kernel, planes, height),
        grid_spec=pltpu.PrefetchScalarGridSpec(
            num_scalar_prefetch=1,
            grid=(tiles,),
            in_specs=[tile_of(rows), tile_of(rows), tile_of(rows), tile_of(rows), tile_of(SUB)],
            out_specs=[
                pl.BlockSpec((padded, LANES), lambda c, w: (0, jnp.minimum(c, half_tiles - 1))),
                pl.BlockSpec((padded, LANES), lambda c, w: (0, jnp.maximum(c - half_tiles, 0))),
            ],
            scratch_shapes=[
                spread_of(2 * MARGIN + planes),
                pltpu.VMEM((2, KS, SUB * SUB, LANES), F32),
                pltpu.VMEM((9, KS, SUB, LANES), F32),
                pltpu.VMEM((padded, LANES), F32),
            ],
        ),
        out_shape=[jax.ShapeDtypeStruct((padded, wide), BF16)] * 2,
        compiler_params=params(),
        cost_estimate=NO_COST,
        name="kernel_grad_terms",
    )(jnp.stack([core, 1 - core]), inner, own, outer, conv_grad, small)

    corners = [part[: 2 * SUB, :LANES] for part in (grad_inner, grad_outer)]
    half_sent, norm_line[2], *corners = lax.optimization_barrier(
        (half_sent, norm_line[2], *corners)
    )
    half_got = lax.ppermute(half_sent, "row", other_core)
    sums, gathered = pl.pallas_call(
        follow(chip_sum_kernel, 0, 2 + line, 2),
        in_specs=[whole_block(padded, wide)] * 2 + [whole] * line + [IN_PLACE] * 2,
        out_specs=[whole_block(padded, wide), whole_block(line, rows, channels)],
        out_shape=[
            jax.ShapeDtypeStruct((padded, wide), BF16),
            jax.ShapeDtypeStruct((line, rows, channels), BF16),
        ],
        grid=(1,),
        compiler_params=params(),
        cost_estimate=NO_COST,
        name="kernel_grad_chip_sum",
    )(half_kept, half_got, *norm_line, *corners)

    share = units // count
    tokens = line * rows
    base = me // quad * quad
    side = lax.rem(me, quad) // 2
    far = base + 2 * (1 - side)
    near = base + 2 * side
    which = jnp.stack([far + core, near + core]).astype(jnp.int32)
    other_gathered = lax.ppermute(gathered, "row", other_core)
    other_cotangents = lax.ppermute(cotangents, "row", other_core)

    def side_terms(kernel, number, more, after, outs, name):
        chunk = pl.BlockSpec((share, channels), lambda _, w: (w[number], 0))
        return pl.pallas_call(
            follow(kernel, 1, 7 + len(more), 1),
            grid_spec=pltpu.PrefetchScalarGridSpec(
                num_scalar_prefetch=1,
                grid=(1,),
                in_specs=[chunk, chunk, whole_block(channels)]
                + [pl.BlockSpec(memory_space=pltpu.VMEM)] * 4
                + [whole_block(*part.shape) for part in more]
                + [IN_PLACE],
                out_specs=[whole_block(*out.shape) for out in outs],
            ),
            out_shape=outs,
            compiler_params=params(),
            cost_estimate=NO_COST,
            name=name,
        )(
            which,
            weight_in,
            weight_out,
            layer_scale,
            gathered,
            cotangents,
            other_gathered,
            other_cotangents,
            *more,
            after,
        )

    pair = jax.ShapeDtypeStruct((2, share, channels), BF16)
    single = jax.ShapeDtypeStruct((share, channels), F32)
    (sent,) = side_terms(far_side_kernel, 0, [], sums, [pair], "weight_grads_far_side")
    got = lax.ppermute(sent, "row", other_side)
    scattered = lax.all_to_all(
        sums.reshape(half, piece, wide),
        "row",
        split_axis=0,
        concat_axis=0,
        tiled=True,
        axis_index_groups=alike,
    )
    voxel_grad, token = pl.pallas_call(
        follow(functools.partial(input_grad_kernel, planes, height), 1, 5, 1),
        grid_spec=pltpu.PrefetchScalarGridSpec(
            num_scalar_prefetch=1,
            grid=(tiles,),
            in_specs=[
                lane_block(rows),
                lane_block(rows),
                lane_block(rows),
                lane_block(TAP_ROWS),
                lane_block(rows),
                IN_PLACE,
            ],
            out_specs=[lane_block(rows), whole_block(SUB, LANES)],
            scratch_shapes=[
                spread_of(2 * MARGIN + planes),
                pltpu.VMEM((9, KS, SUB, LANES), F32),
            ],
        ),
        out_shape=[
            jax.ShapeDtypeStruct((rows, channels), BF16),
            jax.ShapeDtypeStruct((SUB, LANES), F32),
        ],
        compiler_params=params(),
        cost_estimate=NO_COST,
        name="input_grad_conv",
    )(parity, grad_inner, conv_grad, grad_outer, dw_kernel, upstream, sent)

    copies = pl.pallas_call(
        follow(spread_sum_kernel, 0, 1, 1),
        in_specs=[whole_block(half, piece, wide), IN_PLACE],
        out_specs=whole_block(half, piece, wide),
        out_shape=jax.ShapeDtypeStruct((half, piece, wide), BF16),
        grid=(1,),
        compiler_params=params(),
        cost_estimate=NO_COST,
        name="kernel_grad_sum",
    )(scattered, token)
    totals = lax.all_to_all(
        copies, "row", split_axis=0, concat_axis=0, tiled=True, axis_index_groups=alike
    )
    weight_in_grad, weight_out_grad = side_terms(
        near_side_kernel, 1, [got], copies, [single, single], "weight_grads_near_side"
    )
    totals, weight_in_grad = lax.optimization_barrier((totals, weight_in_grad))
    other_totals = lax.ppermute(totals, "row", other_core)
    kernel_grad, *vector_grads = pl.pallas_call(
        unpack_kernel,
        grid_spec=pltpu.PrefetchScalarGridSpec(
            num_scalar_prefetch=1,
            grid=(1,),
            in_specs=[whole_block(half, piece, wide)] * 2,
            out_specs=[whole_block(TAP_ROWS, channels)] + [whole_block(channels)] * 3,
        ),
        out_shape=[jax.ShapeDtypeStruct((TAP_ROWS, channels), F32)]
        + [jax.ShapeDtypeStruct((channels,), F32)] * 3,
        compiler_params=params(),
        cost_estimate=NO_COST,
        name="kernel_grad_unpack",
    )(parity, totals, other_totals)

    return (
        block_out.reshape(voxels.shape),
        voxel_grad.reshape(voxels.shape),
        kernel_grad,
        *vector_grads,
        weight_in_grad,
        weight_out_grad,
    )


def solution(mesh):
    in_specs = (
        P(("group", "row"), None, None, None),
        P(),
        P(),
        P(),
        P(),
        P(),
        P(),
        P(("group", "row"), None, None, None),
    )
    out_specs = (
        P(("group", "row"), None, None, None),
        P(("group", "row"), None, None, None),
        P("group", None),
        P("group"),
        P("group"),
        P("group"),
        P(("group", "row"), None),
        P(("group", "row"), None),
    )
    return jax.shard_map(
        on_device, mesh=mesh, in_specs=in_specs, out_specs=out_specs, check_vma=False
    )
```
